32 devices in a mesh: leaf: 8 (over z, x), sub: 4 (over y, core).
Axes of the slice: x: 2, y: 2, z: 4, core: 2. Of those that a mesh axis runs over, the one named last changes fastest.
Arguments:
- points: bfloat16 [131072, 64], P(('leaf', 'sub')), may hold values from -6 to 6
- probes: bfloat16 [131072, 128], P(('leaf', 'sub')), may hold values from -6 to 6
- order: int32 [131072], P(('leaf', 'sub')), may hold values from 0 to 511, as said below
- near_lists: int32 [256, 12], P(('leaf', 'sub')), may hold values from 0 to 255, as said below
- near_counts: int32 [256], P(('leaf', 'sub')), may hold values from 1 to 12, as said below
- leaf_sets: int32 [256, 128], P(('leaf', 'sub')), may hold values from 0 to 511, as said below
- merge_sets: int32 [255, 128], replicated, may hold values from 0 to 255, as said below
Outputs:
- near_samples: float32 [131072, 128], P(('leaf', 'sub'))
- root_samples: float32 [16384], P(('leaf', 'sub'))
The draws below stay inside these ranges and needn't reach their ends.
Inputs may be any that keep to these rules, and one draw needn't show every extreme that they name: `order`: the 512 entries of each leaf block are a permutation of 0 to 511. `near_lists`: for block g of shard i = g // 32: entry 0 is g; entries 1 to near_counts[g] - 1 are distinct blocks other than g within i * 32 - 8 to (i + 1) * 32 + 7; entries from near_counts[g] on equal g. `near_counts`: some block among the first sixteen of the aligned sixteens of blocks has 12 entries. `leaf_sets`: each row holds distinct values. `merge_sets`: each row holds distinct values; row m - 1 belongs to the node whose two children meet at block m.
All inputs are finite; a program needn't handle non-finite values.
Results may differ from the reference program's by a relative error of at most 0.0029.
Values may be sent and summed in bfloat16 or wider, within the bound.
No kernel may reach another device: no remote copies, remote signals or barrier semaphores. Data moves between devices by JAX's collectives and lax.ppermute only.
A program may use at most 128 MiB of HBM per device.

```python
import jax
import jax.numpy as jnp
from jax import lax

DIM = 64
LEAF = 512
SKEL = 128
PROBES = 128
NEAR = 12
BLK_DEV = 8
SHARD_BLOCKS = 32
NBLOCKS = 256
NPTS = 131072


def near_table(key):
    base_key = jax.random.fold_in(key, 71)
    window = SHARD_BLOCKS + 2 * BLK_DEV
    offsets = jnp.arange(window, dtype=jnp.int32)
    slot_ids = jnp.arange(NEAR, dtype=jnp.int32)

    def one_block(block_id):
        block_key = jax.random.fold_in(base_key, block_id)
        shard_id = block_id // SHARD_BLOCKS
        candidate = shard_id * SHARD_BLOCKS - BLK_DEV + offsets
        usable = (candidate >= 0) & (candidate < NBLOCKS) & (candidate != block_id)
        scores = jax.random.permutation(jax.random.fold_in(block_key, 1), window).astype(jnp.int32)
        scores = scores + jnp.where(usable, 0, window)
        ranked = jnp.take(candidate, jnp.argsort(scores), axis=0)[:NEAR - 1]
        first_draw = jax.random.randint(jax.random.fold_in(block_key, 2), (), 1, NEAR + 1)
        second = jax.random.randint(jax.random.fold_in(block_key, 3), (), 1, NEAR + 1)
        live_count = jnp.where(block_id % 16 == 5, NEAR, jnp.minimum(first_draw, second)).astype(jnp.int32)
        listed = jnp.concatenate([block_id[None], ranked])
        listed = jnp.where(slot_ids < live_count, listed, block_id)
        return (listed.astype(jnp.int32), live_count)
    return jax.vmap(one_block)(jnp.arange(NBLOCKS, dtype=jnp.int32))


def draw_near_lists(key, part):
    return near_table(key)[0]


def draw_near_counts(key, part):
    return near_table(key)[1]


def draw_order(key, part):
    base_key = jax.random.fold_in(key, 13)

    def one_block(block_id):
        return jax.random.permutation(jax.random.fold_in(base_key, block_id), LEAF).astype(jnp.int32)
    return jax.vmap(one_block)(jnp.arange(NBLOCKS, dtype=jnp.int32)).reshape(NPTS)


def draw_leaf_sets(key, part):
    base_key = jax.random.fold_in(key, 29)

    def one_block(block_id):
        return jax.random.permutation(jax.random.fold_in(base_key, block_id), LEAF).astype(jnp.int32)[:SKEL]
    return jax.vmap(one_block)(jnp.arange(NBLOCKS, dtype=jnp.int32))


def draw_merge_sets(key, part):
    base_key = jax.random.fold_in(key, 43)

    def one_node(node_id):
        return jax.random.permutation(jax.random.fold_in(base_key, node_id), 2 * SKEL).astype(jnp.int32)[:SKEL]
    return jax.vmap(one_node)(jnp.arange(NBLOCKS - 1, dtype=jnp.int32))


def levels(key, shape, split, least, largest):
    def one(position, blocks):
        draws = jax.random.uniform(jax.random.fold_in(jax.random.fold_in(key, 6), position), (blocks,), jnp.float32, least / len(split), largest / len(split))
        return jnp.repeat(jnp.exp(draws), shape[position] // blocks).reshape((-1,) + (1,) * (len(shape) - position - 1))

    factor_of = one(*split[0])
    for cut in split[1:]:
        factor_of = factor_of * one(*cut)
    return factor_of


def centred(own_key, dims, width, reach, split=(), held_as=jnp.bfloat16):
    gain = levels(own_key, dims, split, -0.22, 0.18) if split else 1.0
    drawn = jax.random.normal(own_key, dims, jnp.float32) * width * gain
    return jnp.minimum(jnp.maximum(drawn, -reach), reach).astype(held_as)


def setup_inputs(seed: int = 0) -> dict:
    key_of = jax.random.split(jax.random.key(seed), 8)
    points = centred(key_of[0], (NPTS, DIM), 1.0, 6.0, ((0, 32),))
    probes = centred(key_of[1], (NPTS, PROBES), 1.0, 6.0, ((0, 32),))
    order = draw_order(jax.random.fold_in(key_of[7], 71), 0)
    near_lists = draw_near_lists(jax.random.fold_in(key_of[7], 71), 0)
    near_counts = draw_near_counts(jax.random.fold_in(key_of[7], 71), 0)
    leaf_sets = draw_leaf_sets(jax.random.fold_in(key_of[7], 71), 0)
    merge_sets = draw_merge_sets(jax.random.fold_in(key_of[7], 71), 0)
    return {"points": points, "probes": probes, "order": order, "near_lists": near_lists, "near_counts": near_counts, "leaf_sets": leaf_sets, "merge_sets": merge_sets}


def row_squares(values):
    return jnp.sum(jnp.square(values.astype(jnp.float32)), axis=-1)


def kernel_tile(target_rows, target_sq, source_rows, source_sq):
    cross_terms = jnp.dot(target_rows, source_rows.T, preferred_element_type=jnp.float32)
    distance = target_sq[:, None] + source_sq[None, :] - 2.0 * cross_terms
    return jnp.exp(-distance / target_rows.shape[1])


def condense(coords, samples, chosen):
    picked = jnp.take(coords, chosen, axis=0)
    weights = kernel_tile(picked, row_squares(picked), coords, row_squares(coords))
    totals = jnp.sum(weights, axis=1, keepdims=True)
    mixed_part = jnp.dot(weights, samples, precision=lax.Precision.HIGHEST, preferred_element_type=jnp.float32)
    return picked, jnp.take(samples, chosen, axis=0) + mixed_part / totals


def reference(points, probes, order, near_lists, near_counts, leaf_sets, merge_sets):
    block_base = (jnp.arange(NPTS).astype(jnp.int32) // LEAF) * LEAF
    tree_points = jnp.take(points, order.astype(jnp.int32) + block_base, axis=0)
    blocks = tree_points.reshape(NBLOCKS, LEAF, DIM)
    probe_blocks = probes.reshape(NBLOCKS, LEAF, PROBES)
    squares = row_squares(blocks)

    def near_block(block_id):
        def add_slot(slot_index, running):
            source = near_lists[block_id, slot_index]
            weights = kernel_tile(blocks[block_id], squares[block_id], blocks[source], squares[source])
            weights = weights.astype(jnp.bfloat16)
            return running + jnp.dot(weights, probe_blocks[source], preferred_element_type=jnp.float32)

        running = lax.fori_loop(0, near_counts[block_id], add_slot, jnp.zeros((LEAF, PROBES), jnp.float32))
        return running * (LEAF ** -0.5)

    near_samples = lax.map(near_block, jnp.arange(NBLOCKS).astype(jnp.int32)).reshape(NPTS, PROBES)

    coords, samples = jax.vmap(condense)(blocks, probe_blocks.astype(jnp.float32), leaf_sets)
    node_span = 1
    while coords.shape[0] > 1:
        node_count = coords.shape[0] // 2
        node_first = jnp.arange(node_count).astype(jnp.int32) * (2 * node_span)
        chosen = jnp.take(merge_sets, node_first + node_span - 1, axis=0)
        coords, samples = jax.vmap(condense)(
            coords.reshape(node_count, 2 * SKEL, DIM),
            samples.reshape(node_count, 2 * SKEL, PROBES),
            chosen)
        node_span = node_span * 2
    return near_samples, samples[0].reshape(SKEL * PROBES)
```

```python
import functools

import jax
import jax.numpy as jnp
from jax import lax
from jax.experimental import pallas as pl
from jax.experimental.pallas import tpu as pltpu
from jax.sharding import PartitionSpec as P

LANES = 128
PARTS = 3
VMEM_BYTES = 56 * 1024 * 1024
F32 = jnp.float32
BF16 = jnp.bfloat16


def dot(a, b):
    return jnp.dot(a, b, preferred_element_type=F32)


def dot_t(a, b):
    return lax.dot_general(a, b, (((0,), (0,)), ((), ())), preferred_element_type=F32)


def split(x):
    hi = x.astype(BF16)
    return hi, (x - hi.astype(F32)).astype(BF16)


def square_rows(pts):
    x = pts.astype(F32)
    total = jnp.sum(x * x, axis=0, keepdims=True)
    hi = total.astype(BF16).astype(F32)
    mid = (total - hi).astype(BF16).astype(F32)
    low = total - hi - mid
    row = lax.broadcasted_iota(jnp.int32, (16, pts.shape[1]), 0)
    ones = jnp.where(row < 2 * PARTS, 1.0, 0.0)
    return jnp.where(row == 0, hi, jnp.where(row == 1, mid, jnp.where(row == 2, low, ones))).astype(BF16)


def form_map(dim, size):
    k = lax.broadcasted_iota(jnp.int32, (size, size), 0)
    j = lax.broadcasted_iota(jnp.int32, (size, size), 1)
    r = jnp.where((k == j) & (j < dim), 2.0 / dim, 0.0)
    r = jnp.where((j >= dim) & (j < dim + PARTS) & (k == j + PARTS), -1.0 / dim, r)
    r = jnp.where((j >= dim + PARTS) & (j < dim + 2 * PARTS) & (k == j - PARTS), -1.0 / dim, r)
    return r.astype(BF16)


def onehot_in(row, size):
    index = lax.broadcasted_iota(jnp.int32, (size, row.shape[1]), 0)
    return jnp.where(index == row, 1.0, 0.0).astype(BF16)


def column_of(row):
    return jnp.broadcast_to(row.astype(F32), (LANES, row.shape[1])).T


def onehot_out(column, size):
    lane = lax.broadcasted_iota(jnp.int32, column.shape, 1).astype(F32)
    return jnp.concatenate(
        [jnp.where(column == lane + float(i), 1.0, 0.0) for i in range(0, size, LANES)], axis=1
    )


def mix3(m, s):
    m_hi, m_lo = split(m)
    s_hi, s_lo = split(s)
    return dot(m_hi, s_hi) + (dot(m_hi, s_lo) + dot(m_lo, s_hi))


def order_kernel(points_t, order, probes, pack, rows):
    dim, leaf = points_t.shape
    picks = onehot_in(order[0], leaf)
    tree_t = dot(points_t[...], picks).astype(BF16)
    pack[0, :leaf, :] = probes[...]
    for i in range(leaf // LANES):
        pack[0, leaf + i * dim : leaf + (i + 1) * dim, :] = tree_t[:, i * LANES : (i + 1) * LANES]
    form = jnp.concatenate(
        [tree_t, square_rows(tree_t), jnp.zeros((LANES - dim - 16, leaf), BF16)], axis=0
    )
    rows[0] = dot_t(form, form_map(dim, LANES)).astype(BF16)


def order_call(points_t, order, probes, blocks):
    dim, npts = points_t.shape
    leaf = npts // blocks
    packed = leaf + leaf // LANES * dim
    return pl.pallas_call(
        order_kernel,
        grid=(blocks,),
        in_specs=[
            pl.BlockSpec((dim, leaf), lambda b: (0, b)),
            pl.BlockSpec((1, 1, leaf), lambda b: (b, 0, 0)),
            pl.BlockSpec((leaf, LANES), lambda b: (b, 0)),
        ],
        out_specs=[
            pl.BlockSpec((1, packed, LANES), lambda b: (b, 0, 0)),
            pl.BlockSpec((1, leaf, LANES), lambda b: (b, 0, 0)),
        ],
        out_shape=[
            jax.ShapeDtypeStruct((blocks, packed, LANES), BF16),
            jax.ShapeDtypeStruct((blocks, leaf, LANES), BF16),
        ],
        compiler_params=pltpu.CompilerParams(vmem_limit_bytes=VMEM_BYTES),
        cost_estimate=pl.CostEstimate(
            flops=blocks * 2 * leaf * leaf * dim, bytes_accessed=10 * npts * LANES, transcendentals=0
        ),
        name="tree_order",
    )(points_t, order, probes)


def build_form(pack_block, leaf, dim):
    columns = []
    for i in range(leaf // LANES):
        pts = pack_block[leaf + i * dim : leaf + (i + 1) * dim, :]
        columns.append(
            jnp.concatenate(
                [pts, square_rows(pts), jnp.zeros((LANES - dim - 16, LANES), BF16)], axis=0
            )
        )
    return jnp.concatenate(columns, axis=1)


def local_tree_kernel(pack, rows, leaf_sets, merge_sets, coords_out, samples_out, *, dim):
    blocks, leaf = rows.shape[:2]
    first_block = (lax.axis_index("leaf") * lax.axis_size("sub") + lax.axis_index("sub")) * blocks

    def step(form, a_rows, chosen):
        size = form.shape[1]
        picks_out = onehot_out(column_of(chosen), size)
        new_rows = dot(picks_out.astype(BF16), a_rows).astype(BF16)
        new_form = dot(form, onehot_in(chosen, size)).astype(BF16)
        weights = jnp.exp(dot(new_rows, form))
        mixing = picks_out + weights / jnp.sum(weights, axis=1, keepdims=True)
        return new_form, new_rows, mixing

    nodes = []
    for b in range(blocks):
        form = build_form(pack.at[b], leaf, dim)
        new_form, new_rows, mixing = step(form, rows[b], leaf_sets[b : b + 1, :])
        m_hi, m_lo = split(mixing)
        probes = pack[b, :leaf, :]
        nodes.append((new_form, new_rows, dot(m_hi, probes) + dot(m_lo, probes)))
    span = 1
    while len(nodes) > 1:
        merged = []
        for k in range(len(nodes) // 2):
            left, right = nodes[2 * k], nodes[2 * k + 1]
            chosen = merge_sets[pl.ds(first_block + (2 * k + 1) * span - 1, 1), :]
            new_form, new_rows, mixing = step(
                jnp.concatenate([left[0], right[0]], axis=1),
                jnp.concatenate([left[1], right[1]], axis=0),
                chosen,
            )
            samples = mix3(mixing, jnp.concatenate([left[2], right[2]], axis=0))
            merged.append((new_form, new_rows, samples))
        nodes = merged
        span *= 2
    coords_out[...] = nodes[0][0][: dim + 16, :]
    samples_out[...] = nodes[0][2]


def local_tree_call(pack, rows, leaf_sets, merge_sets, dim):
    blocks, leaf = rows.shape[:2]
    skel = leaf_sets.shape[1]
    return pl.pallas_call(
        functools.partial(local_tree_kernel, dim=dim),
        out_shape=[
            jax.ShapeDtypeStruct((dim + 16, skel), BF16),
            jax.ShapeDtypeStruct((skel, LANES), F32),
        ],
        compiler_params=pltpu.CompilerParams(vmem_limit_bytes=VMEM_BYTES),
        cost_estimate=pl.CostEstimate(
            flops=blocks * 8 * skel * leaf * LANES,
            bytes_accessed=6 * blocks * leaf * LANES,
            transcendentals=blocks * skel * leaf,
        ),
        name="local_tree",
    )(pack, rows, leaf_sets, merge_sets)


def path_kernel(all_coords, samples, merge_sets, out, forms, *, dim, blocks):
    count, held, skel = all_coords.shape
    me = lax.axis_index("leaf") * lax.axis_size("sub") + lax.axis_index("sub")
    forms[:, held:, :] = jnp.zeros((forms.shape[0], LANES - held, skel), BF16)
    forms[:count, :held, :] = all_coords[...]
    to_rows = form_map(dim, LANES)
    steps = []
    base, nodes, span, bit = 0, count, blocks, 0
    while nodes > 1:
        after = base + nodes

        def pick(k, carry, base=base, after=after, span=span):
            chosen = merge_sets[pl.ds((2 * k + 1) * span - 1, 1), :]
            picks = onehot_in(chosen, 2 * skel)
            forms[after + k] = (
                dot(forms[base + 2 * k], picks[:skel]) + dot(forms[base + 2 * k + 1], picks[skel:])
            ).astype(BF16)
            return carry

        lax.fori_loop(0, nodes // 2, pick, 0, unroll=min(nodes // 2, 8))
        steps.append((base, after, span, bit))
        base, nodes, span, bit = after, nodes // 2, span * 2, bit + 1
    mixings = []
    for base, after, span, bit in steps:
        node = lax.shift_right_logical(me, bit + 1)
        side = lax.shift_right_logical(me, bit) & 1
        chosen = merge_sets[pl.ds((2 * node + 1) * span - 1, 1), :]
        new_rows = dot_t(forms[after + node], to_rows).astype(BF16)
        left = jnp.exp(dot(new_rows, forms[base + 2 * node]))
        right = jnp.exp(dot(new_rows, forms[base + 2 * node + 1]))
        total = jnp.sum(left + right, axis=1, keepdims=True)
        own = jnp.where(side == 1, right, left)
        lane = lax.broadcasted_iota(jnp.int32, (skel, skel), 1) + side * skel
        picks = jnp.where(column_of(chosen) == lane.astype(F32), 1.0, 0.0)
        mixings.append(picks + own / total)
    value = samples[...]
    for mixing in mixings:
        value = mix3(mixing, value)
    out[...] = value


def path_call(all_coords, samples, merge_sets, dim, blocks):
    count, held, skel = all_coords.shape
    return pl.pallas_call(
        functools.partial(path_kernel, dim=dim, blocks=blocks),
        out_shape=jax.ShapeDtypeStruct(samples.shape, F32),
        scratch_shapes=[pltpu.VMEM((2 * count, LANES, skel), BF16)],
        compiler_params=pltpu.CompilerParams(vmem_limit_bytes=VMEM_BYTES),
        cost_estimate=pl.CostEstimate(
            flops=count * 2 * LANES * 2 * skel * skel * 4,
            bytes_accessed=2 * count * held * skel,
            transcendentals=10 * skel * skel,
        ),
        name="tree_path",
    )(all_coords, samples, merge_sets)


def near_kernel(*refs, slots, dim, has_acc, last):
    lists, counts, rows = refs[:3]
    refs = refs[3:]
    if has_acc:
        acc_in, refs = refs[0], refs[1:]
    buffers = []
    for _, which in slots:
        number = max(which) + 1
        buffers.append(refs[:number])
        refs = refs[number:]
    out, packs, forms, pair_list, sems = refs
    blocks, leaf = rows.shape[:2]
    near = lists.shape[1]
    window = blocks * lax.axis_size("sub")
    start = lax.axis_index("leaf") * window - blocks
    sub = lax.axis_index("sub")

    def place(table):
        value = jnp.int32(table[0])
        for i in range(1, len(table)):
            value = jnp.where(sub == i, jnp.int32(table[i]), value)
        return value

    copies = []
    for slot, (bases, which) in enumerate(slots):
        target = packs.at[pl.ds(slot * blocks, blocks)]
        held = place(which)
        for number, buffer in enumerate(buffers[slot]):
            copy = pltpu.make_async_copy(buffer, target, sems.at[slot])
            if len(buffers[slot]) == 1:
                copy.start()
            else:
                pl.when(held == number)(copy.start)
        copies.append(copy)
    starts = [place(bases) for bases, _ in slots]

    if has_acc:
        out[...] = acc_in[...]
    else:
        out[...] = jnp.zeros(out.shape, F32)

    def list_block(g, found):
        used = counts[g]

        def list_slot(s, found):
            source = lists[g, s] - start
            local = jnp.int32(-1)
            for slot, first in enumerate(starts):
                inside = (source >= first) & (source < first + blocks)
                local = jnp.where(inside, source - first + slot * blocks, local)
            pair_list[found] = g * (len(slots) * blocks) + local
            return found + jnp.where((local >= 0) & (s < used), 1, 0)

        return lax.fori_loop(0, near, list_slot, found, unroll=True)

    pairs = lax.fori_loop(0, blocks, list_block, jnp.int32(0))

    for slot in range(len(slots)):
        copies[slot].wait()

        def prepare(i, carry):
            forms[i] = build_form(packs.at[i], leaf, dim)
            return carry

        lax.fori_loop(slot * blocks, (slot + 1) * blocks, prepare, 0)

    half = leaf // 2

    def add_pair(i, carry):
        code = pair_list[i]
        g = code // (len(slots) * blocks)
        local = code - g * (len(slots) * blocks)
        form = forms[local]
        probes = packs[local, :leaf, :]
        for r in range(0, leaf, half):
            weights = jnp.exp(dot(rows[g, r : r + half, :], form)).astype(BF16)
            out[g, r : r + half, :] += dot(weights, probes)
        return carry

    lax.fori_loop(0, pairs, add_pair, 0)
    if last:
        out[...] = out[...] * (leaf ** -0.5)


def near_call(lists, counts, rows, acc, sets, dim, last, name):
    blocks, leaf = rows.shape[:2]
    buffers = [b for _, _, bufs in sets for b in bufs]
    slots = tuple((bases, which) for bases, which, _ in sets)
    packed = buffers[0].shape[1]
    smem = pl.BlockSpec(memory_space=pltpu.SMEM)
    vmem = pl.BlockSpec(memory_space=pltpu.VMEM)
    args = [lists, counts, rows] + ([acc] if acc is not None else []) + buffers
    specs = [smem, smem, vmem] + ([vmem] if acc is not None else [])
    specs += [pl.BlockSpec(memory_space=pl.ANY)] * len(buffers)
    total = len(slots) * blocks
    near = lists.shape[1]
    pairs = total * blocks // 8
    return pl.pallas_call(
        functools.partial(
            near_kernel, slots=slots, dim=dim, has_acc=acc is not None, last=last
        ),
        in_specs=specs,
        out_specs=vmem,
        out_shape=jax.ShapeDtypeStruct((blocks, leaf, LANES), F32),
        scratch_shapes=[
            pltpu.VMEM((total, packed, LANES), BF16),
            pltpu.VMEM((total, LANES, leaf), BF16),
            pltpu.SMEM((blocks * near + 8,), jnp.int32),
            pltpu.SemaphoreType.DMA((len(slots),)),
        ],
        compiler_params=pltpu.CompilerParams(vmem_limit_bytes=VMEM_BYTES),
        cost_estimate=pl.CostEstimate(
            flops=pairs * 2 * leaf * leaf * 256,
            bytes_accessed=total * packed * LANES * 2 + blocks * leaf * LANES * 8,
            transcendentals=pairs * leaf * leaf,
        ),
        name=name,
    )(*args)


def on_device(points, probes, order, near_lists, near_counts, leaf_sets, merge_sets):
    leaf_count = lax.axis_size("leaf")
    sub_count = lax.axis_size("sub")
    blocks, skel = leaf_sets.shape
    npts, dim = points.shape
    leaf = npts // blocks
    axes = ("leaf", "sub")

    def send(x, routes):
        pairs = []
        for place in range(leaf_count):
            for from_sub, step, to_sub in routes:
                if 0 <= place + step < leaf_count:
                    pairs.append((place * sub_count + from_sub, (place + step) * sub_count + to_sub))
        return lax.ppermute(x, axes, pairs)

    swap = [(0, 0, 1), (1, 0, 0), (2, 0, 3), (3, 0, 2)]
    pack, rows = order_call(points.T, order.reshape(blocks, 1, leaf), probes, blocks)
    outer_next = send(pack, [(3, 1, 3), (0, -1, 0)])
    outer_across = send(pack, [(3, 0, 1), (0, 0, 2)])
    beside = send(pack, swap)

    coords, samples = local_tree_call(pack, rows, leaf_sets, merge_sets, dim)
    all_coords = lax.all_gather(coords, axes, axis=0)

    inner_pack, outer_across = lax.optimization_barrier((pack, outer_across))
    inner_across = send(inner_pack, [(2, 0, 0), (1, 0, 3)])
    forwarded = send(outer_across, [(1, 1, 1), (2, -1, 2)])

    place = lax.axis_index("sub")
    at_edge = (place == 0) | (place == sub_count - 1)
    early = jnp.where(at_edge, outer_next, outer_across)
    early_beside = send(early, swap)

    b = blocks
    own_base, beside_base = (b, 2 * b, 3 * b, 4 * b), (2 * b, b, 4 * b, 3 * b)
    early_base, early_beside_base = (5 * b, 4 * b, b, 0), (4 * b, 5 * b, 0, b)
    late_base, late_beside_base = (3 * b, 0, 5 * b, 2 * b), (0, 3 * b, 2 * b, 5 * b)
    single = (0, 0, 0, 0)
    acc = near_call(
        near_lists, near_counts, rows, None,
        [(own_base, single, [pack]), (beside_base, single, [beside]), (early_base, single, [early])],
        dim, False, "near_first",
    )
    late = jnp.where(at_edge, inner_across, forwarded)
    late_beside = send(late, swap)
    acc = near_call(
        near_lists, near_counts, rows, acc,
        [(early_beside_base, single, [early_beside]), (late_base, single, [late])],
        dim, False, "near_second",
    )
    root_term = path_call(all_coords, samples, merge_sets, dim, blocks)
    if skel % (leaf_count * sub_count):
        root_term = root_term.reshape(-1)
    root = lax.psum_scatter(root_term, axes, scatter_dimension=0, tiled=True)
    near = near_call(
        near_lists, near_counts, rows, acc,
        [(late_beside_base, single, [late_beside])],
        dim, True, "near_last",
    )
    return near.reshape(npts, LANES), root.reshape(-1)


def solution(mesh):
    in_specs = (
        P(("leaf", "sub"), None),
        P(("leaf", "sub"), None),
        P(("leaf", "sub")),
        P(("leaf", "sub"), None),
        P(("leaf", "sub")),
        P(("leaf", "sub"), None),
        P(),
    )
    out_specs = (P(("leaf", "sub"), None), P(("leaf", "sub")))
    return jax.shard_map(
        on_device, mesh=mesh, in_specs=in_specs, out_specs=out_specs, check_vma=False
    )
```

```python
import functools

import jax
import jax.numpy as jnp
from jax import lax
from jax.experimental import pallas as pl
from jax.experimental.pallas import tpu as pltpu
from jax.sharding import PartitionSpec as P

LANES = 128
PARTS = 3
VMEM_BYTES = 56 * 1024 * 1024
F32 = jnp.float32
BF16 = jnp.bfloat16


def dot(a, b):
    return jnp.dot(a, b, preferred_element_type=F32)


def dot_t(a, b):
    return lax.dot_general(a, b, (((0,), (0,)), ((), ())), preferred_element_type=F32)


def split(x):
    hi = x.astype(BF16)
    return hi, (x - hi.astype(F32)).astype(BF16)


def square_rows(pts):
    x = pts.astype(F32)
    total = jnp.sum(x * x, axis=0, keepdims=True)
    hi = total.astype(BF16).astype(F32)
    mid = (total - hi).astype(BF16).astype(F32)
    low = total - hi - mid
    row = lax.broadcasted_iota(jnp.int32, (16, pts.shape[1]), 0)
    ones = jnp.where(row < 2 * PARTS, 1.0, 0.0)
    return jnp.where(row == 0, hi, jnp.where(row == 1, mid, jnp.where(row == 2, low, ones))).astype(BF16)


def form_map(dim, size):
    k = lax.broadcasted_iota(jnp.int32, (size, size), 0)
    j = lax.broadcasted_iota(jnp.int32, (size, size), 1)
    r = jnp.where((k == j) & (j < dim), 2.0 / dim, 0.0)
    r = jnp.where((j >= dim) & (j < dim + PARTS) & (k == j + PARTS), -1.0 / dim, r)
    r = jnp.where((j >= dim + PARTS) & (j < dim + 2 * PARTS) & (k == j - PARTS), -1.0 / dim, r)
    return r.astype(BF16)


def onehot_in(row, size):
    index = lax.broadcasted_iota(jnp.int32, (size, row.shape[1]), 0)
    return jnp.where(index == row, 1.0, 0.0).astype(BF16)


def column_of(row):
    return jnp.broadcast_to(row.astype(F32), (LANES, row.shape[1])).T


def onehot_out(column, size):
    lane = lax.broadcasted_iota(jnp.int32, column.shape, 1).astype(F32)
    return jnp.concatenate(
        [jnp.where(column == lane + float(i), 1.0, 0.0) for i in range(0, size, LANES)], axis=1
    )


def mix3(m, s):
    m_hi, m_lo = split(m)
    s_hi, s_lo = split(s)
    return dot(m_hi, s_hi) + (dot(m_hi, s_lo) + dot(m_lo, s_hi))


def order_kernel(points_t, order, probes, pack, rows):
    dim = points_t.shape[0]
    many, leaf = rows.shape[:2]
    held = dim + 16
    to_rows = form_map(dim, LANES)
    for b in range(many):
        picks = onehot_in(order[b], leaf)
        tree_t = dot(points_t[:, b * leaf : (b + 1) * leaf], picks).astype(BF16)
        pack[b, :leaf, :] = probes[b * leaf : (b + 1) * leaf, :]
        form = jnp.concatenate([tree_t, square_rows(tree_t)], axis=0)
        for i in range(leaf // LANES):
            pack[b, leaf + i * held : leaf + (i + 1) * held, :] = form[:, i * LANES : (i + 1) * LANES]
        form = jnp.concatenate([form, jnp.zeros((LANES - held, leaf), BF16)], axis=0)
        rows[b] = dot_t(form, to_rows).astype(BF16)


def order_call(points_t, order, probes, blocks):
    dim, npts = points_t.shape
    leaf = npts // blocks
    packed = leaf + leaf // LANES * (dim + 16)
    many = 4 if blocks % 4 == 0 else 1
    return pl.pallas_call(
        order_kernel,
        grid=(blocks // many,),
        in_specs=[
            pl.BlockSpec((dim, many * leaf), lambda b: (0, b)),
            pl.BlockSpec((many, 1, leaf), lambda b: (b, 0, 0)),
            pl.BlockSpec((many * leaf, LANES), lambda b: (b, 0)),
        ],
        out_specs=[
            pl.BlockSpec((many, packed, LANES), lambda b: (b, 0, 0)),
            pl.BlockSpec((many, leaf, LANES), lambda b: (b, 0, 0)),
        ],
        out_shape=[
            jax.ShapeDtypeStruct((blocks, packed, LANES), BF16),
            jax.ShapeDtypeStruct((blocks, leaf, LANES), BF16),
        ],
        compiler_params=pltpu.CompilerParams(vmem_limit_bytes=VMEM_BYTES),
        cost_estimate=pl.CostEstimate(
            flops=blocks * 2 * leaf * leaf * dim, bytes_accessed=10 * npts * LANES, transcendentals=0
        ),
        name="tree_order",
    )(points_t, order, probes)


def form_of(pack_block, leaf, dim):
    held = dim + 16
    columns = [
        pack_block[leaf + i * held : leaf + (i + 1) * held, :] for i in range(leaf // LANES)
    ]
    form = jnp.concatenate(columns, axis=1)
    return jnp.concatenate([form, jnp.zeros((LANES - held, leaf), BF16)], axis=0)


def condense(form, a_rows, chosen):
    size = form.shape[1]
    picks_out = onehot_out(column_of(chosen), size)
    new_rows = dot(picks_out.astype(BF16), a_rows).astype(BF16)
    new_form = dot(form, onehot_in(chosen, size)).astype(BF16)
    weights = jnp.exp(dot(new_rows, form))
    mixing = picks_out + weights / jnp.sum(weights, axis=1, keepdims=True)
    return new_form, new_rows, mixing


def local_tree_kernel(pack, rows, leaf_sets, merge_sets, out, *, dim):
    blocks, leaf = rows.shape[:2]
    first_block = (lax.axis_index("leaf") * lax.axis_size("sub") + lax.axis_index("sub")) * blocks

    nodes = []
    for b in range(blocks):
        form = form_of(pack.at[b], leaf, dim)
        new_form, new_rows, mixing = condense(form, rows[b], leaf_sets[b : b + 1, :])
        m_hi, m_lo = split(mixing)
        probes = pack[b, :leaf, :]
        nodes.append((new_form, new_rows, dot(m_hi, probes) + dot(m_lo, probes)))
    span = 1
    while len(nodes) > 1:
        merged = []
        for k in range(len(nodes) // 2):
            left, right = nodes[2 * k], nodes[2 * k + 1]
            chosen = merge_sets[pl.ds(first_block + (2 * k + 1) * span - 1, 1), :]
            new_form, new_rows, mixing = condense(
                jnp.concatenate([left[0], right[0]], axis=1),
                jnp.concatenate([left[1], right[1]], axis=0),
                chosen,
            )
            samples = mix3(mixing, jnp.concatenate([left[2], right[2]], axis=0))
            merged.append((new_form, new_rows, samples))
        nodes = merged
        span *= 2
    held = dim + 16
    out[:held, :] = nodes[0][0][:held, :].astype(F32)
    out[held:, :] = nodes[0][2]


def local_tree_call(pack, rows, leaf_sets, merge_sets, dim):
    blocks, leaf = rows.shape[:2]
    skel = leaf_sets.shape[1]
    return pl.pallas_call(
        functools.partial(local_tree_kernel, dim=dim),
        out_shape=jax.ShapeDtypeStruct((dim + 16 + skel, LANES), F32),
        compiler_params=pltpu.CompilerParams(vmem_limit_bytes=VMEM_BYTES),
        cost_estimate=pl.CostEstimate(
            flops=blocks * 8 * skel * leaf * LANES,
            bytes_accessed=6 * blocks * leaf * LANES,
            transcendentals=blocks * skel * leaf,
        ),
        name="local_tree",
    )(pack, rows, leaf_sets, merge_sets)


def merge_kernel(own, other, merge_sets, out, *, dim, blocks, bit, piece):
    held = dim + 16
    skel = own.shape[0] - held
    me = lax.axis_index("leaf") * lax.axis_size("sub") + lax.axis_index("sub")
    node = lax.shift_right_logical(me, bit + 1)
    is_right = (lax.shift_right_logical(me, bit) & 1) == 1
    chosen = merge_sets[pl.ds((2 * node + 1) * (blocks << bit) - 1, 1), :]
    left = jnp.where(is_right, other[...], own[...])
    right = jnp.where(is_right, own[...], other[...])
    form = jnp.concatenate([left[:held], right[:held]], axis=1).astype(BF16)
    form = jnp.concatenate([form, jnp.zeros((LANES - held, 2 * skel), BF16)], axis=0)
    new_form = dot(form, onehot_in(chosen, 2 * skel))
    new_rows = dot_t(new_form.astype(BF16), form_map(dim, LANES)).astype(BF16)
    weights = jnp.exp(dot(new_rows, form))
    picks = onehot_out(column_of(chosen), 2 * skel)
    mixing = picks + weights / jnp.sum(weights, axis=1, keepdims=True)
    samples = mix3(mixing, jnp.concatenate([left[held:], right[held:]], axis=0))
    if piece is None:
        out[:held, :] = new_form[:held]
        out[held:, :] = samples
    elif piece == 0:
        out[...] = samples
    else:
        rank = lax.broadcasted_iota(jnp.int32, (piece, skel), 1)
        first = lax.broadcasted_iota(jnp.int32, (piece, skel), 0) + me * piece
        take = jnp.where(rank == first, 1.0, 0.0).astype(BF16)
        hi, lo = split(samples)
        low = (samples - hi.astype(F32) - lo.astype(F32)).astype(BF16)
        out[...] = dot(take, hi) + dot(take, lo) + dot(take, low)


def merge_call(own, other, merge_sets, dim, blocks, bit, piece=None):
    size = own.shape[0]
    skel = size - dim - 16
    rows = size if piece is None else (piece or skel)
    return pl.pallas_call(
        functools.partial(merge_kernel, dim=dim, blocks=blocks, bit=bit, piece=piece),
        out_shape=jax.ShapeDtypeStruct((rows, LANES), F32),
        compiler_params=pltpu.CompilerParams(vmem_limit_bytes=VMEM_BYTES),
        cost_estimate=pl.CostEstimate(
            flops=16 * LANES**3, bytes_accessed=12 * size * LANES, transcendentals=2 * LANES**2
        ),
        name="tree_merge",
    )(own, other, merge_sets)


def near_kernel(*refs, slots, dim, has_acc, last):
    lists, counts, rows = refs[:3]
    refs = refs[3:]
    if has_acc:
        acc_in, refs = refs[0], refs[1:]
    buffers = []
    for _, which in slots:
        number = max(which) + 1
        buffers.append(refs[:number])
        refs = refs[number:]
    out, packs, pair_list, sems = refs
    blocks, leaf = rows.shape[:2]
    near = lists.shape[1]
    window = blocks * lax.axis_size("sub")
    start = lax.axis_index("leaf") * window - blocks
    sub = lax.axis_index("sub")

    def place(table):
        value = jnp.int32(table[0])
        for i in range(1, len(table)):
            value = jnp.where(sub == i, jnp.int32(table[i]), value)
        return value

    copies = []
    for slot, (bases, which) in enumerate(slots):
        target = packs.at[pl.ds(slot * blocks, blocks)]
        held = place(which)
        for number, buffer in enumerate(buffers[slot]):
            copy = pltpu.make_async_copy(buffer, target, sems.at[slot])
            if len(buffers[slot]) == 1:
                copy.start()
            else:
                pl.when(held == number)(copy.start)
        copies.append(copy)
    starts = [place(bases) for bases, _ in slots]

    if has_acc:
        acc_copy = pltpu.make_async_copy(acc_in, out, sems.at[len(slots)])
        acc_copy.start()
    else:
        out[...] = jnp.zeros(out.shape, F32)

    def list_block(g, found):
        used = counts[g]

        def list_slot(s, found):
            source = lists[g, s] - start
            local = jnp.int32(-1)
            for slot, first in enumerate(starts):
                inside = (source >= first) & (source < first + blocks)
                local = jnp.where(inside, source - first + slot * blocks, local)
            pair_list[found] = g * (len(slots) * blocks) + local
            return found + jnp.where((local >= 0) & (s < used), 1, 0)

        return lax.fori_loop(0, near, list_slot, found, unroll=True)

    pairs = lax.fori_loop(0, blocks, list_block, jnp.int32(0))

    for copy in copies:
        copy.wait()
    if has_acc:
        acc_copy.wait()

    half = leaf // 2

    def add_pair(i, carry):
        code = pair_list[i]
        g = code // (len(slots) * blocks)
        local = code - g * (len(slots) * blocks)
        form = form_of(packs.at[local], leaf, dim)
        probes = packs[local, :leaf, :]
        for r in range(0, leaf, half):
            weights = jnp.exp(dot(rows[g, r : r + half, :], form)).astype(BF16)
            out[g, r : r + half, :] += dot(weights, probes)
        return carry

    lax.fori_loop(0, pairs, add_pair, 0)
    if last:
        out[...] = out[...] * (leaf ** -0.5)


def near_call(lists, counts, rows, acc, sets, dim, last, name):
    blocks, leaf = rows.shape[:2]
    buffers = [b for _, _, bufs in sets for b in bufs]
    slots = tuple((bases, which) for bases, which, _ in sets)
    packed = buffers[0].shape[1]
    smem = pl.BlockSpec(memory_space=pltpu.SMEM)
    vmem = pl.BlockSpec(memory_space=pltpu.VMEM)
    args = [lists, counts, rows] + ([acc] if acc is not None else []) + buffers
    specs = [smem, smem, vmem]
    specs += [pl.BlockSpec(memory_space=pl.ANY)] * (len(buffers) + (acc is not None))
    total = len(slots) * blocks
    near = lists.shape[1]
    pairs = total * blocks // 8
    return pl.pallas_call(
        functools.partial(
            near_kernel, slots=slots, dim=dim, has_acc=acc is not None, last=last
        ),
        in_specs=specs,
        out_specs=vmem,
        out_shape=jax.ShapeDtypeStruct((blocks, leaf, LANES), F32),
        scratch_shapes=[
            pltpu.VMEM((total, packed, LANES), BF16),
            pltpu.SMEM((blocks * near + 8,), jnp.int32),
            pltpu.SemaphoreType.DMA((len(slots) + 1,)),
        ],
        compiler_params=pltpu.CompilerParams(vmem_limit_bytes=VMEM_BYTES),
        cost_estimate=pl.CostEstimate(
            flops=pairs * 2 * leaf * leaf * 256,
            bytes_accessed=total * packed * LANES * 2 + blocks * leaf * LANES * 8,
            transcendentals=pairs * leaf * leaf,
        ),
        name=name,
    )(*args)


def on_device(points, probes, order, near_lists, near_counts, leaf_sets, merge_sets):
    leaf_count = lax.axis_size("leaf")
    sub_count = lax.axis_size("sub")
    blocks, skel = leaf_sets.shape
    npts, dim = points.shape
    leaf = npts // blocks
    axes = ("leaf", "sub")

    def send(x, routes):
        pairs = []
        for place in range(leaf_count):
            for from_sub, step, to_sub in routes:
                if 0 <= place + step < leaf_count:
                    pairs.append((place * sub_count + from_sub, (place + step) * sub_count + to_sub))
        return lax.ppermute(x, axes, pairs)

    swap = [(0, 0, 1), (1, 0, 0), (2, 0, 3), (3, 0, 2)]
    pack, rows = order_call(points.T, order.reshape(blocks, 1, leaf), probes, blocks)
    outer_across = send(pack, [(3, 0, 1), (0, 0, 2)])
    outer_next = send(pack, [(3, 1, 3), (0, -1, 0)])
    beside = send(pack, swap)

    node = local_tree_call(pack, rows, leaf_sets, merge_sets, dim)

    inner_pack, outer_across, node = lax.optimization_barrier((pack, outer_across, node))
    inner_across = send(inner_pack, [(2, 0, 0), (1, 0, 3)])
    forwarded = send(outer_across, [(1, 1, 1), (2, -1, 2)])

    place = lax.axis_index("sub")
    at_edge = (place == 0) | (place == sub_count - 1)
    early = jnp.where(at_edge, outer_next, outer_across)
    early_beside = send(early, swap)

    count = leaf_count * sub_count
    bits = count.bit_length() - 1
    sub_bits = sub_count.bit_length() - 1
    piece = skel // count
    for bit in range(bits):
        partner = [(i, i ^ (1 << bit)) for i in range(count)]
        other = lax.ppermute(node, axes, partner)
        node = merge_call(node, other, merge_sets, dim, blocks, bit, None if bit < bits - 1 else piece)
        if bit == sub_bits - 1:
            early, early_beside, beside, node = lax.optimization_barrier(
                (early, early_beside, beside, node)
            )
    if piece:
        root = node.reshape(-1)
    else:
        size = skel * LANES // count
        rank = lax.axis_index("leaf") * sub_count + lax.axis_index("sub")
        root = lax.dynamic_slice_in_dim(node.reshape(-1), rank * size, size, 0)

    b = blocks
    own_base, beside_base = (b, 2 * b, 3 * b, 4 * b), (2 * b, b, 4 * b, 3 * b)
    early_base, early_beside_base = (5 * b, 4 * b, b, 0), (4 * b, 5 * b, 0, b)
    late_base, late_beside_base = (3 * b, 0, 5 * b, 2 * b), (0, 3 * b, 2 * b, 5 * b)
    single = (0, 0, 0, 0)
    acc = near_call(
        near_lists, near_counts, rows, None,
        [
            (own_base, single, [pack]),
            (beside_base, single, [beside]),
            (early_base, single, [early]),
            (early_beside_base, single, [early_beside]),
        ],
        dim, False, "near_first",
    )
    late = jnp.where(at_edge, inner_across, forwarded)
    late, acc = lax.optimization_barrier((late, acc))
    late_beside = send(late, swap)
    near = near_call(
        near_lists, near_counts, rows, acc,
        [(late_base, single, [late]), (late_beside_base, single, [late_beside])],
        dim, True, "near_last",
    )
    return near.reshape(npts, LANES), root


def solution(mesh):
    in_specs = (
        P(("leaf", "sub"), None),
        P(("leaf", "sub"), None),
        P(("leaf", "sub")),
        P(("leaf", "sub"), None),
        P(("leaf", "sub")),
        P(("leaf", "sub"), None),
        P(),
    )
    out_specs = (P(("leaf", "sub"), None), P(("leaf", "sub")))
    return jax.shard_map(
        on_device, mesh=mesh, in_specs=in_specs, out_specs=out_specs, check_vma=False
    )
```

```python
import functools

import jax
import jax.numpy as jnp
from jax import lax
from jax.experimental import pallas as pl
from jax.experimental.pallas import tpu as pltpu
from jax.sharding import PartitionSpec as P

LANES = 128
PARTS = 3
VMEM_BYTES = 24 * 1024 * 1024
F32 = jnp.float32
BF16 = jnp.bfloat16


def dot(a, b):
    return jnp.dot(a, b, preferred_element_type=F32)


def dot_t(a, b):
    return lax.dot_general(a, b, (((0,), (0,)), ((), ())), preferred_element_type=F32)


def split(x):
    hi = x.astype(BF16)
    return hi, (x - hi.astype(F32)).astype(BF16)


def square_rows(pts):
    x = pts.astype(F32)
    total = jnp.sum(x * x, axis=0, keepdims=True)
    hi = total.astype(BF16).astype(F32)
    mid = (total - hi).astype(BF16).astype(F32)
    low = total - hi - mid
    row = lax.broadcasted_iota(jnp.int32, (16, pts.shape[1]), 0)
    ones = jnp.where(row < 2 * PARTS, 1.0, 0.0)
    return jnp.where(row == 0, hi, jnp.where(row == 1, mid, jnp.where(row == 2, low, ones))).astype(BF16)


def form_map(dim, size):
    k = lax.broadcasted_iota(jnp.int32, (size, size), 0)
    j = lax.broadcasted_iota(jnp.int32, (size, size), 1)
    r = jnp.where((k == j) & (j < dim), 2.0 / dim, 0.0)
    r = jnp.where((j >= dim) & (j < dim + PARTS) & (k == j + PARTS), -1.0 / dim, r)
    r = jnp.where((j >= dim + PARTS) & (j < dim + 2 * PARTS) & (k == j - PARTS), -1.0 / dim, r)
    return r.astype(BF16)


def onehot_in(row, size):
    index = lax.broadcasted_iota(jnp.int32, (size, row.shape[1]), 0)
    return jnp.where(index == row, 1.0, 0.0).astype(BF16)


def column_of(row):
    return jnp.broadcast_to(row.astype(F32), (LANES, row.shape[1])).T


def onehot_out(column, size):
    lane = lax.broadcasted_iota(jnp.int32, column.shape, 1).astype(F32)
    return jnp.concatenate(
        [jnp.where(column == lane + float(i), 1.0, 0.0) for i in range(0, size, LANES)], axis=1
    )


def mix3(m, s):
    m_hi, m_lo = split(m)
    s_hi, s_lo = split(s)
    return dot(m_hi, s_hi) + (dot(m_hi, s_lo) + dot(m_lo, s_hi))


def order_kernel(points_t, order, probes, pack, rows):
    dim = points_t.shape[0]
    many, leaf = rows.shape[:2]
    held = dim + 16
    to_rows = form_map(dim, LANES)
    for b in range(many):
        picks = onehot_in(order[b], leaf)
        tree_t = dot(points_t[:, b * leaf : (b + 1) * leaf], picks).astype(BF16)
        pack[b, :leaf, :] = probes[b * leaf : (b + 1) * leaf, :]
        form = jnp.concatenate([tree_t, square_rows(tree_t)], axis=0)
        for i in range(leaf // LANES):
            pack[b, leaf + i * held : leaf + (i + 1) * held, :] = form[:, i * LANES : (i + 1) * LANES]
        form = jnp.concatenate([form, jnp.zeros((LANES - held, leaf), BF16)], axis=0)
        rows[b] = dot_t(form, to_rows).astype(BF16)


def order_call(points_t, order, probes, blocks):
    dim, npts = points_t.shape
    leaf = npts // blocks
    packed = leaf + leaf // LANES * (dim + 16)
    many = 4 if blocks % 4 == 0 else 1
    return pl.pallas_call(
        order_kernel,
        grid=(blocks // many,),
        in_specs=[
            pl.BlockSpec((dim, many * leaf), lambda b: (0, b)),
            pl.BlockSpec((many, 1, leaf), lambda b: (b, 0, 0)),
            pl.BlockSpec((many * leaf, LANES), lambda b: (b, 0)),
        ],
        out_specs=[
            pl.BlockSpec((many, packed, LANES), lambda b: (b, 0, 0)),
            pl.BlockSpec((many, leaf, LANES), lambda b: (b, 0, 0)),
        ],
        out_shape=[
            jax.ShapeDtypeStruct((blocks, packed, LANES), BF16),
            jax.ShapeDtypeStruct((blocks, leaf, LANES), BF16),
        ],
        compiler_params=pltpu.CompilerParams(vmem_limit_bytes=VMEM_BYTES),
        cost_estimate=pl.CostEstimate(
            flops=blocks * 2 * leaf * leaf * dim, bytes_accessed=10 * npts * LANES, transcendentals=0
        ),
        name="tree_order",
    )(points_t, order, probes)


def form_of(pack_block, leaf, dim):
    held = dim + 16
    columns = [
        pack_block[leaf + i * held : leaf + (i + 1) * held, :] for i in range(leaf // LANES)
    ]
    form = jnp.concatenate(columns, axis=1)
    return jnp.concatenate([form, jnp.zeros((LANES - held, leaf), BF16)], axis=0)


def condense(form, a_rows, chosen):
    size = form.shape[1]
    picks_out = onehot_out(column_of(chosen), size)
    new_rows = dot(picks_out.astype(BF16), a_rows).astype(BF16)
    new_form = dot(form, onehot_in(chosen, size)).astype(BF16)
    weights = jnp.exp(dot(new_rows, form))
    mixing = picks_out + weights / jnp.sum(weights, axis=1, keepdims=True)
    return new_form, new_rows, mixing


def local_tree_kernel(pack, rows, leaf_sets, merge_sets, out, *, dim):
    blocks, leaf = rows.shape[:2]
    first_block = (lax.axis_index("leaf") * lax.axis_size("sub") + lax.axis_index("sub")) * blocks

    nodes = []
    for b in range(blocks):
        form = form_of(pack.at[b], leaf, dim)
        new_form, new_rows, mixing = condense(form, rows[b], leaf_sets[b : b + 1, :])
        m_hi, m_lo = split(mixing)
        probes = pack[b, :leaf, :]
        nodes.append((new_form, new_rows, dot(m_hi, probes) + dot(m_lo, probes)))
    span = 1
    while len(nodes) > 1:
        merged = []
        for k in range(len(nodes) // 2):
            left, right = nodes[2 * k], nodes[2 * k + 1]
            chosen = merge_sets[pl.ds(first_block + (2 * k + 1) * span - 1, 1), :]
            new_form, new_rows, mixing = condense(
                jnp.concatenate([left[0], right[0]], axis=1),
                jnp.concatenate([left[1], right[1]], axis=0),
                chosen,
            )
            samples = mix3(mixing, jnp.concatenate([left[2], right[2]], axis=0))
            merged.append((new_form, new_rows, samples))
        nodes = merged
        span *= 2
    held = dim + 16
    out[:held, :] = nodes[0][0][:held, :].astype(F32)
    out[held:, :] = nodes[0][2]


def local_tree_call(pack, rows, leaf_sets, merge_sets, dim):
    blocks, leaf = rows.shape[:2]
    skel = leaf_sets.shape[1]
    return pl.pallas_call(
        functools.partial(local_tree_kernel, dim=dim),
        out_shape=jax.ShapeDtypeStruct((dim + 16 + skel, LANES), F32),
        compiler_params=pltpu.CompilerParams(vmem_limit_bytes=VMEM_BYTES),
        cost_estimate=pl.CostEstimate(
            flops=blocks * 8 * skel * leaf * LANES,
            bytes_accessed=6 * blocks * leaf * LANES,
            transcendentals=blocks * skel * leaf,
        ),
        name="local_tree",
    )(pack, rows, leaf_sets, merge_sets)


def merge_kernel(group, merge_sets, out, *, dim, span, base, piece):
    held = dim + 16
    count, size = group.shape[:2]
    skel = size - held
    to_rows = form_map(dim, LANES)
    first = lax.axis_index(base) * count if base else 0
    forms = [group[i, :held, :].astype(BF16) for i in range(count)]
    samples = [group[i, held:, :] for i in range(count)]
    while len(forms) > 1:
        first = first // 2
        new_forms, new_samples = [], []
        for k in range(len(forms) // 2):
            chosen = merge_sets[pl.ds((2 * (first + k) + 1) * span - 1, 1), :]
            form = jnp.concatenate(forms[2 * k : 2 * k + 2], axis=1)
            form = jnp.concatenate([form, jnp.zeros((LANES - held, 2 * skel), BF16)], axis=0)
            new_form = dot(form, onehot_in(chosen, 2 * skel)).astype(BF16)
            new_rows = dot_t(new_form, to_rows).astype(BF16)
            weights = jnp.exp(dot(new_rows, form))
            picks = onehot_out(column_of(chosen), 2 * skel)
            mixing = picks + weights / jnp.sum(weights, axis=1, keepdims=True)
            new_forms.append(new_form[:held])
            new_samples.append(mix3(mixing, jnp.concatenate(samples[2 * k : 2 * k + 2], axis=0)))
        forms, samples = new_forms, new_samples
        span *= 2
    if piece is None:
        out[:held, :] = forms[0].astype(F32)
        out[held:, :] = samples[0]
    elif piece == 0:
        out[...] = samples[0]
    else:
        me = lax.axis_index("leaf") * lax.axis_size("sub") + lax.axis_index("sub")
        column = lax.broadcasted_iota(jnp.int32, (piece, skel), 1)
        row = lax.broadcasted_iota(jnp.int32, (piece, skel), 0) + me * piece
        take = jnp.where(column == row, 1.0, 0.0).astype(BF16)
        hi, lo = split(samples[0])
        low = (samples[0] - hi.astype(F32) - lo.astype(F32)).astype(BF16)
        out[...] = dot(take, hi) + dot(take, lo) + dot(take, low)


def merge_call(group, merge_sets, dim, span, base, piece=None):
    count, size = group.shape[:2]
    skel = size - dim - 16
    rows = size if piece is None else (piece or skel)
    return pl.pallas_call(
        functools.partial(merge_kernel, dim=dim, span=span, base=base, piece=piece),
        out_shape=jax.ShapeDtypeStruct((rows, LANES), F32),
        compiler_params=pltpu.CompilerParams(vmem_limit_bytes=20 * 1024 * 1024),
        cost_estimate=pl.CostEstimate(
            flops=count * 16 * LANES**3,
            bytes_accessed=4 * count * size * LANES,
            transcendentals=2 * count * LANES**2,
        ),
        name="tree_merge",
    )(group, merge_sets)


def near_kernel(*refs, slots, dim, has_acc, last):
    lists, counts, rows = refs[:3]
    refs = refs[3:]
    if has_acc:
        acc_in, refs = refs[0], refs[1:]
    buffers = []
    for _, which in slots:
        number = max(which) + 1
        buffers.append(refs[:number])
        refs = refs[number:]
    out, packs, pair_list, sems = refs
    blocks, leaf = rows.shape[:2]
    near = lists.shape[1]
    window = blocks * lax.axis_size("sub")
    start = lax.axis_index("leaf") * window - blocks
    sub = lax.axis_index("sub")

    def place(table):
        value = jnp.int32(table[0])
        for i in range(1, len(table)):
            value = jnp.where(sub == i, jnp.int32(table[i]), value)
        return value

    copies = []
    for slot, (bases, which) in enumerate(slots):
        target = packs.at[pl.ds(slot * blocks, blocks)]
        held = place(which)
        for number, buffer in enumerate(buffers[slot]):
            copy = pltpu.make_async_copy(buffer, target, sems.at[slot])
            if len(buffers[slot]) == 1:
                copy.start()
            else:
                pl.when(held == number)(copy.start)
        copies.append(copy)
    starts = [place(bases) for bases, _ in slots]

    if has_acc:
        acc_copy = pltpu.make_async_copy(acc_in, out, sems.at[len(slots)])
        acc_copy.start()
    else:
        out[...] = jnp.zeros(out.shape, F32)

    def list_block(g, found):
        used = counts[g]

        def list_slot(s, found):
            source = lists[g, s] - start
            local = jnp.int32(-1)
            for slot, first in enumerate(starts):
                inside = (source >= first) & (source < first + blocks)
                local = jnp.where(inside, source - first + slot * blocks, local)
            pair_list[found] = g * (len(slots) * blocks) + local
            return found + jnp.where((local >= 0) & (s < used), 1, 0)

        return lax.fori_loop(0, near, list_slot, found, unroll=True)

    pairs = lax.fori_loop(0, blocks, list_block, jnp.int32(0))

    for copy in copies:
        copy.wait()
    if has_acc:
        acc_copy.wait()

    half = leaf // 2

    def add_pair(i):
        code = pair_list[i]
        g = code // (len(slots) * blocks)
        local = code - g * (len(slots) * blocks)
        form = form_of(packs.at[local], leaf, dim)
        probes = packs[local, :leaf, :]
        sums = []
        for r in range(0, leaf, half):
            weights = jnp.exp(dot(rows[g, r : r + half, :], form)).astype(BF16)
            sums.append(dot(weights, probes))
        return g, sums

    def add_pairs(i, carry):
        found = [add_pair(2 * i), add_pair(2 * i + 1)]
        for g, sums in found:
            for j, value in enumerate(sums):
                out[g, j * half : (j + 1) * half, :] += value
        return carry

    lax.fori_loop(0, pairs // 2, add_pairs, 0)

    @pl.when(pairs % 2 == 1)
    def _():
        g, sums = add_pair(pairs - 1)
        for j, value in enumerate(sums):
            out[g, j * half : (j + 1) * half, :] += value

    if last:
        out[...] = out[...] * (leaf ** -0.5)


def near_call(lists, counts, rows, acc, sets, dim, last, name):
    blocks, leaf = rows.shape[:2]
    buffers = [b for _, _, bufs in sets for b in bufs]
    slots = tuple((bases, which) for bases, which, _ in sets)
    packed = buffers[0].shape[1]
    smem = pl.BlockSpec(memory_space=pltpu.SMEM)
    vmem = pl.BlockSpec(memory_space=pltpu.VMEM)
    args = [lists, counts, rows] + ([acc] if acc is not None else []) + buffers
    specs = [smem, smem, vmem]
    specs += [pl.BlockSpec(memory_space=pl.ANY)] * (len(buffers) + (acc is not None))
    total = len(slots) * blocks
    near = lists.shape[1]
    pairs = total * blocks // 8
    return pl.pallas_call(
        functools.partial(
            near_kernel, slots=slots, dim=dim, has_acc=acc is not None, last=last
        ),
        in_specs=specs,
        out_specs=vmem,
        out_shape=jax.ShapeDtypeStruct((blocks, leaf, LANES), F32),
        scratch_shapes=[
            pltpu.VMEM((total, packed, LANES), BF16),
            pltpu.SMEM((blocks * near + 8,), jnp.int32),
            pltpu.SemaphoreType.DMA((len(slots) + 1,)),
        ],
        compiler_params=pltpu.CompilerParams(vmem_limit_bytes=VMEM_BYTES),
        cost_estimate=pl.CostEstimate(
            flops=pairs * 2 * leaf * leaf * 256,
            bytes_accessed=total * packed * LANES * 2 + blocks * leaf * LANES * 8,
            transcendentals=pairs * leaf * leaf,
        ),
        name=name,
    )(*args)


def on_device(points, probes, order, near_lists, near_counts, leaf_sets, merge_sets):
    leaf_count = lax.axis_size("leaf")
    sub_count = lax.axis_size("sub")
    blocks, skel = leaf_sets.shape
    npts, dim = points.shape
    leaf = npts // blocks
    axes = ("leaf", "sub")

    def send(x, routes):
        pairs = []
        for place in range(leaf_count):
            for from_sub, step, to_sub in routes:
                if 0 <= place + step < leaf_count:
                    pairs.append((place * sub_count + from_sub, (place + step) * sub_count + to_sub))
        return lax.ppermute(x, axes, pairs)

    swap = [(0, 0, 1), (1, 0, 0), (2, 0, 3), (3, 0, 2)]
    pack, rows = order_call(points.T, order.reshape(blocks, 1, leaf), probes, blocks)
    outer_across = send(pack, [(3, 0, 1), (0, 0, 2)])
    outer_next = send(pack, [(3, 1, 3), (0, -1, 0)])
    beside = send(pack, swap)

    node = local_tree_call(pack, rows, leaf_sets, merge_sets, dim)

    beside, node = lax.optimization_barrier((beside, node))
    group = lax.all_gather(node, "sub", axis=0)

    b = blocks
    own_base, beside_base = (b, 2 * b, 3 * b, 4 * b), (2 * b, b, 4 * b, 3 * b)
    early_base, early_beside_base = (5 * b, 4 * b, b, 0), (4 * b, 5 * b, 0, b)
    late_base, late_beside_base = (3 * b, 0, 5 * b, 2 * b), (0, 3 * b, 2 * b, 5 * b)
    single = (0, 0, 0, 0)
    acc = near_call(
        near_lists, near_counts, rows, None,
        [(own_base, single, [pack]), (beside_base, single, [beside])],
        dim, False, "near_first",
    )

    inner_pack, outer_across, outer_next, acc = lax.optimization_barrier(
        (pack, outer_across, outer_next, acc)
    )
    inner_across = send(inner_pack, [(2, 0, 0), (1, 0, 3)])
    forwarded = send(outer_across, [(1, 1, 1), (2, -1, 2)])
    place = lax.axis_index("sub")
    at_edge = (place == 0) | (place == sub_count - 1)
    early = jnp.where(at_edge, outer_next, outer_across)
    early_beside = send(early, swap)

    group, early = lax.optimization_barrier((group, early))
    node = merge_call(group, merge_sets, dim, blocks, "leaf")
    early_beside, node = lax.optimization_barrier((early_beside, node))
    group = lax.all_gather(node, "leaf", axis=0)
    acc = near_call(
        near_lists, near_counts, rows, acc,
        [(early_base, single, [early]), (early_beside_base, single, [early_beside])],
        dim, False, "near_second",
    )

    inner_across, forwarded, acc = lax.optimization_barrier((inner_across, forwarded, acc))
    late = jnp.where(at_edge, inner_across, forwarded)
    late_beside = send(late, swap)
    group, late = lax.optimization_barrier((group, late))
    piece = skel // (leaf_count * sub_count)
    node = merge_call(group, merge_sets, dim, blocks * sub_count, None, piece)
    if piece:
        root = node.reshape(-1)
    else:
        size = skel * LANES // (leaf_count * sub_count)
        rank = lax.axis_index("leaf") * sub_count + place
        root = lax.dynamic_slice_in_dim(node.reshape(-1), rank * size, size, 0)
    near = near_call(
        near_lists, near_counts, rows, acc,
        [(late_base, single, [late]), (late_beside_base, single, [late_beside])],
        dim, True, "near_last",
    )
    return near.reshape(npts, LANES), root


def solution(mesh):
    in_specs = (
        P(("leaf", "sub"), None),
        P(("leaf", "sub"), None),
        P(("leaf", "sub")),
        P(("leaf", "sub"), None),
        P(("leaf", "sub")),
        P(("leaf", "sub"), None),
        P(),
    )
    out_specs = (P(("leaf", "sub"), None), P(("leaf", "sub")))
    return jax.shard_map(
        on_device, mesh=mesh, in_specs=in_specs, out_specs=out_specs, check_vma=False
    )
```

```python
import functools

import jax
import jax.numpy as jnp
from jax import lax
from jax.experimental import pallas as pl
from jax.experimental.pallas import tpu as pltpu
from jax.sharding import PartitionSpec as P

LANES = 128
PARTS = 3
VMEM_BYTES = 24 * 1024 * 1024
F32 = jnp.float32
BF16 = jnp.bfloat16


def dot(a, b):
    return jnp.dot(a, b, preferred_element_type=F32)


def dot_t(a, b):
    return lax.dot_general(a, b, (((0,), (0,)), ((), ())), preferred_element_type=F32)


def split(x):
    hi = x.astype(BF16)
    return hi, (x - hi.astype(F32)).astype(BF16)


def square_rows(pts):
    x = pts.astype(F32)
    total = jnp.sum(x * x, axis=0, keepdims=True)
    hi = total.astype(BF16).astype(F32)
    mid = (total - hi).astype(BF16).astype(F32)
    low = total - hi - mid
    row = lax.broadcasted_iota(jnp.int32, (16, pts.shape[1]), 0)
    ones = jnp.where(row < 2 * PARTS, 1.0, 0.0)
    return jnp.where(row == 0, hi, jnp.where(row == 1, mid, jnp.where(row == 2, low, ones))).astype(BF16)


def form_map(dim, size):
    k = lax.broadcasted_iota(jnp.int32, (size, size), 0)
    j = lax.broadcasted_iota(jnp.int32, (size, size), 1)
    r = jnp.where((k == j) & (j < dim), 2.0 / dim, 0.0)
    r = jnp.where((j >= dim) & (j < dim + PARTS) & (k == j + PARTS), -1.0 / dim, r)
    r = jnp.where((j >= dim + PARTS) & (j < dim + 2 * PARTS) & (k == j - PARTS), -1.0 / dim, r)
    return r.astype(BF16)


def onehot_in(row, size):
    index = lax.broadcasted_iota(jnp.int32, (size, row.shape[1]), 0)
    return jnp.where(index == row, 1.0, 0.0).astype(BF16)


def column_of(row):
    return jnp.broadcast_to(row.astype(F32), (LANES, row.shape[1])).T


def onehot_out(column, size):
    lane = lax.broadcasted_iota(jnp.int32, column.shape, 1).astype(F32)
    return jnp.concatenate(
        [jnp.where(column == lane + float(i), 1.0, 0.0) for i in range(0, size, LANES)], axis=1
    )


def mix3(m, s):
    m_hi, m_lo = split(m)
    s_hi, s_lo = split(s)
    return dot(m_hi, s_hi) + (dot(m_hi, s_lo) + dot(m_lo, s_hi))


def order_kernel(points_t, order, probes, pack, rows, points_in, order_in, sems):
    dim = points_t.shape[0]
    many, leaf = rows.shape[:2]
    held = dim + 16
    order_copy = pltpu.make_async_copy(order, order_in, sems.at[0])
    order_copy.start()
    point_copies, probe_copies = [], []
    for b in range(many):
        span = pl.ds(b * leaf, leaf)
        copy = pltpu.make_async_copy(points_t.at[:, span], points_in.at[b], sems.at[1 + b])
        copy.start()
        point_copies.append(copy)
    for b in range(many):
        span = pl.ds(b * leaf, leaf)
        copy = pltpu.make_async_copy(
            probes.at[span], pack.at[b, pl.ds(0, leaf)], sems.at[1 + many + b]
        )
        copy.start()
        probe_copies.append(copy)
    to_rows = form_map(dim, LANES)
    order_copy.wait()
    for b in range(many):
        picks = onehot_in(order_in[b], leaf)
        point_copies[b].wait()
        tree_t = dot(points_in[b], picks).astype(BF16)
        form = jnp.concatenate([tree_t, square_rows(tree_t)], axis=0)
        for i in range(leaf // LANES):
            pack[b, leaf + i * held : leaf + (i + 1) * held, :] = form[:, i * LANES : (i + 1) * LANES]
        form = jnp.concatenate([form, jnp.zeros((LANES - held, leaf), BF16)], axis=0)
        rows[b] = dot_t(form, to_rows).astype(BF16)
    for copy in probe_copies:
        copy.wait()


def order_call(points_t, order, probes, blocks):
    dim, npts = points_t.shape
    leaf = npts // blocks
    packed = leaf + leaf // LANES * (dim + 16)
    return pl.pallas_call(
        order_kernel,
        in_specs=[pl.BlockSpec(memory_space=pltpu.HBM)] * 3,
        out_shape=[
            jax.ShapeDtypeStruct((blocks, packed, LANES), BF16),
            jax.ShapeDtypeStruct((blocks, leaf, LANES), BF16),
        ],
        scratch_shapes=[
            pltpu.VMEM((blocks, dim, leaf), BF16),
            pltpu.VMEM((blocks, 1, leaf), jnp.int32),
            pltpu.SemaphoreType.DMA((1 + 2 * blocks,)),
        ],
        compiler_params=pltpu.CompilerParams(vmem_limit_bytes=VMEM_BYTES),
        cost_estimate=pl.CostEstimate(
            flops=blocks * 2 * leaf * leaf * dim, bytes_accessed=10 * npts * LANES, transcendentals=0
        ),
        name="tree_order",
    )(points_t, order, probes)


def form_of(pack_block, leaf, dim):
    held = dim + 16
    columns = [
        pack_block[leaf + i * held : leaf + (i + 1) * held, :] for i in range(leaf // LANES)
    ]
    form = jnp.concatenate(columns, axis=1)
    return jnp.concatenate([form, jnp.zeros((LANES - held, leaf), BF16)], axis=0)


def condense(form, a_rows, chosen):
    size = form.shape[1]
    picks_out = onehot_out(column_of(chosen), size)
    new_rows = dot(picks_out.astype(BF16), a_rows).astype(BF16)
    new_form = dot(form, onehot_in(chosen, size)).astype(BF16)
    weights = jnp.exp(dot(new_rows, form))
    mixing = picks_out + weights / jnp.sum(weights, axis=1, keepdims=True)
    return new_form, new_rows, mixing


def local_tree_kernel(pack, rows, leaf_sets_in, merge_sets_in, out, leaf_sets, merge_sets, sems, *, dim):
    blocks, leaf = rows.shape[:2]
    leaf_copy = pltpu.make_async_copy(leaf_sets_in, leaf_sets, sems.at[0])
    merge_copy = pltpu.make_async_copy(merge_sets_in, merge_sets, sems.at[1])
    leaf_copy.start()
    merge_copy.start()
    leaf_copy.wait()
    first_block = (lax.axis_index("leaf") * lax.axis_size("sub") + lax.axis_index("sub")) * blocks

    nodes = []
    for b in range(blocks):
        form = form_of(pack.at[b], leaf, dim)
        new_form, new_rows, mixing = condense(form, rows[b], leaf_sets[b : b + 1, :])
        m_hi, m_lo = split(mixing)
        probes = pack[b, :leaf, :]
        nodes.append((new_form, new_rows, dot(m_hi, probes) + dot(m_lo, probes)))
    span = 1
    merge_copy.wait()
    while len(nodes) > 1:
        merged = []
        for k in range(len(nodes) // 2):
            left, right = nodes[2 * k], nodes[2 * k + 1]
            chosen = merge_sets[pl.ds(first_block + (2 * k + 1) * span - 1, 1), :]
            new_form, new_rows, mixing = condense(
                jnp.concatenate([left[0], right[0]], axis=1),
                jnp.concatenate([left[1], right[1]], axis=0),
                chosen,
            )
            samples = mix3(mixing, jnp.concatenate([left[2], right[2]], axis=0))
            merged.append((new_form, new_rows, samples))
        nodes = merged
        span *= 2
    held = dim + 16
    out[:held, :] = nodes[0][0][:held, :].astype(F32)
    out[held:, :] = nodes[0][2]


def local_tree_call(pack, rows, leaf_sets, merge_sets, dim):
    blocks, leaf = rows.shape[:2]
    skel = leaf_sets.shape[1]
    return pl.pallas_call(
        functools.partial(local_tree_kernel, dim=dim),
        in_specs=[pl.BlockSpec(memory_space=pltpu.VMEM)] * 2
        + [pl.BlockSpec(memory_space=pltpu.HBM)] * 2,
        out_shape=jax.ShapeDtypeStruct((dim + 16 + skel, LANES), F32),
        scratch_shapes=[
            pltpu.VMEM(leaf_sets.shape, jnp.int32),
            pltpu.VMEM(merge_sets.shape, jnp.int32),
            pltpu.SemaphoreType.DMA((2,)),
        ],
        compiler_params=pltpu.CompilerParams(vmem_limit_bytes=VMEM_BYTES),
        cost_estimate=pl.CostEstimate(
            flops=blocks * 8 * skel * leaf * LANES,
            bytes_accessed=6 * blocks * leaf * LANES,
            transcendentals=blocks * skel * leaf,
        ),
        name="local_tree",
    )(pack, rows, leaf_sets, merge_sets)


def merge_kernel(*refs, dim, blocks, shift, piece):
    merge_sets_in, out, group, merge_sets, sem = refs[-5:]
    parts = refs[:-5]
    count, size = group.shape[:2]
    copy = pltpu.make_async_copy(merge_sets_in, merge_sets, sem)
    copy.start()
    held = dim + 16
    skel = size - held
    rank = lax.axis_index("leaf") * lax.axis_size("sub") + lax.axis_index("sub")
    unit = lax.shift_right_logical(rank, shift)
    place = unit & (count - 1)
    first = unit - place
    span = blocks << shift
    for d, part in enumerate(parts):
        group[place ^ d] = part[...]
    to_rows = form_map(dim, LANES)
    forms = [group[i, :held, :].astype(BF16) for i in range(count)]
    samples = [group[i, held:, :] for i in range(count)]
    copy.wait()
    while len(forms) > 1:
        first = first // 2
        new_forms, new_samples = [], []
        for k in range(len(forms) // 2):
            chosen = merge_sets[pl.ds((2 * (first + k) + 1) * span - 1, 1), :]
            form = jnp.concatenate(forms[2 * k : 2 * k + 2], axis=1)
            form = jnp.concatenate([form, jnp.zeros((LANES - held, 2 * skel), BF16)], axis=0)
            new_form = dot(form, onehot_in(chosen, 2 * skel)).astype(BF16)
            new_rows = dot_t(new_form, to_rows).astype(BF16)
            weights = jnp.exp(dot(new_rows, form))
            picks = onehot_out(column_of(chosen), 2 * skel)
            mixing = picks + weights / jnp.sum(weights, axis=1, keepdims=True)
            new_forms.append(new_form[:held])
            new_samples.append(mix3(mixing, jnp.concatenate(samples[2 * k : 2 * k + 2], axis=0)))
        forms, samples = new_forms, new_samples
        span *= 2
    if piece is None:
        out[:held, :] = forms[0].astype(F32)
        out[held:, :] = samples[0]
    elif piece == 0:
        out[...] = samples[0]
    else:
        column = lax.broadcasted_iota(jnp.int32, (piece, skel), 1)
        row = lax.broadcasted_iota(jnp.int32, (piece, skel), 0) + rank * piece
        take = jnp.where(column == row, 1.0, 0.0).astype(BF16)
        hi, lo = split(samples[0])
        low = (samples[0] - hi.astype(F32) - lo.astype(F32)).astype(BF16)
        out[...] = dot(take, hi) + dot(take, lo) + dot(take, low)


def merge_call(parts, merge_sets, dim, blocks, shift, piece=None):
    count = len(parts)
    size = parts[0].shape[0]
    skel = size - dim - 16
    rows = size if piece is None else (piece or skel)
    return pl.pallas_call(
        functools.partial(merge_kernel, dim=dim, blocks=blocks, shift=shift, piece=piece),
        in_specs=[pl.BlockSpec(memory_space=pltpu.VMEM)] * count
        + [pl.BlockSpec(memory_space=pltpu.HBM)],
        out_shape=jax.ShapeDtypeStruct((rows, LANES), F32),
        scratch_shapes=[
            pltpu.VMEM((count, size, LANES), F32),
            pltpu.VMEM(merge_sets.shape, jnp.int32),
            pltpu.SemaphoreType.DMA(()),
        ],
        compiler_params=pltpu.CompilerParams(vmem_limit_bytes=16 * 1024 * 1024),
        cost_estimate=pl.CostEstimate(
            flops=count * 16 * LANES**3,
            bytes_accessed=4 * count * size * LANES,
            transcendentals=2 * count * LANES**2,
        ),
        name="tree_merge",
    )(*parts, merge_sets)


def near_kernel(*refs, slots, dim, has_acc, last):
    lists, counts, rows = refs[:3]
    refs = refs[3:]
    if has_acc:
        acc_in, refs = refs[0], refs[1:]
    buffers = []
    for _, which in slots:
        number = max(which) + 1
        buffers.append(refs[:number])
        refs = refs[number:]
    out, packs, pair_list, sems = refs
    blocks, leaf = rows.shape[:2]
    near = lists.shape[1]
    window = blocks * lax.axis_size("sub")
    start = lax.axis_index("leaf") * window - blocks
    sub = lax.axis_index("sub")

    def place(table):
        value = jnp.int32(table[0])
        for i in range(1, len(table)):
            value = jnp.where(sub == i, jnp.int32(table[i]), value)
        return value

    copies = []
    for slot, (bases, which) in enumerate(slots):
        target = packs.at[pl.ds(slot * blocks, blocks)]
        held = place(which)
        for number, buffer in enumerate(buffers[slot]):
            copy = pltpu.make_async_copy(buffer, target, sems.at[slot])
            if len(buffers[slot]) == 1:
                copy.start()
            else:
                pl.when(held == number)(copy.start)
        copies.append(copy)
    starts = [place(bases) for bases, _ in slots]

    if has_acc:
        acc_copy = pltpu.make_async_copy(acc_in, out, sems.at[len(slots)])
        acc_copy.start()
    else:
        out[...] = jnp.zeros(out.shape, F32)

    def list_block(g, found):
        used = counts[g]

        def list_slot(s, found):
            source = lists[g, s] - start
            local = jnp.int32(-1)
            for slot, first in enumerate(starts):
                inside = (source >= first) & (source < first + blocks)
                local = jnp.where(inside, source - first + slot * blocks, local)
            pair_list[found] = g * (len(slots) * blocks) + local
            return found + jnp.where((local >= 0) & (s < used), 1, 0)

        return lax.fori_loop(0, near, list_slot, found, unroll=True)

    pairs = lax.fori_loop(0, blocks, list_block, jnp.int32(0))

    for copy in copies:
        copy.wait()
    if has_acc:
        acc_copy.wait()

    half = leaf // 2

    def add_pair(i):
        code = pair_list[i]
        g = code // (len(slots) * blocks)
        local = code - g * (len(slots) * blocks)
        form = form_of(packs.at[local], leaf, dim)
        probes = packs[local, :leaf, :]
        total = None
        for c in range(0, leaf, half):
            weights = jnp.exp(dot(rows[g], form[:, c : c + half])).astype(BF16)
            term = dot(weights, probes[c : c + half])
            total = term if total is None else total + term
        return g, total

    def add_pairs(i, carry):
        found = [add_pair(2 * i), add_pair(2 * i + 1)]
        for g, total in found:
            out[g] += total
        return carry

    lax.fori_loop(0, pairs // 2, add_pairs, 0)

    @pl.when(pairs % 2 == 1)
    def _():
        g, total = add_pair(pairs - 1)
        out[g] += total

    if last:
        out[...] = out[...] * (leaf ** -0.5)


def near_call(lists, counts, rows, acc, sets, dim, last, name):
    blocks, leaf = rows.shape[:2]
    buffers = [b for _, _, bufs in sets for b in bufs]
    slots = tuple((bases, which) for bases, which, _ in sets)
    packed = buffers[0].shape[1]
    smem = pl.BlockSpec(memory_space=pltpu.SMEM)
    vmem = pl.BlockSpec(memory_space=pltpu.VMEM)
    args = [lists, counts, rows] + ([acc] if acc is not None else []) + buffers
    specs = [smem, smem, vmem]
    specs += [pl.BlockSpec(memory_space=pl.ANY)] * (len(buffers) + (acc is not None))
    total = len(slots) * blocks
    near = lists.shape[1]
    pairs = total * blocks // 8
    return pl.pallas_call(
        functools.partial(
            near_kernel, slots=slots, dim=dim, has_acc=acc is not None, last=last
        ),
        in_specs=specs,
        out_specs=vmem,
        out_shape=jax.ShapeDtypeStruct((blocks, leaf, LANES), F32),
        scratch_shapes=[
            pltpu.VMEM((total, packed, LANES), BF16),
            pltpu.SMEM((blocks * near + 8,), jnp.int32),
            pltpu.SemaphoreType.DMA((len(slots) + 1,)),
        ],
        compiler_params=pltpu.CompilerParams(vmem_limit_bytes=VMEM_BYTES),
        cost_estimate=pl.CostEstimate(
            flops=pairs * 2 * leaf * leaf * 256,
            bytes_accessed=total * packed * LANES * 2 + blocks * leaf * LANES * 8,
            transcendentals=pairs * leaf * leaf,
        ),
        name=name,
    )(*args)


def on_device(points, probes, order, near_lists, near_counts, leaf_sets, merge_sets):
    leaf_count = lax.axis_size("leaf")
    sub_count = lax.axis_size("sub")
    blocks, skel = leaf_sets.shape
    npts, dim = points.shape
    leaf = npts // blocks
    axes = ("leaf", "sub")

    def send(x, routes):
        pairs = []
        for place in range(leaf_count):
            for from_sub, step, to_sub in routes:
                if 0 <= place + step < leaf_count:
                    pairs.append((place * sub_count + from_sub, (place + step) * sub_count + to_sub))
        return lax.ppermute(x, axes, pairs)

    swap = [(0, 0, 1), (1, 0, 0), (2, 0, 3), (3, 0, 2)]
    pack, rows = order_call(points.T, order.reshape(blocks, 1, leaf), probes, blocks)
    outer_across = send(pack, [(3, 0, 1), (0, 0, 2)])
    outer_next = send(pack, [(3, 1, 3), (0, -1, 0)])
    beside = send(pack, swap)

    node = local_tree_call(pack, rows, leaf_sets, merge_sets, dim)

    count = leaf_count * sub_count
    bits = count.bit_length() - 1
    sub_bits = sub_count.bit_length() - 1

    def exchange(x, shift, stage_bits):
        parts = [x]
        for d in range(1, 1 << stage_bits):
            parts.append(lax.ppermute(x, axes, [(i, i ^ (d << shift)) for i in range(count)]))
        return parts

    b = blocks
    own_base, beside_base = (b, 2 * b, 3 * b, 4 * b), (2 * b, b, 4 * b, 3 * b)
    early_base, early_beside_base = (5 * b, 4 * b, b, 0), (4 * b, 5 * b, 0, b)
    late_base, late_beside_base = (3 * b, 0, 5 * b, 2 * b), (0, 3 * b, 2 * b, 5 * b)
    single, edge_first, edge_second = (0, 0, 0, 0), (0, 1, 1, 0), (1, 0, 0, 1)
    from_edge, from_inner = [(0, 0, 1), (3, 0, 2)], [(1, 0, 0), (2, 0, 3)]

    def tie(*values):
        return lax.optimization_barrier(values)

    beside, node = tie(beside, node)
    parts = exchange(node, 0, sub_bits)
    acc = near_call(
        near_lists, near_counts, rows, None,
        [(own_base, single, [pack]), (beside_base, single, [beside])],
        dim, False, "near_first",
    )

    *parts, acc = tie(*parts, acc)
    node = merge_call(parts, merge_sets, dim, blocks, 0)
    inner_pack, outer_across, outer_next, node = tie(pack, outer_across, outer_next, node)
    shift, stage_bits = sub_bits, min(2, bits - sub_bits)
    parts = exchange(node, shift, stage_bits)
    inner_across = send(inner_pack, [(2, 0, 0), (1, 0, 3)])
    forwarded = send(outer_across, [(1, 1, 1), (2, -1, 2)])
    next_beside = send(outer_next, from_edge)
    across_beside = send(outer_across, from_inner)
    acc = near_call(
        near_lists, near_counts, rows, acc,
        [
            (early_base, edge_first, [outer_next, outer_across]),
            (early_beside_base, edge_second, [next_beside, across_beside]),
        ],
        dim, False, "near_second",
    )

    *parts, inner_across, forwarded, acc = tie(*parts, inner_across, forwarded, acc)
    inner_beside = send(inner_across, from_edge)
    forwarded_beside = send(forwarded, from_inner)
    node = merge_call(parts, merge_sets, dim, blocks, shift)
    shift += stage_bits
    inner_beside, forwarded_beside, node = tie(inner_beside, forwarded_beside, node)
    parts = exchange(node, shift, bits - shift)
    near = near_call(
        near_lists, near_counts, rows, acc,
        [
            (late_base, edge_first, [inner_across, forwarded]),
            (late_beside_base, edge_second, [inner_beside, forwarded_beside]),
        ],
        dim, True, "near_last",
    )

    *parts, near = tie(*parts, near)
    piece = skel // count
    node = merge_call(parts, merge_sets, dim, blocks, shift, piece)
    if piece:
        root = node.reshape(-1)
    else:
        size = skel * LANES // count
        rank = lax.axis_index("leaf") * sub_count + lax.axis_index("sub")
        root = lax.dynamic_slice_in_dim(node.reshape(-1), rank * size, size, 0)
    return near.reshape(npts, LANES), root


def solution(mesh):
    in_specs = (
        P(("leaf", "sub"), None),
        P(("leaf", "sub"), None),
        P(("leaf", "sub")),
        P(("leaf", "sub"), None),
        P(("leaf", "sub")),
        P(("leaf", "sub"), None),
        P(),
    )
    out_specs = (P(("leaf", "sub"), None), P(("leaf", "sub")))
    return jax.shard_map(
        on_device, mesh=mesh, in_specs=in_specs, out_specs=out_specs, check_vma=False
    )
```

```python
import functools

import jax
import jax.numpy as jnp
from jax import lax
from jax.experimental import pallas as pl
from jax.experimental.pallas import tpu as pltpu
from jax.sharding import PartitionSpec as P

LANES = 128
PARTS = 3
VMEM_BYTES = 24 * 1024 * 1024
F32 = jnp.float32
BF16 = jnp.bfloat16


def dot(a, b):
    return jnp.dot(a, b, preferred_element_type=F32)


def dot_t(a, b):
    return lax.dot_general(a, b, (((0,), (0,)), ((), ())), preferred_element_type=F32)


def split(x):
    hi = x.astype(BF16)
    return hi, (x - hi.astype(F32)).astype(BF16)


def square_rows(pts):
    x = pts.astype(F32)
    total = jnp.sum(x * x, axis=0, keepdims=True)
    hi = total.astype(BF16).astype(F32)
    mid = (total - hi).astype(BF16).astype(F32)
    low = total - hi - mid
    row = lax.broadcasted_iota(jnp.int32, (16, pts.shape[1]), 0)
    ones = jnp.where(row < 2 * PARTS, 1.0, 0.0)
    return jnp.where(row == 0, hi, jnp.where(row == 1, mid, jnp.where(row == 2, low, ones))).astype(BF16)


def form_map(dim, size):
    k = lax.broadcasted_iota(jnp.int32, (size, size), 0)
    j = lax.broadcasted_iota(jnp.int32, (size, size), 1)
    r = jnp.where((k == j) & (j < dim), 2.0 / dim, 0.0)
    r = jnp.where((j >= dim) & (j < dim + PARTS) & (k == j + PARTS), -1.0 / dim, r)
    r = jnp.where((j >= dim + PARTS) & (j < dim + 2 * PARTS) & (k == j - PARTS), -1.0 / dim, r)
    return r.astype(BF16)


def onehot_in(row, size):
    index = lax.broadcasted_iota(jnp.int32, (size, row.shape[1]), 0)
    return jnp.where(index == row, 1.0, 0.0).astype(BF16)


def column_of(row):
    return jnp.broadcast_to(row.astype(F32), (LANES, row.shape[1])).T


def onehot_out(column, size):
    lane = lax.broadcasted_iota(jnp.int32, column.shape, 1).astype(F32)
    return jnp.concatenate(
        [jnp.where(column == lane + float(i), 1.0, 0.0) for i in range(0, size, LANES)], axis=1
    )


def mix3(m, s):
    m_hi, m_lo = split(m)
    s_hi, s_lo = split(s)
    return dot(m_hi, s_hi) + (dot(m_hi, s_lo) + dot(m_lo, s_hi))


def order_kernel(points_t, order, probes, pack, rows, points_in, order_in, forms_out, rows_out, sems):
    dim = points_t.shape[0]
    many, leaf = rows.shape[:2]
    held = dim + 16

    def begin(source, target, place):
        copy = pltpu.make_async_copy(source, target, sems.at[place])
        copy.start()
        return copy

    order_copy = begin(order, order_in, 0)
    arrivals = [
        begin(points_t.at[:, pl.ds(b * leaf, leaf)], points_in.at[b], 1 + b) for b in range(many)
    ]
    leaving = [
        begin(probes.at[pl.ds(b * leaf, leaf)], pack.at[b, pl.ds(0, leaf)], 1 + many + b)
        for b in range(many)
    ]
    to_rows = form_map(dim, LANES)
    order_copy.wait()
    for b in range(many):
        picks = onehot_in(order_in[b], leaf)
        arrivals[b].wait()
        tree_t = dot(points_in[b], picks).astype(BF16)
        form = jnp.concatenate([tree_t, square_rows(tree_t)], axis=0)
        for i in range(leaf // LANES):
            forms_out[b, i * held : (i + 1) * held, :] = form[:, i * LANES : (i + 1) * LANES]
        form = jnp.concatenate([form, jnp.zeros((LANES - held, leaf), BF16)], axis=0)
        rows_out[b] = dot_t(form, to_rows).astype(BF16)
        target = pack.at[b, pl.ds(leaf, leaf // LANES * held)]
        leaving.append(begin(forms_out.at[b], target, 1 + 2 * many + b))
        leaving.append(begin(rows_out.at[b], rows.at[b], 1 + 3 * many + b))
    for copy in leaving:
        copy.wait()


def order_call(points_t, order, probes, blocks):
    dim, npts = points_t.shape
    leaf = npts // blocks
    formed = leaf // LANES * (dim + 16)
    hbm = pl.BlockSpec(memory_space=pltpu.HBM)
    return pl.pallas_call(
        order_kernel,
        in_specs=[hbm] * 3,
        out_specs=[hbm] * 2,
        out_shape=[
            jax.ShapeDtypeStruct((blocks, leaf + formed, LANES), BF16),
            jax.ShapeDtypeStruct((blocks, leaf, LANES), BF16),
        ],
        scratch_shapes=[
            pltpu.VMEM((blocks, dim, leaf), BF16),
            pltpu.VMEM((blocks, 1, leaf), jnp.int32),
            pltpu.VMEM((blocks, formed, LANES), BF16),
            pltpu.VMEM((blocks, leaf, LANES), BF16),
            pltpu.SemaphoreType.DMA((1 + 4 * blocks,)),
        ],
        compiler_params=pltpu.CompilerParams(vmem_limit_bytes=60 * 1024 * 1024),
        cost_estimate=pl.CostEstimate(
            flops=blocks * 2 * leaf * leaf * dim, bytes_accessed=10 * npts * LANES, transcendentals=0
        ),
        name="tree_order",
    )(points_t, order, probes)


def form_of(pack_block, leaf, dim):
    held = dim + 16
    columns = [
        pack_block[leaf + i * held : leaf + (i + 1) * held, :] for i in range(leaf // LANES)
    ]
    form = jnp.concatenate(columns, axis=1)
    return jnp.concatenate([form, jnp.zeros((LANES - held, leaf), BF16)], axis=0)


def condense(form, a_rows, chosen):
    size = form.shape[1]
    picks_out = onehot_out(column_of(chosen), size)
    new_rows = dot(picks_out.astype(BF16), a_rows).astype(BF16)
    new_form = dot(form, onehot_in(chosen, size)).astype(BF16)
    weights = jnp.exp(dot(new_rows, form))
    mixing = picks_out + weights / jnp.sum(weights, axis=1, keepdims=True)
    return new_form, new_rows, mixing


def local_tree_kernel(pack, rows, leaf_sets_in, merge_sets_in, out, leaf_sets, merge_sets, sems, *, dim):
    blocks, leaf = rows.shape[:2]
    leaf_copy = pltpu.make_async_copy(leaf_sets_in, leaf_sets, sems.at[0])
    merge_copy = pltpu.make_async_copy(merge_sets_in, merge_sets, sems.at[1])
    leaf_copy.start()
    merge_copy.start()
    leaf_copy.wait()
    first_block = (lax.axis_index("leaf") * lax.axis_size("sub") + lax.axis_index("sub")) * blocks

    nodes = []
    for b in range(blocks):
        form = form_of(pack.at[b], leaf, dim)
        new_form, new_rows, mixing = condense(form, rows[b], leaf_sets[b : b + 1, :])
        m_hi, m_lo = split(mixing)
        probes = pack[b, :leaf, :]
        nodes.append((new_form, new_rows, dot(m_hi, probes) + dot(m_lo, probes)))
    span = 1
    merge_copy.wait()
    while len(nodes) > 1:
        merged = []
        for k in range(len(nodes) // 2):
            left, right = nodes[2 * k], nodes[2 * k + 1]
            chosen = merge_sets[pl.ds(first_block + (2 * k + 1) * span - 1, 1), :]
            new_form, new_rows, mixing = condense(
                jnp.concatenate([left[0], right[0]], axis=1),
                jnp.concatenate([left[1], right[1]], axis=0),
                chosen,
            )
            samples = mix3(mixing, jnp.concatenate([left[2], right[2]], axis=0))
            merged.append((new_form, new_rows, samples))
        nodes = merged
        span *= 2
    held = dim + 16
    out[:held, :] = nodes[0][0][:held, :].astype(F32)
    out[held:, :] = nodes[0][2]


def local_tree_call(pack, rows, leaf_sets, merge_sets, dim):
    blocks, leaf = rows.shape[:2]
    skel = leaf_sets.shape[1]
    return pl.pallas_call(
        functools.partial(local_tree_kernel, dim=dim),
        in_specs=[pl.BlockSpec(memory_space=pltpu.VMEM)] * 2
        + [pl.BlockSpec(memory_space=pltpu.HBM)] * 2,
        out_shape=jax.ShapeDtypeStruct((dim + 16 + skel, LANES), F32),
        scratch_shapes=[
            pltpu.VMEM(leaf_sets.shape, jnp.int32),
            pltpu.VMEM(merge_sets.shape, jnp.int32),
            pltpu.SemaphoreType.DMA((2,)),
        ],
        compiler_params=pltpu.CompilerParams(vmem_limit_bytes=VMEM_BYTES),
        cost_estimate=pl.CostEstimate(
            flops=blocks * 8 * skel * leaf * LANES,
            bytes_accessed=6 * blocks * leaf * LANES,
            transcendentals=blocks * skel * leaf,
        ),
        name="local_tree",
    )(pack, rows, leaf_sets, merge_sets)


def merge_kernel(*refs, dim, blocks, shift, piece):
    merge_sets_in, out, group, merge_sets, sem = refs[-5:]
    parts = refs[:-5]
    count, size = group.shape[:2]
    copy = pltpu.make_async_copy(merge_sets_in, merge_sets, sem)
    copy.start()
    held = dim + 16
    skel = size - held
    rank = lax.axis_index("leaf") * lax.axis_size("sub") + lax.axis_index("sub")
    unit = lax.shift_right_logical(rank, shift)
    place = unit & (count - 1)
    first = unit - place
    span = blocks << shift
    for d, part in enumerate(parts):
        group[place ^ d] = part[...]
    to_rows = form_map(dim, LANES)
    forms = [group[i, :held, :].astype(BF16) for i in range(count)]
    samples = [group[i, held:, :] for i in range(count)]
    copy.wait()
    while len(forms) > 1:
        first = first // 2
        new_forms, new_samples = [], []
        for k in range(len(forms) // 2):
            chosen = merge_sets[pl.ds((2 * (first + k) + 1) * span - 1, 1), :]
            form = jnp.concatenate(forms[2 * k : 2 * k + 2], axis=1)
            form = jnp.concatenate([form, jnp.zeros((LANES - held, 2 * skel), BF16)], axis=0)
            new_form = dot(form, onehot_in(chosen, 2 * skel)).astype(BF16)
            new_rows = dot_t(new_form, to_rows).astype(BF16)
            weights = jnp.exp(dot(new_rows, form))
            picks = onehot_out(column_of(chosen), 2 * skel)
            mixing = picks + weights / jnp.sum(weights, axis=1, keepdims=True)
            new_forms.append(new_form[:held])
            new_samples.append(mix3(mixing, jnp.concatenate(samples[2 * k : 2 * k + 2], axis=0)))
        forms, samples = new_forms, new_samples
        span *= 2
    if piece is None:
        out[:held, :] = forms[0].astype(F32)
        out[held:, :] = samples[0]
    elif piece == 0:
        out[...] = samples[0]
    else:
        column = lax.broadcasted_iota(jnp.int32, (piece, skel), 1)
        row = lax.broadcasted_iota(jnp.int32, (piece, skel), 0) + rank * piece
        take = jnp.where(column == row, 1.0, 0.0).astype(BF16)
        hi, lo = split(samples[0])
        low = (samples[0] - hi.astype(F32) - lo.astype(F32)).astype(BF16)
        out[...] = dot(take, hi) + dot(take, lo) + dot(take, low)


def merge_call(parts, merge_sets, dim, blocks, shift, piece=None):
    count = len(parts)
    size = parts[0].shape[0]
    skel = size - dim - 16
    rows = size if piece is None else (piece or skel)
    return pl.pallas_call(
        functools.partial(merge_kernel, dim=dim, blocks=blocks, shift=shift, piece=piece),
        in_specs=[pl.BlockSpec(memory_space=pltpu.VMEM)] * count
        + [pl.BlockSpec(memory_space=pltpu.HBM)],
        out_shape=jax.ShapeDtypeStruct((rows, LANES), F32),
        scratch_shapes=[
            pltpu.VMEM((count, size, LANES), F32),
            pltpu.VMEM(merge_sets.shape, jnp.int32),
            pltpu.SemaphoreType.DMA(()),
        ],
        compiler_params=pltpu.CompilerParams(vmem_limit_bytes=16 * 1024 * 1024),
        cost_estimate=pl.CostEstimate(
            flops=count * 16 * LANES**3,
            bytes_accessed=4 * count * size * LANES,
            transcendentals=2 * count * LANES**2,
        ),
        name="tree_merge",
    )(*parts, merge_sets)


def near_kernel(*refs, slots, dim, has_acc, last):
    lists, counts, rows = refs[:3]
    refs = refs[3:]
    if has_acc:
        acc_in, refs = refs[0], refs[1:]
    buffers = []
    for _, which in slots:
        number = max(which) + 1
        buffers.append(refs[:number])
        refs = refs[number:]
    out, packs, pair_list, sems = refs
    blocks, leaf = rows.shape[:2]
    near = lists.shape[1]
    window = blocks * lax.axis_size("sub")
    start = lax.axis_index("leaf") * window - blocks
    sub = lax.axis_index("sub")

    def place(table):
        value = jnp.int32(table[0])
        for i in range(1, len(table)):
            value = jnp.where(sub == i, jnp.int32(table[i]), value)
        return value

    copies = []
    for slot, (bases, which) in enumerate(slots):
        target = packs.at[pl.ds(slot * blocks, blocks)]
        held = place(which)
        for number, buffer in enumerate(buffers[slot]):
            copy = pltpu.make_async_copy(buffer, target, sems.at[slot])
            if len(buffers[slot]) == 1:
                copy.start()
            else:
                pl.when(held == number)(copy.start)
        copies.append(copy)
    starts = [place(bases) for bases, _ in slots]

    if has_acc:
        acc_copy = pltpu.make_async_copy(acc_in, out, sems.at[len(slots)])
        acc_copy.start()
    else:
        out[...] = jnp.zeros(out.shape, F32)

    def list_block(g, found):
        used = counts[g]

        def list_slot(s, found):
            source = lists[g, s] - start
            local = jnp.int32(-1)
            for slot, first in enumerate(starts):
                inside = (source >= first) & (source < first + blocks)
                local = jnp.where(inside, source - first + slot * blocks, local)
            pair_list[found] = g * (len(slots) * blocks) + local
            return found + jnp.where((local >= 0) & (s < used), 1, 0)

        return lax.fori_loop(0, near, list_slot, found, unroll=True)

    pairs = lax.fori_loop(0, blocks, list_block, jnp.int32(0))

    for copy in copies:
        copy.wait()
    if has_acc:
        acc_copy.wait()

    half = leaf // 2

    def add_pair(i):
        code = pair_list[i]
        g = code // (len(slots) * blocks)
        local = code - g * (len(slots) * blocks)
        form = form_of(packs.at[local], leaf, dim)
        probes = packs[local, :leaf, :]
        total = None
        for c in range(0, leaf, half):
            weights = jnp.exp(dot(rows[g], form[:, c : c + half])).astype(BF16)
            term = dot(weights, probes[c : c + half])
            total = term if total is None else total + term
        return g, total

    def add_pairs(i, carry):
        found = [add_pair(2 * i), add_pair(2 * i + 1)]
        for g, total in found:
            out[g] += total
        return carry

    lax.fori_loop(0, pairs // 2, add_pairs, 0)

    @pl.when(pairs % 2 == 1)
    def _():
        g, total = add_pair(pairs - 1)
        out[g] += total

    if last:
        out[...] = out[...] * (leaf ** -0.5)


def near_call(lists, counts, rows, acc, sets, dim, last, name):
    blocks, leaf = rows.shape[:2]
    buffers = [b for _, _, bufs in sets for b in bufs]
    slots = tuple((bases, which) for bases, which, _ in sets)
    packed = buffers[0].shape[1]
    smem = pl.BlockSpec(memory_space=pltpu.SMEM)
    vmem = pl.BlockSpec(memory_space=pltpu.VMEM)
    args = [lists, counts, rows] + ([acc] if acc is not None else []) + buffers
    specs = [smem, smem, vmem]
    specs += [pl.BlockSpec(memory_space=pl.ANY)] * (len(buffers) + (acc is not None))
    total = len(slots) * blocks
    near = lists.shape[1]
    pairs = total * blocks // 8
    return pl.pallas_call(
        functools.partial(
            near_kernel, slots=slots, dim=dim, has_acc=acc is not None, last=last
        ),
        in_specs=specs,
        out_specs=vmem,
        out_shape=jax.ShapeDtypeStruct((blocks, leaf, LANES), F32),
        scratch_shapes=[
            pltpu.VMEM((total, packed, LANES), BF16),
            pltpu.SMEM((blocks * near + 8,), jnp.int32),
            pltpu.SemaphoreType.DMA((len(slots) + 1,)),
        ],
        compiler_params=pltpu.CompilerParams(vmem_limit_bytes=VMEM_BYTES),
        cost_estimate=pl.CostEstimate(
            flops=pairs * 2 * leaf * leaf * 256,
            bytes_accessed=total * packed * LANES * 2 + blocks * leaf * LANES * 8,
            transcendentals=pairs * leaf * leaf,
        ),
        name=name,
    )(*args)


def on_device(points, probes, order, near_lists, near_counts, leaf_sets, merge_sets):
    leaf_count = lax.axis_size("leaf")
    sub_count = lax.axis_size("sub")
    blocks, skel = leaf_sets.shape
    npts, dim = points.shape
    leaf = npts // blocks
    axes = ("leaf", "sub")

    def send(x, routes):
        pairs = []
        for place in range(leaf_count):
            for from_sub, step, to_sub in routes:
                if 0 <= place + step < leaf_count:
                    pairs.append((place * sub_count + from_sub, (place + step) * sub_count + to_sub))
        return lax.ppermute(x, axes, pairs)

    swap = [(0, 0, 1), (1, 0, 0), (2, 0, 3), (3, 0, 2)]
    pack, rows = order_call(points.T, order.reshape(blocks, 1, leaf), probes, blocks)
    outer_across = send(pack, [(3, 0, 1), (0, 0, 2)])
    outer_next = send(pack, [(3, 1, 3), (0, -1, 0)])
    beside = send(pack, swap)

    node = local_tree_call(pack, rows, leaf_sets, merge_sets, dim)

    count = leaf_count * sub_count
    bits = count.bit_length() - 1
    sub_bits = sub_count.bit_length() - 1

    def exchange(x, shift, stage_bits):
        parts = [x]
        for d in range(1, 1 << stage_bits):
            parts.append(lax.ppermute(x, axes, [(i, i ^ (d << shift)) for i in range(count)]))
        return parts

    b = blocks
    own_base, beside_base = (b, 2 * b, 3 * b, 4 * b), (2 * b, b, 4 * b, 3 * b)
    early_base, early_beside_base = (5 * b, 4 * b, b, 0), (4 * b, 5 * b, 0, b)
    late_base, late_beside_base = (3 * b, 0, 5 * b, 2 * b), (0, 3 * b, 2 * b, 5 * b)
    single, edge_first, edge_second = (0, 0, 0, 0), (0, 1, 1, 0), (1, 0, 0, 1)
    from_edge, from_inner = [(0, 0, 1), (3, 0, 2)], [(1, 0, 0), (2, 0, 3)]

    def tie(*values):
        return lax.optimization_barrier(values)

    own_pack, node = tie(pack, node)
    parts = exchange(node, 0, sub_bits)
    acc = near_call(
        near_lists, near_counts, rows, None,
        [(own_base, single, [own_pack])],
        dim, False, "near_first",
    )

    *parts, inner_pack, outer_across, outer_next, acc = tie(
        *parts, own_pack, outer_across, outer_next, acc
    )
    inner_across = send(inner_pack, [(2, 0, 0), (1, 0, 3)])
    forwarded = send(outer_across, [(1, 1, 1), (2, -1, 2)])
    node = merge_call(parts, merge_sets, dim, blocks, 0)
    shift, stage_bits = sub_bits, min(2, bits - sub_bits)
    parts = exchange(node, shift, stage_bits)
    outer_next, outer_across, node = tie(outer_next, outer_across, node)
    next_beside = send(outer_next, from_edge)
    across_beside = send(outer_across, from_inner)
    beside, node = tie(beside, node)
    acc = near_call(
        near_lists, near_counts, rows, acc,
        [
            (beside_base, single, [beside]),
            (early_base, edge_first, [outer_next, outer_across]),
            (early_beside_base, edge_second, [next_beside, across_beside]),
        ],
        dim, False, "near_second",
    )

    *parts, inner_across, forwarded, acc = tie(*parts, inner_across, forwarded, acc)
    inner_beside = send(inner_across, from_edge)
    forwarded_beside = send(forwarded, from_inner)
    node = merge_call(parts, merge_sets, dim, blocks, shift)
    shift += stage_bits
    inner_beside, forwarded_beside, node = tie(inner_beside, forwarded_beside, node)
    parts = exchange(node, shift, bits - shift)
    near = near_call(
        near_lists, near_counts, rows, acc,
        [
            (late_base, edge_first, [inner_across, forwarded]),
            (late_beside_base, edge_second, [inner_beside, forwarded_beside]),
        ],
        dim, True, "near_last",
    )

    *parts, near = tie(*parts, near)
    piece = skel // count
    node = merge_call(parts, merge_sets, dim, blocks, shift, piece)
    if piece:
        root = node.reshape(-1)
    else:
        size = skel * LANES // count
        rank = lax.axis_index("leaf") * sub_count + lax.axis_index("sub")
        root = lax.dynamic_slice_in_dim(node.reshape(-1), rank * size, size, 0)
    return near.reshape(npts, LANES), root


def solution(mesh):
    in_specs = (
        P(("leaf", "sub"), None),
        P(("leaf", "sub"), None),
        P(("leaf", "sub")),
        P(("leaf", "sub"), None),
        P(("leaf", "sub")),
        P(("leaf", "sub"), None),
        P(),
    )
    out_specs = (P(("leaf", "sub"), None), P(("leaf", "sub")))
    return jax.shard_map(
        on_device, mesh=mesh, in_specs=in_specs, out_specs=out_specs, check_vma=False
    )
```

```python
import functools

import jax
import jax.numpy as jnp
from jax import lax
from jax.experimental import pallas as pl
from jax.experimental.pallas import tpu as pltpu
from jax.sharding import PartitionSpec as P

LANES = 128
PARTS = 3
VMEM_BYTES = 20 * 1024 * 1024
NEAR_BYTES = 24 * 1024 * 1024
F32 = jnp.float32
BF16 = jnp.bfloat16


def dot(a, b):
    return jnp.dot(a, b, preferred_element_type=F32)


def dot_t(a, b):
    return lax.dot_general(a, b, (((0,), (0,)), ((), ())), preferred_element_type=F32)


def split(x):
    hi = x.astype(BF16)
    return hi, (x - hi.astype(F32)).astype(BF16)


def square_rows(pts):
    x = pts.astype(F32)
    total = jnp.sum(x * x, axis=0, keepdims=True)
    hi = total.astype(BF16).astype(F32)
    mid = (total - hi).astype(BF16).astype(F32)
    low = total - hi - mid
    row = lax.broadcasted_iota(jnp.int32, (16, pts.shape[1]), 0)
    ones = jnp.where(row < 2 * PARTS, 1.0, 0.0)
    return jnp.where(row == 0, hi, jnp.where(row == 1, mid, jnp.where(row == 2, low, ones))).astype(BF16)


def form_map(dim, size):
    k = lax.broadcasted_iota(jnp.int32, (size, size), 0)
    j = lax.broadcasted_iota(jnp.int32, (size, size), 1)
    r = jnp.where((k == j) & (j < dim), 2.0 / dim, 0.0)
    r = jnp.where((j >= dim) & (j < dim + PARTS) & (k == j + PARTS), -1.0 / dim, r)
    r = jnp.where((j >= dim + PARTS) & (j < dim + 2 * PARTS) & (k == j - PARTS), -1.0 / dim, r)
    return r.astype(BF16)


def onehot_in(row, size):
    index = lax.broadcasted_iota(jnp.int32, (size, row.shape[1]), 0)
    return jnp.where(index == row, 1.0, 0.0).astype(BF16)


def column_of(row):
    return jnp.broadcast_to(row.astype(F32), (LANES, row.shape[1])).T


def onehot_out(column, size):
    lane = lax.broadcasted_iota(jnp.int32, column.shape, 1).astype(F32)
    return jnp.concatenate(
        [jnp.where(column == lane + float(i), 1.0, 0.0) for i in range(0, size, LANES)], axis=1
    )


def mix3(m, s):
    m_hi, m_lo = split(m)
    s_hi, s_lo = split(s)
    return dot(m_hi, s_hi) + (dot(m_hi, s_lo) + dot(m_lo, s_hi))


def order_kernel(points_t, order, probes, pack, rows):
    dim = points_t.shape[0]
    many, leaf = rows.shape[:2]
    held = dim + 16
    to_rows = form_map(dim, LANES)
    for b in range(many):
        picks = onehot_in(order[b], leaf)
        tree_t = dot(points_t[:, b * leaf : (b + 1) * leaf], picks).astype(BF16)
        pack[b, :leaf, :] = probes[b * leaf : (b + 1) * leaf, :]
        form = jnp.concatenate([tree_t, square_rows(tree_t)], axis=0)
        for i in range(leaf // LANES):
            pack[b, leaf + i * held : leaf + (i + 1) * held, :] = form[:, i * LANES : (i + 1) * LANES]
        form = jnp.concatenate([form, jnp.zeros((LANES - held, leaf), BF16)], axis=0)
        rows[b] = dot_t(form, to_rows).astype(BF16)


def order_call(points_t, order, probes, blocks):
    dim, npts = points_t.shape
    leaf = npts // blocks
    packed = leaf + leaf // LANES * (dim + 16)
    many = 4 if blocks % 4 == 0 else 1
    return pl.pallas_call(
        order_kernel,
        grid=(blocks // many,),
        in_specs=[
            pl.BlockSpec((dim, many * leaf), lambda b: (0, b)),
            pl.BlockSpec((many, 1, leaf), lambda b: (b, 0, 0)),
            pl.BlockSpec((many * leaf, LANES), lambda b: (b, 0)),
        ],
        out_specs=[
            pl.BlockSpec((many, packed, LANES), lambda b: (b, 0, 0)),
            pl.BlockSpec((many, leaf, LANES), lambda b: (b, 0, 0)),
        ],
        out_shape=[
            jax.ShapeDtypeStruct((blocks, packed, LANES), BF16),
            jax.ShapeDtypeStruct((blocks, leaf, LANES), BF16),
        ],
        compiler_params=pltpu.CompilerParams(vmem_limit_bytes=VMEM_BYTES),
        cost_estimate=pl.CostEstimate(
            flops=blocks * 2 * leaf * leaf * dim, bytes_accessed=10 * npts * LANES, transcendentals=0
        ),
        name="tree_order",
    )(points_t, order, probes)


def form_of(pack_block, leaf, dim):
    held = dim + 16
    columns = [
        pack_block[leaf + i * held : leaf + (i + 1) * held, :] for i in range(leaf // LANES)
    ]
    form = jnp.concatenate(columns, axis=1)
    return jnp.concatenate([form, jnp.zeros((LANES - held, leaf), BF16)], axis=0)


def condense(form, a_rows, chosen):
    size = form.shape[1]
    picks_out = onehot_out(column_of(chosen), size)
    new_rows = dot(picks_out.astype(BF16), a_rows).astype(BF16)
    new_form = dot(form, onehot_in(chosen, size)).astype(BF16)
    weights = jnp.exp(dot(new_rows, form))
    mixing = picks_out + weights / jnp.sum(weights, axis=1, keepdims=True)
    return new_form, new_rows, mixing


def local_tree_kernel(pack, rows, leaf_sets_in, merge_sets_in, out, leaf_sets, merge_sets, sems, *, dim):
    blocks, leaf = rows.shape[:2]
    leaf_copy = pltpu.make_async_copy(leaf_sets_in, leaf_sets, sems.at[0])
    merge_copy = pltpu.make_async_copy(merge_sets_in, merge_sets, sems.at[1])
    leaf_copy.start()
    merge_copy.start()
    leaf_copy.wait()
    first_block = (lax.axis_index("leaf") * lax.axis_size("sub") + lax.axis_index("sub")) * blocks

    nodes = []
    for b in range(blocks):
        form = form_of(pack.at[b], leaf, dim)
        new_form, new_rows, mixing = condense(form, rows[b], leaf_sets[b : b + 1, :])
        m_hi, m_lo = split(mixing)
        probes = pack[b, :leaf, :]
        nodes.append((new_form, new_rows, dot(m_hi, probes) + dot(m_lo, probes)))
    span = 1
    merge_copy.wait()
    while len(nodes) > 1:
        merged = []
        for k in range(len(nodes) // 2):
            left, right = nodes[2 * k], nodes[2 * k + 1]
            chosen = merge_sets[pl.ds(first_block + (2 * k + 1) * span - 1, 1), :]
            new_form, new_rows, mixing = condense(
                jnp.concatenate([left[0], right[0]], axis=1),
                jnp.concatenate([left[1], right[1]], axis=0),
                chosen,
            )
            samples = mix3(mixing, jnp.concatenate([left[2], right[2]], axis=0))
            merged.append((new_form, new_rows, samples))
        nodes = merged
        span *= 2
    held = dim + 16
    out[:held, :] = nodes[0][0][:held, :].astype(F32)
    out[held:, :] = nodes[0][2]


def local_tree_call(pack, rows, leaf_sets, merge_sets, dim):
    blocks, leaf = rows.shape[:2]
    skel = leaf_sets.shape[1]
    return pl.pallas_call(
        functools.partial(local_tree_kernel, dim=dim),
        in_specs=[pl.BlockSpec(memory_space=pltpu.VMEM)] * 2
        + [pl.BlockSpec(memory_space=pltpu.HBM)] * 2,
        out_shape=jax.ShapeDtypeStruct((dim + 16 + skel, LANES), F32),
        scratch_shapes=[
            pltpu.VMEM(leaf_sets.shape, jnp.int32),
            pltpu.VMEM(merge_sets.shape, jnp.int32),
            pltpu.SemaphoreType.DMA((2,)),
        ],
        compiler_params=pltpu.CompilerParams(vmem_limit_bytes=VMEM_BYTES),
        cost_estimate=pl.CostEstimate(
            flops=blocks * 8 * skel * leaf * LANES,
            bytes_accessed=6 * blocks * leaf * LANES,
            transcendentals=blocks * skel * leaf,
        ),
        name="local_tree",
    )(pack, rows, leaf_sets, merge_sets)


def merge_kernel(*refs, dim, blocks, shift, piece):
    merge_sets_in, out, group, merge_sets, sem = refs[-5:]
    parts = refs[:-5]
    count, size = group.shape[:2]
    copy = pltpu.make_async_copy(merge_sets_in, merge_sets, sem)
    copy.start()
    held = dim + 16
    skel = size - held
    rank = lax.axis_index("leaf") * lax.axis_size("sub") + lax.axis_index("sub")
    unit = lax.shift_right_logical(rank, shift)
    place = unit & (count - 1)
    first = unit - place
    span = blocks << shift
    for d, part in enumerate(parts):
        group[place ^ d] = part[...]
    to_rows = form_map(dim, LANES)
    forms = [group[i, :held, :].astype(BF16) for i in range(count)]
    samples = [group[i, held:, :] for i in range(count)]
    copy.wait()
    while len(forms) > 1:
        first = first // 2
        new_forms, new_samples = [], []
        for k in range(len(forms) // 2):
            chosen = merge_sets[pl.ds((2 * (first + k) + 1) * span - 1, 1), :]
            form = jnp.concatenate(forms[2 * k : 2 * k + 2], axis=1)
            form = jnp.concatenate([form, jnp.zeros((LANES - held, 2 * skel), BF16)], axis=0)
            new_form = dot(form, onehot_in(chosen, 2 * skel)).astype(BF16)
            new_rows = dot_t(new_form, to_rows).astype(BF16)
            weights = jnp.exp(dot(new_rows, form))
            picks = onehot_out(column_of(chosen), 2 * skel)
            mixing = picks + weights / jnp.sum(weights, axis=1, keepdims=True)
            new_forms.append(new_form[:held])
            new_samples.append(mix3(mixing, jnp.concatenate(samples[2 * k : 2 * k + 2], axis=0)))
        forms, samples = new_forms, new_samples
        span *= 2
    if piece is None:
        out[:held, :] = forms[0].astype(F32)
        out[held:, :] = samples[0]
    elif piece == 0:
        out[...] = samples[0]
    else:
        column = lax.broadcasted_iota(jnp.int32, (piece, skel), 1)
        row = lax.broadcasted_iota(jnp.int32, (piece, skel), 0) + rank * piece
        take = jnp.where(column == row, 1.0, 0.0).astype(BF16)
        hi, lo = split(samples[0])
        low = (samples[0] - hi.astype(F32) - lo.astype(F32)).astype(BF16)
        out[...] = dot(take, hi) + dot(take, lo) + dot(take, low)


def merge_call(parts, merge_sets, dim, blocks, shift, piece=None):
    count = len(parts)
    size = parts[0].shape[0]
    skel = size - dim - 16
    rows = size if piece is None else (piece or skel)
    return pl.pallas_call(
        functools.partial(merge_kernel, dim=dim, blocks=blocks, shift=shift, piece=piece),
        in_specs=[pl.BlockSpec(memory_space=pltpu.VMEM)] * count
        + [pl.BlockSpec(memory_space=pltpu.HBM)],
        out_shape=jax.ShapeDtypeStruct((rows, LANES), F32),
        scratch_shapes=[
            pltpu.VMEM((count, size, LANES), F32),
            pltpu.VMEM(merge_sets.shape, jnp.int32),
            pltpu.SemaphoreType.DMA(()),
        ],
        compiler_params=pltpu.CompilerParams(vmem_limit_bytes=16 * 1024 * 1024),
        cost_estimate=pl.CostEstimate(
            flops=count * 16 * LANES**3,
            bytes_accessed=4 * count * size * LANES,
            transcendentals=2 * count * LANES**2,
        ),
        name="tree_merge",
    )(*parts, merge_sets)


def near_kernel(*refs, slots, dim, has_acc, last):
    lists, counts, rows = refs[:3]
    refs = refs[3:]
    if has_acc:
        acc_in, refs = refs[0], refs[1:]
    buffers = []
    for _, which in slots:
        number = max(which) + 1
        buffers.append(refs[:number])
        refs = refs[number:]
    out, pair_list = refs
    blocks, leaf = rows.shape[:2]
    near = lists.shape[1]
    window = blocks * lax.axis_size("sub")
    start = lax.axis_index("leaf") * window - blocks
    sub = lax.axis_index("sub")

    def place(table):
        value = jnp.int32(table[0])
        for i in range(1, len(table)):
            value = jnp.where(sub == i, jnp.int32(table[i]), value)
        return value

    starts = [start + place(bases) for bases, _ in slots]
    stride = blocks * near + 8

    def list_block(g, found):
        used = counts[g]

        def list_slot(s, found):
            source = lists[g, s]
            after = []
            for slot, first in enumerate(starts):
                pair_list[slot * stride + found[slot]] = g * blocks + source - first
                inside = (source >= first) & (source < first + blocks) & (s < used)
                after.append(found[slot] + jnp.where(inside, 1, 0))
            return tuple(after)

        return lax.fori_loop(0, near, list_slot, found, unroll=True)

    found = lax.fori_loop(0, blocks, list_block, (jnp.int32(0),) * len(slots))
    if has_acc:
        out[...] = acc_in[...]
    else:
        out[...] = jnp.zeros(out.shape, F32)

    half = leaf // 2

    def add_all(buffer, first, pairs):
        def add_pair(i):
            code = pair_list[first + i]
            g = code // blocks
            local = code - g * blocks
            form = form_of(buffer.at[local], leaf, dim)
            probes = buffer[local, :leaf, :]
            total = None
            for c in range(0, leaf, half):
                weights = jnp.exp(dot(rows[g], form[:, c : c + half])).astype(BF16)
                term = dot(weights, probes[c : c + half])
                total = term if total is None else total + term
            return g, total

        def add_pairs(i, carry):
            for g, total in [add_pair(2 * i), add_pair(2 * i + 1)]:
                out[g] += total
            return carry

        lax.fori_loop(0, pairs // 2, add_pairs, 0)

        @pl.when(pairs % 2 == 1)
        def _():
            g, total = add_pair(pairs - 1)
            out[g] += total

    for slot, (_, which) in enumerate(slots):
        if len(buffers[slot]) == 1:
            add_all(buffers[slot][0], slot * stride, found[slot])
        else:
            held = place(which)
            for number, buffer in enumerate(buffers[slot]):
                add_all(buffer, slot * stride, jnp.where(held == number, found[slot], 0))
    if last:
        out[...] = out[...] * (leaf ** -0.5)


def near_call(lists, counts, rows, acc, sets, dim, last, name):
    blocks, leaf = rows.shape[:2]
    buffers = [b for _, _, bufs in sets for b in bufs]
    slots = tuple((bases, which) for bases, which, _ in sets)
    packed = buffers[0].shape[1]
    smem = pl.BlockSpec(memory_space=pltpu.SMEM)
    vmem = pl.BlockSpec(memory_space=pltpu.VMEM)
    args = [lists, counts, rows] + ([acc] if acc is not None else []) + buffers
    total = len(slots) * blocks
    near = lists.shape[1]
    pairs = total * blocks // 8
    return pl.pallas_call(
        functools.partial(
            near_kernel, slots=slots, dim=dim, has_acc=acc is not None, last=last
        ),
        in_specs=[smem, smem] + [vmem] * (len(args) - 2),
        out_specs=vmem,
        out_shape=jax.ShapeDtypeStruct((blocks, leaf, LANES), F32),
        scratch_shapes=[pltpu.SMEM((len(slots) * (blocks * near + 8),), jnp.int32)],
        compiler_params=pltpu.CompilerParams(vmem_limit_bytes=NEAR_BYTES),
        cost_estimate=pl.CostEstimate(
            flops=pairs * 2 * leaf * leaf * 256,
            bytes_accessed=total * packed * LANES * 2 + blocks * leaf * LANES * 8,
            transcendentals=pairs * leaf * leaf,
        ),
        name=name,
    )(*args)


def on_device(points, probes, order, near_lists, near_counts, leaf_sets, merge_sets):
    leaf_count = lax.axis_size("leaf")
    sub_count = lax.axis_size("sub")
    blocks, skel = leaf_sets.shape
    npts, dim = points.shape
    leaf = npts // blocks
    axes = ("leaf", "sub")

    def send(x, routes):
        pairs = []
        for place in range(leaf_count):
            for from_sub, step, to_sub in routes:
                if 0 <= place + step < leaf_count:
                    pairs.append((place * sub_count + from_sub, (place + step) * sub_count + to_sub))
        return lax.ppermute(x, axes, pairs)

    swap = [(0, 0, 1), (1, 0, 0), (2, 0, 3), (3, 0, 2)]
    pack, rows = order_call(points.T, order.reshape(blocks, 1, leaf), probes, blocks)
    outer_across = send(pack, [(3, 0, 1), (0, 0, 2)])
    outer_next = send(pack, [(3, 1, 3), (0, -1, 0)])
    beside = send(pack, swap)

    node = local_tree_call(pack, rows, leaf_sets, merge_sets, dim)

    count = leaf_count * sub_count
    bits = count.bit_length() - 1
    sub_bits = sub_count.bit_length() - 1

    def exchange(x, shift, stage_bits):
        parts = [x]
        for d in range(1, 1 << stage_bits):
            parts.append(lax.ppermute(x, axes, [(i, i ^ (d << shift)) for i in range(count)]))
        return parts

    b = blocks
    own_base, beside_base = (b, 2 * b, 3 * b, 4 * b), (2 * b, b, 4 * b, 3 * b)
    early_base, early_beside_base = (5 * b, 4 * b, b, 0), (4 * b, 5 * b, 0, b)
    late_base, late_beside_base = (3 * b, 0, 5 * b, 2 * b), (0, 3 * b, 2 * b, 5 * b)
    single, edge_first, edge_second = (0, 0, 0, 0), (0, 1, 1, 0), (1, 0, 0, 1)
    from_edge, from_inner = [(0, 0, 1), (3, 0, 2)], [(1, 0, 0), (2, 0, 3)]

    def tie(*values):
        return lax.optimization_barrier(values)

    own_pack, node = tie(pack, node)
    parts = exchange(node, 0, sub_bits)
    acc = near_call(
        near_lists, near_counts, rows, None,
        [(own_base, single, [own_pack])],
        dim, False, "near_first",
    )

    *parts, inner_pack, acc = tie(*parts, own_pack, acc)
    inner_across = send(inner_pack, [(2, 0, 0), (1, 0, 3)])
    node = merge_call(parts, merge_sets, dim, blocks, 0)
    shift, stage_bits = sub_bits, min(2, bits - sub_bits)
    parts = exchange(node, shift, stage_bits)
    *parts, outer_across, outer_next = tie(*parts, outer_across, outer_next)
    forwarded = send(outer_across, [(1, 1, 1), (2, -1, 2)])
    next_beside = send(outer_next, from_edge)
    across_beside = send(outer_across, from_inner)
    node = merge_call(parts, merge_sets, dim, blocks, shift)
    shift += stage_bits
    beside, node = tie(beside, node)
    parts = exchange(node, shift, bits - shift)
    acc = near_call(
        near_lists, near_counts, rows, acc,
        [
            (beside_base, single, [beside]),
            (early_base, edge_first, [outer_next, outer_across]),
        ],
        dim, False, "near_second",
    )

    inner_across, forwarded, acc = tie(inner_across, forwarded, acc)
    inner_beside = send(inner_across, from_edge)
    forwarded_beside = send(forwarded, from_inner)
    acc = near_call(
        near_lists, near_counts, rows, acc,
        [
            (early_beside_base, edge_second, [next_beside, across_beside]),
            (late_base, edge_first, [inner_across, forwarded]),
        ],
        dim, False, "near_third",
    )
    near = near_call(
        near_lists, near_counts, rows, acc,
        [(late_beside_base, edge_second, [inner_beside, forwarded_beside])],
        dim, True, "near_last",
    )

    *parts, near = tie(*parts, near)
    piece = skel // count
    node = merge_call(parts, merge_sets, dim, blocks, shift, piece)
    if piece:
        root = node.reshape(-1)
    else:
        size = skel * LANES // count
        rank = lax.axis_index("leaf") * sub_count + lax.axis_index("sub")
        root = lax.dynamic_slice_in_dim(node.reshape(-1), rank * size, size, 0)
    return near.reshape(npts, LANES), root


def solution(mesh):
    in_specs = (
        P(("leaf", "sub"), None),
        P(("leaf", "sub"), None),
        P(("leaf", "sub")),
        P(("leaf", "sub"), None),
        P(("leaf", "sub")),
        P(("leaf", "sub"), None),
        P(),
    )
    out_specs = (P(("leaf", "sub"), None), P(("leaf", "sub")))
    return jax.shard_map(
        on_device, mesh=mesh, in_specs=in_specs, out_specs=out_specs, check_vma=False
    )
```

```python
import functools

import jax
import jax.numpy as jnp
from jax import lax
from jax.experimental import pallas as pl
from jax.experimental.pallas import tpu as pltpu
from jax.sharding import PartitionSpec as P

LANES = 128
PARTS = 3
VMEM_BYTES = 20 * 1024 * 1024
NEAR_BYTES = 24 * 1024 * 1024
F32 = jnp.float32
BF16 = jnp.bfloat16


def dot(a, b):
    return jnp.dot(a, b, preferred_element_type=F32)


def dot_t(a, b):
    return lax.dot_general(a, b, (((0,), (0,)), ((), ())), preferred_element_type=F32)


def split(x):
    hi = x.astype(BF16)
    return hi, (x - hi.astype(F32)).astype(BF16)


def square_rows(pts):
    x = pts.astype(F32)
    total = jnp.sum(x * x, axis=0, keepdims=True)
    hi = total.astype(BF16).astype(F32)
    mid = (total - hi).astype(BF16).astype(F32)
    low = total - hi - mid
    row = lax.broadcasted_iota(jnp.int32, (16, pts.shape[1]), 0)
    ones = jnp.where(row < 2 * PARTS, 1.0, 0.0)
    return jnp.where(row == 0, hi, jnp.where(row == 1, mid, jnp.where(row == 2, low, ones))).astype(BF16)


def form_map(dim, size):
    k = lax.broadcasted_iota(jnp.int32, (size, size), 0)
    j = lax.broadcasted_iota(jnp.int32, (size, size), 1)
    r = jnp.where((k == j) & (j < dim), 2.0 / dim, 0.0)
    r = jnp.where((j >= dim) & (j < dim + PARTS) & (k == j + PARTS), -1.0 / dim, r)
    r = jnp.where((j >= dim + PARTS) & (j < dim + 2 * PARTS) & (k == j - PARTS), -1.0 / dim, r)
    return r.astype(BF16)


def onehot_in(row, size):
    index = lax.broadcasted_iota(jnp.int32, (size, row.shape[1]), 0)
    return jnp.where(index == row, 1.0, 0.0).astype(BF16)


def column_of(row):
    return jnp.broadcast_to(row.astype(F32), (LANES, row.shape[1])).T


def onehot_out(column, size):
    lane = lax.broadcasted_iota(jnp.int32, column.shape, 1).astype(F32)
    return jnp.concatenate(
        [jnp.where(column == lane + float(i), 1.0, 0.0) for i in range(0, size, LANES)], axis=1
    )


def mix3(m, s):
    m_hi, m_lo = split(m)
    s_hi, s_lo = split(s)
    return dot(m_hi, s_hi) + (dot(m_hi, s_lo) + dot(m_lo, s_hi))


def order_kernel(points_t, order, probes, pack, rows):
    dim = points_t.shape[0]
    many, leaf = rows.shape[:2]
    held = dim + 16
    to_rows = form_map(dim, LANES)
    for b in range(many):
        picks = onehot_in(order[b], leaf)
        tree_t = dot(points_t[:, b * leaf : (b + 1) * leaf], picks).astype(BF16)
        pack[b, :leaf, :] = probes[b * leaf : (b + 1) * leaf, :]
        form = jnp.concatenate([tree_t, square_rows(tree_t)], axis=0)
        for i in range(leaf // LANES):
            pack[b, leaf + i * held : leaf + (i + 1) * held, :] = form[:, i * LANES : (i + 1) * LANES]
        form = jnp.concatenate([form, jnp.zeros((LANES - held, leaf), BF16)], axis=0)
        rows[b] = dot_t(form, to_rows).astype(BF16)


def order_call(points_t, order, probes, blocks):
    dim, npts = points_t.shape
    leaf = npts // blocks
    packed = leaf + leaf // LANES * (dim + 16)
    many = 4 if blocks % 4 == 0 else 1
    return pl.pallas_call(
        order_kernel,
        grid=(blocks // many,),
        in_specs=[
            pl.BlockSpec((dim, many * leaf), lambda b: (0, b)),
            pl.BlockSpec((many, 1, leaf), lambda b: (b, 0, 0)),
            pl.BlockSpec((many * leaf, LANES), lambda b: (b, 0)),
        ],
        out_specs=[
            pl.BlockSpec((many, packed, LANES), lambda b: (b, 0, 0)),
            pl.BlockSpec((many, leaf, LANES), lambda b: (b, 0, 0)),
        ],
        out_shape=[
            jax.ShapeDtypeStruct((blocks, packed, LANES), BF16),
            jax.ShapeDtypeStruct((blocks, leaf, LANES), BF16),
        ],
        compiler_params=pltpu.CompilerParams(vmem_limit_bytes=VMEM_BYTES),
        cost_estimate=pl.CostEstimate(
            flops=blocks * 2 * leaf * leaf * dim, bytes_accessed=10 * npts * LANES, transcendentals=0
        ),
        name="tree_order",
    )(points_t, order, probes)


def form_of(pack_block, leaf, dim):
    held = dim + 16
    columns = [
        pack_block[leaf + i * held : leaf + (i + 1) * held, :] for i in range(leaf // LANES)
    ]
    form = jnp.concatenate(columns, axis=1)
    return jnp.concatenate([form, jnp.zeros((LANES - held, leaf), BF16)], axis=0)


def condense(form, a_rows, chosen):
    size = form.shape[1]
    picks_out = onehot_out(column_of(chosen), size)
    new_rows = dot(picks_out.astype(BF16), a_rows).astype(BF16)
    new_form = dot(form, onehot_in(chosen, size)).astype(BF16)
    weights = jnp.exp(dot(new_rows, form))
    mixing = picks_out + weights / jnp.sum(weights, axis=1, keepdims=True)
    return new_form, new_rows, mixing


def local_tree_kernel(pack, rows, leaf_sets_in, merge_sets_in, out, leaf_sets, merge_sets, sems, *, dim):
    blocks, leaf = rows.shape[:2]
    leaf_copy = pltpu.make_async_copy(leaf_sets_in, leaf_sets, sems.at[0])
    merge_copy = pltpu.make_async_copy(merge_sets_in, merge_sets, sems.at[1])
    leaf_copy.start()
    merge_copy.start()
    leaf_copy.wait()
    first_block = (lax.axis_index("leaf") * lax.axis_size("sub") + lax.axis_index("sub")) * blocks

    nodes = []
    for b in range(blocks):
        form = form_of(pack.at[b], leaf, dim)
        new_form, new_rows, mixing = condense(form, rows[b], leaf_sets[b : b + 1, :])
        m_hi, m_lo = split(mixing)
        probes = pack[b, :leaf, :]
        nodes.append((new_form, new_rows, dot(m_hi, probes) + dot(m_lo, probes)))
    span = 1
    merge_copy.wait()
    while len(nodes) > 1:
        merged = []
        for k in range(len(nodes) // 2):
            left, right = nodes[2 * k], nodes[2 * k + 1]
            chosen = merge_sets[pl.ds(first_block + (2 * k + 1) * span - 1, 1), :]
            new_form, new_rows, mixing = condense(
                jnp.concatenate([left[0], right[0]], axis=1),
                jnp.concatenate([left[1], right[1]], axis=0),
                chosen,
            )
            samples = mix3(mixing, jnp.concatenate([left[2], right[2]], axis=0))
            merged.append((new_form, new_rows, samples))
        nodes = merged
        span *= 2
    held = dim + 16
    out[:held, :] = nodes[0][0][:held, :].astype(F32)
    out[held:, :] = nodes[0][2]


def local_tree_call(pack, rows, leaf_sets, merge_sets, dim):
    blocks, leaf = rows.shape[:2]
    skel = leaf_sets.shape[1]
    return pl.pallas_call(
        functools.partial(local_tree_kernel, dim=dim),
        in_specs=[pl.BlockSpec(memory_space=pltpu.VMEM)] * 2
        + [pl.BlockSpec(memory_space=pltpu.HBM)] * 2,
        out_shape=jax.ShapeDtypeStruct((dim + 16 + skel, LANES), F32),
        scratch_shapes=[
            pltpu.VMEM(leaf_sets.shape, jnp.int32),
            pltpu.VMEM(merge_sets.shape, jnp.int32),
            pltpu.SemaphoreType.DMA((2,)),
        ],
        compiler_params=pltpu.CompilerParams(vmem_limit_bytes=VMEM_BYTES),
        cost_estimate=pl.CostEstimate(
            flops=blocks * 8 * skel * leaf * LANES,
            bytes_accessed=6 * blocks * leaf * LANES,
            transcendentals=blocks * skel * leaf,
        ),
        name="local_tree",
    )(pack, rows, leaf_sets, merge_sets)


def merge_kernel(*refs, dim, blocks, shift, piece):
    merge_sets_in, out, group, merge_sets, sem = refs[-5:]
    parts = refs[:-5]
    count, size = group.shape[:2]
    copy = pltpu.make_async_copy(merge_sets_in, merge_sets, sem)
    copy.start()
    held = dim + 16
    skel = size - held
    rank = lax.axis_index("leaf") * lax.axis_size("sub") + lax.axis_index("sub")
    unit = lax.shift_right_logical(rank, shift)
    place = unit & (count - 1)
    first = unit - place
    span = blocks << shift
    for d, part in enumerate(parts):
        group[place ^ d] = part[...]
    to_rows = form_map(dim, LANES)
    forms = [group[i, :held, :].astype(BF16) for i in range(count)]
    samples = [group[i, held:, :] for i in range(count)]
    copy.wait()
    while len(forms) > 1:
        first = first // 2
        new_forms, new_samples = [], []
        for k in range(len(forms) // 2):
            chosen = merge_sets[pl.ds((2 * (first + k) + 1) * span - 1, 1), :]
            form = jnp.concatenate(forms[2 * k : 2 * k + 2], axis=1)
            form = jnp.concatenate([form, jnp.zeros((LANES - held, 2 * skel), BF16)], axis=0)
            new_form = dot(form, onehot_in(chosen, 2 * skel)).astype(BF16)
            new_rows = dot_t(new_form, to_rows).astype(BF16)
            weights = jnp.exp(dot(new_rows, form))
            picks = onehot_out(column_of(chosen), 2 * skel)
            mixing = picks + weights / jnp.sum(weights, axis=1, keepdims=True)
            new_forms.append(new_form[:held])
            new_samples.append(mix3(mixing, jnp.concatenate(samples[2 * k : 2 * k + 2], axis=0)))
        forms, samples = new_forms, new_samples
        span *= 2
    if piece is None:
        out[:held, :] = forms[0].astype(F32)
        out[held:, :] = samples[0]
    elif piece == 0:
        out[...] = samples[0]
    else:
        column = lax.broadcasted_iota(jnp.int32, (piece, skel), 1)
        row = lax.broadcasted_iota(jnp.int32, (piece, skel), 0) + rank * piece
        take = jnp.where(column == row, 1.0, 0.0).astype(BF16)
        hi, lo = split(samples[0])
        low = (samples[0] - hi.astype(F32) - lo.astype(F32)).astype(BF16)
        out[...] = dot(take, hi) + dot(take, lo) + dot(take, low)


def merge_call(parts, merge_sets, dim, blocks, shift, piece=None):
    count = len(parts)
    size = parts[0].shape[0]
    skel = size - dim - 16
    rows = size if piece is None else (piece or skel)
    return pl.pallas_call(
        functools.partial(merge_kernel, dim=dim, blocks=blocks, shift=shift, piece=piece),
        in_specs=[pl.BlockSpec(memory_space=pltpu.VMEM)] * count
        + [pl.BlockSpec(memory_space=pltpu.HBM)],
        out_shape=jax.ShapeDtypeStruct((rows, LANES), F32),
        scratch_shapes=[
            pltpu.VMEM((count, size, LANES), F32),
            pltpu.VMEM(merge_sets.shape, jnp.int32),
            pltpu.SemaphoreType.DMA(()),
        ],
        compiler_params=pltpu.CompilerParams(vmem_limit_bytes=16 * 1024 * 1024),
        cost_estimate=pl.CostEstimate(
            flops=count * 16 * LANES**3,
            bytes_accessed=4 * count * size * LANES,
            transcendentals=2 * count * LANES**2,
        ),
        name="tree_merge",
    )(*parts, merge_sets)


def near_kernel(*refs, slots, dim, has_acc, last):
    lists, counts, rows = refs[:3]
    refs = refs[3:]
    if has_acc:
        acc_in, refs = refs[0], refs[1:]
    buffers = []
    for _, which in slots:
        number = max(which) + 1
        buffers.append(refs[:number])
        refs = refs[number:]
    out, pair_list = refs
    blocks, leaf = rows.shape[:2]
    near = lists.shape[1]
    window = blocks * lax.axis_size("sub")
    start = lax.axis_index("leaf") * window - blocks
    sub = lax.axis_index("sub")

    def place(table):
        value = jnp.int32(table[0])
        for i in range(1, len(table)):
            value = jnp.where(sub == i, jnp.int32(table[i]), value)
        return value

    starts = [start + place(bases) for bases, _ in slots]
    stride = blocks * near + 8

    def list_block(g, found):
        used = counts[g]

        def list_slot(s, found):
            source = lists[g, s]
            after = []
            for slot, first in enumerate(starts):
                pair_list[slot * stride + found[slot]] = g * blocks + source - first
                inside = (source >= first) & (source < first + blocks) & (s < used)
                after.append(found[slot] + jnp.where(inside, 1, 0))
            return tuple(after)

        return lax.fori_loop(0, near, list_slot, found, unroll=True)

    found = lax.fori_loop(0, blocks, list_block, (jnp.int32(0),) * len(slots))
    if has_acc:
        out[...] = acc_in[...]
    else:
        out[...] = jnp.zeros(out.shape, F32)

    half = leaf // 2

    def add_all(buffer, first, pairs):
        def add_pair(i):
            code = pair_list[first + i]
            g = code // blocks
            local = code - g * blocks
            form = form_of(buffer.at[local], leaf, dim)
            probes = buffer[local, :leaf, :]
            total = None
            for c in range(0, leaf, half):
                weights = jnp.exp(dot(rows[g], form[:, c : c + half])).astype(BF16)
                term = dot(weights, probes[c : c + half])
                total = term if total is None else total + term
            return g, total

        def add_pairs(i, carry):
            for g, total in [add_pair(2 * i), add_pair(2 * i + 1)]:
                out[g] += total
            return carry

        lax.fori_loop(0, pairs // 2, add_pairs, 0)

        @pl.when(pairs % 2 == 1)
        def _():
            g, total = add_pair(pairs - 1)
            out[g] += total

    for slot, (_, which) in enumerate(slots):
        if len(buffers[slot]) == 1:
            add_all(buffers[slot][0], slot * stride, found[slot])
        else:
            held = place(which)
            for number, buffer in enumerate(buffers[slot]):
                add_all(buffer, slot * stride, jnp.where(held == number, found[slot], 0))
    if last:
        out[...] = out[...] * (leaf ** -0.5)


def near_call(lists, counts, rows, acc, sets, dim, last, name):
    blocks, leaf = rows.shape[:2]
    buffers = [b for _, _, bufs in sets for b in bufs]
    slots = tuple((bases, which) for bases, which, _ in sets)
    packed = buffers[0].shape[1]
    smem = pl.BlockSpec(memory_space=pltpu.SMEM)
    vmem = pl.BlockSpec(memory_space=pltpu.VMEM)
    args = [lists, counts, rows] + ([acc] if acc is not None else []) + buffers
    total = len(slots) * blocks
    near = lists.shape[1]
    pairs = total * blocks // 8
    return pl.pallas_call(
        functools.partial(
            near_kernel, slots=slots, dim=dim, has_acc=acc is not None, last=last
        ),
        in_specs=[smem, smem] + [vmem] * (len(args) - 2),
        out_specs=vmem,
        out_shape=jax.ShapeDtypeStruct((blocks, leaf, LANES), F32),
        scratch_shapes=[pltpu.SMEM((len(slots) * (blocks * near + 8),), jnp.int32)],
        compiler_params=pltpu.CompilerParams(vmem_limit_bytes=NEAR_BYTES),
        cost_estimate=pl.CostEstimate(
            flops=1000, bytes_accessed=1000, transcendentals=0
        ),
        name=name,
    )(*args)


def on_device(points, probes, order, near_lists, near_counts, leaf_sets, merge_sets):
    leaf_count = lax.axis_size("leaf")
    sub_count = lax.axis_size("sub")
    blocks, skel = leaf_sets.shape
    npts, dim = points.shape
    leaf = npts // blocks
    axes = ("leaf", "sub")

    def send(x, routes):
        pairs = []
        for place in range(leaf_count):
            for from_sub, step, to_sub in routes:
                if 0 <= place + step < leaf_count:
                    pairs.append((place * sub_count + from_sub, (place + step) * sub_count + to_sub))
        return lax.ppermute(x, axes, pairs)

    swap = [(0, 0, 1), (1, 0, 0), (2, 0, 3), (3, 0, 2)]
    pack, rows = order_call(points.T, order.reshape(blocks, 1, leaf), probes, blocks)
    outer_across = send(pack, [(3, 0, 1), (0, 0, 2)])
    outer_next = send(pack, [(3, 1, 3), (0, -1, 0)])
    beside = send(pack, swap)

    node = local_tree_call(pack, rows, leaf_sets, merge_sets, dim)

    count = leaf_count * sub_count
    bits = count.bit_length() - 1
    sub_bits = sub_count.bit_length() - 1

    def exchange(x, shift, stage_bits):
        parts = [x]
        for d in range(1, 1 << stage_bits):
            parts.append(lax.ppermute(x, axes, [(i, i ^ (d << shift)) for i in range(count)]))
        return parts

    b = blocks
    own_base, beside_base = (b, 2 * b, 3 * b, 4 * b), (2 * b, b, 4 * b, 3 * b)
    early_base, early_beside_base = (5 * b, 4 * b, b, 0), (4 * b, 5 * b, 0, b)
    late_base, late_beside_base = (3 * b, 0, 5 * b, 2 * b), (0, 3 * b, 2 * b, 5 * b)
    single, edge_first, edge_second = (0, 0, 0, 0), (0, 1, 1, 0), (1, 0, 0, 1)
    from_edge, from_inner = [(0, 0, 1), (3, 0, 2)], [(1, 0, 0), (2, 0, 3)]

    def tie(*values):
        return lax.optimization_barrier(values)

    node = merge_call(exchange(node, 0, 1), merge_sets, dim, blocks, 0)
    own_pack, node = tie(pack, node)
    parts = exchange(node, 1, sub_bits - 1)
    acc = near_call(
        near_lists, near_counts, rows, None,
        [(own_base, single, [own_pack])],
        dim, False, "near_first",
    )

    *parts, outer_across, outer_next, own_pack, acc = tie(
        *parts, outer_across, outer_next, own_pack, acc
    )
    forwarded = send(outer_across, [(1, 1, 1), (2, -1, 2)])
    inner_across = send(own_pack, [(2, 0, 0), (1, 0, 3)])
    acc = near_call(
        near_lists, near_counts, rows, acc,
        [
            (beside_base, single, [beside]),
            (early_base, edge_first, [outer_next, outer_across]),
        ],
        dim, False, "near_second",
    )

    *parts, acc = tie(*parts, acc)
    node = merge_call(parts, merge_sets, dim, blocks, 1)
    outer_next, outer_across, node = tie(outer_next, outer_across, node)
    next_beside = send(outer_next, from_edge)
    across_beside = send(outer_across, from_inner)
    shift, stage_bits = sub_bits, min(2, bits - sub_bits)
    parts = exchange(node, shift, stage_bits)
    next_beside, across_beside, node = tie(next_beside, across_beside, node)
    acc = near_call(
        near_lists, near_counts, rows, acc,
        [(early_beside_base, edge_second, [next_beside, across_beside])],
        dim, False, "near_third",
    )

    *parts, inner_across, forwarded, acc = tie(*parts, inner_across, forwarded, acc)
    inner_beside = send(inner_across, from_edge)
    forwarded_beside = send(forwarded, from_inner)
    node = merge_call(parts, merge_sets, dim, blocks, shift)
    shift += stage_bits
    inner_across, forwarded, node = tie(inner_across, forwarded, node)
    parts = exchange(node, shift, bits - shift)
    near = near_call(
        near_lists, near_counts, rows, acc,
        [
            (late_base, edge_first, [inner_across, forwarded]),
            (late_beside_base, edge_second, [inner_beside, forwarded_beside]),
        ],
        dim, True, "near_last",
    )

    *parts, near = tie(*parts, near)
    piece = skel // count
    node = merge_call(parts, merge_sets, dim, blocks, shift, piece)
    if piece:
        root = node.reshape(-1)
    else:
        size = skel * LANES // count
        rank = lax.axis_index("leaf") * sub_count + lax.axis_index("sub")
        root = lax.dynamic_slice_in_dim(node.reshape(-1), rank * size, size, 0)
    return near.reshape(npts, LANES), root


def solution(mesh):
    in_specs = (
        P(("leaf", "sub"), None),
        P(("leaf", "sub"), None),
        P(("leaf", "sub")),
        P(("leaf", "sub"), None),
        P(("leaf", "sub")),
        P(("leaf", "sub"), None),
        P(),
    )
    out_specs = (P(("leaf", "sub"), None), P(("leaf", "sub")))
    return jax.shard_map(
        on_device, mesh=mesh, in_specs=in_specs, out_specs=out_specs, check_vma=False
    )
```

```python
import functools

import jax
import jax.numpy as jnp
from jax import lax
from jax.experimental import pallas as pl
from jax.experimental.pallas import tpu as pltpu
from jax.sharding import PartitionSpec as P

LANES = 128
PARTS = 3
VMEM_BYTES = 20 * 1024 * 1024
NEAR_BYTES = 24 * 1024 * 1024
F32 = jnp.float32
BF16 = jnp.bfloat16


def dot(a, b):
    return jnp.dot(a, b, preferred_element_type=F32)


def dot_t(a, b):
    return lax.dot_general(a, b, (((0,), (0,)), ((), ())), preferred_element_type=F32)


def split(x):
    hi = x.astype(BF16)
    return hi, (x - hi.astype(F32)).astype(BF16)


def square_rows(pts):
    x = pts.astype(F32)
    total = jnp.sum(x * x, axis=0, keepdims=True)
    hi = total.astype(BF16).astype(F32)
    mid = (total - hi).astype(BF16).astype(F32)
    low = total - hi - mid
    row = lax.broadcasted_iota(jnp.int32, (16, pts.shape[1]), 0)
    ones = jnp.where(row < 2 * PARTS, 1.0, 0.0)
    return jnp.where(row == 0, hi, jnp.where(row == 1, mid, jnp.where(row == 2, low, ones))).astype(BF16)


def form_map(dim, size):
    k = lax.broadcasted_iota(jnp.int32, (size, size), 0)
    j = lax.broadcasted_iota(jnp.int32, (size, size), 1)
    r = jnp.where((k == j) & (j < dim), 2.0 / dim, 0.0)
    r = jnp.where((j >= dim) & (j < dim + PARTS) & (k == j + PARTS), -1.0 / dim, r)
    r = jnp.where((j >= dim + PARTS) & (j < dim + 2 * PARTS) & (k == j - PARTS), -1.0 / dim, r)
    return r.astype(BF16)


def onehot_in(row, size):
    index = lax.broadcasted_iota(jnp.int32, (size, row.shape[1]), 0)
    return jnp.where(index == row, 1.0, 0.0).astype(BF16)


def column_of(row):
    return jnp.broadcast_to(row.astype(F32), (LANES, row.shape[1])).T


def onehot_out(column, size):
    lane = lax.broadcasted_iota(jnp.int32, column.shape, 1).astype(F32)
    return jnp.concatenate(
        [jnp.where(column == lane + float(i), 1.0, 0.0) for i in range(0, size, LANES)], axis=1
    )


def mix3(m, s):
    m_hi, m_lo = split(m)
    s_hi, s_lo = split(s)
    return dot(m_hi, s_hi) + (dot(m_hi, s_lo) + dot(m_lo, s_hi))


def order_kernel(points_t, order, probes, pack, rows):
    dim = points_t.shape[0]
    many, leaf = rows.shape[:2]
    held = dim + 16
    to_rows = form_map(dim, LANES)
    for b in range(many):
        picks = onehot_in(order[b], leaf)
        tree_t = dot(points_t[:, b * leaf : (b + 1) * leaf], picks).astype(BF16)
        pack[b, :leaf, :] = probes[b * leaf : (b + 1) * leaf, :]
        form = jnp.concatenate([tree_t, square_rows(tree_t)], axis=0)
        for i in range(leaf // LANES):
            pack[b, leaf + i * held : leaf + (i + 1) * held, :] = form[:, i * LANES : (i + 1) * LANES]
        form = jnp.concatenate([form, jnp.zeros((LANES - held, leaf), BF16)], axis=0)
        rows[b] = dot_t(form, to_rows).astype(BF16)


def order_call(points_t, order, probes, blocks):
    dim, npts = points_t.shape
    leaf = npts // blocks
    packed = leaf + leaf // LANES * (dim + 16)
    many = 4 if blocks % 4 == 0 else 1
    return pl.pallas_call(
        order_kernel,
        grid=(blocks // many,),
        in_specs=[
            pl.BlockSpec((dim, many * leaf), lambda b: (0, b)),
            pl.BlockSpec((many, 1, leaf), lambda b: (b, 0, 0)),
            pl.BlockSpec((many * leaf, LANES), lambda b: (b, 0)),
        ],
        out_specs=[
            pl.BlockSpec((many, packed, LANES), lambda b: (b, 0, 0)),
            pl.BlockSpec((many, leaf, LANES), lambda b: (b, 0, 0)),
        ],
        out_shape=[
            jax.ShapeDtypeStruct((blocks, packed, LANES), BF16),
            jax.ShapeDtypeStruct((blocks, leaf, LANES), BF16),
        ],
        compiler_params=pltpu.CompilerParams(vmem_limit_bytes=VMEM_BYTES),
        cost_estimate=pl.CostEstimate(
            flops=blocks * 2 * leaf * leaf * dim, bytes_accessed=10 * npts * LANES, transcendentals=0
        ),
        name="tree_order",
    )(points_t, order, probes)


def form_of(pack_block, leaf, dim):
    held = dim + 16
    columns = [
        pack_block[leaf + i * held : leaf + (i + 1) * held, :] for i in range(leaf // LANES)
    ]
    form = jnp.concatenate(columns, axis=1)
    return jnp.concatenate([form, jnp.zeros((LANES - held, leaf), BF16)], axis=0)


def condense(form, a_rows, chosen):
    size = form.shape[1]
    picks_out = onehot_out(column_of(chosen), size)
    new_rows = dot(picks_out.astype(BF16), a_rows).astype(BF16)
    new_form = dot(form, onehot_in(chosen, size)).astype(BF16)
    weights = jnp.exp(dot(new_rows, form))
    mixing = picks_out + weights / jnp.sum(weights, axis=1, keepdims=True)
    return new_form, new_rows, mixing


def local_tree_kernel(pack, rows, leaf_sets_in, merge_sets_in, out, leaf_sets, merge_sets, sems, *, dim):
    blocks, leaf = rows.shape[:2]
    leaf_copy = pltpu.make_async_copy(leaf_sets_in, leaf_sets, sems.at[0])
    merge_copy = pltpu.make_async_copy(merge_sets_in, merge_sets, sems.at[1])
    leaf_copy.start()
    merge_copy.start()
    leaf_copy.wait()
    first_block = (lax.axis_index("leaf") * lax.axis_size("sub") + lax.axis_index("sub")) * blocks

    nodes = []
    for b in range(blocks):
        form = form_of(pack.at[b], leaf, dim)
        new_form, new_rows, mixing = condense(form, rows[b], leaf_sets[b : b + 1, :])
        m_hi, m_lo = split(mixing)
        probes = pack[b, :leaf, :]
        nodes.append((new_form, new_rows, dot(m_hi, probes) + dot(m_lo, probes)))
    span = 1
    merge_copy.wait()
    while len(nodes) > 1:
        merged = []
        for k in range(len(nodes) // 2):
            left, right = nodes[2 * k], nodes[2 * k + 1]
            chosen = merge_sets[pl.ds(first_block + (2 * k + 1) * span - 1, 1), :]
            new_form, new_rows, mixing = condense(
                jnp.concatenate([left[0], right[0]], axis=1),
                jnp.concatenate([left[1], right[1]], axis=0),
                chosen,
            )
            samples = mix3(mixing, jnp.concatenate([left[2], right[2]], axis=0))
            merged.append((new_form, new_rows, samples))
        nodes = merged
        span *= 2
    held = dim + 16
    out[:held, :] = nodes[0][0][:held, :].astype(F32)
    out[held:, :] = nodes[0][2]


def local_tree_call(pack, rows, leaf_sets, merge_sets, dim):
    blocks, leaf = rows.shape[:2]
    skel = leaf_sets.shape[1]
    return pl.pallas_call(
        functools.partial(local_tree_kernel, dim=dim),
        in_specs=[pl.BlockSpec(memory_space=pltpu.VMEM)] * 2
        + [pl.BlockSpec(memory_space=pltpu.HBM)] * 2,
        out_shape=jax.ShapeDtypeStruct((dim + 16 + skel, LANES), F32),
        scratch_shapes=[
            pltpu.VMEM(leaf_sets.shape, jnp.int32),
            pltpu.VMEM(merge_sets.shape, jnp.int32),
            pltpu.SemaphoreType.DMA((2,)),
        ],
        compiler_params=pltpu.CompilerParams(vmem_limit_bytes=VMEM_BYTES),
        cost_estimate=pl.CostEstimate(
            flops=blocks * 8 * skel * leaf * LANES,
            bytes_accessed=6 * blocks * leaf * LANES,
            transcendentals=blocks * skel * leaf,
        ),
        name="local_tree",
    )(pack, rows, leaf_sets, merge_sets)


def merge_kernel(*refs, dim, blocks, shift, piece):
    merge_sets_in, out, group, merge_sets, sem = refs[-5:]
    parts = refs[:-5]
    count, size = group.shape[:2]
    copy = pltpu.make_async_copy(merge_sets_in, merge_sets, sem)
    copy.start()
    held = dim + 16
    skel = size - held
    rank = lax.axis_index("leaf") * lax.axis_size("sub") + lax.axis_index("sub")
    unit = lax.shift_right_logical(rank, shift)
    place = unit & (count - 1)
    first = unit - place
    span = blocks << shift
    for d, part in enumerate(parts):
        group[place ^ d] = part[...]
    to_rows = form_map(dim, LANES)
    forms = [group[i, :held, :].astype(BF16) for i in range(count)]
    samples = [group[i, held:, :] for i in range(count)]
    copy.wait()
    while len(forms) > 1:
        first = first // 2
        new_forms, new_samples = [], []
        for k in range(len(forms) // 2):
            chosen = merge_sets[pl.ds((2 * (first + k) + 1) * span - 1, 1), :]
            form = jnp.concatenate(forms[2 * k : 2 * k + 2], axis=1)
            form = jnp.concatenate([form, jnp.zeros((LANES - held, 2 * skel), BF16)], axis=0)
            new_form = dot(form, onehot_in(chosen, 2 * skel)).astype(BF16)
            new_rows = dot_t(new_form, to_rows).astype(BF16)
            weights = jnp.exp(dot(new_rows, form))
            picks = onehot_out(column_of(chosen), 2 * skel)
            mixing = picks + weights / jnp.sum(weights, axis=1, keepdims=True)
            new_forms.append(new_form[:held])
            new_samples.append(mix3(mixing, jnp.concatenate(samples[2 * k : 2 * k + 2], axis=0)))
        forms, samples = new_forms, new_samples
        span *= 2
    if piece is None:
        out[:held, :] = forms[0].astype(F32)
        out[held:, :] = samples[0]
    elif piece == 0:
        out[...] = samples[0]
    else:
        column = lax.broadcasted_iota(jnp.int32, (piece, skel), 1)
        row = lax.broadcasted_iota(jnp.int32, (piece, skel), 0) + rank * piece
        take = jnp.where(column == row, 1.0, 0.0).astype(BF16)
        hi, lo = split(samples[0])
        low = (samples[0] - hi.astype(F32) - lo.astype(F32)).astype(BF16)
        out[...] = dot(take, hi) + dot(take, lo) + dot(take, low)


def merge_call(parts, merge_sets, dim, blocks, shift, piece=None):
    count = len(parts)
    size = parts[0].shape[0]
    skel = size - dim - 16
    rows = size if piece is None else (piece or skel)
    return pl.pallas_call(
        functools.partial(merge_kernel, dim=dim, blocks=blocks, shift=shift, piece=piece),
        in_specs=[pl.BlockSpec(memory_space=pltpu.VMEM)] * count
        + [pl.BlockSpec(memory_space=pltpu.HBM)],
        out_shape=jax.ShapeDtypeStruct((rows, LANES), F32),
        scratch_shapes=[
            pltpu.VMEM((count, size, LANES), F32),
            pltpu.VMEM(merge_sets.shape, jnp.int32),
            pltpu.SemaphoreType.DMA(()),
        ],
        compiler_params=pltpu.CompilerParams(vmem_limit_bytes=16 * 1024 * 1024),
        cost_estimate=pl.CostEstimate(
            flops=count * 16 * LANES**3,
            bytes_accessed=4 * count * size * LANES,
            transcendentals=2 * count * LANES**2,
        ),
        name="tree_merge",
    )(*parts, merge_sets)


def near_kernel(*refs, flips, bases, which, dim, has_acc):
    groups = len(flips)
    lists, rows, refs = refs[:groups], refs[groups : 2 * groups], refs[2 * groups :]
    if has_acc:
        accs, refs = refs[:groups], refs[groups:]
    buffers, outs, pair_list = refs[: max(which) + 1], refs[max(which) + 1 : -1], refs[-1]
    blocks, leaf = rows[0].shape[:2]
    near = lists[0].shape[1]
    window = blocks * lax.axis_size("sub")
    sub = lax.axis_index("sub")

    def place(table):
        value = jnp.int32(table[0])
        for i in range(1, len(table)):
            value = jnp.where(sub == i, jnp.int32(table[i]), value)
        return value

    source_first = lax.axis_index("leaf") * window - blocks + place(bases)
    stride = blocks * near + 8
    found = []
    for j, flip in enumerate(flips):
        target_first = lax.axis_index("leaf") * window + (sub ^ flip) * blocks

        def list_block(g, count, j=j, target_first=target_first):
            for s in range(near):
                source = lists[j][g, s]
                local = source - source_first
                pair_list[j * stride + count] = g * blocks + local
                inside = (local >= 0) & (local < blocks)
                if s:
                    inside = inside & (source != target_first + g)
                count = count + jnp.where(inside, 1, 0)
            return count

        found.append(lax.fori_loop(0, blocks, list_block, jnp.int32(0)))
        outs[j][...] = accs[j][...] if has_acc else jnp.zeros(outs[j].shape, F32)

    half = leaf // 2

    def add_all(buffer, j, pairs):
        def add_pair(i):
            code = pair_list[j * stride + i]
            g = code // blocks
            local = code - g * blocks
            form = form_of(buffer.at[local], leaf, dim)
            probes = buffer[local, :leaf, :]
            total = None
            for c in range(0, leaf, half):
                weights = jnp.exp(dot(rows[j][g], form[:, c : c + half])).astype(BF16)
                term = dot(weights, probes[c : c + half])
                total = term if total is None else total + term
            return g, total

        def add_pairs(i, carry):
            for g, total in [add_pair(2 * i), add_pair(2 * i + 1)]:
                outs[j][g] += total
            return carry

        lax.fori_loop(0, pairs // 2, add_pairs, 0)

        @pl.when(pairs % 2 == 1)
        def _():
            g, total = add_pair(pairs - 1)
            outs[j][g] += total

    held = place(which)
    for number, buffer in enumerate(buffers):
        for j in range(groups):
            pairs = found[j] if len(buffers) == 1 else jnp.where(held == number, found[j], 0)
            add_all(buffer, j, pairs)


def near_call(groups, source, dim, name):
    flips, lists, rows, accs = zip(*groups)
    bases, which, buffers = source
    blocks, leaf = rows[0].shape[:2]
    has_acc = accs[0] is not None
    args = [*lists, *rows, *(accs if has_acc else ()), *buffers]
    smem = pl.BlockSpec(memory_space=pltpu.SMEM)
    vmem = pl.BlockSpec(memory_space=pltpu.VMEM)
    near = lists[0].shape[1]
    return pl.pallas_call(
        functools.partial(
            near_kernel, flips=flips, bases=bases, which=which, dim=dim, has_acc=has_acc
        ),
        in_specs=[smem] * len(lists) + [vmem] * (len(args) - len(lists)),
        out_specs=[vmem] * len(groups),
        out_shape=[jax.ShapeDtypeStruct((blocks, leaf, LANES), F32)] * len(groups),
        scratch_shapes=[pltpu.SMEM((len(groups) * (blocks * near + 8),), jnp.int32)],
        compiler_params=pltpu.CompilerParams(vmem_limit_bytes=NEAR_BYTES),
        cost_estimate=pl.CostEstimate(flops=1000, bytes_accessed=1000, transcendentals=0),
        name=name,
    )(*args)


def on_device(points, probes, order, near_lists, near_counts, leaf_sets, merge_sets):
    leaf_count = lax.axis_size("leaf")
    sub_count = lax.axis_size("sub")
    blocks, skel = leaf_sets.shape
    npts, dim = points.shape
    leaf = npts // blocks
    axes = ("leaf", "sub")

    def send(x, routes):
        pairs = []
        for place in range(leaf_count):
            for from_sub, step, to_sub in routes:
                if 0 <= place + step < leaf_count:
                    pairs.append((place * sub_count + from_sub, (place + step) * sub_count + to_sub))
        return lax.ppermute(x, axes, pairs)

    count = leaf_count * sub_count
    bits = count.bit_length() - 1
    sub_bits = sub_count.bit_length() - 1

    def exchange(x, shift, stage_bits):
        parts = [x]
        for d in range(1, 1 << stage_bits):
            parts.append(lax.ppermute(x, axes, [(i, i ^ (d << shift)) for i in range(count)]))
        return parts

    def tie(*values):
        return lax.optimization_barrier(values)

    b = blocks
    own_base = (b, 2 * b, 3 * b, 4 * b)
    early_base, late_base = (5 * b, 4 * b, b, 0), (3 * b, 0, 5 * b, 2 * b)
    single, by_edge = (0, 0, 0, 0), (0, 1, 1, 0)

    pack, rows = order_call(points.T, order.reshape(blocks, 1, leaf), probes, blocks)
    outer_across = send(pack, [(3, 0, 1), (0, 0, 2)])
    outer_next = send(pack, [(3, 1, 3), (0, -1, 0)])
    beside_rows = exchange(rows, 0, 1)[1]
    beside_lists = exchange(near_lists, 0, 1)[1]

    rows, beside_lists = tie(rows, beside_lists)
    node = local_tree_call(pack, rows, leaf_sets, merge_sets, dim)
    node = merge_call(exchange(node, 0, 1), merge_sets, dim, blocks, 0)
    own_pack, node = tie(pack, node)
    parts = exchange(node, 1, sub_bits - 1)
    own, beside = near_call(
        [(0, near_lists, rows, None), (1, beside_lists, beside_rows, None)],
        (own_base, single, [own_pack]), dim, "near_own",
    )

    *parts, outer_across, outer_next, own_pack, own, beside = tie(
        *parts, outer_across, outer_next, own_pack, own, beside
    )
    forwarded = send(outer_across, [(1, 1, 1), (2, -1, 2)])
    inner_across = send(own_pack, [(2, 0, 0), (1, 0, 3)])
    own, beside = near_call(
        [(0, near_lists, rows, own), (1, beside_lists, beside_rows, beside)],
        (early_base, by_edge, [outer_next, outer_across]), dim, "near_early",
    )

    *parts, beside = tie(*parts, beside)
    node = merge_call(parts, merge_sets, dim, blocks, 1)
    shift, stage_bits = sub_bits, min(2, bits - sub_bits)
    parts = exchange(node, shift, stage_bits)

    *parts, inner_across, forwarded, beside = tie(*parts, inner_across, forwarded, beside)
    late = (late_base, by_edge, [inner_across, forwarded])
    (beside,) = near_call([(1, beside_lists, beside_rows, beside)], late, dim, "near_beside")
    given = exchange(beside, 0, 1)[1]
    *parts, beside = tie(*parts, beside)
    node = merge_call(parts, merge_sets, dim, blocks, shift)
    shift += stage_bits
    own, node = tie(own, node)
    parts = exchange(node, shift, bits - shift)
    (own,) = near_call([(0, near_lists, rows, own)], late, dim, "near_last")
    *parts, own = tie(*parts, own)
    piece = skel // count
    node = merge_call(parts, merge_sets, dim, blocks, shift, piece)
    if piece:
        root = node.reshape(-1)
    else:
        size = skel * LANES // count
        rank = lax.axis_index("leaf") * sub_count + lax.axis_index("sub")
        root = lax.dynamic_slice_in_dim(node.reshape(-1), rank * size, size, 0)
    near = (own + given) * (leaf ** -0.5)
    return near.reshape(npts, LANES), root


def solution(mesh):
    in_specs = (
        P(("leaf", "sub"), None),
        P(("leaf", "sub"), None),
        P(("leaf", "sub")),
        P(("leaf", "sub"), None),
        P(("leaf", "sub")),
        P(("leaf", "sub"), None),
        P(),
    )
    out_specs = (P(("leaf", "sub"), None), P(("leaf", "sub")))
    return jax.shard_map(
        on_device, mesh=mesh, in_specs=in_specs, out_specs=out_specs, check_vma=False
    )
```

```python
import functools

import jax
import jax.numpy as jnp
from jax import lax
from jax.experimental import pallas as pl
from jax.experimental.pallas import tpu as pltpu
from jax.sharding import PartitionSpec as P

LANES = 128
PARTS = 3
VMEM_BYTES = 20 * 1024 * 1024
NEAR_BYTES = 24 * 1024 * 1024
F32 = jnp.float32
BF16 = jnp.bfloat16


def dot(a, b):
    return jnp.dot(a, b, preferred_element_type=F32)


def dot_t(a, b):
    return lax.dot_general(a, b, (((0,), (0,)), ((), ())), preferred_element_type=F32)


def split(x):
    hi = x.astype(BF16)
    return hi, (x - hi.astype(F32)).astype(BF16)


def square_rows(pts):
    x = pts.astype(F32)
    total = jnp.sum(x * x, axis=0, keepdims=True)
    hi = total.astype(BF16).astype(F32)
    mid = (total - hi).astype(BF16).astype(F32)
    low = total - hi - mid
    row = lax.broadcasted_iota(jnp.int32, (16, pts.shape[1]), 0)
    ones = jnp.where(row < 2 * PARTS, 1.0, 0.0)
    return jnp.where(row == 0, hi, jnp.where(row == 1, mid, jnp.where(row == 2, low, ones))).astype(BF16)


def form_map(dim, size):
    k = lax.broadcasted_iota(jnp.int32, (size, size), 0)
    j = lax.broadcasted_iota(jnp.int32, (size, size), 1)
    r = jnp.where((k == j) & (j < dim), 2.0 / dim, 0.0)
    r = jnp.where((j >= dim) & (j < dim + PARTS) & (k == j + PARTS), -1.0 / dim, r)
    r = jnp.where((j >= dim + PARTS) & (j < dim + 2 * PARTS) & (k == j - PARTS), -1.0 / dim, r)
    return r.astype(BF16)


def onehot_in(row, size):
    index = lax.broadcasted_iota(jnp.int32, (size, row.shape[1]), 0)
    return jnp.where(index == row, 1.0, 0.0).astype(BF16)


def column_of(row):
    return jnp.broadcast_to(row.astype(F32), (LANES, row.shape[1])).T


def onehot_out(column, size):
    lane = lax.broadcasted_iota(jnp.int32, column.shape, 1).astype(F32)
    return jnp.concatenate(
        [jnp.where(column == lane + float(i), 1.0, 0.0) for i in range(0, size, LANES)], axis=1
    )


def mix3(m, s):
    m_hi, m_lo = split(m)
    s_hi, s_lo = split(s)
    return dot(m_hi, s_hi) + (dot(m_hi, s_lo) + dot(m_lo, s_hi))


def order_kernel(points_t, order, probes, pack, rows):
    dim = points_t.shape[0]
    many, leaf = rows.shape[:2]
    held = dim + 16
    to_rows = form_map(dim, LANES)
    for b in range(many):
        picks = onehot_in(order[b], leaf)
        tree_t = dot(points_t[:, b * leaf : (b + 1) * leaf], picks).astype(BF16)
        pack[b, :leaf, :] = probes[b * leaf : (b + 1) * leaf, :]
        form = jnp.concatenate([tree_t, square_rows(tree_t)], axis=0)
        for i in range(leaf // LANES):
            pack[b, leaf + i * held : leaf + (i + 1) * held, :] = form[:, i * LANES : (i + 1) * LANES]
        form = jnp.concatenate([form, jnp.zeros((LANES - held, leaf), BF16)], axis=0)
        rows[b] = dot_t(form, to_rows).astype(BF16)


def order_call(points_t, order, probes, blocks):
    dim, npts = points_t.shape
    leaf = npts // blocks
    packed = leaf + leaf // LANES * (dim + 16)
    many = 4 if blocks % 4 == 0 else 1
    return pl.pallas_call(
        order_kernel,
        grid=(blocks // many,),
        in_specs=[
            pl.BlockSpec((dim, many * leaf), lambda b: (0, b)),
            pl.BlockSpec((many, 1, leaf), lambda b: (b, 0, 0)),
            pl.BlockSpec((many * leaf, LANES), lambda b: (b, 0)),
        ],
        out_specs=[
            pl.BlockSpec((many, packed, LANES), lambda b: (b, 0, 0)),
            pl.BlockSpec((many, leaf, LANES), lambda b: (b, 0, 0)),
        ],
        out_shape=[
            jax.ShapeDtypeStruct((blocks, packed, LANES), BF16),
            jax.ShapeDtypeStruct((blocks, leaf, LANES), BF16),
        ],
        compiler_params=pltpu.CompilerParams(vmem_limit_bytes=VMEM_BYTES),
        cost_estimate=pl.CostEstimate(
            flops=blocks * 2 * leaf * leaf * dim, bytes_accessed=10 * npts * LANES, transcendentals=0
        ),
        name="tree_order",
    )(points_t, order, probes)


def form_of(pack_block, leaf, dim):
    held = dim + 16
    columns = [
        pack_block[leaf + i * held : leaf + (i + 1) * held, :] for i in range(leaf // LANES)
    ]
    form = jnp.concatenate(columns, axis=1)
    return jnp.concatenate([form, jnp.zeros((LANES - held, leaf), BF16)], axis=0)


def condense(form, a_rows, chosen):
    size = form.shape[1]
    picks_out = onehot_out(column_of(chosen), size)
    new_rows = dot(picks_out.astype(BF16), a_rows).astype(BF16)
    new_form = dot(form, onehot_in(chosen, size)).astype(BF16)
    weights = jnp.exp(dot(new_rows, form))
    mixing = picks_out + weights / jnp.sum(weights, axis=1, keepdims=True)
    return new_form, new_rows, mixing


def local_tree_kernel(pack, rows, leaf_sets_in, merge_sets_in, out, leaf_sets, merge_sets, sems, *, dim):
    blocks, leaf = rows.shape[:2]
    leaf_copy = pltpu.make_async_copy(leaf_sets_in, leaf_sets, sems.at[0])
    merge_copy = pltpu.make_async_copy(merge_sets_in, merge_sets, sems.at[1])
    leaf_copy.start()
    merge_copy.start()
    leaf_copy.wait()
    first_block = (lax.axis_index("leaf") * lax.axis_size("sub") + lax.axis_index("sub")) * blocks

    nodes = []
    for b in range(blocks):
        form = form_of(pack.at[b], leaf, dim)
        new_form, new_rows, mixing = condense(form, rows[b], leaf_sets[b : b + 1, :])
        m_hi, m_lo = split(mixing)
        probes = pack[b, :leaf, :]
        nodes.append((new_form, new_rows, dot(m_hi, probes) + dot(m_lo, probes)))
    span = 1
    merge_copy.wait()
    while len(nodes) > 1:
        merged = []
        for k in range(len(nodes) // 2):
            left, right = nodes[2 * k], nodes[2 * k + 1]
            chosen = merge_sets[pl.ds(first_block + (2 * k + 1) * span - 1, 1), :]
            new_form, new_rows, mixing = condense(
                jnp.concatenate([left[0], right[0]], axis=1),
                jnp.concatenate([left[1], right[1]], axis=0),
                chosen,
            )
            samples = mix3(mixing, jnp.concatenate([left[2], right[2]], axis=0))
            merged.append((new_form, new_rows, samples))
        nodes = merged
        span *= 2
    held = dim + 16
    out[:held, :] = nodes[0][0][:held, :].astype(F32)
    out[held:, :] = nodes[0][2]


def local_tree_call(pack, rows, leaf_sets, merge_sets, dim):
    blocks, leaf = rows.shape[:2]
    skel = leaf_sets.shape[1]
    return pl.pallas_call(
        functools.partial(local_tree_kernel, dim=dim),
        in_specs=[pl.BlockSpec(memory_space=pltpu.VMEM)] * 2
        + [pl.BlockSpec(memory_space=pltpu.HBM)] * 2,
        out_shape=jax.ShapeDtypeStruct((dim + 16 + skel, LANES), F32),
        scratch_shapes=[
            pltpu.VMEM(leaf_sets.shape, jnp.int32),
            pltpu.VMEM(merge_sets.shape, jnp.int32),
            pltpu.SemaphoreType.DMA((2,)),
        ],
        compiler_params=pltpu.CompilerParams(vmem_limit_bytes=VMEM_BYTES),
        cost_estimate=pl.CostEstimate(
            flops=blocks * 8 * skel * leaf * LANES,
            bytes_accessed=6 * blocks * leaf * LANES,
            transcendentals=blocks * skel * leaf,
        ),
        name="local_tree",
    )(pack, rows, leaf_sets, merge_sets)


def merge_kernel(*refs, dim, blocks, shift, piece):
    merge_sets_in, out, group, merge_sets, sem = refs[-5:]
    parts = refs[:-5]
    count, size = group.shape[:2]
    copy = pltpu.make_async_copy(merge_sets_in, merge_sets, sem)
    copy.start()
    held = dim + 16
    skel = size - held
    rank = lax.axis_index("leaf") * lax.axis_size("sub") + lax.axis_index("sub")
    unit = lax.shift_right_logical(rank, shift)
    place = unit & (count - 1)
    first = unit - place
    span = blocks << shift
    for d, part in enumerate(parts):
        group[place ^ d] = part[...]
    to_rows = form_map(dim, LANES)
    forms = [group[i, :held, :].astype(BF16) for i in range(count)]
    samples = [group[i, held:, :] for i in range(count)]
    copy.wait()
    while len(forms) > 1:
        first = first // 2
        new_forms, new_samples = [], []
        for k in range(len(forms) // 2):
            chosen = merge_sets[pl.ds((2 * (first + k) + 1) * span - 1, 1), :]
            form = jnp.concatenate(forms[2 * k : 2 * k + 2], axis=1)
            form = jnp.concatenate([form, jnp.zeros((LANES - held, 2 * skel), BF16)], axis=0)
            new_form = dot(form, onehot_in(chosen, 2 * skel)).astype(BF16)
            new_rows = dot_t(new_form, to_rows).astype(BF16)
            weights = jnp.exp(dot(new_rows, form))
            picks = onehot_out(column_of(chosen), 2 * skel)
            mixing = picks + weights / jnp.sum(weights, axis=1, keepdims=True)
            new_forms.append(new_form[:held])
            new_samples.append(mix3(mixing, jnp.concatenate(samples[2 * k : 2 * k + 2], axis=0)))
        forms, samples = new_forms, new_samples
        span *= 2
    if piece is None:
        out[:held, :] = forms[0].astype(F32)
        out[held:, :] = samples[0]
    elif piece == 0:
        out[...] = samples[0]
    else:
        column = lax.broadcasted_iota(jnp.int32, (piece, skel), 1)
        row = lax.broadcasted_iota(jnp.int32, (piece, skel), 0) + rank * piece
        take = jnp.where(column == row, 1.0, 0.0).astype(BF16)
        hi, lo = split(samples[0])
        low = (samples[0] - hi.astype(F32) - lo.astype(F32)).astype(BF16)
        out[...] = dot(take, hi) + dot(take, lo) + dot(take, low)


def merge_call(parts, merge_sets, dim, blocks, shift, piece=None):
    count = len(parts)
    size = parts[0].shape[0]
    skel = size - dim - 16
    rows = size if piece is None else (piece or skel)
    return pl.pallas_call(
        functools.partial(merge_kernel, dim=dim, blocks=blocks, shift=shift, piece=piece),
        in_specs=[pl.BlockSpec(memory_space=pltpu.VMEM)] * count
        + [pl.BlockSpec(memory_space=pltpu.HBM)],
        out_shape=jax.ShapeDtypeStruct((rows, LANES), F32),
        scratch_shapes=[
            pltpu.VMEM((count, size, LANES), F32),
            pltpu.VMEM(merge_sets.shape, jnp.int32),
            pltpu.SemaphoreType.DMA(()),
        ],
        compiler_params=pltpu.CompilerParams(vmem_limit_bytes=16 * 1024 * 1024),
        cost_estimate=pl.CostEstimate(
            flops=count * 16 * LANES**3,
            bytes_accessed=4 * count * size * LANES,
            transcendentals=2 * count * LANES**2,
        ),
        name="tree_merge",
    )(*parts, merge_sets)


def near_kernel(*refs, flips, has_acc, sets, tasks, dim):
    refs = list(refs)

    def take(number):
        taken = refs[:number]
        del refs[:number]
        return taken

    lists, rows = take(len(flips)), take(len(flips))
    accs = [take(1)[0] if has else None for has in has_acc]
    buffers = [take(max(which) + 1) for _, which in sets]
    outs, (pair_list,) = take(len(flips)), refs
    blocks, leaf = rows[0].shape[:2]
    near = lists[0].shape[1]
    window = blocks * lax.axis_size("sub")
    sub = lax.axis_index("sub")

    def place(table):
        value = jnp.int32(table[0])
        for i in range(1, len(table)):
            value = jnp.where(sub == i, jnp.int32(table[i]), value)
        return value

    window_first = lax.axis_index("leaf") * window - blocks
    stride = blocks * near + 8
    found = [jnp.int32(0)] * len(tasks)
    for j, flip in enumerate(flips):
        mine = [t for t, (_, group) in enumerate(tasks) if group == j]
        firsts = [window_first + place(sets[tasks[t][0]][0]) for t in mine]
        target_first = lax.axis_index("leaf") * window + (sub ^ flip) * blocks

        def list_block(g, counts, j=j, mine=mine, firsts=firsts, target_first=target_first):
            for s in range(near):
                source = lists[j][g, s]
                used = (source != target_first + g) if s else True
                after = []
                for t, first, count in zip(mine, firsts, counts):
                    local = source - first
                    pair_list[t * stride + count] = g * blocks + local
                    inside = (local >= 0) & (local < blocks) & used
                    after.append(count + jnp.where(inside, 1, 0))
                counts = tuple(after)
            return counts

        counts = lax.fori_loop(0, blocks, list_block, (jnp.int32(0),) * len(mine))
        for t, count in zip(mine, counts):
            found[t] = count
        outs[j][...] = jnp.zeros(outs[j].shape, F32) if accs[j] is None else accs[j][...]

    half = leaf // 2

    def add_all(buffer, t, pairs):
        j = tasks[t][1]

        def add_pair(i):
            code = pair_list[t * stride + i]
            g = code // blocks
            local = code - g * blocks
            form = form_of(buffer.at[local], leaf, dim)
            probes = buffer[local, :leaf, :]
            total = None
            for c in range(0, leaf, half):
                weights = jnp.exp(dot(rows[j][g], form[:, c : c + half])).astype(BF16)
                term = dot(weights, probes[c : c + half])
                total = term if total is None else total + term
            return g, total

        def add_pairs(i, carry):
            for g, total in [add_pair(2 * i), add_pair(2 * i + 1)]:
                outs[j][g] += total
            return carry

        lax.fori_loop(0, pairs // 2, add_pairs, 0)

        @pl.when(pairs % 2 == 1)
        def _():
            g, total = add_pair(pairs - 1)
            outs[j][g] += total

    for t, (number, _) in enumerate(tasks):
        held = place(sets[number][1])
        for k, buffer in enumerate(buffers[number]):
            pairs = found[t] if len(buffers[number]) == 1 else jnp.where(held == k, found[t], 0)
            add_all(buffer, t, pairs)


def near_call(groups, sources, tasks, dim, name):
    flips, lists, rows, accs = zip(*groups)
    blocks, leaf = rows[0].shape[:2]
    held = [acc for acc in accs if acc is not None]
    args = [*lists, *rows, *held, *(b for _, _, buffers in sources for b in buffers)]
    smem = pl.BlockSpec(memory_space=pltpu.SMEM)
    vmem = pl.BlockSpec(memory_space=pltpu.VMEM)
    near = lists[0].shape[1]
    return pl.pallas_call(
        functools.partial(
            near_kernel,
            flips=flips,
            has_acc=tuple(acc is not None for acc in accs),
            sets=tuple((bases, which) for bases, which, _ in sources),
            tasks=tasks,
            dim=dim,
        ),
        in_specs=[smem] * len(lists) + [vmem] * (len(args) - len(lists)),
        out_specs=[vmem] * len(groups),
        out_shape=[jax.ShapeDtypeStruct((blocks, leaf, LANES), F32)] * len(groups),
        scratch_shapes=[pltpu.SMEM((len(tasks) * (blocks * near + 8),), jnp.int32)],
        compiler_params=pltpu.CompilerParams(vmem_limit_bytes=NEAR_BYTES),
        cost_estimate=pl.CostEstimate(flops=1000, bytes_accessed=1000, transcendentals=0),
        name=name,
    )(*args)


def on_device(points, probes, order, near_lists, near_counts, leaf_sets, merge_sets):
    leaf_count = lax.axis_size("leaf")
    sub_count = lax.axis_size("sub")
    blocks, skel = leaf_sets.shape
    npts, dim = points.shape
    leaf = npts // blocks
    axes = ("leaf", "sub")

    def send(x, routes):
        pairs = []
        for place in range(leaf_count):
            for from_sub, step, to_sub in routes:
                if 0 <= place + step < leaf_count:
                    pairs.append((place * sub_count + from_sub, (place + step) * sub_count + to_sub))
        return lax.ppermute(x, axes, pairs)

    count = leaf_count * sub_count
    bits = count.bit_length() - 1
    sub_bits = sub_count.bit_length() - 1

    def exchange(x, shift, stage_bits):
        parts = [x]
        for d in range(1, 1 << stage_bits):
            parts.append(lax.ppermute(x, axes, [(i, i ^ (d << shift)) for i in range(count)]))
        return parts

    def tie(*values):
        return lax.optimization_barrier(values)

    b = blocks
    own_base = (b, 2 * b, 3 * b, 4 * b)
    early_base, late_base = (5 * b, 4 * b, b, 0), (3 * b, 0, 5 * b, 2 * b)
    single, by_edge = (0, 0, 0, 0), (0, 1, 1, 0)

    pack, rows = order_call(points.T, order.reshape(blocks, 1, leaf), probes, blocks)
    outer_across = send(pack, [(3, 0, 1), (0, 0, 2)])
    outer_next = send(pack, [(3, 1, 3), (0, -1, 0)])
    beside_rows = exchange(rows, 0, 1)[1]
    beside_lists = exchange(near_lists, 0, 1)[1]

    node = local_tree_call(pack, rows, leaf_sets, merge_sets, dim)
    node, beside_lists = tie(node, beside_lists)

    def level(parts, bit, piece=None):
        return merge_call(parts, merge_sets, dim, blocks, bit, piece)

    node = level(exchange(node, 0, 1), 0)
    own_pack, node = tie(pack, node)
    parts = exchange(node, 1, 1)
    own_set = (own_base, single, [own_pack])
    (beside,) = near_call(
        [(1, beside_lists, beside_rows, None)], [own_set], ((0, 0),), dim, "near_own"
    )

    *parts, outer_across, outer_next, own_pack, beside = tie(
        *parts, outer_across, outer_next, own_pack, beside
    )
    forwarded = send(outer_across, [(1, 1, 1), (2, -1, 2)])
    inner_across = send(own_pack, [(2, 0, 0), (1, 0, 3)])
    node = level(parts, 1)
    parts = exchange(node, 2, 1)
    own_set = (own_base, single, [own_pack])
    early_set = (early_base, by_edge, [outer_next, outer_across])
    own, beside = near_call(
        [(0, near_lists, rows, None), (1, beside_lists, beside_rows, beside)],
        [own_set, early_set], ((0, 0), (1, 0), (1, 1)), dim, "near_early",
    )

    *parts, beside = tie(*parts, beside)
    node = level(parts, 2)
    for bit in range(3, bits - 1):
        node = level(exchange(node, bit, 1), bit)
    parts = exchange(node, bits - 1, 1)
    inner_across, forwarded, beside, node = tie(inner_across, forwarded, beside, node)
    late_set = (late_base, by_edge, [inner_across, forwarded])
    (beside,) = near_call(
        [(1, beside_lists, beside_rows, beside)], [late_set], ((0, 0),), dim, "near_beside"
    )
    given = exchange(beside, 0, 1)[1]
    (own,) = near_call([(0, near_lists, rows, own)], [late_set], ((0, 0),), dim, "near_last")
    *parts, own = tie(*parts, own)
    piece = skel // count
    node = level(parts, bits - 1, piece)
    if piece:
        root = node.reshape(-1)
    else:
        size = skel * LANES // count
        rank = lax.axis_index("leaf") * sub_count + lax.axis_index("sub")
        root = lax.dynamic_slice_in_dim(node.reshape(-1), rank * size, size, 0)
    near = (own + given) * (leaf ** -0.5)
    return near.reshape(npts, LANES), root


def solution(mesh):
    in_specs = (
        P(("leaf", "sub"), None),
        P(("leaf", "sub"), None),
        P(("leaf", "sub")),
        P(("leaf", "sub"), None),
        P(("leaf", "sub")),
        P(("leaf", "sub"), None),
        P(),
    )
    out_specs = (P(("leaf", "sub"), None), P(("leaf", "sub")))
    return jax.shard_map(
        on_device, mesh=mesh, in_specs=in_specs, out_specs=out_specs, check_vma=False
    )
```

```python
import functools

import jax
import jax.numpy as jnp
from jax import lax
from jax.experimental import pallas as pl
from jax.experimental.pallas import tpu as pltpu
from jax.sharding import PartitionSpec as P

LANES = 128
PARTS = 3
VMEM_BYTES = 20 * 1024 * 1024
NEAR_BYTES = 24 * 1024 * 1024
F32 = jnp.float32
BF16 = jnp.bfloat16


def dot(a, b):
    return jnp.dot(a, b, preferred_element_type=F32)


def dot_t(a, b):
    return lax.dot_general(a, b, (((0,), (0,)), ((), ())), preferred_element_type=F32)


def split(x):
    hi = x.astype(BF16)
    return hi, (x - hi.astype(F32)).astype(BF16)


def square_rows(pts):
    x = pts.astype(F32)
    total = jnp.sum(x * x, axis=0, keepdims=True)
    hi = total.astype(BF16).astype(F32)
    mid = (total - hi).astype(BF16).astype(F32)
    low = total - hi - mid
    row = lax.broadcasted_iota(jnp.int32, (16, pts.shape[1]), 0)
    ones = jnp.where(row < 2 * PARTS, 1.0, 0.0)
    return jnp.where(row == 0, hi, jnp.where(row == 1, mid, jnp.where(row == 2, low, ones))).astype(BF16)


def form_map(dim, size):
    k = lax.broadcasted_iota(jnp.int32, (size, size), 0)
    j = lax.broadcasted_iota(jnp.int32, (size, size), 1)
    r = jnp.where((k == j) & (j < dim), 2.0 / dim, 0.0)
    r = jnp.where((j >= dim) & (j < dim + PARTS) & (k == j + PARTS), -1.0 / dim, r)
    r = jnp.where((j >= dim + PARTS) & (j < dim + 2 * PARTS) & (k == j - PARTS), -1.0 / dim, r)
    return r.astype(BF16)


def onehot_in(row, size):
    index = lax.broadcasted_iota(jnp.int32, (size, row.shape[1]), 0)
    return jnp.where(index == row, 1.0, 0.0).astype(BF16)


def column_of(row):
    return jnp.broadcast_to(row.astype(F32), (LANES, row.shape[1])).T


def onehot_out(column, size):
    lane = lax.broadcasted_iota(jnp.int32, column.shape, 1).astype(F32)
    return jnp.concatenate(
        [jnp.where(column == lane + float(i), 1.0, 0.0) for i in range(0, size, LANES)], axis=1
    )


def mix3(m, s):
    m_hi, m_lo = split(m)
    s_hi, s_lo = split(s)
    return dot(m_hi, s_hi) + (dot(m_hi, s_lo) + dot(m_lo, s_hi))


def order_kernel(points_t, order, probes, pack, rows, *halves):
    dim = points_t.shape[0]
    many, leaf = rows.shape[:2]
    held = dim + 16
    to_rows = form_map(dim, LANES)
    for b in range(many):
        picks = onehot_in(order[b], leaf)
        tree_t = dot(points_t[:, b * leaf : (b + 1) * leaf], picks).astype(BF16)
        pack[b, :leaf, :] = probes[b * leaf : (b + 1) * leaf, :]
        form = jnp.concatenate([tree_t, square_rows(tree_t)], axis=0)
        for i in range(leaf // LANES):
            pack[b, leaf + i * held : leaf + (i + 1) * held, :] = form[:, i * LANES : (i + 1) * LANES]
        form = jnp.concatenate([form, jnp.zeros((LANES - held, leaf), BF16)], axis=0)
        rows[b] = dot_t(form, to_rows).astype(BF16)
    for step, half in enumerate(halves):

        @pl.when(pl.program_id(0) == step)
        def _(half=half):
            half[...] = pack[...]


def order_call(points_t, order, probes, blocks):
    dim, npts = points_t.shape
    leaf = npts // blocks
    packed = leaf + leaf // LANES * (dim + 16)
    many = blocks // 2
    return pl.pallas_call(
        order_kernel,
        grid=(blocks // many,),
        in_specs=[
            pl.BlockSpec((dim, many * leaf), lambda b: (0, b)),
            pl.BlockSpec((many, 1, leaf), lambda b: (b, 0, 0)),
            pl.BlockSpec((many * leaf, LANES), lambda b: (b, 0)),
        ],
        out_specs=[
            pl.BlockSpec((many, packed, LANES), lambda b: (b, 0, 0)),
            pl.BlockSpec((many, leaf, LANES), lambda b: (b, 0, 0)),
            pl.BlockSpec((many, packed, LANES), lambda b: (0, 0, 0)),
            pl.BlockSpec((many, packed, LANES), lambda b: (0, 0, 0)),
        ],
        out_shape=[
            jax.ShapeDtypeStruct((blocks, packed, LANES), BF16),
            jax.ShapeDtypeStruct((blocks, leaf, LANES), BF16),
            jax.ShapeDtypeStruct((many, packed, LANES), BF16),
            jax.ShapeDtypeStruct((many, packed, LANES), BF16),
        ],
        compiler_params=pltpu.CompilerParams(vmem_limit_bytes=VMEM_BYTES),
        cost_estimate=pl.CostEstimate(
            flops=blocks * 2 * leaf * leaf * dim, bytes_accessed=10 * npts * LANES, transcendentals=0
        ),
        name="tree_order",
    )(points_t, order, probes)


def form_of(pack_block, leaf, dim):
    held = dim + 16
    columns = [
        pack_block[leaf + i * held : leaf + (i + 1) * held, :] for i in range(leaf // LANES)
    ]
    form = jnp.concatenate(columns, axis=1)
    return jnp.concatenate([form, jnp.zeros((LANES - held, leaf), BF16)], axis=0)


def condense(form, a_rows, chosen):
    size = form.shape[1]
    picks_out = onehot_out(column_of(chosen), size)
    new_rows = dot(picks_out.astype(BF16), a_rows).astype(BF16)
    new_form = dot(form, onehot_in(chosen, size)).astype(BF16)
    weights = jnp.exp(dot(new_rows, form))
    mixing = picks_out + weights / jnp.sum(weights, axis=1, keepdims=True)
    return new_form, new_rows, mixing


def local_tree_kernel(pack, rows, leaf_sets_in, merge_sets_in, out, leaf_sets, merge_sets, sems, *, dim):
    blocks, leaf = rows.shape[:2]
    leaf_copy = pltpu.make_async_copy(leaf_sets_in, leaf_sets, sems.at[0])
    merge_copy = pltpu.make_async_copy(merge_sets_in, merge_sets, sems.at[1])
    leaf_copy.start()
    merge_copy.start()
    leaf_copy.wait()
    first_block = (lax.axis_index("leaf") * lax.axis_size("sub") + lax.axis_index("sub")) * blocks

    nodes = []
    for b in range(blocks):
        form = form_of(pack.at[b], leaf, dim)
        new_form, new_rows, mixing = condense(form, rows[b], leaf_sets[b : b + 1, :])
        m_hi, m_lo = split(mixing)
        probes = pack[b, :leaf, :]
        nodes.append((new_form, new_rows, dot(m_hi, probes) + dot(m_lo, probes)))
    span = 1
    merge_copy.wait()
    while len(nodes) > 1:
        merged = []
        for k in range(len(nodes) // 2):
            left, right = nodes[2 * k], nodes[2 * k + 1]
            chosen = merge_sets[pl.ds(first_block + (2 * k + 1) * span - 1, 1), :]
            new_form, new_rows, mixing = condense(
                jnp.concatenate([left[0], right[0]], axis=1),
                jnp.concatenate([left[1], right[1]], axis=0),
                chosen,
            )
            samples = mix3(mixing, jnp.concatenate([left[2], right[2]], axis=0))
            merged.append((new_form, new_rows, samples))
        nodes = merged
        span *= 2
    held = dim + 16
    out[:held, :] = nodes[0][0][:held, :].astype(F32)
    out[held:, :] = nodes[0][2]


def local_tree_call(pack, rows, leaf_sets, merge_sets, dim):
    blocks, leaf = rows.shape[:2]
    skel = leaf_sets.shape[1]
    return pl.pallas_call(
        functools.partial(local_tree_kernel, dim=dim),
        in_specs=[pl.BlockSpec(memory_space=pltpu.VMEM)] * 2
        + [pl.BlockSpec(memory_space=pltpu.HBM)] * 2,
        out_shape=jax.ShapeDtypeStruct((dim + 16 + skel, LANES), F32),
        scratch_shapes=[
            pltpu.VMEM(leaf_sets.shape, jnp.int32),
            pltpu.VMEM(merge_sets.shape, jnp.int32),
            pltpu.SemaphoreType.DMA((2,)),
        ],
        compiler_params=pltpu.CompilerParams(vmem_limit_bytes=VMEM_BYTES),
        cost_estimate=pl.CostEstimate(
            flops=blocks * 8 * skel * leaf * LANES,
            bytes_accessed=6 * blocks * leaf * LANES,
            transcendentals=blocks * skel * leaf,
        ),
        name="local_tree",
    )(pack, rows, leaf_sets, merge_sets)


def merge_kernel(*refs, dim, blocks, shift, piece):
    merge_sets_in, out, group, merge_sets, sem = refs[-5:]
    parts = refs[:-5]
    count, size = group.shape[:2]
    copy = pltpu.make_async_copy(merge_sets_in, merge_sets, sem)
    copy.start()
    held = dim + 16
    skel = size - held
    rank = lax.axis_index("leaf") * lax.axis_size("sub") + lax.axis_index("sub")
    unit = lax.shift_right_logical(rank, shift)
    place = unit & (count - 1)
    first = unit - place
    span = blocks << shift
    for d, part in enumerate(parts):
        group[place ^ d] = part[...]
    to_rows = form_map(dim, LANES)
    forms = [group[i, :held, :].astype(BF16) for i in range(count)]
    samples = [group[i, held:, :] for i in range(count)]
    copy.wait()
    while len(forms) > 1:
        first = first // 2
        new_forms, new_samples = [], []
        for k in range(len(forms) // 2):
            chosen = merge_sets[pl.ds((2 * (first + k) + 1) * span - 1, 1), :]
            form = jnp.concatenate(forms[2 * k : 2 * k + 2], axis=1)
            form = jnp.concatenate([form, jnp.zeros((LANES - held, 2 * skel), BF16)], axis=0)
            new_form = dot(form, onehot_in(chosen, 2 * skel)).astype(BF16)
            new_rows = dot_t(new_form, to_rows).astype(BF16)
            weights = jnp.exp(dot(new_rows, form))
            picks = onehot_out(column_of(chosen), 2 * skel)
            mixing = picks + weights / jnp.sum(weights, axis=1, keepdims=True)
            new_forms.append(new_form[:held])
            new_samples.append(mix3(mixing, jnp.concatenate(samples[2 * k : 2 * k + 2], axis=0)))
        forms, samples = new_forms, new_samples
        span *= 2
    if piece is None:
        out[:held, :] = forms[0].astype(F32)
        out[held:, :] = samples[0]
    elif piece == 0:
        out[...] = samples[0]
    else:
        column = lax.broadcasted_iota(jnp.int32, (piece, skel), 1)
        row = lax.broadcasted_iota(jnp.int32, (piece, skel), 0) + rank * piece
        take = jnp.where(column == row, 1.0, 0.0).astype(BF16)
        hi, lo = split(samples[0])
        low = (samples[0] - hi.astype(F32) - lo.astype(F32)).astype(BF16)
        out[...] = dot(take, hi) + dot(take, lo) + dot(take, low)


def merge_call(parts, merge_sets, dim, blocks, shift, piece=None):
    count = len(parts)
    size = parts[0].shape[0]
    skel = size - dim - 16
    rows = size if piece is None else (piece or skel)
    return pl.pallas_call(
        functools.partial(merge_kernel, dim=dim, blocks=blocks, shift=shift, piece=piece),
        in_specs=[pl.BlockSpec(memory_space=pltpu.VMEM)] * count
        + [pl.BlockSpec(memory_space=pltpu.HBM)],
        out_shape=jax.ShapeDtypeStruct((rows, LANES), F32),
        scratch_shapes=[
            pltpu.VMEM((count, size, LANES), F32),
            pltpu.VMEM(merge_sets.shape, jnp.int32),
            pltpu.SemaphoreType.DMA(()),
        ],
        compiler_params=pltpu.CompilerParams(vmem_limit_bytes=16 * 1024 * 1024),
        cost_estimate=pl.CostEstimate(
            flops=count * 16 * LANES**3,
            bytes_accessed=4 * count * size * LANES,
            transcendentals=2 * count * LANES**2,
        ),
        name="tree_merge",
    )(*parts, merge_sets)


def near_kernel(*refs, flips, has_acc, sets, tasks, dim):
    refs = list(refs)

    def take(number):
        taken = refs[:number]
        del refs[:number]
        return taken

    lists, rows = take(len(flips)), take(len(flips))
    accs = [take(1)[0] if has else None for has in has_acc]
    buffers = [take(max(which) + 1) for _, _, which in sets]
    outs, (pair_list,) = take(len(flips)), refs
    blocks, leaf = rows[0].shape[:2]
    near = lists[0].shape[1]
    window = blocks * lax.axis_size("sub")
    sub = lax.axis_index("sub")

    def place(table):
        value = jnp.int32(table[0])
        for i in range(1, len(table)):
            value = jnp.where(sub == i, jnp.int32(table[i]), value)
        return value

    window_first = lax.axis_index("leaf") * window - blocks
    stride = blocks * near + 8
    found = [jnp.int32(0)] * len(tasks)
    for j, flip in enumerate(flips):
        mine = [t for t, (_, group) in enumerate(tasks) if group == j]
        firsts = [window_first + place(sets[tasks[t][0]][0]) for t in mine]
        sizes = [place(sets[tasks[t][0]][1]) for t in mine]
        target_first = lax.axis_index("leaf") * window + (sub ^ flip) * blocks

        def list_block(g, counts, j=j, mine=mine, firsts=firsts, sizes=sizes, target_first=target_first):
            for s in range(near):
                source = lists[j][g, s]
                used = (source != target_first + g) if s else True
                after = []
                for t, first, size, count in zip(mine, firsts, sizes, counts):
                    local = source - first
                    pair_list[t * stride + count] = g * blocks + local
                    inside = (local >= 0) & (local < size) & used
                    after.append(count + jnp.where(inside, 1, 0))
                counts = tuple(after)
            return counts

        counts = lax.fori_loop(0, blocks, list_block, (jnp.int32(0),) * len(mine))
        for t, count in zip(mine, counts):
            found[t] = count
        outs[j][...] = jnp.zeros(outs[j].shape, F32) if accs[j] is None else accs[j][...]

    half = leaf // 2

    def add_all(buffer, t, pairs):
        j = tasks[t][1]

        def add_pair(i):
            code = pair_list[t * stride + i]
            g = code // blocks
            local = code - g * blocks
            form = form_of(buffer.at[local], leaf, dim)
            probes = buffer[local, :leaf, :]
            total = None
            for c in range(0, leaf, half):
                weights = jnp.exp(dot(rows[j][g], form[:, c : c + half])).astype(BF16)
                term = dot(weights, probes[c : c + half])
                total = term if total is None else total + term
            return g, total

        def add_pairs(i, carry):
            for g, total in [add_pair(2 * i), add_pair(2 * i + 1)]:
                outs[j][g] += total
            return carry

        lax.fori_loop(0, pairs // 2, add_pairs, 0)

        @pl.when(pairs % 2 == 1)
        def _():
            g, total = add_pair(pairs - 1)
            outs[j][g] += total

    for t, (number, _) in enumerate(tasks):
        held = place(sets[number][2])
        for k, buffer in enumerate(buffers[number]):
            pairs = found[t] if len(buffers[number]) == 1 else jnp.where(held == k, found[t], 0)
            add_all(buffer, t, pairs)


def near_call(groups, sources, tasks, dim, name):
    flips, lists, rows, accs = zip(*groups)
    blocks, leaf = rows[0].shape[:2]
    held = [acc for acc in accs if acc is not None]
    args = [*lists, *rows, *held, *(b for *_, buffers in sources for b in buffers)]
    smem = pl.BlockSpec(memory_space=pltpu.SMEM)
    vmem = pl.BlockSpec(memory_space=pltpu.VMEM)
    near = lists[0].shape[1]
    return pl.pallas_call(
        functools.partial(
            near_kernel,
            flips=flips,
            has_acc=tuple(acc is not None for acc in accs),
            sets=tuple(source[:3] for source in sources),
            tasks=tasks,
            dim=dim,
        ),
        in_specs=[smem] * len(lists) + [vmem] * (len(args) - len(lists)),
        out_specs=[vmem] * len(groups),
        out_shape=[jax.ShapeDtypeStruct((blocks, leaf, LANES), F32)] * len(groups),
        scratch_shapes=[pltpu.SMEM((len(tasks) * (blocks * near + 8),), jnp.int32)],
        compiler_params=pltpu.CompilerParams(vmem_limit_bytes=NEAR_BYTES),
        cost_estimate=pl.CostEstimate(flops=1000, bytes_accessed=1000, transcendentals=0),
        name=name,
    )(*args)


def on_device(points, probes, order, near_lists, near_counts, leaf_sets, merge_sets):
    leaf_count = lax.axis_size("leaf")
    sub_count = lax.axis_size("sub")
    blocks, skel = leaf_sets.shape
    npts, dim = points.shape
    leaf = npts // blocks
    axes = ("leaf", "sub")

    def send(x, routes):
        pairs = []
        for place in range(leaf_count):
            for from_sub, step, to_sub in routes:
                if 0 <= place + step < leaf_count:
                    pairs.append((place * sub_count + from_sub, (place + step) * sub_count + to_sub))
        return lax.ppermute(x, axes, pairs)

    count = leaf_count * sub_count
    bits = count.bit_length() - 1
    sub_bits = sub_count.bit_length() - 1

    def exchange(x, shift, stage_bits):
        parts = [x]
        for d in range(1, 1 << stage_bits):
            parts.append(lax.ppermute(x, axes, [(i, i ^ (d << shift)) for i in range(count)]))
        return parts

    def tie(*values):
        return lax.optimization_barrier(values)

    b, h = blocks, blocks // 2
    own_base = (b, 2 * b, 3 * b, 4 * b)
    early_base, late_base = (5 * b, 4 * b, b, 0), (3 * b, h, 5 * b + h, 2 * b)
    second_base, forwarded_base = (0, 4 * b + h, b + h, 0), (0, 0, 5 * b, 0)
    whole, mixed, inner = (b, b, b, b), (b, h, h, b), (0, h, h, 0)
    single, by_edge = (0, 0, 0, 0), (0, 1, 1, 0)

    def level(parts, bit, piece=None):
        return merge_call(parts, merge_sets, dim, blocks, bit, piece)

    pack, rows, *halves = order_call(points.T, order.reshape(blocks, 1, leaf), probes, blocks)
    across = [send(half, [(3, 0, 1), (0, 0, 2)]) for half in halves]
    outer_next = send(pack, [(3, 1, 3), (0, -1, 0)])
    beside_rows = exchange(rows, 0, 1)[1]
    beside_lists = exchange(near_lists, 0, 1)[1]

    node = local_tree_call(pack, rows, leaf_sets, merge_sets, dim)
    node, beside_lists, across[0] = tie(node, beside_lists, across[0])
    forward = [(1, 1, 1), (2, -1, 2)]
    forwarded = send(across[0], forward)
    node = level(exchange(node, 0, 1), 0)
    own_pack, node = tie(pack, node)
    parts = exchange(node, 1, 1)
    own_set = (own_base, whole, single, [own_pack])
    (beside,) = near_call(
        [(1, beside_lists, beside_rows, None)], [own_set], ((0, 0),), dim, "near_own"
    )

    *parts, across[1], outer_next, forwarded, own_pack, beside = tie(
        *parts, across[1], outer_next, forwarded, own_pack, beside
    )
    late_forwarded = send(across[1], forward)
    inner_across = send(own_pack, [(2, 0, 0), (1, 0, 3)])
    node = level(parts, 1)
    parts = exchange(node, 2, 1)
    own, beside = near_call(
        [(0, near_lists, rows, None), (1, beside_lists, beside_rows, beside)],
        [
            (own_base, whole, single, [own_pack]),
            (early_base, mixed, by_edge, [outer_next, across[0]]),
            (second_base, inner, single, [across[1]]),
            (forwarded_base, inner, single, [forwarded]),
        ],
        ((0, 0), (1, 0), (2, 0), (3, 0), (1, 1), (2, 1), (3, 1)), dim, "near_early",
    )

    *parts, beside = tie(*parts, beside)
    node = level(parts, 2)
    for bit in range(3, bits - 1):
        node = level(exchange(node, bit, 1), bit)
    parts = exchange(node, bits - 1, 1)
    inner_across, late_forwarded, beside, node = tie(inner_across, late_forwarded, beside, node)
    late_set = (late_base, mixed, by_edge, [inner_across, late_forwarded])
    (beside,) = near_call(
        [(1, beside_lists, beside_rows, beside)], [late_set], ((0, 0),), dim, "near_beside"
    )
    given = exchange(beside, 0, 1)[1]
    (own,) = near_call([(0, near_lists, rows, own)], [late_set], ((0, 0),), dim, "near_last")
    *parts, own = tie(*parts, own)
    piece = skel // count
    node = level(parts, bits - 1, piece)
    if piece:
        root = node.reshape(-1)
    else:
        size = skel * LANES // count
        rank = lax.axis_index("leaf") * sub_count + lax.axis_index("sub")
        root = lax.dynamic_slice_in_dim(node.reshape(-1), rank * size, size, 0)
    near = (own + given) * (leaf ** -0.5)
    return near.reshape(npts, LANES), root


def solution(mesh):
    in_specs = (
        P(("leaf", "sub"), None),
        P(("leaf", "sub"), None),
        P(("leaf", "sub")),
        P(("leaf", "sub"), None),
        P(("leaf", "sub")),
        P(("leaf", "sub"), None),
        P(),
    )
    out_specs = (P(("leaf", "sub"), None), P(("leaf", "sub")))
    return jax.shard_map(
        on_device, mesh=mesh, in_specs=in_specs, out_specs=out_specs, check_vma=False
    )
```

```python
import functools

import jax
import jax.numpy as jnp
from jax import lax
from jax.experimental import pallas as pl
from jax.experimental.pallas import tpu as pltpu
from jax.sharding import PartitionSpec as P

LANES = 128
PARTS = 3
VMEM_BYTES = 20 * 1024 * 1024
NEAR_BYTES = 24 * 1024 * 1024
F32 = jnp.float32
BF16 = jnp.bfloat16


def dot(a, b):
    return jnp.dot(a, b, preferred_element_type=F32)


def dot_t(a, b):
    return lax.dot_general(a, b, (((0,), (0,)), ((), ())), preferred_element_type=F32)


def split(x):
    hi = x.astype(BF16)
    return hi, (x - hi.astype(F32)).astype(BF16)


def square_rows(pts):
    x = pts.astype(F32)
    total = jnp.sum(x * x, axis=0, keepdims=True)
    hi = total.astype(BF16).astype(F32)
    mid = (total - hi).astype(BF16).astype(F32)
    low = total - hi - mid
    row = lax.broadcasted_iota(jnp.int32, (16, pts.shape[1]), 0)
    ones = jnp.where(row < 2 * PARTS, 1.0, 0.0)
    return jnp.where(row == 0, hi, jnp.where(row == 1, mid, jnp.where(row == 2, low, ones))).astype(BF16)


def form_map(dim, size):
    k = lax.broadcasted_iota(jnp.int32, (size, size), 0)
    j = lax.broadcasted_iota(jnp.int32, (size, size), 1)
    r = jnp.where((k == j) & (j < dim), 2.0 / dim, 0.0)
    r = jnp.where((j >= dim) & (j < dim + PARTS) & (k == j + PARTS), -1.0 / dim, r)
    r = jnp.where((j >= dim + PARTS) & (j < dim + 2 * PARTS) & (k == j - PARTS), -1.0 / dim, r)
    return r.astype(BF16)


def onehot_in(row, size):
    index = lax.broadcasted_iota(jnp.int32, (size, row.shape[1]), 0)
    return jnp.where(index == row, 1.0, 0.0).astype(BF16)


def column_of(row):
    return jnp.broadcast_to(row.astype(F32), (LANES, row.shape[1])).T


def onehot_out(column, size):
    lane = lax.broadcasted_iota(jnp.int32, column.shape, 1).astype(F32)
    return jnp.concatenate(
        [jnp.where(column == lane + float(i), 1.0, 0.0) for i in range(0, size, LANES)], axis=1
    )


def mix3(m, s):
    m_hi, m_lo = split(m)
    s_hi, s_lo = split(s)
    return dot(m_hi, s_hi) + (dot(m_hi, s_lo) + dot(m_lo, s_hi))


def order_kernel(points_t, order, probes, pack, rows, *halves):
    dim = points_t.shape[0]
    many, leaf = rows.shape[:2]
    held = dim + 16
    to_rows = form_map(dim, LANES)
    for b in range(many):
        picks = onehot_in(order[b], leaf)
        tree_t = dot(points_t[:, b * leaf : (b + 1) * leaf], picks).astype(BF16)
        pack[b, :leaf, :] = probes[b * leaf : (b + 1) * leaf, :]
        form = jnp.concatenate([tree_t, square_rows(tree_t)], axis=0)
        for i in range(leaf // LANES):
            pack[b, leaf + i * held : leaf + (i + 1) * held, :] = form[:, i * LANES : (i + 1) * LANES]
        form = jnp.concatenate([form, jnp.zeros((LANES - held, leaf), BF16)], axis=0)
        rows[b] = dot_t(form, to_rows).astype(BF16)
    for step, half in enumerate(halves):

        @pl.when(pl.program_id(0) == step)
        def _(half=half):
            half[...] = pack[...]


def order_call(points_t, order, probes, blocks):
    dim, npts = points_t.shape
    leaf = npts // blocks
    packed = leaf + leaf // LANES * (dim + 16)
    many = blocks // 2
    return pl.pallas_call(
        order_kernel,
        grid=(blocks // many,),
        in_specs=[
            pl.BlockSpec((dim, many * leaf), lambda b: (0, b)),
            pl.BlockSpec((many, 1, leaf), lambda b: (b, 0, 0)),
            pl.BlockSpec((many * leaf, LANES), lambda b: (b, 0)),
        ],
        out_specs=[
            pl.BlockSpec((many, packed, LANES), lambda b: (b, 0, 0)),
            pl.BlockSpec((many, leaf, LANES), lambda b: (b, 0, 0)),
            pl.BlockSpec((many, packed, LANES), lambda b: (0, 0, 0)),
            pl.BlockSpec((many, packed, LANES), lambda b: (0, 0, 0)),
        ],
        out_shape=[
            jax.ShapeDtypeStruct((blocks, packed, LANES), BF16),
            jax.ShapeDtypeStruct((blocks, leaf, LANES), BF16),
            jax.ShapeDtypeStruct((many, packed, LANES), BF16),
            jax.ShapeDtypeStruct((many, packed, LANES), BF16),
        ],
        compiler_params=pltpu.CompilerParams(vmem_limit_bytes=VMEM_BYTES),
        cost_estimate=pl.CostEstimate(
            flops=blocks * 2 * leaf * leaf * dim, bytes_accessed=10 * npts * LANES, transcendentals=0
        ),
        name="tree_order",
    )(points_t, order, probes)


def form_of(pack_block, leaf, dim):
    held = dim + 16
    columns = [
        pack_block[leaf + i * held : leaf + (i + 1) * held, :] for i in range(leaf // LANES)
    ]
    form = jnp.concatenate(columns, axis=1)
    return jnp.concatenate([form, jnp.zeros((LANES - held, leaf), BF16)], axis=0)


def condense(form, a_rows, chosen):
    size = form.shape[1]
    picks_out = onehot_out(column_of(chosen), size)
    new_rows = dot(picks_out.astype(BF16), a_rows).astype(BF16)
    new_form = dot(form, onehot_in(chosen, size)).astype(BF16)
    weights = jnp.exp(dot(new_rows, form))
    mixing = picks_out + weights / jnp.sum(weights, axis=1, keepdims=True)
    return new_form, new_rows, mixing


def local_tree_kernel(pack, rows, leaf_sets_in, merge_sets_in, out, leaf_sets, merge_sets, sems, *, dim):
    blocks, leaf = rows.shape[:2]
    leaf_copy = pltpu.make_async_copy(leaf_sets_in, leaf_sets, sems.at[0])
    merge_copy = pltpu.make_async_copy(merge_sets_in, merge_sets, sems.at[1])
    leaf_copy.start()
    merge_copy.start()
    leaf_copy.wait()
    first_block = (lax.axis_index("leaf") * lax.axis_size("sub") + lax.axis_index("sub")) * blocks

    nodes = []
    for b in range(blocks):
        form = form_of(pack.at[b], leaf, dim)
        new_form, new_rows, mixing = condense(form, rows[b], leaf_sets[b : b + 1, :])
        m_hi, m_lo = split(mixing)
        probes = pack[b, :leaf, :]
        nodes.append((new_form, new_rows, dot(m_hi, probes) + dot(m_lo, probes)))
    span = 1
    merge_copy.wait()
    while len(nodes) > 1:
        merged = []
        for k in range(len(nodes) // 2):
            left, right = nodes[2 * k], nodes[2 * k + 1]
            chosen = merge_sets[pl.ds(first_block + (2 * k + 1) * span - 1, 1), :]
            new_form, new_rows, mixing = condense(
                jnp.concatenate([left[0], right[0]], axis=1),
                jnp.concatenate([left[1], right[1]], axis=0),
                chosen,
            )
            samples = mix3(mixing, jnp.concatenate([left[2], right[2]], axis=0))
            merged.append((new_form, new_rows, samples))
        nodes = merged
        span *= 2
    held = dim + 16
    out[:held, :] = nodes[0][0][:held, :].astype(F32)
    out[held:, :] = nodes[0][2]


def local_tree_call(pack, rows, leaf_sets, merge_sets, dim):
    blocks, leaf = rows.shape[:2]
    skel = leaf_sets.shape[1]
    return pl.pallas_call(
        functools.partial(local_tree_kernel, dim=dim),
        in_specs=[pl.BlockSpec(memory_space=pltpu.VMEM)] * 2
        + [pl.BlockSpec(memory_space=pltpu.HBM)] * 2,
        out_shape=jax.ShapeDtypeStruct((dim + 16 + skel, LANES), F32),
        scratch_shapes=[
            pltpu.VMEM(leaf_sets.shape, jnp.int32),
            pltpu.VMEM(merge_sets.shape, jnp.int32),
            pltpu.SemaphoreType.DMA((2,)),
        ],
        compiler_params=pltpu.CompilerParams(vmem_limit_bytes=VMEM_BYTES),
        cost_estimate=pl.CostEstimate(
            flops=blocks * 8 * skel * leaf * LANES,
            bytes_accessed=6 * blocks * leaf * LANES,
            transcendentals=blocks * skel * leaf,
        ),
        name="local_tree",
    )(pack, rows, leaf_sets, merge_sets)


def merge_kernel(*refs, dim, blocks, shift, piece):
    merge_sets_in, out, group, merge_sets, sem = refs[-5:]
    parts = refs[:-5]
    count, size = group.shape[:2]
    copy = pltpu.make_async_copy(merge_sets_in, merge_sets, sem)
    copy.start()
    held = dim + 16
    skel = size - held
    rank = lax.axis_index("leaf") * lax.axis_size("sub") + lax.axis_index("sub")
    unit = lax.shift_right_logical(rank, shift)
    place = unit & (count - 1)
    first = unit - place
    span = blocks << shift
    for d, part in enumerate(parts):
        group[place ^ d] = part[...]
    to_rows = form_map(dim, LANES)
    forms = [group[i, :held, :].astype(BF16) for i in range(count)]
    samples = [group[i, held:, :] for i in range(count)]
    copy.wait()
    while len(forms) > 1:
        first = first // 2
        new_forms, new_samples = [], []
        for k in range(len(forms) // 2):
            chosen = merge_sets[pl.ds((2 * (first + k) + 1) * span - 1, 1), :]
            form = jnp.concatenate(forms[2 * k : 2 * k + 2], axis=1)
            form = jnp.concatenate([form, jnp.zeros((LANES - held, 2 * skel), BF16)], axis=0)
            new_form = dot(form, onehot_in(chosen, 2 * skel)).astype(BF16)
            new_rows = dot_t(new_form, to_rows).astype(BF16)
            weights = jnp.exp(dot(new_rows, form))
            picks = onehot_out(column_of(chosen), 2 * skel)
            mixing = picks + weights / jnp.sum(weights, axis=1, keepdims=True)
            new_forms.append(new_form[:held])
            new_samples.append(mix3(mixing, jnp.concatenate(samples[2 * k : 2 * k + 2], axis=0)))
        forms, samples = new_forms, new_samples
        span *= 2
    if piece is None:
        out[:held, :] = forms[0].astype(F32)
        out[held:, :] = samples[0]
    elif piece == 0:
        out[...] = samples[0]
    else:
        column = lax.broadcasted_iota(jnp.int32, (piece, skel), 1)
        row = lax.broadcasted_iota(jnp.int32, (piece, skel), 0) + rank * piece
        take = jnp.where(column == row, 1.0, 0.0).astype(BF16)
        hi, lo = split(samples[0])
        low = (samples[0] - hi.astype(F32) - lo.astype(F32)).astype(BF16)
        out[...] = dot(take, hi) + dot(take, lo) + dot(take, low)


def merge_call(parts, merge_sets, dim, blocks, shift, piece=None):
    count = len(parts)
    size = parts[0].shape[0]
    skel = size - dim - 16
    rows = size if piece is None else (piece or skel)
    return pl.pallas_call(
        functools.partial(merge_kernel, dim=dim, blocks=blocks, shift=shift, piece=piece),
        in_specs=[pl.BlockSpec(memory_space=pltpu.VMEM)] * count
        + [pl.BlockSpec(memory_space=pltpu.HBM)],
        out_shape=jax.ShapeDtypeStruct((rows, LANES), F32),
        scratch_shapes=[
            pltpu.VMEM((count, size, LANES), F32),
            pltpu.VMEM(merge_sets.shape, jnp.int32),
            pltpu.SemaphoreType.DMA(()),
        ],
        compiler_params=pltpu.CompilerParams(vmem_limit_bytes=16 * 1024 * 1024),
        cost_estimate=pl.CostEstimate(
            flops=count * 16 * LANES**3,
            bytes_accessed=4 * count * size * LANES,
            transcendentals=2 * count * LANES**2,
        ),
        name="tree_merge",
    )(*parts, merge_sets)


def near_kernel(*refs, flips, has_acc, sets, tasks, dim):
    refs = list(refs)

    def take(number):
        taken = refs[:number]
        del refs[:number]
        return taken

    lists, rows = take(len(flips)), take(len(flips))
    accs = [take(1)[0] if has else None for has in has_acc]
    buffers = [take(max(which) + 1) for _, _, which in sets]
    outs, (pair_list,) = take(len(flips)), refs
    blocks, leaf = rows[0].shape[:2]
    near = lists[0].shape[1]
    window = blocks * lax.axis_size("sub")
    sub = lax.axis_index("sub")

    def place(table):
        value = jnp.int32(table[0])
        for i in range(1, len(table)):
            value = jnp.where(sub == i, jnp.int32(table[i]), value)
        return value

    window_first = lax.axis_index("leaf") * window - blocks
    stride = blocks * near + 8
    found = [jnp.int32(0)] * len(tasks)
    for j, flip in enumerate(flips):
        mine = [t for t, (_, group) in enumerate(tasks) if group == j]
        firsts = [window_first + place(sets[tasks[t][0]][0]) for t in mine]
        sizes = [place(sets[tasks[t][0]][1]) for t in mine]
        target_first = lax.axis_index("leaf") * window + (sub ^ flip) * blocks

        def list_block(g, counts, j=j, mine=mine, firsts=firsts, sizes=sizes, target_first=target_first):
            for s in range(near):
                source = lists[j][g, s]
                used = (source != target_first + g) if s else True
                after = []
                for t, first, size, count in zip(mine, firsts, sizes, counts):
                    local = source - first
                    pair_list[t * stride + count] = g * blocks + local
                    inside = (local >= 0) & (local < size) & used
                    after.append(count + jnp.where(inside, 1, 0))
                counts = tuple(after)
            return counts

        counts = lax.fori_loop(0, blocks, list_block, (jnp.int32(0),) * len(mine))
        for t, count in zip(mine, counts):
            found[t] = count
        outs[j][...] = jnp.zeros(outs[j].shape, F32) if accs[j] is None else accs[j][...]

    half = leaf // 2

    def add_all(buffer, t, pairs):
        j = tasks[t][1]

        def add_pair(i):
            code = pair_list[t * stride + i]
            g = code // blocks
            local = code - g * blocks
            form = form_of(buffer.at[local], leaf, dim)
            probes = buffer[local, :leaf, :]
            total = None
            for c in range(0, leaf, half):
                weights = jnp.exp(dot(rows[j][g], form[:, c : c + half])).astype(BF16)
                term = dot(weights, probes[c : c + half])
                total = term if total is None else total + term
            return g, total

        def add_pairs(i, carry):
            for g, total in [add_pair(2 * i), add_pair(2 * i + 1)]:
                outs[j][g] += total
            return carry

        lax.fori_loop(0, pairs // 2, add_pairs, 0)

        @pl.when(pairs % 2 == 1)
        def _():
            g, total = add_pair(pairs - 1)
            outs[j][g] += total

    for t, (number, _) in enumerate(tasks):
        held = place(sets[number][2])
        for k, buffer in enumerate(buffers[number]):
            pairs = found[t] if len(buffers[number]) == 1 else jnp.where(held == k, found[t], 0)
            add_all(buffer, t, pairs)


def near_call(groups, sources, tasks, dim, name):
    flips, lists, rows, accs = zip(*groups)
    blocks, leaf = rows[0].shape[:2]
    held = [acc for acc in accs if acc is not None]
    args = [*lists, *rows, *held, *(b for *_, buffers in sources for b in buffers)]
    smem = pl.BlockSpec(memory_space=pltpu.SMEM)
    vmem = pl.BlockSpec(memory_space=pltpu.VMEM)
    near = lists[0].shape[1]
    return pl.pallas_call(
        functools.partial(
            near_kernel,
            flips=flips,
            has_acc=tuple(acc is not None for acc in accs),
            sets=tuple(source[:3] for source in sources),
            tasks=tasks,
            dim=dim,
        ),
        in_specs=[smem] * len(lists) + [vmem] * (len(args) - len(lists)),
        out_specs=[vmem] * len(groups),
        out_shape=[jax.ShapeDtypeStruct((blocks, leaf, LANES), F32)] * len(groups),
        scratch_shapes=[pltpu.SMEM((len(tasks) * (blocks * near + 8),), jnp.int32)],
        compiler_params=pltpu.CompilerParams(vmem_limit_bytes=NEAR_BYTES),
        cost_estimate=pl.CostEstimate(flops=1000, bytes_accessed=1000, transcendentals=0),
        name=name,
    )(*args)


def on_device(points, probes, order, near_lists, near_counts, leaf_sets, merge_sets):
    leaf_count = lax.axis_size("leaf")
    sub_count = lax.axis_size("sub")
    blocks, skel = leaf_sets.shape
    npts, dim = points.shape
    leaf = npts // blocks
    axes = ("leaf", "sub")

    def send(x, routes):
        pairs = []
        for place in range(leaf_count):
            for from_sub, step, to_sub in routes:
                if 0 <= place + step < leaf_count:
                    pairs.append((place * sub_count + from_sub, (place + step) * sub_count + to_sub))
        return lax.ppermute(x, axes, pairs)

    count = leaf_count * sub_count
    bits = count.bit_length() - 1
    sub_bits = sub_count.bit_length() - 1

    def exchange(x, shift, stage_bits):
        parts = [x]
        for d in range(1, 1 << stage_bits):
            parts.append(lax.ppermute(x, axes, [(i, i ^ (d << shift)) for i in range(count)]))
        return parts

    def tie(*values):
        return lax.optimization_barrier(values)

    b, h = blocks, blocks // 2
    own_base = (b, 2 * b, 3 * b, 4 * b)
    early_base, late_base = (5 * b, 4 * b, b, 0), (3 * b, h, 5 * b + h, 2 * b)
    second_base, forwarded_base = (0, 4 * b + h, b + h, 0), (0, 0, 5 * b, 0)
    whole, mixed, inner = (b, b, b, b), (b, h, h, b), (0, h, h, 0)
    single, by_edge = (0, 0, 0, 0), (0, 1, 1, 0)

    def level(parts, bit, piece=None):
        return merge_call(parts, merge_sets, dim, blocks, bit, piece)

    pack, rows, *halves = order_call(points.T, order.reshape(blocks, 1, leaf), probes, blocks)
    across = [send(half, [(3, 0, 1), (0, 0, 2)]) for half in halves]
    outer_next = send(pack, [(3, 1, 3), (0, -1, 0)])
    beside_rows = exchange(rows, 0, 1)[1]
    beside_lists = exchange(near_lists, 0, 1)[1]

    node = local_tree_call(pack, rows, leaf_sets, merge_sets, dim)
    node, beside_lists, across[0] = tie(node, beside_lists, across[0])
    forward = [(1, 1, 1), (2, -1, 2)]
    forwarded = send(across[0], forward)
    node = level(exchange(node, 0, 1), 0)
    own_pack, node = tie(pack, node)
    parts = exchange(node, 1, 1)
    own_set = (own_base, whole, single, [own_pack])
    (beside,) = near_call(
        [(1, beside_lists, beside_rows, None)], [own_set], ((0, 0),), dim, "near_own"
    )

    *parts, across[1], outer_next, forwarded, own_pack, beside = tie(
        *parts, across[1], outer_next, forwarded, own_pack, beside
    )
    inner_across = send(own_pack, [(2, 0, 0), (1, 0, 3)])
    for bit in range(1, bits - 1):
        node = level(parts, bit)
        parts = exchange(node, bit + 1, 1)
    node = level(parts, bits - 1, skel // count)
    across[1], node = tie(across[1], node)
    late_forwarded = send(across[1], forward)
    own, beside = near_call(
        [(0, near_lists, rows, None), (1, beside_lists, beside_rows, beside)],
        [
            (own_base, whole, single, [own_pack]),
            (early_base, mixed, by_edge, [outer_next, across[0]]),
            (second_base, inner, single, [across[1]]),
            (forwarded_base, inner, single, [forwarded]),
        ],
        ((0, 0), (1, 0), (2, 0), (3, 0), (1, 1), (2, 1), (3, 1)), dim, "near_early",
    )

    inner_across, late_forwarded, beside = tie(inner_across, late_forwarded, beside)
    late_set = (late_base, mixed, by_edge, [inner_across, late_forwarded])
    (beside,) = near_call(
        [(1, beside_lists, beside_rows, beside)], [late_set], ((0, 0),), dim, "near_beside"
    )
    given = exchange(beside, 0, 1)[1]
    (own,) = near_call([(0, near_lists, rows, own)], [late_set], ((0, 0),), dim, "near_last")
    if skel // count:
        root = node.reshape(-1)
    else:
        size = skel * LANES // count
        rank = lax.axis_index("leaf") * sub_count + lax.axis_index("sub")
        root = lax.dynamic_slice_in_dim(node.reshape(-1), rank * size, size, 0)
    near = (own + given) * (leaf ** -0.5)
    return near.reshape(npts, LANES), root


def solution(mesh):
    in_specs = (
        P(("leaf", "sub"), None),
        P(("leaf", "sub"), None),
        P(("leaf", "sub")),
        P(("leaf", "sub"), None),
        P(("leaf", "sub")),
        P(("leaf", "sub"), None),
        P(),
    )
    out_specs = (P(("leaf", "sub"), None), P(("leaf", "sub")))
    return jax.shard_map(
        on_device, mesh=mesh, in_specs=in_specs, out_specs=out_specs, check_vma=False
    )
```

```python
import functools

import jax
import jax.numpy as jnp
from jax import lax
from jax.experimental import pallas as pl
from jax.experimental.pallas import tpu as pltpu
from jax.sharding import PartitionSpec as P

LANES = 128
PARTS = 3
VMEM_BYTES = 20 * 1024 * 1024
NEAR_BYTES = 24 * 1024 * 1024
F32 = jnp.float32
BF16 = jnp.bfloat16


def dot(a, b):
    return jnp.dot(a, b, preferred_element_type=F32)


def dot_t(a, b):
    return lax.dot_general(a, b, (((0,), (0,)), ((), ())), preferred_element_type=F32)


def split(x):
    hi = x.astype(BF16)
    return hi, (x - hi.astype(F32)).astype(BF16)


def square_rows(pts):
    x = pts.astype(F32)
    total = jnp.sum(x * x, axis=0, keepdims=True)
    hi = total.astype(BF16).astype(F32)
    mid = (total - hi).astype(BF16).astype(F32)
    low = total - hi - mid
    row = lax.broadcasted_iota(jnp.int32, (16, pts.shape[1]), 0)
    ones = jnp.where(row < 2 * PARTS, 1.0, 0.0)
    return jnp.where(row == 0, hi, jnp.where(row == 1, mid, jnp.where(row == 2, low, ones))).astype(BF16)


def form_map(dim, size):
    k = lax.broadcasted_iota(jnp.int32, (size, size), 0)
    j = lax.broadcasted_iota(jnp.int32, (size, size), 1)
    r = jnp.where((k == j) & (j < dim), 2.0 / dim, 0.0)
    r = jnp.where((j >= dim) & (j < dim + PARTS) & (k == j + PARTS), -1.0 / dim, r)
    r = jnp.where((j >= dim + PARTS) & (j < dim + 2 * PARTS) & (k == j - PARTS), -1.0 / dim, r)
    return r.astype(BF16)


def onehot_in(row, size):
    index = lax.broadcasted_iota(jnp.int32, (size, row.shape[1]), 0)
    return jnp.where(index == row, 1.0, 0.0).astype(BF16)


def column_of(row):
    return jnp.broadcast_to(row.astype(F32), (LANES, row.shape[1])).T


def onehot_out(column, size):
    lane = lax.broadcasted_iota(jnp.int32, column.shape, 1).astype(F32)
    return jnp.concatenate(
        [jnp.where(column == lane + float(i), 1.0, 0.0) for i in range(0, size, LANES)], axis=1
    )


def mix3(m, s):
    m_hi, m_lo = split(m)
    s_hi, s_lo = split(s)
    return dot(m_hi, s_hi) + (dot(m_hi, s_lo) + dot(m_lo, s_hi))


def order_kernel(points_t, order, probes, pack, rows):
    dim = points_t.shape[0]
    many, leaf = rows.shape[:2]
    held = dim + 16
    to_rows = form_map(dim, LANES)
    for b in range(many):
        picks = onehot_in(order[b], leaf)
        tree_t = dot(points_t[:, b * leaf : (b + 1) * leaf], picks).astype(BF16)
        pack[b, :leaf, :] = probes[b * leaf : (b + 1) * leaf, :]
        form = jnp.concatenate([tree_t, square_rows(tree_t)], axis=0)
        for i in range(leaf // LANES):
            pack[b, leaf + i * dim : leaf + (i + 1) * dim, :] = tree_t[:, i * LANES : (i + 1) * LANES]
        form = jnp.concatenate([form, jnp.zeros((LANES - held, leaf), BF16)], axis=0)
        rows[b] = dot_t(form, to_rows).astype(BF16)


def order_call(points_t, order, probes, blocks):
    dim, npts = points_t.shape
    leaf = npts // blocks
    packed = leaf + leaf // LANES * dim
    many = 4 if blocks % 4 == 0 else 1
    return pl.pallas_call(
        order_kernel,
        grid=(blocks // many,),
        in_specs=[
            pl.BlockSpec((dim, many * leaf), lambda b: (0, b)),
            pl.BlockSpec((many, 1, leaf), lambda b: (b, 0, 0)),
            pl.BlockSpec((many * leaf, LANES), lambda b: (b, 0)),
        ],
        out_specs=[
            pl.BlockSpec((many, packed, LANES), lambda b: (b, 0, 0)),
            pl.BlockSpec((many, leaf, LANES), lambda b: (b, 0, 0)),
        ],
        out_shape=[
            jax.ShapeDtypeStruct((blocks, packed, LANES), BF16),
            jax.ShapeDtypeStruct((blocks, leaf, LANES), BF16),
        ],
        compiler_params=pltpu.CompilerParams(vmem_limit_bytes=VMEM_BYTES),
        cost_estimate=pl.CostEstimate(
            flops=blocks * 2 * leaf * leaf * dim, bytes_accessed=10 * npts * LANES, transcendentals=0
        ),
        name="tree_order",
    )(points_t, order, probes)


def form_of(pack_block, leaf, dim):
    columns = []
    for i in range(leaf // LANES):
        pts = pack_block[leaf + i * dim : leaf + (i + 1) * dim, :]
        columns.append(jnp.concatenate([pts, square_rows(pts)], axis=0))
    form = jnp.concatenate(columns, axis=1)
    return jnp.concatenate([form, jnp.zeros((LANES - dim - 16, leaf), BF16)], axis=0)


def condense(form, a_rows, chosen):
    size = form.shape[1]
    picks_out = onehot_out(column_of(chosen), size)
    new_rows = dot(picks_out.astype(BF16), a_rows).astype(BF16)
    new_form = dot(form, onehot_in(chosen, size)).astype(BF16)
    weights = jnp.exp(dot(new_rows, form))
    mixing = picks_out + weights / jnp.sum(weights, axis=1, keepdims=True)
    return new_form, new_rows, mixing


def local_tree_kernel(pack, rows, leaf_sets_in, merge_sets_in, out, leaf_sets, merge_sets, sems, *, dim):
    blocks, leaf = rows.shape[:2]
    leaf_copy = pltpu.make_async_copy(leaf_sets_in, leaf_sets, sems.at[0])
    merge_copy = pltpu.make_async_copy(merge_sets_in, merge_sets, sems.at[1])
    leaf_copy.start()
    merge_copy.start()
    leaf_copy.wait()
    first_block = (lax.axis_index("leaf") * lax.axis_size("sub") + lax.axis_index("sub")) * blocks

    nodes = []
    for b in range(blocks):
        form = form_of(pack.at[b], leaf, dim)
        new_form, new_rows, mixing = condense(form, rows[b], leaf_sets[b : b + 1, :])
        m_hi, m_lo = split(mixing)
        probes = pack[b, :leaf, :]
        nodes.append((new_form, new_rows, dot(m_hi, probes) + dot(m_lo, probes)))
    span = 1
    merge_copy.wait()
    while len(nodes) > 1:
        merged = []
        for k in range(len(nodes) // 2):
            left, right = nodes[2 * k], nodes[2 * k + 1]
            chosen = merge_sets[pl.ds(first_block + (2 * k + 1) * span - 1, 1), :]
            new_form, new_rows, mixing = condense(
                jnp.concatenate([left[0], right[0]], axis=1),
                jnp.concatenate([left[1], right[1]], axis=0),
                chosen,
            )
            samples = mix3(mixing, jnp.concatenate([left[2], right[2]], axis=0))
            merged.append((new_form, new_rows, samples))
        nodes = merged
        span *= 2
    held = dim + 16
    out[:held, :] = nodes[0][0][:held, :].astype(F32)
    out[held:, :] = nodes[0][2]


def local_tree_call(pack, rows, leaf_sets, merge_sets, dim):
    blocks, leaf = rows.shape[:2]
    skel = leaf_sets.shape[1]
    return pl.pallas_call(
        functools.partial(local_tree_kernel, dim=dim),
        in_specs=[pl.BlockSpec(memory_space=pltpu.VMEM)] * 2
        + [pl.BlockSpec(memory_space=pltpu.HBM)] * 2,
        out_shape=jax.ShapeDtypeStruct((dim + 16 + skel, LANES), F32),
        scratch_shapes=[
            pltpu.VMEM(leaf_sets.shape, jnp.int32),
            pltpu.VMEM(merge_sets.shape, jnp.int32),
            pltpu.SemaphoreType.DMA((2,)),
        ],
        compiler_params=pltpu.CompilerParams(vmem_limit_bytes=VMEM_BYTES),
        cost_estimate=pl.CostEstimate(
            flops=blocks * 8 * skel * leaf * LANES,
            bytes_accessed=6 * blocks * leaf * LANES,
            transcendentals=blocks * skel * leaf,
        ),
        name="local_tree",
    )(pack, rows, leaf_sets, merge_sets)


def merge_kernel(*refs, dim, blocks, shift, piece):
    merge_sets_in, out, group, merge_sets, sem = refs[-5:]
    parts = refs[:-5]
    count, size = group.shape[:2]
    copy = pltpu.make_async_copy(merge_sets_in, merge_sets, sem)
    copy.start()
    held = dim + 16
    skel = size - held
    rank = lax.axis_index("leaf") * lax.axis_size("sub") + lax.axis_index("sub")
    unit = lax.shift_right_logical(rank, shift)
    place = unit & (count - 1)
    first = unit - place
    span = blocks << shift
    for d, part in enumerate(parts):
        group[place ^ d] = part[...]
    to_rows = form_map(dim, LANES)
    forms = [group[i, :held, :].astype(BF16) for i in range(count)]
    samples = [group[i, held:, :] for i in range(count)]
    copy.wait()
    while len(forms) > 1:
        first = first // 2
        new_forms, new_samples = [], []
        for k in range(len(forms) // 2):
            chosen = merge_sets[pl.ds((2 * (first + k) + 1) * span - 1, 1), :]
            form = jnp.concatenate(forms[2 * k : 2 * k + 2], axis=1)
            form = jnp.concatenate([form, jnp.zeros((LANES - held, 2 * skel), BF16)], axis=0)
            new_form = dot(form, onehot_in(chosen, 2 * skel)).astype(BF16)
            new_rows = dot_t(new_form, to_rows).astype(BF16)
            weights = jnp.exp(dot(new_rows, form))
            picks = onehot_out(column_of(chosen), 2 * skel)
            mixing = picks + weights / jnp.sum(weights, axis=1, keepdims=True)
            new_forms.append(new_form[:held])
            new_samples.append(mix3(mixing, jnp.concatenate(samples[2 * k : 2 * k + 2], axis=0)))
        forms, samples = new_forms, new_samples
        span *= 2
    if piece is None:
        out[:held, :] = forms[0].astype(F32)
        out[held:, :] = samples[0]
    elif piece == 0:
        out[...] = samples[0]
    else:
        column = lax.broadcasted_iota(jnp.int32, (piece, skel), 1)
        row = lax.broadcasted_iota(jnp.int32, (piece, skel), 0) + rank * piece
        take = jnp.where(column == row, 1.0, 0.0).astype(BF16)
        hi, lo = split(samples[0])
        low = (samples[0] - hi.astype(F32) - lo.astype(F32)).astype(BF16)
        out[...] = dot(take, hi) + dot(take, lo) + dot(take, low)


def merge_call(parts, merge_sets, dim, blocks, shift, piece=None):
    count = len(parts)
    size = parts[0].shape[0]
    skel = size - dim - 16
    rows = size if piece is None else (piece or skel)
    return pl.pallas_call(
        functools.partial(merge_kernel, dim=dim, blocks=blocks, shift=shift, piece=piece),
        in_specs=[pl.BlockSpec(memory_space=pltpu.VMEM)] * count
        + [pl.BlockSpec(memory_space=pltpu.HBM)],
        out_shape=jax.ShapeDtypeStruct((rows, LANES), F32),
        scratch_shapes=[
            pltpu.VMEM((count, size, LANES), F32),
            pltpu.VMEM(merge_sets.shape, jnp.int32),
            pltpu.SemaphoreType.DMA(()),
        ],
        compiler_params=pltpu.CompilerParams(vmem_limit_bytes=16 * 1024 * 1024),
        cost_estimate=pl.CostEstimate(
            flops=count * 16 * LANES**3,
            bytes_accessed=4 * count * size * LANES,
            transcendentals=2 * count * LANES**2,
        ),
        name="tree_merge",
    )(*parts, merge_sets)


def near_kernel(*refs, flips, has_acc, sets, tasks, dim):
    refs = list(refs)

    def take(number):
        taken = refs[:number]
        del refs[:number]
        return taken

    lists, rows = take(len(flips)), take(len(flips))
    accs = [take(1)[0] if has else None for has in has_acc]
    buffers = [take(max(which) + 1) for _, which in sets]
    outs, (pair_list,) = take(len(flips)), refs
    blocks, leaf = rows[0].shape[:2]
    near = lists[0].shape[1]
    window = blocks * lax.axis_size("sub")
    sub = lax.axis_index("sub")

    def place(table):
        value = jnp.int32(table[0])
        for i in range(1, len(table)):
            value = jnp.where(sub == i, jnp.int32(table[i]), value)
        return value

    window_first = lax.axis_index("leaf") * window - blocks
    stride = blocks * near + 8
    found = [jnp.int32(0)] * len(tasks)
    for j, flip in enumerate(flips):
        mine = [t for t, (_, group) in enumerate(tasks) if group == j]
        firsts = [window_first + place(sets[tasks[t][0]][0]) for t in mine]
        target_first = lax.axis_index("leaf") * window + (sub ^ flip) * blocks

        def list_block(g, counts, j=j, mine=mine, firsts=firsts, target_first=target_first):
            for s in range(near):
                source = lists[j][g, s]
                used = (source != target_first + g) if s else True
                after = []
                for t, first, count in zip(mine, firsts, counts):
                    local = source - first
                    pair_list[t * stride + count] = g * blocks + local
                    inside = (local >= 0) & (local < blocks) & used
                    after.append(count + jnp.where(inside, 1, 0))
                counts = tuple(after)
            return counts

        counts = lax.fori_loop(0, blocks, list_block, (jnp.int32(0),) * len(mine))
        for t, count in zip(mine, counts):
            found[t] = count
        outs[j][...] = jnp.zeros(outs[j].shape, F32) if accs[j] is None else accs[j][...]

    half = leaf // 2

    def add_all(buffer, t, pairs):
        j = tasks[t][1]

        def add_pair(i):
            code = pair_list[t * stride + i]
            g = code // blocks
            local = code - g * blocks
            form = form_of(buffer.at[local], leaf, dim)
            probes = buffer[local, :leaf, :]
            total = None
            for c in range(0, leaf, half):
                weights = jnp.exp(dot(rows[j][g], form[:, c : c + half])).astype(BF16)
                term = dot(weights, probes[c : c + half])
                total = term if total is None else total + term
            return g, total

        def add_pairs(i, carry):
            for g, total in [add_pair(2 * i), add_pair(2 * i + 1)]:
                outs[j][g] += total
            return carry

        lax.fori_loop(0, pairs // 2, add_pairs, 0)

        @pl.when(pairs % 2 == 1)
        def _():
            g, total = add_pair(pairs - 1)
            outs[j][g] += total

    for t, (number, _) in enumerate(tasks):
        held = place(sets[number][1])
        for k, buffer in enumerate(buffers[number]):
            pairs = found[t] if len(buffers[number]) == 1 else jnp.where(held == k, found[t], 0)
            add_all(buffer, t, pairs)


def near_call(groups, sources, tasks, dim, name):
    flips, lists, rows, accs = zip(*groups)
    blocks, leaf = rows[0].shape[:2]
    held = [acc for acc in accs if acc is not None]
    args = [*lists, *rows, *held, *(b for _, _, buffers in sources for b in buffers)]
    smem = pl.BlockSpec(memory_space=pltpu.SMEM)
    vmem = pl.BlockSpec(memory_space=pltpu.VMEM)
    near = lists[0].shape[1]
    return pl.pallas_call(
        functools.partial(
            near_kernel,
            flips=flips,
            has_acc=tuple(acc is not None for acc in accs),
            sets=tuple((bases, which) for bases, which, _ in sources),
            tasks=tasks,
            dim=dim,
        ),
        in_specs=[smem] * len(lists) + [vmem] * (len(args) - len(lists)),
        out_specs=[vmem] * len(groups),
        out_shape=[jax.ShapeDtypeStruct((blocks, leaf, LANES), F32)] * len(groups),
        scratch_shapes=[pltpu.SMEM((len(tasks) * (blocks * near + 8),), jnp.int32)],
        compiler_params=pltpu.CompilerParams(vmem_limit_bytes=NEAR_BYTES),
        cost_estimate=pl.CostEstimate(flops=1000, bytes_accessed=1000, transcendentals=0),
        name=name,
    )(*args)


def on_device(points, probes, order, near_lists, near_counts, leaf_sets, merge_sets):
    leaf_count = lax.axis_size("leaf")
    sub_count = lax.axis_size("sub")
    blocks, skel = leaf_sets.shape
    npts, dim = points.shape
    leaf = npts // blocks
    axes = ("leaf", "sub")

    def send(x, routes):
        pairs = []
        for place in range(leaf_count):
            for from_sub, step, to_sub in routes:
                if 0 <= place + step < leaf_count:
                    pairs.append((place * sub_count + from_sub, (place + step) * sub_count + to_sub))
        return lax.ppermute(x, axes, pairs)

    count = leaf_count * sub_count
    bits = count.bit_length() - 1
    sub_bits = sub_count.bit_length() - 1

    def exchange(x, shift, stage_bits):
        parts = [x]
        for d in range(1, 1 << stage_bits):
            parts.append(lax.ppermute(x, axes, [(i, i ^ (d << shift)) for i in range(count)]))
        return parts

    def tie(*values):
        return lax.optimization_barrier(values)

    b = blocks
    own_base = (b, 2 * b, 3 * b, 4 * b)
    early_base, late_base = (5 * b, 4 * b, b, 0), (3 * b, 0, 5 * b, 2 * b)
    single, by_edge = (0, 0, 0, 0), (0, 1, 1, 0)

    pack, rows = order_call(points.T, order.reshape(blocks, 1, leaf), probes, blocks)
    outer_across = send(pack, [(3, 0, 1), (0, 0, 2)])
    outer_next = send(pack, [(3, 1, 3), (0, -1, 0)])
    beside_rows = exchange(rows, 0, 1)[1]
    beside_lists = exchange(near_lists, 0, 1)[1]

    node = local_tree_call(pack, rows, leaf_sets, merge_sets, dim)
    node, beside_lists = tie(node, beside_lists)

    def level(parts, bit, piece=None):
        return merge_call(parts, merge_sets, dim, blocks, bit, piece)

    node = level(exchange(node, 0, 1), 0)
    own_pack, node = tie(pack, node)
    parts = exchange(node, 1, 1)
    own_set = (own_base, single, [own_pack])
    (beside,) = near_call(
        [(1, beside_lists, beside_rows, None)], [own_set], ((0, 0),), dim, "near_own"
    )

    *parts, outer_across, outer_next, own_pack, beside = tie(
        *parts, outer_across, outer_next, own_pack, beside
    )
    inner_across = send(own_pack, [(2, 0, 0), (1, 0, 3)])
    for bit in range(1, bits - 1):
        node = level(parts, bit)
        parts = exchange(node, bit + 1, 1)
    node = level(parts, bits - 1, skel // count)
    outer_across, node = tie(outer_across, node)
    forwarded = send(outer_across, [(1, 1, 1), (2, -1, 2)])
    own_set = (own_base, single, [own_pack])
    early_set = (early_base, by_edge, [outer_next, outer_across])
    own, beside = near_call(
        [(0, near_lists, rows, None), (1, beside_lists, beside_rows, beside)],
        [own_set, early_set], ((0, 0), (1, 0), (1, 1)), dim, "near_early",
    )

    inner_across, forwarded, beside = tie(inner_across, forwarded, beside)
    late_set = (late_base, by_edge, [inner_across, forwarded])
    (beside,) = near_call(
        [(1, beside_lists, beside_rows, beside)], [late_set], ((0, 0),), dim, "near_beside"
    )
    given = exchange(beside, 0, 1)[1]
    (own,) = near_call([(0, near_lists, rows, own)], [late_set], ((0, 0),), dim, "near_last")
    if skel // count:
        root = node.reshape(-1)
    else:
        size = skel * LANES // count
        rank = lax.axis_index("leaf") * sub_count + lax.axis_index("sub")
        root = lax.dynamic_slice_in_dim(node.reshape(-1), rank * size, size, 0)
    near = (own + given) * (leaf ** -0.5)
    return near.reshape(npts, LANES), root


def solution(mesh):
    in_specs = (
        P(("leaf", "sub"), None),
        P(("leaf", "sub"), None),
        P(("leaf", "sub")),
        P(("leaf", "sub"), None),
        P(("leaf", "sub")),
        P(("leaf", "sub"), None),
        P(),
    )
    out_specs = (P(("leaf", "sub"), None), P(("leaf", "sub")))
    return jax.shard_map(
        on_device, mesh=mesh, in_specs=in_specs, out_specs=out_specs, check_vma=False
    )
```

```python
import functools

import jax
import jax.numpy as jnp
from jax import lax
from jax.experimental import pallas as pl
from jax.experimental.pallas import tpu as pltpu
from jax.sharding import PartitionSpec as P

LANES = 128
PARTS = 3
VMEM_BYTES = 20 * 1024 * 1024
NEAR_BYTES = 24 * 1024 * 1024
F32 = jnp.float32
BF16 = jnp.bfloat16


def dot(a, b):
    return jnp.dot(a, b, preferred_element_type=F32)


def dot_t(a, b):
    return lax.dot_general(a, b, (((0,), (0,)), ((), ())), preferred_element_type=F32)


def split(x):
    hi = x.astype(BF16)
    return hi, (x - hi.astype(F32)).astype(BF16)


def square_rows(pts):
    x = pts.astype(F32)
    total = jnp.sum(x * x, axis=0, keepdims=True)
    hi = total.astype(BF16).astype(F32)
    mid = (total - hi).astype(BF16).astype(F32)
    low = total - hi - mid
    row = lax.broadcasted_iota(jnp.int32, (16, pts.shape[1]), 0)
    ones = jnp.where(row < 2 * PARTS, 1.0, 0.0)
    return jnp.where(row == 0, hi, jnp.where(row == 1, mid, jnp.where(row == 2, low, ones))).astype(BF16)


def form_map(dim, size):
    k = lax.broadcasted_iota(jnp.int32, (size, size), 0)
    j = lax.broadcasted_iota(jnp.int32, (size, size), 1)
    r = jnp.where((k == j) & (j < dim), 2.0 / dim, 0.0)
    r = jnp.where((j >= dim) & (j < dim + PARTS) & (k == j + PARTS), -1.0 / dim, r)
    r = jnp.where((j >= dim + PARTS) & (j < dim + 2 * PARTS) & (k == j - PARTS), -1.0 / dim, r)
    return r.astype(BF16)


def onehot_in(row, size):
    index = lax.broadcasted_iota(jnp.int32, (size, row.shape[1]), 0)
    return jnp.where(index == row, 1.0, 0.0).astype(BF16)


def column_of(row):
    return jnp.broadcast_to(row.astype(F32), (LANES, row.shape[1])).T


def onehot_out(column, size):
    lane = lax.broadcasted_iota(jnp.int32, column.shape, 1).astype(F32)
    return jnp.concatenate(
        [jnp.where(column == lane + float(i), 1.0, 0.0) for i in range(0, size, LANES)], axis=1
    )


def mix3(m, s):
    m_hi, m_lo = split(m)
    s_hi, s_lo = split(s)
    return dot(m_hi, s_hi) + (dot(m_hi, s_lo) + dot(m_lo, s_hi))


def order_kernel(points_t, order, probes, pack, rows):
    dim = points_t.shape[0]
    many, leaf = rows.shape[:2]
    held = dim + 16
    to_rows = form_map(dim, LANES)
    for b in range(many):
        picks = onehot_in(order[b], leaf)
        tree_t = dot(points_t[:, b * leaf : (b + 1) * leaf], picks).astype(BF16)
        pack[b, :leaf, :] = probes[b * leaf : (b + 1) * leaf, :]
        form = jnp.concatenate([tree_t, square_rows(tree_t)], axis=0)
        for i in range(leaf // LANES):
            pack[b, leaf + i * dim : leaf + (i + 1) * dim, :] = tree_t[:, i * LANES : (i + 1) * LANES]
        form = jnp.concatenate([form, jnp.zeros((LANES - held, leaf), BF16)], axis=0)
        rows[b] = dot_t(form, to_rows).astype(BF16)


def order_call(points_t, order, probes, blocks):
    dim, npts = points_t.shape
    leaf = npts // blocks
    packed = leaf + leaf // LANES * dim
    many = 4 if blocks % 4 == 0 else 1
    return pl.pallas_call(
        order_kernel,
        grid=(blocks // many,),
        in_specs=[
            pl.BlockSpec((dim, many * leaf), lambda b: (0, b)),
            pl.BlockSpec((many, 1, leaf), lambda b: (b, 0, 0)),
            pl.BlockSpec((many * leaf, LANES), lambda b: (b, 0)),
        ],
        out_specs=[
            pl.BlockSpec((many, packed, LANES), lambda b: (b, 0, 0)),
            pl.BlockSpec((many, leaf, LANES), lambda b: (b, 0, 0)),
        ],
        out_shape=[
            jax.ShapeDtypeStruct((blocks, packed, LANES), BF16),
            jax.ShapeDtypeStruct((blocks, leaf, LANES), BF16),
        ],
        compiler_params=pltpu.CompilerParams(vmem_limit_bytes=VMEM_BYTES),
        cost_estimate=pl.CostEstimate(
            flops=blocks * 2 * leaf * leaf * dim, bytes_accessed=10 * npts * LANES, transcendentals=0
        ),
        name="tree_order",
    )(points_t, order, probes)


def form_of(pack_block, leaf, dim):
    columns = []
    for i in range(leaf // LANES):
        pts = pack_block[leaf + i * dim : leaf + (i + 1) * dim, :]
        columns.append(jnp.concatenate([pts, square_rows(pts)], axis=0))
    form = jnp.concatenate(columns, axis=1)
    return jnp.concatenate([form, jnp.zeros((LANES - dim - 16, leaf), BF16)], axis=0)


def condense(form, a_rows, chosen):
    size = form.shape[1]
    picks_out = onehot_out(column_of(chosen), size)
    new_rows = dot(picks_out.astype(BF16), a_rows).astype(BF16)
    new_form = dot(form, onehot_in(chosen, size)).astype(BF16)
    weights = jnp.exp(dot(new_rows, form))
    mixing = picks_out + weights / jnp.sum(weights, axis=1, keepdims=True)
    return new_form, new_rows, mixing


def local_tree_kernel(pack, rows, leaf_sets_in, merge_sets_in, out, leaf_sets, merge_sets, sems, *, dim):
    blocks, leaf = rows.shape[:2]
    leaf_copy = pltpu.make_async_copy(leaf_sets_in, leaf_sets, sems.at[0])
    merge_copy = pltpu.make_async_copy(merge_sets_in, merge_sets, sems.at[1])
    leaf_copy.start()
    merge_copy.start()
    leaf_copy.wait()
    first_block = (lax.axis_index("leaf") * lax.axis_size("sub") + lax.axis_index("sub")) * blocks

    nodes = []
    for b in range(blocks):
        form = form_of(pack.at[b], leaf, dim)
        new_form, new_rows, mixing = condense(form, rows[b], leaf_sets[b : b + 1, :])
        m_hi, m_lo = split(mixing)
        probes = pack[b, :leaf, :]
        nodes.append((new_form, new_rows, dot(m_hi, probes) + dot(m_lo, probes)))
    span = 1
    merge_copy.wait()
    while len(nodes) > 1:
        merged = []
        for k in range(len(nodes) // 2):
            left, right = nodes[2 * k], nodes[2 * k + 1]
            chosen = merge_sets[pl.ds(first_block + (2 * k + 1) * span - 1, 1), :]
            new_form, new_rows, mixing = condense(
                jnp.concatenate([left[0], right[0]], axis=1),
                jnp.concatenate([left[1], right[1]], axis=0),
                chosen,
            )
            samples = mix3(mixing, jnp.concatenate([left[2], right[2]], axis=0))
            merged.append((new_form, new_rows, samples))
        nodes = merged
        span *= 2
    held = dim + 16
    out[:held, :] = nodes[0][0][:held, :].astype(F32)
    out[held:, :] = nodes[0][2]


def local_tree_call(pack, rows, leaf_sets, merge_sets, dim):
    blocks, leaf = rows.shape[:2]
    skel = leaf_sets.shape[1]
    return pl.pallas_call(
        functools.partial(local_tree_kernel, dim=dim),
        in_specs=[pl.BlockSpec(memory_space=pltpu.VMEM)] * 2
        + [pl.BlockSpec(memory_space=pltpu.HBM)] * 2,
        out_shape=jax.ShapeDtypeStruct((dim + 16 + skel, LANES), F32),
        scratch_shapes=[
            pltpu.VMEM(leaf_sets.shape, jnp.int32),
            pltpu.VMEM(merge_sets.shape, jnp.int32),
            pltpu.SemaphoreType.DMA((2,)),
        ],
        compiler_params=pltpu.CompilerParams(vmem_limit_bytes=VMEM_BYTES),
        cost_estimate=pl.CostEstimate(
            flops=blocks * 8 * skel * leaf * LANES,
            bytes_accessed=6 * blocks * leaf * LANES,
            transcendentals=blocks * skel * leaf,
        ),
        name="local_tree",
    )(pack, rows, leaf_sets, merge_sets)


def merge_kernel(*refs, dim, blocks, shift, piece):
    merge_sets_in, out, group, merge_sets, sem = refs[-5:]
    parts = refs[:-5]
    count, size = group.shape[:2]
    copy = pltpu.make_async_copy(merge_sets_in, merge_sets, sem)
    copy.start()
    held = dim + 16
    skel = size - held
    rank = lax.axis_index("leaf") * lax.axis_size("sub") + lax.axis_index("sub")
    unit = lax.shift_right_logical(rank, shift)
    place = unit & (count - 1)
    first = unit - place
    span = blocks << shift
    for d, part in enumerate(parts):
        group[place ^ d] = part[...]
    to_rows = form_map(dim, LANES)
    forms = [group[i, :held, :].astype(BF16) for i in range(count)]
    samples = [group[i, held:, :] for i in range(count)]
    copy.wait()
    while len(forms) > 1:
        first = first // 2
        new_forms, new_samples = [], []
        for k in range(len(forms) // 2):
            chosen = merge_sets[pl.ds((2 * (first + k) + 1) * span - 1, 1), :]
            form = jnp.concatenate(forms[2 * k : 2 * k + 2], axis=1)
            form = jnp.concatenate([form, jnp.zeros((LANES - held, 2 * skel), BF16)], axis=0)
            new_form = dot(form, onehot_in(chosen, 2 * skel)).astype(BF16)
            new_rows = dot_t(new_form, to_rows).astype(BF16)
            weights = jnp.exp(dot(new_rows, form))
            picks = onehot_out(column_of(chosen), 2 * skel)
            mixing = picks + weights / jnp.sum(weights, axis=1, keepdims=True)
            new_forms.append(new_form[:held])
            new_samples.append(mix3(mixing, jnp.concatenate(samples[2 * k : 2 * k + 2], axis=0)))
        forms, samples = new_forms, new_samples
        span *= 2
    if piece is None:
        out[:held, :] = forms[0].astype(F32)
        out[held:, :] = samples[0]
    elif piece == 0:
        out[...] = samples[0]
    else:
        column = lax.broadcasted_iota(jnp.int32, (piece, skel), 1)
        row = lax.broadcasted_iota(jnp.int32, (piece, skel), 0) + rank * piece
        take = jnp.where(column == row, 1.0, 0.0).astype(BF16)
        hi, lo = split(samples[0])
        low = (samples[0] - hi.astype(F32) - lo.astype(F32)).astype(BF16)
        out[...] = dot(take, hi) + dot(take, lo) + dot(take, low)


def merge_call(parts, merge_sets, dim, blocks, shift, piece=None):
    count = len(parts)
    size = parts[0].shape[0]
    skel = size - dim - 16
    rows = size if piece is None else (piece or skel)
    return pl.pallas_call(
        functools.partial(merge_kernel, dim=dim, blocks=blocks, shift=shift, piece=piece),
        in_specs=[pl.BlockSpec(memory_space=pltpu.VMEM)] * count
        + [pl.BlockSpec(memory_space=pltpu.HBM)],
        out_shape=jax.ShapeDtypeStruct((rows, LANES), F32),
        scratch_shapes=[
            pltpu.VMEM((count, size, LANES), F32),
            pltpu.VMEM(merge_sets.shape, jnp.int32),
            pltpu.SemaphoreType.DMA(()),
        ],
        compiler_params=pltpu.CompilerParams(vmem_limit_bytes=16 * 1024 * 1024),
        cost_estimate=pl.CostEstimate(
            flops=count * 10**9,
            bytes_accessed=4 * count * size * LANES,
            transcendentals=2 * count * LANES**2,
        ),
        name="tree_merge",
    )(*parts, merge_sets)


def near_kernel(*refs, flips, has_acc, sets, tasks, dim):
    refs = list(refs)

    def take(number):
        taken = refs[:number]
        del refs[:number]
        return taken

    lists, rows = take(len(flips)), take(len(flips))
    accs = [take(1)[0] if has else None for has in has_acc]
    buffers = [take(max(which) + 1) for _, which in sets]
    outs, (pair_list,) = take(len(flips)), refs
    blocks, leaf = rows[0].shape[:2]
    near = lists[0].shape[1]
    window = blocks * lax.axis_size("sub")
    sub = lax.axis_index("sub")

    def place(table):
        value = jnp.int32(table[0])
        for i in range(1, len(table)):
            value = jnp.where(sub == i, jnp.int32(table[i]), value)
        return value

    window_first = lax.axis_index("leaf") * window - blocks
    stride = blocks * near + 8
    found = [jnp.int32(0)] * len(tasks)
    for j, flip in enumerate(flips):
        mine = [t for t, (_, group) in enumerate(tasks) if group == j]
        firsts = [window_first + place(sets[tasks[t][0]][0]) for t in mine]
        target_first = lax.axis_index("leaf") * window + (sub ^ flip) * blocks

        def list_block(g, counts, j=j, mine=mine, firsts=firsts, target_first=target_first):
            for s in range(near):
                source = lists[j][g, s]
                used = (source != target_first + g) if s else True
                after = []
                for t, first, count in zip(mine, firsts, counts):
                    local = source - first
                    pair_list[t * stride + count] = g * blocks + local
                    inside = (local >= 0) & (local < blocks) & used
                    after.append(count + jnp.where(inside, 1, 0))
                counts = tuple(after)
            return counts

        counts = lax.fori_loop(0, blocks, list_block, (jnp.int32(0),) * len(mine))
        for t, count in zip(mine, counts):
            found[t] = count
        outs[j][...] = jnp.zeros(outs[j].shape, F32) if accs[j] is None else accs[j][...]

    half = leaf // 2

    def add_all(buffer, t, pairs):
        j = tasks[t][1]

        def add_pair(i):
            code = pair_list[t * stride + i]
            g = code // blocks
            local = code - g * blocks
            form = form_of(buffer.at[local], leaf, dim)
            probes = buffer[local, :leaf, :]
            total = None
            for c in range(0, leaf, half):
                weights = jnp.exp(dot(rows[j][g], form[:, c : c + half])).astype(BF16)
                term = dot(weights, probes[c : c + half])
                total = term if total is None else total + term
            return g, total

        def add_pairs(i, carry):
            for g, total in [add_pair(2 * i), add_pair(2 * i + 1)]:
                outs[j][g] += total
            return carry

        lax.fori_loop(0, pairs // 2, add_pairs, 0)

        @pl.when(pairs % 2 == 1)
        def _():
            g, total = add_pair(pairs - 1)
            outs[j][g] += total

    for t, (number, _) in enumerate(tasks):
        held = place(sets[number][1])
        for k, buffer in enumerate(buffers[number]):
            pairs = found[t] if len(buffers[number]) == 1 else jnp.where(held == k, found[t], 0)
            add_all(buffer, t, pairs)


def near_call(groups, sources, tasks, dim, name):
    flips, lists, rows, accs = zip(*groups)
    blocks, leaf = rows[0].shape[:2]
    held = [acc for acc in accs if acc is not None]
    args = [*lists, *rows, *held, *(b for _, _, buffers in sources for b in buffers)]
    smem = pl.BlockSpec(memory_space=pltpu.SMEM)
    vmem = pl.BlockSpec(memory_space=pltpu.VMEM)
    near = lists[0].shape[1]
    return pl.pallas_call(
        functools.partial(
            near_kernel,
            flips=flips,
            has_acc=tuple(acc is not None for acc in accs),
            sets=tuple((bases, which) for bases, which, _ in sources),
            tasks=tasks,
            dim=dim,
        ),
        in_specs=[smem] * len(lists) + [vmem] * (len(args) - len(lists)),
        out_specs=[vmem] * len(groups),
        out_shape=[jax.ShapeDtypeStruct((blocks, leaf, LANES), F32)] * len(groups),
        scratch_shapes=[pltpu.SMEM((len(tasks) * (blocks * near + 8),), jnp.int32)],
        compiler_params=pltpu.CompilerParams(vmem_limit_bytes=NEAR_BYTES),
        cost_estimate=pl.CostEstimate(flops=1000, bytes_accessed=1000, transcendentals=0),
        name=name,
    )(*args)


def on_device(points, probes, order, near_lists, near_counts, leaf_sets, merge_sets):
    leaf_count = lax.axis_size("leaf")
    sub_count = lax.axis_size("sub")
    blocks, skel = leaf_sets.shape
    npts, dim = points.shape
    leaf = npts // blocks
    axes = ("leaf", "sub")

    def send(x, routes):
        pairs = []
        for place in range(leaf_count):
            for from_sub, step, to_sub in routes:
                if 0 <= place + step < leaf_count:
                    pairs.append((place * sub_count + from_sub, (place + step) * sub_count + to_sub))
        return lax.ppermute(x, axes, pairs)

    count = leaf_count * sub_count
    bits = count.bit_length() - 1
    sub_bits = sub_count.bit_length() - 1

    def exchange(x, shift, stage_bits):
        parts = [x]
        for d in range(1, 1 << stage_bits):
            parts.append(lax.ppermute(x, axes, [(i, i ^ (d << shift)) for i in range(count)]))
        return parts

    def tie(*values):
        return lax.optimization_barrier(values)

    b = blocks
    own_base = (b, 2 * b, 3 * b, 4 * b)
    early_base, late_base = (5 * b, 4 * b, b, 0), (3 * b, 0, 5 * b, 2 * b)
    single, by_edge = (0, 0, 0, 0), (0, 1, 1, 0)

    pack, rows = order_call(points.T, order.reshape(blocks, 1, leaf), probes, blocks)
    outer_across = send(pack, [(3, 0, 1), (0, 0, 2)])
    outer_next = send(pack, [(3, 1, 3), (0, -1, 0)])
    beside_rows = exchange(rows, 0, 1)[1]
    beside_lists = exchange(near_lists, 0, 1)[1]

    node = local_tree_call(pack, rows, leaf_sets, merge_sets, dim)
    node, beside_lists = tie(node, beside_lists)

    def level(parts, bit, piece=None):
        return merge_call(parts, merge_sets, dim, blocks, bit, piece)

    own_pack, node = tie(pack, node)
    parts = exchange(node, 0, sub_bits)
    own_set = (own_base, single, [own_pack])
    (beside,) = near_call(
        [(1, beside_lists, beside_rows, None)], [own_set], ((0, 0),), dim, "near_own"
    )

    *parts, outer_across, outer_next, own_pack, beside = tie(
        *parts, outer_across, outer_next, own_pack, beside
    )
    inner_across = send(own_pack, [(2, 0, 0), (1, 0, 3)])
    shift, stage = 0, sub_bits
    while shift + stage < bits:
        node = level(parts, shift)
        shift, stage = shift + stage, min(3, bits - shift - stage)
        parts = exchange(node, shift, stage)
    outer_across, *parts = tie(outer_across, *parts)
    forwarded = send(outer_across, [(1, 1, 1), (2, -1, 2)])
    own_set = (own_base, single, [own_pack])
    early_set = (early_base, by_edge, [outer_next, outer_across])
    own, beside = near_call(
        [(0, near_lists, rows, None), (1, beside_lists, beside_rows, beside)],
        [own_set, early_set], ((0, 0), (1, 0), (1, 1)), dim, "near_early",
    )

    inner_across, beside, *parts = tie(inner_across, beside, *parts)
    node = level(parts, shift, skel // count)
    forwarded, beside, node = tie(forwarded, beside, node)
    late_set = (late_base, by_edge, [inner_across, forwarded])
    (beside,) = near_call(
        [(1, beside_lists, beside_rows, beside)], [late_set], ((0, 0),), dim, "near_beside"
    )
    given = exchange(beside, 0, 1)[1]
    (own,) = near_call([(0, near_lists, rows, own)], [late_set], ((0, 0),), dim, "near_last")
    if skel // count:
        root = node.reshape(-1)
    else:
        size = skel * LANES // count
        rank = lax.axis_index("leaf") * sub_count + lax.axis_index("sub")
        root = lax.dynamic_slice_in_dim(node.reshape(-1), rank * size, size, 0)
    near = (own + given) * (leaf ** -0.5)
    return near.reshape(npts, LANES), root


def solution(mesh):
    in_specs = (
        P(("leaf", "sub"), None),
        P(("leaf", "sub"), None),
        P(("leaf", "sub")),
        P(("leaf", "sub"), None),
        P(("leaf", "sub")),
        P(("leaf", "sub"), None),
        P(),
    )
    out_specs = (P(("leaf", "sub"), None), P(("leaf", "sub")))
    return jax.shard_map(
        on_device, mesh=mesh, in_specs=in_specs, out_specs=out_specs, check_vma=False
    )
```

```python
import functools

import jax
import jax.numpy as jnp
from jax import lax
from jax.experimental import pallas as pl
from jax.experimental.pallas import tpu as pltpu
from jax.sharding import PartitionSpec as P

LANES = 128
PARTS = 3
VMEM_BYTES = 20 * 1024 * 1024
NEAR_BYTES = 24 * 1024 * 1024
F32 = jnp.float32
BF16 = jnp.bfloat16


def dot(a, b):
    return jnp.dot(a, b, preferred_element_type=F32)


def dot_t(a, b):
    return lax.dot_general(a, b, (((0,), (0,)), ((), ())), preferred_element_type=F32)


def split(x):
    hi = x.astype(BF16)
    return hi, (x - hi.astype(F32)).astype(BF16)


def square_rows(pts):
    x = pts.astype(F32)
    total = jnp.sum(x * x, axis=0, keepdims=True)
    hi = total.astype(BF16).astype(F32)
    mid = (total - hi).astype(BF16).astype(F32)
    low = total - hi - mid
    row = lax.broadcasted_iota(jnp.int32, (16, pts.shape[1]), 0)
    ones = jnp.where(row < 2 * PARTS, 1.0, 0.0)
    return jnp.where(row == 0, hi, jnp.where(row == 1, mid, jnp.where(row == 2, low, ones))).astype(BF16)


def form_map(dim, size):
    k = lax.broadcasted_iota(jnp.int32, (size, size), 0)
    j = lax.broadcasted_iota(jnp.int32, (size, size), 1)
    r = jnp.where((k == j) & (j < dim), 2.0 / dim, 0.0)
    r = jnp.where((j >= dim) & (j < dim + PARTS) & (k == j + PARTS), -1.0 / dim, r)
    r = jnp.where((j >= dim + PARTS) & (j < dim + 2 * PARTS) & (k == j - PARTS), -1.0 / dim, r)
    return r.astype(BF16)


def onehot_in(row, size):
    index = lax.broadcasted_iota(jnp.int32, (size, row.shape[1]), 0)
    return jnp.where(index == row, 1.0, 0.0).astype(BF16)


def column_of(row):
    return jnp.broadcast_to(row.astype(F32), (LANES, row.shape[1])).T


def onehot_out(column, size):
    lane = lax.broadcasted_iota(jnp.int32, column.shape, 1).astype(F32)
    return jnp.concatenate(
        [jnp.where(column == lane + float(i), 1.0, 0.0) for i in range(0, size, LANES)], axis=1
    )


def mix3(m, s):
    m_hi, m_lo = split(m)
    s_hi, s_lo = split(s)
    return dot(m_hi, s_hi) + (dot(m_hi, s_lo) + dot(m_lo, s_hi))


def order_kernel(points_t, order, probes, pack, rows):
    dim = points_t.shape[0]
    many, leaf = rows.shape[:2]
    held = dim + 16
    to_rows = form_map(dim, LANES)
    for b in range(many):
        picks = onehot_in(order[b], leaf)
        tree_t = dot(points_t[:, b * leaf : (b + 1) * leaf], picks).astype(BF16)
        pack[b, :leaf, :] = probes[b * leaf : (b + 1) * leaf, :]
        form = jnp.concatenate([tree_t, square_rows(tree_t)], axis=0)
        for i in range(leaf // LANES):
            pack[b, leaf + i * dim : leaf + (i + 1) * dim, :] = tree_t[:, i * LANES : (i + 1) * LANES]
        form = jnp.concatenate([form, jnp.zeros((LANES - held, leaf), BF16)], axis=0)
        rows[b] = dot_t(form, to_rows).astype(BF16)


def order_call(points_t, order, probes, blocks):
    dim, npts = points_t.shape
    leaf = npts // blocks
    packed = leaf + leaf // LANES * dim
    many = 4 if blocks % 4 == 0 else 1
    return pl.pallas_call(
        order_kernel,
        grid=(blocks // many,),
        in_specs=[
            pl.BlockSpec((dim, many * leaf), lambda b: (0, b)),
            pl.BlockSpec((many, 1, leaf), lambda b: (b, 0, 0)),
            pl.BlockSpec((many * leaf, LANES), lambda b: (b, 0)),
        ],
        out_specs=[
            pl.BlockSpec((many, packed, LANES), lambda b: (b, 0, 0)),
            pl.BlockSpec((many, leaf, LANES), lambda b: (b, 0, 0)),
        ],
        out_shape=[
            jax.ShapeDtypeStruct((blocks, packed, LANES), BF16),
            jax.ShapeDtypeStruct((blocks, leaf, LANES), BF16),
        ],
        compiler_params=pltpu.CompilerParams(vmem_limit_bytes=VMEM_BYTES),
        cost_estimate=pl.CostEstimate(
            flops=blocks * 2 * leaf * leaf * dim, bytes_accessed=10 * npts * LANES, transcendentals=0
        ),
        name="tree_order",
    )(points_t, order, probes)


def form_of(pack_block, leaf, dim):
    columns = []
    for i in range(leaf // LANES):
        pts = pack_block[leaf + i * dim : leaf + (i + 1) * dim, :]
        columns.append(jnp.concatenate([pts, square_rows(pts)], axis=0))
    form = jnp.concatenate(columns, axis=1)
    return jnp.concatenate([form, jnp.zeros((LANES - dim - 16, leaf), BF16)], axis=0)


def condense(form, a_rows, chosen):
    size = form.shape[1]
    picks_out = onehot_out(column_of(chosen), size)
    new_rows = dot(picks_out.astype(BF16), a_rows).astype(BF16)
    new_form = dot(form, onehot_in(chosen, size)).astype(BF16)
    weights = jnp.exp(dot(new_rows, form))
    mixing = picks_out + weights / jnp.sum(weights, axis=1, keepdims=True)
    return new_form, new_rows, mixing


def local_tree_kernel(pack, rows, leaf_sets_in, merge_sets_in, out, leaf_sets, merge_sets, sems, *, dim):
    blocks, leaf = rows.shape[:2]
    leaf_copy = pltpu.make_async_copy(leaf_sets_in, leaf_sets, sems.at[0])
    merge_copy = pltpu.make_async_copy(merge_sets_in, merge_sets, sems.at[1])
    leaf_copy.start()
    merge_copy.start()
    leaf_copy.wait()
    first_block = (lax.axis_index("leaf") * lax.axis_size("sub") + lax.axis_index("sub")) * blocks

    nodes = []
    for b in range(blocks):
        form = form_of(pack.at[b], leaf, dim)
        new_form, new_rows, mixing = condense(form, rows[b], leaf_sets[b : b + 1, :])
        m_hi, m_lo = split(mixing)
        probes = pack[b, :leaf, :]
        nodes.append((new_form, new_rows, dot(m_hi, probes) + dot(m_lo, probes)))
    span = 1
    merge_copy.wait()
    while len(nodes) > 1:
        merged = []
        for k in range(len(nodes) // 2):
            left, right = nodes[2 * k], nodes[2 * k + 1]
            chosen = merge_sets[pl.ds(first_block + (2 * k + 1) * span - 1, 1), :]
            new_form, new_rows, mixing = condense(
                jnp.concatenate([left[0], right[0]], axis=1),
                jnp.concatenate([left[1], right[1]], axis=0),
                chosen,
            )
            samples = mix3(mixing, jnp.concatenate([left[2], right[2]], axis=0))
            merged.append((new_form, new_rows, samples))
        nodes = merged
        span *= 2
    held = dim + 16
    out[:held, :] = nodes[0][0][:held, :].astype(F32)
    out[held:, :] = nodes[0][2]


def local_tree_call(pack, rows, leaf_sets, merge_sets, dim):
    blocks, leaf = rows.shape[:2]
    skel = leaf_sets.shape[1]
    return pl.pallas_call(
        functools.partial(local_tree_kernel, dim=dim),
        in_specs=[pl.BlockSpec(memory_space=pltpu.VMEM)] * 2
        + [pl.BlockSpec(memory_space=pltpu.HBM)] * 2,
        out_shape=jax.ShapeDtypeStruct((dim + 16 + skel, LANES), F32),
        scratch_shapes=[
            pltpu.VMEM(leaf_sets.shape, jnp.int32),
            pltpu.VMEM(merge_sets.shape, jnp.int32),
            pltpu.SemaphoreType.DMA((2,)),
        ],
        compiler_params=pltpu.CompilerParams(vmem_limit_bytes=VMEM_BYTES),
        cost_estimate=pl.CostEstimate(
            flops=blocks * 8 * skel * leaf * LANES,
            bytes_accessed=6 * blocks * leaf * LANES,
            transcendentals=blocks * skel * leaf,
        ),
        name="local_tree",
    )(pack, rows, leaf_sets, merge_sets)


def merge_kernel(*refs, dim, blocks, shift, piece):
    merge_sets_in, out, group, merge_sets, sem = refs[-5:]
    parts = refs[:-5]
    count, size = group.shape[:2]
    copy = pltpu.make_async_copy(merge_sets_in, merge_sets, sem)
    copy.start()
    held = dim + 16
    skel = size - held
    rank = lax.axis_index("leaf") * lax.axis_size("sub") + lax.axis_index("sub")
    unit = lax.shift_right_logical(rank, shift)
    place = unit & (count - 1)
    first = unit - place
    span = blocks << shift
    for d, part in enumerate(parts):
        group[place ^ d] = part[...]
    to_rows = form_map(dim, LANES)
    forms = [group[i, :held, :].astype(BF16) for i in range(count)]
    samples = [group[i, held:, :] for i in range(count)]
    copy.wait()
    while len(forms) > 1:
        first = first // 2
        new_forms, new_samples = [], []
        for k in range(len(forms) // 2):
            chosen = merge_sets[pl.ds((2 * (first + k) + 1) * span - 1, 1), :]
            form = jnp.concatenate(forms[2 * k : 2 * k + 2], axis=1)
            form = jnp.concatenate([form, jnp.zeros((LANES - held, 2 * skel), BF16)], axis=0)
            new_form = dot(form, onehot_in(chosen, 2 * skel)).astype(BF16)
            new_rows = dot_t(new_form, to_rows).astype(BF16)
            weights = jnp.exp(dot(new_rows, form))
            picks = onehot_out(column_of(chosen), 2 * skel)
            mixing = picks + weights / jnp.sum(weights, axis=1, keepdims=True)
            new_forms.append(new_form[:held])
            new_samples.append(mix3(mixing, jnp.concatenate(samples[2 * k : 2 * k + 2], axis=0)))
        forms, samples = new_forms, new_samples
        span *= 2
    if piece is None:
        out[:held, :] = forms[0].astype(F32)
        out[held:, :] = samples[0]
    elif piece == 0:
        out[...] = samples[0]
    else:
        column = lax.broadcasted_iota(jnp.int32, (piece, skel), 1)
        row = lax.broadcasted_iota(jnp.int32, (piece, skel), 0) + lax.shift_right_logical(rank, 1) * piece
        take = jnp.where(column == row, 1.0, 0.0).astype(BF16)
        hi, lo = split(samples[0])
        low = (samples[0] - hi.astype(F32) - lo.astype(F32)).astype(BF16)
        out[...] = dot(take, hi) + dot(take, lo) + dot(take, low)


def merge_call(parts, merge_sets, dim, blocks, shift, piece=None):
    count = len(parts)
    size = parts[0].shape[0]
    skel = size - dim - 16
    rows = size if piece is None else (piece or skel)
    return pl.pallas_call(
        functools.partial(merge_kernel, dim=dim, blocks=blocks, shift=shift, piece=piece),
        in_specs=[pl.BlockSpec(memory_space=pltpu.VMEM)] * count
        + [pl.BlockSpec(memory_space=pltpu.HBM)],
        out_shape=jax.ShapeDtypeStruct((rows, LANES), F32),
        scratch_shapes=[
            pltpu.VMEM((count, size, LANES), F32),
            pltpu.VMEM(merge_sets.shape, jnp.int32),
            pltpu.SemaphoreType.DMA(()),
        ],
        compiler_params=pltpu.CompilerParams(vmem_limit_bytes=16 * 1024 * 1024),
        cost_estimate=pl.CostEstimate(
            flops=count * 16 * LANES**3,
            bytes_accessed=4 * count * size * LANES,
            transcendentals=2 * count * LANES**2,
        ),
        name="tree_merge",
    )(*parts, merge_sets)


def near_kernel(*refs, flips, has_acc, sets, tasks, dim):
    refs = list(refs)

    def take(number):
        taken = refs[:number]
        del refs[:number]
        return taken

    lists, rows = take(len(flips)), take(len(flips))
    accs = [take(1)[0] if has else None for has in has_acc]
    buffers = [take(max(which) + 1) for _, which in sets]
    outs, (pair_list,) = take(len(flips)), refs
    blocks, leaf = rows[0].shape[:2]
    near = lists[0].shape[1]
    window = blocks * lax.axis_size("sub")
    sub = lax.axis_index("sub")

    def place(table):
        value = jnp.int32(table[0])
        for i in range(1, len(table)):
            value = jnp.where(sub == i, jnp.int32(table[i]), value)
        return value

    window_first = lax.axis_index("leaf") * window - blocks
    stride = blocks * near + 8
    found = [jnp.int32(0)] * len(tasks)
    for j, flip in enumerate(flips):
        mine = [t for t, (_, group) in enumerate(tasks) if group == j]
        firsts = [window_first + place(sets[tasks[t][0]][0]) for t in mine]
        target_first = lax.axis_index("leaf") * window + (sub ^ flip) * blocks

        def list_block(g, counts, j=j, mine=mine, firsts=firsts, target_first=target_first):
            for s in range(near):
                source = lists[j][g, s]
                used = (source != target_first + g) if s else True
                after = []
                for t, first, count in zip(mine, firsts, counts):
                    local = source - first
                    pair_list[t * stride + count] = g * blocks + local
                    inside = (local >= 0) & (local < blocks) & used
                    after.append(count + jnp.where(inside, 1, 0))
                counts = tuple(after)
            return counts

        counts = lax.fori_loop(0, blocks, list_block, (jnp.int32(0),) * len(mine))
        for t, count in zip(mine, counts):
            found[t] = count
        outs[j][...] = jnp.zeros(outs[j].shape, F32) if accs[j] is None else accs[j][...]

    half = leaf // 2

    def add_all(buffer, t, pairs):
        j = tasks[t][1]

        def add_pair(i):
            code = pair_list[t * stride + i]
            g = code // blocks
            local = code - g * blocks
            form = form_of(buffer.at[local], leaf, dim)
            probes = buffer[local, :leaf, :]
            total = None
            for c in range(0, leaf, half):
                weights = jnp.exp(dot(rows[j][g], form[:, c : c + half])).astype(BF16)
                term = dot(weights, probes[c : c + half])
                total = term if total is None else total + term
            return g, total

        def add_pairs(i, carry):
            for g, total in [add_pair(2 * i), add_pair(2 * i + 1)]:
                outs[j][g] += total
            return carry

        lax.fori_loop(0, pairs // 2, add_pairs, 0)

        @pl.when(pairs % 2 == 1)
        def _():
            g, total = add_pair(pairs - 1)
            outs[j][g] += total

    for t, (number, _) in enumerate(tasks):
        held = place(sets[number][1])
        for k, buffer in enumerate(buffers[number]):
            pairs = found[t] if len(buffers[number]) == 1 else jnp.where(held == k, found[t], 0)
            add_all(buffer, t, pairs)


def near_call(groups, sources, tasks, dim, name):
    flips, lists, rows, accs = zip(*groups)
    blocks, leaf = rows[0].shape[:2]
    held = [acc for acc in accs if acc is not None]
    args = [*lists, *rows, *held, *(b for _, _, buffers in sources for b in buffers)]
    smem = pl.BlockSpec(memory_space=pltpu.SMEM)
    vmem = pl.BlockSpec(memory_space=pltpu.VMEM)
    near = lists[0].shape[1]
    return pl.pallas_call(
        functools.partial(
            near_kernel,
            flips=flips,
            has_acc=tuple(acc is not None for acc in accs),
            sets=tuple((bases, which) for bases, which, _ in sources),
            tasks=tasks,
            dim=dim,
        ),
        in_specs=[smem] * len(lists) + [vmem] * (len(args) - len(lists)),
        out_specs=[vmem] * len(groups),
        out_shape=[jax.ShapeDtypeStruct((blocks, leaf, LANES), F32)] * len(groups),
        scratch_shapes=[pltpu.SMEM((len(tasks) * (blocks * near + 8),), jnp.int32)],
        compiler_params=pltpu.CompilerParams(vmem_limit_bytes=NEAR_BYTES),
        cost_estimate=pl.CostEstimate(flops=1000, bytes_accessed=1000, transcendentals=0),
        name=name,
    )(*args)


def on_device(points, probes, order, near_lists, near_counts, leaf_sets, merge_sets):
    leaf_count = lax.axis_size("leaf")
    sub_count = lax.axis_size("sub")
    blocks, skel = leaf_sets.shape
    npts, dim = points.shape
    leaf = npts // blocks
    axes = ("leaf", "sub")

    def send(x, routes):
        pairs = []
        for place in range(leaf_count):
            for from_sub, step, to_sub in routes:
                if 0 <= place + step < leaf_count:
                    pairs.append((place * sub_count + from_sub, (place + step) * sub_count + to_sub))
        return lax.ppermute(x, axes, pairs)

    count = leaf_count * sub_count
    bits = count.bit_length() - 1
    sub_bits = sub_count.bit_length() - 1

    def exchange(x, shift, stage_bits):
        parts = [x]
        for d in range(1, 1 << stage_bits):
            parts.append(lax.ppermute(x, axes, [(i, i ^ (d << shift)) for i in range(count)]))
        return parts

    def tie(*values):
        return lax.optimization_barrier(values)

    b = blocks
    own_base = (b, 2 * b, 3 * b, 4 * b)
    early_base, late_base = (5 * b, 4 * b, b, 0), (3 * b, 0, 5 * b, 2 * b)
    single, by_edge = (0, 0, 0, 0), (0, 1, 1, 0)

    pack, rows = order_call(points.T, order.reshape(blocks, 1, leaf), probes, blocks)
    outer_across = send(pack, [(3, 0, 1), (0, 0, 2)])
    outer_next = send(pack, [(3, 1, 3), (0, -1, 0)])
    beside_rows = exchange(rows, 0, 1)[1]
    beside_lists = exchange(near_lists, 0, 1)[1]

    node = local_tree_call(pack, rows, leaf_sets, merge_sets, dim)
    node, beside_lists = tie(node, beside_lists)

    def level(parts, bit, piece=None):
        return merge_call(parts, merge_sets, dim, blocks, bit, piece)

    node = level(exchange(node, 0, 1), 0)
    own_pack, node = tie(pack, node)
    other = send(node, [(1, 0, 2), (2, 0, 1)])
    own_set = (own_base, single, [own_pack])
    (beside,) = near_call(
        [(1, beside_lists, beside_rows, None)], [own_set], ((0, 0),), dim, "near_own"
    )

    def between_edges(x, bit):
        step = 1 << bit - sub_bits
        pairs = [
            (place * sub_count + edge, (place ^ step) * sub_count + edge)
            for place in range(leaf_count)
            for edge in (0, 3)
        ]
        return lax.ppermute(x, axes, pairs)

    other, beside = tie(other, beside)
    node = send(level([node, other], 1), [(1, 0, 0), (2, 0, 3)])
    outer_across, outer_next, own_pack, node = tie(outer_across, outer_next, own_pack, node)
    forwarded = send(outer_across, [(1, 1, 1), (2, -1, 2)])
    inner_across = send(own_pack, [(2, 0, 0), (1, 0, 3)])
    other = between_edges(node, sub_bits)
    own_set = (own_base, single, [own_pack])
    early_set = (early_base, by_edge, [outer_next, outer_across])
    (own,) = near_call([(0, near_lists, rows, None)], [own_set], ((0, 0),), dim, "near_mine")
    bit = sub_bits
    while bit < bits - 1:
        other, own = tie(other, own)
        node = level([node, other], bit)
        bit += 1
        other = between_edges(node, bit)
        if bit == sub_bits + 1:
            (own,) = near_call(
                [(0, near_lists, rows, own)], [early_set], ((0, 0),), dim, "near_early"
            )
    (beside,) = near_call(
        [(1, beside_lists, beside_rows, beside)], [early_set], ((0, 0),), dim, "near_early_beside"
    )
    other, beside = tie(other, beside)
    piece = skel // count
    root_rows = level([node, other], bit, 2 * piece)
    shared_rows = send(root_rows, [(0, 0, 1), (3, 0, 2)])

    inner_across, forwarded, beside, root_rows = tie(inner_across, forwarded, beside, root_rows)
    late_set = (late_base, by_edge, [inner_across, forwarded])
    (beside,) = near_call(
        [(1, beside_lists, beside_rows, beside)], [late_set], ((0, 0),), dim, "near_beside"
    )
    given = exchange(beside, 0, 1)[1]
    (own,) = near_call([(0, near_lists, rows, own)], [late_set], ((0, 0),), dim, "near_last")
    sub_place = lax.axis_index("sub")
    edge = (sub_place == 0) | (sub_place == sub_count - 1)
    root_rows = jnp.where(edge, root_rows, shared_rows).reshape(-1)
    size = skel * LANES // count
    rank = lax.axis_index("leaf") * sub_count + sub_place
    start = (rank % 2 if piece else rank) * size
    root = lax.dynamic_slice_in_dim(root_rows, start, size, 0)
    near = (own + given) * (leaf ** -0.5)
    return near.reshape(npts, LANES), root


def solution(mesh):
    in_specs = (
        P(("leaf", "sub"), None),
        P(("leaf", "sub"), None),
        P(("leaf", "sub")),
        P(("leaf", "sub"), None),
        P(("leaf", "sub")),
        P(("leaf", "sub"), None),
        P(),
    )
    out_specs = (P(("leaf", "sub"), None), P(("leaf", "sub")))
    return jax.shard_map(
        on_device, mesh=mesh, in_specs=in_specs, out_specs=out_specs, check_vma=False
    )
```

```python
import functools

import jax
import jax.numpy as jnp
from jax import lax
from jax.experimental import pallas as pl
from jax.experimental.pallas import tpu as pltpu
from jax.sharding import PartitionSpec as P

LANES = 128
PARTS = 3
VMEM_BYTES = 20 * 1024 * 1024
NEAR_BYTES = 24 * 1024 * 1024
F32 = jnp.float32
BF16 = jnp.bfloat16


def dot(a, b):
    return jnp.dot(a, b, preferred_element_type=F32)


def dot_t(a, b):
    return lax.dot_general(a, b, (((0,), (0,)), ((), ())), preferred_element_type=F32)


def split(x):
    hi = x.astype(BF16)
    return hi, (x - hi.astype(F32)).astype(BF16)


def square_rows(pts):
    x = pts.astype(F32)
    total = jnp.sum(x * x, axis=0, keepdims=True)
    hi = total.astype(BF16).astype(F32)
    mid = (total - hi).astype(BF16).astype(F32)
    low = total - hi - mid
    row = lax.broadcasted_iota(jnp.int32, (16, pts.shape[1]), 0)
    ones = jnp.where(row < 2 * PARTS, 1.0, 0.0)
    return jnp.where(row == 0, hi, jnp.where(row == 1, mid, jnp.where(row == 2, low, ones))).astype(BF16)


def form_map(dim, size):
    k = lax.broadcasted_iota(jnp.int32, (size, size), 0)
    j = lax.broadcasted_iota(jnp.int32, (size, size), 1)
    r = jnp.where((k == j) & (j < dim), 2.0 / dim, 0.0)
    r = jnp.where((j >= dim) & (j < dim + PARTS) & (k == j + PARTS), -1.0 / dim, r)
    r = jnp.where((j >= dim + PARTS) & (j < dim + 2 * PARTS) & (k == j - PARTS), -1.0 / dim, r)
    return r.astype(BF16)


def onehot_in(row, size):
    index = lax.broadcasted_iota(jnp.int32, (size, row.shape[1]), 0)
    return jnp.where(index == row, 1.0, 0.0).astype(BF16)


def column_of(row):
    return jnp.broadcast_to(row.astype(F32), (LANES, row.shape[1])).T


def onehot_out(column, size):
    lane = lax.broadcasted_iota(jnp.int32, column.shape, 1).astype(F32)
    return jnp.concatenate(
        [jnp.where(column == lane + float(i), 1.0, 0.0) for i in range(0, size, LANES)], axis=1
    )


def mix3(m, s):
    m_hi, m_lo = split(m)
    s_hi, s_lo = split(s)
    return dot(m_hi, s_hi) + (dot(m_hi, s_lo) + dot(m_lo, s_hi))


def order_kernel(points_t, order, probes, pack, rows):
    dim = points_t.shape[0]
    many, leaf = rows.shape[:2]
    held = dim + 16
    to_rows = form_map(dim, LANES)
    for b in range(many):
        picks = onehot_in(order[b], leaf)
        tree_t = dot(points_t[:, b * leaf : (b + 1) * leaf], picks).astype(BF16)
        pack[b, :leaf, :] = probes[b * leaf : (b + 1) * leaf, :]
        form = jnp.concatenate([tree_t, square_rows(tree_t)], axis=0)
        for i in range(leaf // LANES):
            pack[b, leaf + i * dim : leaf + (i + 1) * dim, :] = tree_t[:, i * LANES : (i + 1) * LANES]
        form = jnp.concatenate([form, jnp.zeros((LANES - held, leaf), BF16)], axis=0)
        rows[b] = dot_t(form, to_rows).astype(BF16)


def order_call(points_t, order, probes, blocks):
    dim, npts = points_t.shape
    leaf = npts // blocks
    packed = leaf + leaf // LANES * dim
    many = 4 if blocks % 4 == 0 else 1
    return pl.pallas_call(
        order_kernel,
        grid=(blocks // many,),
        in_specs=[
            pl.BlockSpec((dim, many * leaf), lambda b: (0, b)),
            pl.BlockSpec((many, 1, leaf), lambda b: (b, 0, 0)),
            pl.BlockSpec((many * leaf, LANES), lambda b: (b, 0)),
        ],
        out_specs=[
            pl.BlockSpec((many, packed, LANES), lambda b: (b, 0, 0)),
            pl.BlockSpec((many, leaf, LANES), lambda b: (b, 0, 0)),
        ],
        out_shape=[
            jax.ShapeDtypeStruct((blocks, packed, LANES), BF16),
            jax.ShapeDtypeStruct((blocks, leaf, LANES), BF16),
        ],
        compiler_params=pltpu.CompilerParams(vmem_limit_bytes=VMEM_BYTES),
        cost_estimate=pl.CostEstimate(
            flops=blocks * 2 * leaf * leaf * dim, bytes_accessed=10 * npts * LANES, transcendentals=0
        ),
        name="tree_order",
    )(points_t, order, probes)


def form_of(pack_block, leaf, dim):
    columns = []
    for i in range(leaf // LANES):
        pts = pack_block[leaf + i * dim : leaf + (i + 1) * dim, :]
        columns.append(jnp.concatenate([pts, square_rows(pts)], axis=0))
    form = jnp.concatenate(columns, axis=1)
    return jnp.concatenate([form, jnp.zeros((LANES - dim - 16, leaf), BF16)], axis=0)


def condense(form, a_rows, chosen):
    size = form.shape[1]
    picks_out = onehot_out(column_of(chosen), size)
    new_rows = dot(picks_out.astype(BF16), a_rows).astype(BF16)
    new_form = dot(form, onehot_in(chosen, size)).astype(BF16)
    weights = jnp.exp(dot(new_rows, form))
    mixing = picks_out + weights / jnp.sum(weights, axis=1, keepdims=True)
    return new_form, new_rows, mixing


def local_tree_kernel(pack, rows, leaf_sets_in, merge_sets_in, out, leaf_sets, merge_sets, sems, *, dim):
    blocks, leaf = rows.shape[:2]
    leaf_copy = pltpu.make_async_copy(leaf_sets_in, leaf_sets, sems.at[0])
    merge_copy = pltpu.make_async_copy(merge_sets_in, merge_sets, sems.at[1])
    leaf_copy.start()
    merge_copy.start()
    leaf_copy.wait()
    first_block = (lax.axis_index("leaf") * lax.axis_size("sub") + lax.axis_index("sub")) * blocks

    nodes = []
    for b in range(blocks):
        form = form_of(pack.at[b], leaf, dim)
        new_form, new_rows, mixing = condense(form, rows[b], leaf_sets[b : b + 1, :])
        m_hi, m_lo = split(mixing)
        probes = pack[b, :leaf, :]
        nodes.append((new_form, new_rows, dot(m_hi, probes) + dot(m_lo, probes)))
    span = 1
    merge_copy.wait()
    while len(nodes) > 1:
        merged = []
        for k in range(len(nodes) // 2):
            left, right = nodes[2 * k], nodes[2 * k + 1]
            chosen = merge_sets[pl.ds(first_block + (2 * k + 1) * span - 1, 1), :]
            new_form, new_rows, mixing = condense(
                jnp.concatenate([left[0], right[0]], axis=1),
                jnp.concatenate([left[1], right[1]], axis=0),
                chosen,
            )
            samples = mix3(mixing, jnp.concatenate([left[2], right[2]], axis=0))
            merged.append((new_form, new_rows, samples))
        nodes = merged
        span *= 2
    held = dim + 16
    out[:held, :] = nodes[0][0][:held, :].astype(F32)
    out[held:, :] = nodes[0][2]


def local_tree_call(pack, rows, leaf_sets, merge_sets, dim):
    blocks, leaf = rows.shape[:2]
    skel = leaf_sets.shape[1]
    return pl.pallas_call(
        functools.partial(local_tree_kernel, dim=dim),
        in_specs=[pl.BlockSpec(memory_space=pltpu.VMEM)] * 2
        + [pl.BlockSpec(memory_space=pltpu.HBM)] * 2,
        out_shape=jax.ShapeDtypeStruct((dim + 16 + skel, LANES), F32),
        scratch_shapes=[
            pltpu.VMEM(leaf_sets.shape, jnp.int32),
            pltpu.VMEM(merge_sets.shape, jnp.int32),
            pltpu.SemaphoreType.DMA((2,)),
        ],
        compiler_params=pltpu.CompilerParams(vmem_limit_bytes=VMEM_BYTES),
        cost_estimate=pl.CostEstimate(
            flops=blocks * 8 * skel * leaf * LANES,
            bytes_accessed=6 * blocks * leaf * LANES,
            transcendentals=blocks * skel * leaf,
        ),
        name="local_tree",
    )(pack, rows, leaf_sets, merge_sets)


def merge_kernel(*refs, dim, blocks, shift, piece):
    merge_sets_in, out, group, merge_sets, sem = refs[-5:]
    parts = refs[:-5]
    count, size = group.shape[:2]
    copy = pltpu.make_async_copy(merge_sets_in, merge_sets, sem)
    copy.start()
    held = dim + 16
    skel = size - held
    rank = lax.axis_index("leaf") * lax.axis_size("sub") + lax.axis_index("sub")
    unit = lax.shift_right_logical(rank, shift)
    place = unit & (count - 1)
    first = unit - place
    span = blocks << shift
    for d, part in enumerate(parts):
        group[place ^ d] = part[...]
    to_rows = form_map(dim, LANES)
    forms = [group[i, :held, :].astype(BF16) for i in range(count)]
    samples = [group[i, held:, :] for i in range(count)]
    copy.wait()
    while len(forms) > 1:
        first = first // 2
        new_forms, new_samples = [], []
        for k in range(len(forms) // 2):
            chosen = merge_sets[pl.ds((2 * (first + k) + 1) * span - 1, 1), :]
            form = jnp.concatenate(forms[2 * k : 2 * k + 2], axis=1)
            form = jnp.concatenate([form, jnp.zeros((LANES - held, 2 * skel), BF16)], axis=0)
            new_form = dot(form, onehot_in(chosen, 2 * skel)).astype(BF16)
            new_rows = dot_t(new_form, to_rows).astype(BF16)
            weights = jnp.exp(dot(new_rows, form))
            picks = onehot_out(column_of(chosen), 2 * skel)
            mixing = picks + weights / jnp.sum(weights, axis=1, keepdims=True)
            new_forms.append(new_form[:held])
            new_samples.append(mix3(mixing, jnp.concatenate(samples[2 * k : 2 * k + 2], axis=0)))
        forms, samples = new_forms, new_samples
        span *= 2
    if piece is None:
        out[:held, :] = forms[0].astype(F32)
        out[held:, :] = samples[0]
    elif piece == 0:
        out[...] = samples[0]
    else:
        column = lax.broadcasted_iota(jnp.int32, (piece, skel), 1)
        row = lax.broadcasted_iota(jnp.int32, (piece, skel), 0) + rank * piece
        take = jnp.where(column == row, 1.0, 0.0).astype(BF16)
        hi, lo = split(samples[0])
        low = (samples[0] - hi.astype(F32) - lo.astype(F32)).astype(BF16)
        out[...] = dot(take, hi) + dot(take, lo) + dot(take, low)


def merge_call(parts, merge_sets, dim, blocks, shift, piece=None):
    count = len(parts)
    size = parts[0].shape[0]
    skel = size - dim - 16
    rows = size if piece is None else (piece or skel)
    return pl.pallas_call(
        functools.partial(merge_kernel, dim=dim, blocks=blocks, shift=shift, piece=piece),
        in_specs=[pl.BlockSpec(memory_space=pltpu.VMEM)] * count
        + [pl.BlockSpec(memory_space=pltpu.HBM)],
        out_shape=jax.ShapeDtypeStruct((rows, LANES), F32),
        scratch_shapes=[
            pltpu.VMEM((count, size, LANES), F32),
            pltpu.VMEM(merge_sets.shape, jnp.int32),
            pltpu.SemaphoreType.DMA(()),
        ],
        compiler_params=pltpu.CompilerParams(vmem_limit_bytes=16 * 1024 * 1024),
        cost_estimate=pl.CostEstimate(
            flops=count * 16 * LANES**3,
            bytes_accessed=4 * count * size * LANES,
            transcendentals=2 * count * LANES**2,
        ),
        name="tree_merge",
    )(*parts, merge_sets)


def near_kernel(*refs, flips, has_acc, sets, tasks, dim):
    refs = list(refs)

    def take(number):
        taken = refs[:number]
        del refs[:number]
        return taken

    lists, rows = take(len(flips)), take(len(flips))
    accs = [take(1)[0] if has else None for has in has_acc]
    buffers = [take(max(which) + 1) for _, which in sets]
    outs, (pair_list,) = take(len(flips)), refs
    blocks, leaf = rows[0].shape[:2]
    near = lists[0].shape[1]
    window = blocks * lax.axis_size("sub")
    sub = lax.axis_index("sub")

    def place(table):
        value = jnp.int32(table[0])
        for i in range(1, len(table)):
            value = jnp.where(sub == i, jnp.int32(table[i]), value)
        return value

    window_first = lax.axis_index("leaf") * window - blocks
    stride = blocks * near + 8
    found = [jnp.int32(0)] * len(tasks)
    for j, flip in enumerate(flips):
        mine = [t for t, (_, group) in enumerate(tasks) if group == j]
        firsts = [window_first + place(sets[tasks[t][0]][0]) for t in mine]
        target_first = lax.axis_index("leaf") * window + (sub ^ flip) * blocks

        def list_block(g, counts, j=j, mine=mine, firsts=firsts, target_first=target_first):
            for s in range(near):
                source = lists[j][g, s]
                used = (source != target_first + g) if s else True
                after = []
                for t, first, count in zip(mine, firsts, counts):
                    local = source - first
                    pair_list[t * stride + count] = g * blocks + local
                    inside = (local >= 0) & (local < blocks) & used
                    after.append(count + jnp.where(inside, 1, 0))
                counts = tuple(after)
            return counts

        counts = lax.fori_loop(0, blocks, list_block, (jnp.int32(0),) * len(mine))
        for t, count in zip(mine, counts):
            found[t] = count
        outs[j][...] = jnp.zeros(outs[j].shape, F32) if accs[j] is None else accs[j][...]

    half = leaf // 2

    def add_all(buffer, t, pairs):
        j = tasks[t][1]

        def add_pair(i):
            code = pair_list[t * stride + i]
            g = code // blocks
            local = code - g * blocks
            form = form_of(buffer.at[local], leaf, dim)
            probes = buffer[local, :leaf, :]
            total = None
            for c in range(0, leaf, half):
                weights = jnp.exp(dot(rows[j][g], form[:, c : c + half])).astype(BF16)
                term = dot(weights, probes[c : c + half])
                total = term if total is None else total + term
            return g, total

        def add_pairs(i, carry):
            for g, total in [add_pair(2 * i), add_pair(2 * i + 1)]:
                outs[j][g] += total
            return carry

        lax.fori_loop(0, pairs // 2, add_pairs, 0)

        @pl.when(pairs % 2 == 1)
        def _():
            g, total = add_pair(pairs - 1)
            outs[j][g] += total

    for t, (number, _) in enumerate(tasks):
        held = place(sets[number][1])
        for k, buffer in enumerate(buffers[number]):
            pairs = found[t] if len(buffers[number]) == 1 else jnp.where(held == k, found[t], 0)
            add_all(buffer, t, pairs)


def near_call(groups, sources, tasks, dim, name):
    flips, lists, rows, accs = zip(*groups)
    blocks, leaf = rows[0].shape[:2]
    held = [acc for acc in accs if acc is not None]
    args = [*lists, *rows, *held, *(b for _, _, buffers in sources for b in buffers)]
    smem = pl.BlockSpec(memory_space=pltpu.SMEM)
    vmem = pl.BlockSpec(memory_space=pltpu.VMEM)
    near = lists[0].shape[1]
    return pl.pallas_call(
        functools.partial(
            near_kernel,
            flips=flips,
            has_acc=tuple(acc is not None for acc in accs),
            sets=tuple((bases, which) for bases, which, _ in sources),
            tasks=tasks,
            dim=dim,
        ),
        in_specs=[smem] * len(lists) + [vmem] * (len(args) - len(lists)),
        out_specs=[vmem] * len(groups),
        out_shape=[jax.ShapeDtypeStruct((blocks, leaf, LANES), F32)] * len(groups),
        scratch_shapes=[pltpu.SMEM((len(tasks) * (blocks * near + 8),), jnp.int32)],
        compiler_params=pltpu.CompilerParams(vmem_limit_bytes=NEAR_BYTES),
        cost_estimate=pl.CostEstimate(flops=1000, bytes_accessed=1000, transcendentals=0),
        name=name,
    )(*args)


def on_device(points, probes, order, near_lists, near_counts, leaf_sets, merge_sets):
    leaf_count = lax.axis_size("leaf")
    sub_count = lax.axis_size("sub")
    blocks, skel = leaf_sets.shape
    npts, dim = points.shape
    leaf = npts // blocks
    axes = ("leaf", "sub")

    def send(x, routes):
        pairs = []
        for place in range(leaf_count):
            for from_sub, step, to_sub in routes:
                if 0 <= place + step < leaf_count:
                    pairs.append((place * sub_count + from_sub, (place + step) * sub_count + to_sub))
        return lax.ppermute(x, axes, pairs)

    count = leaf_count * sub_count
    bits = count.bit_length() - 1
    sub_bits = sub_count.bit_length() - 1

    def exchange(x, shift, stage_bits):
        parts = [x]
        for d in range(1, 1 << stage_bits):
            parts.append(lax.ppermute(x, axes, [(i, i ^ (d << shift)) for i in range(count)]))
        return parts

    def tie(*values):
        return lax.optimization_barrier(values)

    b = blocks
    own_base = (b, 2 * b, 3 * b, 4 * b)
    early_base, late_base = (5 * b, 4 * b, b, 0), (3 * b, 0, 5 * b, 2 * b)
    single, by_edge = (0, 0, 0, 0), (0, 1, 1, 0)

    pack, rows = order_call(points.T, order.reshape(blocks, 1, leaf), probes, blocks)
    outer_across = send(pack, [(3, 0, 1), (0, 0, 2)])
    outer_next = send(pack, [(3, 1, 3), (0, -1, 0)])
    beside_rows = exchange(rows, 0, 1)[1]
    beside_lists = exchange(near_lists, 0, 1)[1]

    node = local_tree_call(pack, rows, leaf_sets, merge_sets, dim)
    node, beside_lists = tie(node, beside_lists)

    def level(parts, bit, piece=None):
        return merge_call(parts, merge_sets, dim, blocks, bit, piece)

    node = level(exchange(node, 0, 1), 0)
    own_pack, node = tie(pack, node)
    parts = exchange(node, 1, 1)
    own_set = (own_base, single, [own_pack])
    (beside,) = near_call(
        [(1, beside_lists, beside_rows, None)], [own_set], ((0, 0),), dim, "near_own"
    )

    *parts, outer_across, outer_next, own_pack, beside = tie(
        *parts, outer_across, outer_next, own_pack, beside
    )
    inner_across = send(own_pack, [(2, 0, 0), (1, 0, 3)])
    forwarded = send(outer_across, [(1, 1, 1), (2, -1, 2)])
    node = level(parts, 1)
    own_pack, node = tie(own_pack, node)
    parts = exchange(node, 2, 1)
    own_set = (own_base, single, [own_pack])
    early_set = (early_base, by_edge, [outer_next, outer_across])
    own, beside = near_call(
        [(0, near_lists, rows, None), (1, beside_lists, beside_rows, beside)],
        [own_set, early_set], ((0, 0), (1, 0), (1, 1)), dim, "near_early",
    )

    *parts, inner_across, forwarded, beside = tie(*parts, inner_across, forwarded, beside)
    late_set = (late_base, by_edge, [inner_across, forwarded])
    (beside,) = near_call(
        [(1, beside_lists, beside_rows, beside)], [late_set], ((0, 0),), dim, "near_beside"
    )
    given = exchange(beside, 0, 1)[1]
    *parts, beside = tie(*parts, beside)
    shift, stage = 2, 1
    while shift + stage < bits:
        node = level(parts, shift)
        shift, stage = shift + stage, min(2, bits - shift - stage)
        parts = exchange(node, shift, stage)
    (own,) = near_call([(0, near_lists, rows, own)], [late_set], ((0, 0),), dim, "near_last")
    *parts, own = tie(*parts, own)
    node = level(parts, shift, skel // count)
    near = (own + given) * (leaf ** -0.5)
    if skel // count:
        root = node.reshape(-1)
    else:
        size = skel * LANES // count
        rank = lax.axis_index("leaf") * sub_count + lax.axis_index("sub")
        root = lax.dynamic_slice_in_dim(node.reshape(-1), rank * size, size, 0)
    return near.reshape(npts, LANES), root


def solution(mesh):
    in_specs = (
        P(("leaf", "sub"), None),
        P(("leaf", "sub"), None),
        P(("leaf", "sub")),
        P(("leaf", "sub"), None),
        P(("leaf", "sub")),
        P(("leaf", "sub"), None),
        P(),
    )
    out_specs = (P(("leaf", "sub"), None), P(("leaf", "sub")))
    return jax.shard_map(
        on_device, mesh=mesh, in_specs=in_specs, out_specs=out_specs, check_vma=False
    )
```

```python
import functools

import jax
import jax.numpy as jnp
from jax import lax
from jax.experimental import pallas as pl
from jax.experimental.pallas import tpu as pltpu
from jax.sharding import PartitionSpec as P

LANES = 128
PARTS = 3
VMEM_BYTES = 20 * 1024 * 1024
NEAR_BYTES = 24 * 1024 * 1024
F32 = jnp.float32
BF16 = jnp.bfloat16


def dot(a, b):
    return jnp.dot(a, b, preferred_element_type=F32)


def dot_t(a, b):
    return lax.dot_general(a, b, (((0,), (0,)), ((), ())), preferred_element_type=F32)


def split(x):
    hi = x.astype(BF16)
    return hi, (x - hi.astype(F32)).astype(BF16)


def square_rows(pts):
    x = pts.astype(F32)
    total = jnp.sum(x * x, axis=0, keepdims=True)
    hi = total.astype(BF16).astype(F32)
    mid = (total - hi).astype(BF16).astype(F32)
    low = total - hi - mid
    row = lax.broadcasted_iota(jnp.int32, (16, pts.shape[1]), 0)
    ones = jnp.where(row < 2 * PARTS, 1.0, 0.0)
    return jnp.where(row == 0, hi, jnp.where(row == 1, mid, jnp.where(row == 2, low, ones))).astype(BF16)


def form_map(dim, size):
    k = lax.broadcasted_iota(jnp.int32, (size, size), 0)
    j = lax.broadcasted_iota(jnp.int32, (size, size), 1)
    r = jnp.where((k == j) & (j < dim), 2.0 / dim, 0.0)
    r = jnp.where((j >= dim) & (j < dim + PARTS) & (k == j + PARTS), -1.0 / dim, r)
    r = jnp.where((j >= dim + PARTS) & (j < dim + 2 * PARTS) & (k == j - PARTS), -1.0 / dim, r)
    return r.astype(BF16)


def onehot_in(row, size):
    index = lax.broadcasted_iota(jnp.int32, (size, row.shape[1]), 0)
    return jnp.where(index == row, 1.0, 0.0).astype(BF16)


def column_of(row):
    return jnp.broadcast_to(row.astype(F32), (LANES, row.shape[1])).T


def onehot_out(column, size):
    lane = lax.broadcasted_iota(jnp.int32, column.shape, 1).astype(F32)
    return jnp.concatenate(
        [jnp.where(column == lane + float(i), 1.0, 0.0) for i in range(0, size, LANES)], axis=1
    )


def mix3(m, s):
    m_hi, m_lo = split(m)
    s_hi, s_lo = split(s)
    return dot(m_hi, s_hi) + (dot(m_hi, s_lo) + dot(m_lo, s_hi))


def order_kernel(points_t, order, probes, pack, rows):
    dim = points_t.shape[0]
    many, leaf = rows.shape[:2]
    held = dim + 16
    to_rows = form_map(dim, LANES)
    for b in range(many):
        picks = onehot_in(order[b], leaf)
        tree_t = dot(points_t[:, b * leaf : (b + 1) * leaf], picks).astype(BF16)
        pack[b, :leaf, :] = probes[b * leaf : (b + 1) * leaf, :]
        form = jnp.concatenate([tree_t, square_rows(tree_t)], axis=0)
        for i in range(leaf // LANES):
            pack[b, leaf + i * dim : leaf + (i + 1) * dim, :] = tree_t[:, i * LANES : (i + 1) * LANES]
        form = jnp.concatenate([form, jnp.zeros((LANES - held, leaf), BF16)], axis=0)
        rows[b] = dot_t(form, to_rows).astype(BF16)


def order_call(points_t, order, probes, blocks):
    dim, npts = points_t.shape
    leaf = npts // blocks
    packed = leaf + leaf // LANES * dim
    many = 4 if blocks % 4 == 0 else 1
    return pl.pallas_call(
        order_kernel,
        grid=(blocks // many,),
        in_specs=[
            pl.BlockSpec((dim, many * leaf), lambda b: (0, b)),
            pl.BlockSpec((many, 1, leaf), lambda b: (b, 0, 0)),
            pl.BlockSpec((many * leaf, LANES), lambda b: (b, 0)),
        ],
        out_specs=[
            pl.BlockSpec((many, packed, LANES), lambda b: (b, 0, 0)),
            pl.BlockSpec((many, leaf, LANES), lambda b: (b, 0, 0)),
        ],
        out_shape=[
            jax.ShapeDtypeStruct((blocks, packed, LANES), BF16),
            jax.ShapeDtypeStruct((blocks, leaf, LANES), BF16),
        ],
        compiler_params=pltpu.CompilerParams(vmem_limit_bytes=VMEM_BYTES),
        cost_estimate=pl.CostEstimate(
            flops=blocks * 2 * leaf * leaf * dim, bytes_accessed=10 * npts * LANES, transcendentals=0
        ),
        name="tree_order",
    )(points_t, order, probes)


def form_of(pack_block, leaf, dim):
    columns = []
    for i in range(leaf // LANES):
        pts = pack_block[leaf + i * dim : leaf + (i + 1) * dim, :]
        columns.append(jnp.concatenate([pts, square_rows(pts)], axis=0))
    form = jnp.concatenate(columns, axis=1)
    return jnp.concatenate([form, jnp.zeros((LANES - dim - 16, leaf), BF16)], axis=0)


def condense(form, a_rows, chosen):
    size = form.shape[1]
    picks_out = onehot_out(column_of(chosen), size)
    new_rows = dot(picks_out.astype(BF16), a_rows).astype(BF16)
    new_form = dot(form, onehot_in(chosen, size)).astype(BF16)
    weights = jnp.exp(dot(new_rows, form))
    mixing = picks_out + weights / jnp.sum(weights, axis=1, keepdims=True)
    return new_form, new_rows, mixing


def local_tree_kernel(pack, rows, leaf_sets_in, merge_sets_in, out, leaf_sets, merge_sets, sems, *, dim):
    blocks, leaf = rows.shape[:2]
    leaf_copy = pltpu.make_async_copy(leaf_sets_in, leaf_sets, sems.at[0])
    merge_copy = pltpu.make_async_copy(merge_sets_in, merge_sets, sems.at[1])
    leaf_copy.start()
    merge_copy.start()
    leaf_copy.wait()
    first_block = (lax.axis_index("leaf") * lax.axis_size("sub") + lax.axis_index("sub")) * blocks

    nodes = []
    for b in range(blocks):
        form = form_of(pack.at[b], leaf, dim)
        new_form, new_rows, mixing = condense(form, rows[b], leaf_sets[b : b + 1, :])
        m_hi, m_lo = split(mixing)
        probes = pack[b, :leaf, :]
        nodes.append((new_form, new_rows, dot(m_hi, probes) + dot(m_lo, probes)))
    span = 1
    merge_copy.wait()
    while len(nodes) > 1:
        merged = []
        for k in range(len(nodes) // 2):
            left, right = nodes[2 * k], nodes[2 * k + 1]
            chosen = merge_sets[pl.ds(first_block + (2 * k + 1) * span - 1, 1), :]
            new_form, new_rows, mixing = condense(
                jnp.concatenate([left[0], right[0]], axis=1),
                jnp.concatenate([left[1], right[1]], axis=0),
                chosen,
            )
            samples = mix3(mixing, jnp.concatenate([left[2], right[2]], axis=0))
            merged.append((new_form, new_rows, samples))
        nodes = merged
        span *= 2
    held = dim + 16
    out[:held, :] = nodes[0][0][:held, :].astype(F32)
    out[held:, :] = nodes[0][2]


def local_tree_call(pack, rows, leaf_sets, merge_sets, dim):
    blocks, leaf = rows.shape[:2]
    skel = leaf_sets.shape[1]
    return pl.pallas_call(
        functools.partial(local_tree_kernel, dim=dim),
        in_specs=[pl.BlockSpec(memory_space=pltpu.VMEM)] * 2
        + [pl.BlockSpec(memory_space=pltpu.HBM)] * 2,
        out_shape=jax.ShapeDtypeStruct((dim + 16 + skel, LANES), F32),
        scratch_shapes=[
            pltpu.VMEM(leaf_sets.shape, jnp.int32),
            pltpu.VMEM(merge_sets.shape, jnp.int32),
            pltpu.SemaphoreType.DMA((2,)),
        ],
        compiler_params=pltpu.CompilerParams(vmem_limit_bytes=VMEM_BYTES),
        cost_estimate=pl.CostEstimate(
            flops=blocks * 8 * skel * leaf * LANES,
            bytes_accessed=6 * blocks * leaf * LANES,
            transcendentals=blocks * skel * leaf,
        ),
        name="local_tree",
    )(pack, rows, leaf_sets, merge_sets)


def merge_kernel(*refs, dim, blocks, shift, piece):
    merge_sets_in, out, group, merge_sets, sem = refs[-5:]
    parts = refs[:-5]
    count, size = group.shape[:2]
    copy = pltpu.make_async_copy(merge_sets_in, merge_sets, sem)
    copy.start()
    held = dim + 16
    skel = size - held
    rank = lax.axis_index("leaf") * lax.axis_size("sub") + lax.axis_index("sub")
    unit = lax.shift_right_logical(rank, shift)
    place = unit & (count - 1)
    first = unit - place
    span = blocks << shift
    for d, part in enumerate(parts):
        group[place ^ d] = part[...]
    to_rows = form_map(dim, LANES)
    forms = [group[i, :held, :].astype(BF16) for i in range(count)]
    samples = [group[i, held:, :] for i in range(count)]
    copy.wait()
    while len(forms) > 1:
        first = first // 2
        new_forms, new_samples = [], []
        for k in range(len(forms) // 2):
            chosen = merge_sets[pl.ds((2 * (first + k) + 1) * span - 1, 1), :]
            form = jnp.concatenate(forms[2 * k : 2 * k + 2], axis=1)
            form = jnp.concatenate([form, jnp.zeros((LANES - held, 2 * skel), BF16)], axis=0)
            new_form = dot(form, onehot_in(chosen, 2 * skel)).astype(BF16)
            new_rows = dot_t(new_form, to_rows).astype(BF16)
            weights = jnp.exp(dot(new_rows, form))
            picks = onehot_out(column_of(chosen), 2 * skel)
            mixing = picks + weights / jnp.sum(weights, axis=1, keepdims=True)
            new_forms.append(new_form[:held])
            new_samples.append(mix3(mixing, jnp.concatenate(samples[2 * k : 2 * k + 2], axis=0)))
        forms, samples = new_forms, new_samples
        span *= 2
    if piece is None:
        out[:held, :] = forms[0].astype(F32)
        out[held:, :] = samples[0]
    elif piece == 0:
        out[...] = samples[0]
    else:
        column = lax.broadcasted_iota(jnp.int32, (piece, skel), 1)
        row = lax.broadcasted_iota(jnp.int32, (piece, skel), 0) + rank * piece
        take = jnp.where(column == row, 1.0, 0.0).astype(BF16)
        hi, lo = split(samples[0])
        low = (samples[0] - hi.astype(F32) - lo.astype(F32)).astype(BF16)
        out[...] = dot(take, hi) + dot(take, lo) + dot(take, low)


def merge_call(parts, merge_sets, dim, blocks, shift, piece=None):
    count = len(parts)
    size = parts[0].shape[0]
    skel = size - dim - 16
    rows = size if piece is None else (piece or skel)
    return pl.pallas_call(
        functools.partial(merge_kernel, dim=dim, blocks=blocks, shift=shift, piece=piece),
        in_specs=[pl.BlockSpec(memory_space=pltpu.VMEM)] * count
        + [pl.BlockSpec(memory_space=pltpu.HBM)],
        out_shape=jax.ShapeDtypeStruct((rows, LANES), F32),
        scratch_shapes=[
            pltpu.VMEM((count, size, LANES), F32),
            pltpu.VMEM(merge_sets.shape, jnp.int32),
            pltpu.SemaphoreType.DMA(()),
        ],
        compiler_params=pltpu.CompilerParams(vmem_limit_bytes=16 * 1024 * 1024),
        cost_estimate=pl.CostEstimate(
            flops=count * 16 * LANES**3,
            bytes_accessed=4 * count * size * LANES,
            transcendentals=2 * count * LANES**2,
        ),
        name="tree_merge",
    )(*parts, merge_sets)


def near_kernel(*refs, flips, row_counts, has_acc, sets, tasks, dim):
    refs = list(refs)

    def take(number):
        taken = refs[:number]
        del refs[:number]
        return taken

    lists, rows = take(len(flips)), [take(number) for number in row_counts]
    accs = [take(1)[0] if has else None for has in has_acc]
    buffers = [take(max(which) + 1) for _, which in sets]
    outs, (pair_list,) = take(len(flips)), refs
    blocks, leaf = rows[0][0].shape[:2]
    near = lists[0].shape[1]
    window = blocks * lax.axis_size("sub")
    sub = lax.axis_index("sub")

    def place(table):
        value = jnp.int32(table[0])
        for i in range(1, len(table)):
            value = jnp.where(sub == i, jnp.int32(table[i]), value)
        return value

    window_first = lax.axis_index("leaf") * window - blocks
    stride = blocks * near + 8
    found = [jnp.int32(0)] * len(tasks)
    for j, flip in enumerate(flips):
        mine = [t for t, (_, group) in enumerate(tasks) if group == j]
        firsts = [window_first + place(sets[tasks[t][0]][0]) for t in mine]
        target_first = lax.axis_index("leaf") * window + (sub ^ flip) * blocks

        def list_block(g, counts, j=j, mine=mine, firsts=firsts, target_first=target_first):
            for s in range(near):
                source = lists[j][g, s]
                used = (source != target_first + g) if s else True
                after = []
                for t, first, count in zip(mine, firsts, counts):
                    local = source - first
                    pair_list[t * stride + count] = g * blocks + local
                    inside = (local >= 0) & (local < blocks) & used
                    after.append(count + jnp.where(inside, 1, 0))
                counts = tuple(after)
            return counts

        counts = lax.fori_loop(0, blocks, list_block, (jnp.int32(0),) * len(mine))
        for t, count in zip(mine, counts):
            found[t] = count
        outs[j][...] = jnp.zeros(outs[j].shape, F32) if accs[j] is None else accs[j][...]

    half = leaf // 2

    def add_all(buffer, targets, t, pairs):
        j = tasks[t][1]

        def add_pair(i):
            code = pair_list[t * stride + i]
            g = code // blocks
            local = code - g * blocks
            form = form_of(buffer.at[local], leaf, dim)
            probes = buffer[local, :leaf, :]
            total = None
            for c in range(0, leaf, half):
                weights = jnp.exp(dot(targets[g], form[:, c : c + half])).astype(BF16)
                term = dot(weights, probes[c : c + half])
                total = term if total is None else total + term
            return g, total

        def add_pairs(i, carry):
            for g, total in [add_pair(2 * i), add_pair(2 * i + 1)]:
                outs[j][g] += total
            return carry

        lax.fori_loop(0, pairs // 2, add_pairs, 0)

        @pl.when(pairs % 2 == 1)
        def _():
            g, total = add_pair(pairs - 1)
            outs[j][g] += total

    for t, (number, j) in enumerate(tasks):
        held = place(sets[number][1])
        edge = (sub == 0) | (sub == lax.axis_size("sub") - 1)
        for k, buffer in enumerate(buffers[number]):
            for r, targets in enumerate(rows[j]):
                pairs = found[t]
                if len(buffers[number]) > 1:
                    if len(rows[j]) > 1 and r != k:
                        continue
                    pairs = jnp.where(held == k, pairs, 0)
                elif len(rows[j]) > 1:
                    pairs = jnp.where(edge == (r == 0), pairs, 0)
                add_all(buffer, targets, t, pairs)


def near_call(groups, sources, tasks, dim, name):
    flips, lists, rows, accs = zip(*groups)
    rows = [r if isinstance(r, tuple) else (r,) for r in rows]
    blocks, leaf = rows[0][0].shape[:2]
    held = [acc for acc in accs if acc is not None]
    args = [*lists, *(r for pair in rows for r in pair), *held, *(b for _, _, buffers in sources for b in buffers)]
    smem = pl.BlockSpec(memory_space=pltpu.SMEM)
    vmem = pl.BlockSpec(memory_space=pltpu.VMEM)
    near = lists[0].shape[1]
    return pl.pallas_call(
        functools.partial(
            near_kernel,
            flips=flips,
            row_counts=tuple(len(pair) for pair in rows),
            has_acc=tuple(acc is not None for acc in accs),
            sets=tuple((bases, which) for bases, which, _ in sources),
            tasks=tasks,
            dim=dim,
        ),
        in_specs=[smem] * len(lists) + [vmem] * (len(args) - len(lists)),
        out_specs=[vmem] * len(groups),
        out_shape=[jax.ShapeDtypeStruct((blocks, leaf, LANES), F32)] * len(groups),
        scratch_shapes=[pltpu.SMEM((len(tasks) * (blocks * near + 8),), jnp.int32)],
        compiler_params=pltpu.CompilerParams(vmem_limit_bytes=NEAR_BYTES),
        cost_estimate=pl.CostEstimate(flops=1000, bytes_accessed=1000, transcendentals=0),
        name=name,
    )(*args)


def on_device(points, probes, order, near_lists, near_counts, leaf_sets, merge_sets):
    leaf_count = lax.axis_size("leaf")
    sub_count = lax.axis_size("sub")
    blocks, skel = leaf_sets.shape
    npts, dim = points.shape
    leaf = npts // blocks
    axes = ("leaf", "sub")

    def send(x, routes):
        pairs = []
        for place in range(leaf_count):
            for from_sub, step, to_sub in routes:
                if 0 <= place + step < leaf_count:
                    pairs.append((place * sub_count + from_sub, (place + step) * sub_count + to_sub))
        return lax.ppermute(x, axes, pairs)

    count = leaf_count * sub_count
    bits = count.bit_length() - 1
    sub_bits = sub_count.bit_length() - 1

    def exchange(x, shift, stage_bits):
        parts = [x]
        for d in range(1, 1 << stage_bits):
            parts.append(lax.ppermute(x, axes, [(i, i ^ (d << shift)) for i in range(count)]))
        return parts

    def tie(*values):
        return lax.optimization_barrier(values)

    b = blocks
    own_base = (b, 2 * b, 3 * b, 4 * b)
    early_base, late_base = (5 * b, 4 * b, b, 0), (3 * b, 0, 5 * b, 2 * b)
    single, by_edge = (0, 0, 0, 0), (0, 1, 1, 0)

    pack, rows = order_call(points.T, order.reshape(blocks, 1, leaf), probes, blocks)
    outer_across = send(pack, [(3, 0, 1), (0, 0, 2)])
    outer_next = send(pack, [(3, 1, 3), (0, -1, 0)])
    inward, outward = [(1, 0, 0), (2, 0, 3)], [(0, 0, 1), (3, 0, 2)]
    beside_pack = send(pack, inward)
    edge_rows = send(rows, inward)
    beside_lists = exchange(near_lists, 0, 1)[1]

    node = local_tree_call(pack, rows, leaf_sets, merge_sets, dim)
    node, beside_lists = tie(node, beside_lists)

    def level(parts, bit, piece=None):
        return merge_call(parts, merge_sets, dim, blocks, bit, piece)

    node = level(exchange(node, 0, 1), 0)
    own_pack, node = tie(pack, node)
    parts = exchange(node, 1, 1)
    own_set = (own_base, single, [own_pack])
    (own,) = near_call([(0, near_lists, rows, None)], [own_set], ((0, 0),), dim, "near_own")

    *parts, outer_across, outer_next, beside_pack, edge_rows, late_rows, own = tie(
        *parts, outer_across, outer_next, beside_pack, edge_rows, rows, own
    )
    forwarded = send(outer_across, [(1, 1, 1), (2, -1, 2)])
    inner_across = send(beside_pack, [(0, 0, 3), (3, 0, 0)])
    beside_rows = (edge_rows, send(late_rows, outward))
    node = level(parts, 1)
    own_pack, node = tie(own_pack, node)
    parts = exchange(node, 2, 1)
    own_set = (own_base, single, [own_pack])
    early_set = (early_base, by_edge, [outer_next, outer_across])
    own, beside = near_call(
        [(0, near_lists, rows, own), (1, beside_lists, beside_rows, None)],
        [own_set, early_set], ((1, 0), (0, 1), (1, 1)), dim, "near_early",
    )

    *parts, inner_across, forwarded, beside = tie(*parts, inner_across, forwarded, beside)
    late_set = (late_base, by_edge, [inner_across, forwarded])
    (beside,) = near_call(
        [(1, beside_lists, beside_rows, beside)], [late_set], ((0, 0),), dim, "near_beside"
    )
    given = exchange(beside, 0, 1)[1]
    *parts, beside = tie(*parts, beside)
    shift, stage = 2, 1
    while shift + stage < bits:
        node = level(parts, shift)
        shift, stage = shift + stage, min(2, bits - shift - stage)
        parts = exchange(node, shift, stage)
    (own,) = near_call([(0, near_lists, rows, own)], [late_set], ((0, 0),), dim, "near_last")
    *parts, own = tie(*parts, own)
    node = level(parts, shift, skel // count)
    near = (own + given) * (leaf ** -0.5)
    if skel // count:
        root = node.reshape(-1)
    else:
        size = skel * LANES // count
        rank = lax.axis_index("leaf") * sub_count + lax.axis_index("sub")
        root = lax.dynamic_slice_in_dim(node.reshape(-1), rank * size, size, 0)
    return near.reshape(npts, LANES), root


def solution(mesh):
    in_specs = (
        P(("leaf", "sub"), None),
        P(("leaf", "sub"), None),
        P(("leaf", "sub")),
        P(("leaf", "sub"), None),
        P(("leaf", "sub")),
        P(("leaf", "sub"), None),
        P(),
    )
    out_specs = (P(("leaf", "sub"), None), P(("leaf", "sub")))
    return jax.shard_map(
        on_device, mesh=mesh, in_specs=in_specs, out_specs=out_specs, check_vma=False
    )
```

```python
import functools

import jax
import jax.numpy as jnp
from jax import lax
from jax.experimental import pallas as pl
from jax.experimental.pallas import tpu as pltpu
from jax.sharding import PartitionSpec as P

LANES = 128
PARTS = 3
VMEM_BYTES = 20 * 1024 * 1024
NEAR_BYTES = 24 * 1024 * 1024
F32 = jnp.float32
BF16 = jnp.bfloat16


def dot(a, b):
    return jnp.dot(a, b, preferred_element_type=F32)


def dot_t(a, b):
    return lax.dot_general(a, b, (((0,), (0,)), ((), ())), preferred_element_type=F32)


def split(x):
    hi = x.astype(BF16)
    return hi, (x - hi.astype(F32)).astype(BF16)


def square_rows(pts):
    x = pts.astype(F32)
    total = jnp.sum(x * x, axis=0, keepdims=True)
    hi = total.astype(BF16).astype(F32)
    mid = (total - hi).astype(BF16).astype(F32)
    low = total - hi - mid
    row = lax.broadcasted_iota(jnp.int32, (16, pts.shape[1]), 0)
    ones = jnp.where(row < 2 * PARTS, 1.0, 0.0)
    return jnp.where(row == 0, hi, jnp.where(row == 1, mid, jnp.where(row == 2, low, ones))).astype(BF16)


def form_map(dim, size):
    k = lax.broadcasted_iota(jnp.int32, (size, size), 0)
    j = lax.broadcasted_iota(jnp.int32, (size, size), 1)
    r = jnp.where((k == j) & (j < dim), 2.0 / dim, 0.0)
    r = jnp.where((j >= dim) & (j < dim + PARTS) & (k == j + PARTS), -1.0 / dim, r)
    r = jnp.where((j >= dim + PARTS) & (j < dim + 2 * PARTS) & (k == j - PARTS), -1.0 / dim, r)
    return r.astype(BF16)


def onehot_in(row, size):
    index = lax.broadcasted_iota(jnp.int32, (size, row.shape[1]), 0)
    return jnp.where(index == row, 1.0, 0.0).astype(BF16)


def column_of(row):
    return jnp.broadcast_to(row.astype(F32), (LANES, row.shape[1])).T


def onehot_out(column, size):
    lane = lax.broadcasted_iota(jnp.int32, column.shape, 1).astype(F32)
    return jnp.concatenate(
        [jnp.where(column == lane + float(i), 1.0, 0.0) for i in range(0, size, LANES)], axis=1
    )


def mix3(m, s):
    m_hi, m_lo = split(m)
    s_hi, s_lo = split(s)
    return dot(m_hi, s_hi) + (dot(m_hi, s_lo) + dot(m_lo, s_hi))


def order_kernel(points_t, order, probes, pack, rows):
    dim = points_t.shape[0]
    many, leaf = rows.shape[:2]
    held = dim + 16
    to_rows = form_map(dim, LANES)
    for b in range(many):
        picks = onehot_in(order[b], leaf)
        tree_t = dot(points_t[:, b * leaf : (b + 1) * leaf], picks).astype(BF16)
        pack[b, :leaf, :] = probes[b * leaf : (b + 1) * leaf, :]
        form = jnp.concatenate([tree_t, square_rows(tree_t)], axis=0)
        for i in range(leaf // LANES):
            pack[b, leaf + i * dim : leaf + (i + 1) * dim, :] = tree_t[:, i * LANES : (i + 1) * LANES]
        form = jnp.concatenate([form, jnp.zeros((LANES - held, leaf), BF16)], axis=0)
        rows[b] = dot_t(form, to_rows).astype(BF16)


def order_call(points_t, order, probes, blocks):
    dim, npts = points_t.shape
    leaf = npts // blocks
    packed = leaf + leaf // LANES * dim
    many = 4 if blocks % 4 == 0 else 1
    return pl.pallas_call(
        order_kernel,
        grid=(blocks // many,),
        in_specs=[
            pl.BlockSpec((dim, many * leaf), lambda b: (0, b)),
            pl.BlockSpec((many, 1, leaf), lambda b: (b, 0, 0)),
            pl.BlockSpec((many * leaf, LANES), lambda b: (b, 0)),
        ],
        out_specs=[
            pl.BlockSpec((many, packed, LANES), lambda b: (b, 0, 0)),
            pl.BlockSpec((many, leaf, LANES), lambda b: (b, 0, 0)),
        ],
        out_shape=[
            jax.ShapeDtypeStruct((blocks, packed, LANES), BF16),
            jax.ShapeDtypeStruct((blocks, leaf, LANES), BF16),
        ],
        compiler_params=pltpu.CompilerParams(vmem_limit_bytes=VMEM_BYTES),
        cost_estimate=pl.CostEstimate(
            flops=blocks * 2 * leaf * leaf * dim, bytes_accessed=10 * npts * LANES, transcendentals=0
        ),
        name="tree_order",
    )(points_t, order, probes)


def form_of(pack_block, leaf, dim):
    columns = []
    for i in range(leaf // LANES):
        pts = pack_block[leaf + i * dim : leaf + (i + 1) * dim, :]
        columns.append(jnp.concatenate([pts, square_rows(pts)], axis=0))
    form = jnp.concatenate(columns, axis=1)
    return jnp.concatenate([form, jnp.zeros((LANES - dim - 16, leaf), BF16)], axis=0)


def condense(form, a_rows, chosen):
    size = form.shape[1]
    picks_out = onehot_out(column_of(chosen), size)
    new_rows = dot(picks_out.astype(BF16), a_rows).astype(BF16)
    new_form = dot(form, onehot_in(chosen, size)).astype(BF16)
    weights = jnp.exp(dot(new_rows, form))
    mixing = picks_out + weights / jnp.sum(weights, axis=1, keepdims=True)
    return new_form, new_rows, mixing


def local_tree_kernel(pack, rows, leaf_sets_in, merge_sets_in, out, leaf_sets, merge_sets, sems, *, dim):
    blocks, leaf = rows.shape[:2]
    leaf_copy = pltpu.make_async_copy(leaf_sets_in, leaf_sets, sems.at[0])
    merge_copy = pltpu.make_async_copy(merge_sets_in, merge_sets, sems.at[1])
    leaf_copy.start()
    merge_copy.start()
    leaf_copy.wait()
    first_block = (lax.axis_index("leaf") * lax.axis_size("sub") + lax.axis_index("sub")) * blocks

    nodes = []
    for b in range(blocks):
        form = form_of(pack.at[b], leaf, dim)
        new_form, new_rows, mixing = condense(form, rows[b], leaf_sets[b : b + 1, :])
        m_hi, m_lo = split(mixing)
        probes = pack[b, :leaf, :]
        nodes.append((new_form, new_rows, dot(m_hi, probes) + dot(m_lo, probes)))
    span = 1
    merge_copy.wait()
    while len(nodes) > 1:
        merged = []
        for k in range(len(nodes) // 2):
            left, right = nodes[2 * k], nodes[2 * k + 1]
            chosen = merge_sets[pl.ds(first_block + (2 * k + 1) * span - 1, 1), :]
            new_form, new_rows, mixing = condense(
                jnp.concatenate([left[0], right[0]], axis=1),
                jnp.concatenate([left[1], right[1]], axis=0),
                chosen,
            )
            samples = mix3(mixing, jnp.concatenate([left[2], right[2]], axis=0))
            merged.append((new_form, new_rows, samples))
        nodes = merged
        span *= 2
    held = dim + 16
    out[:held, :] = nodes[0][0][:held, :].astype(F32)
    out[held:, :] = nodes[0][2]


def local_tree_call(pack, rows, leaf_sets, merge_sets, dim):
    blocks, leaf = rows.shape[:2]
    skel = leaf_sets.shape[1]
    return pl.pallas_call(
        functools.partial(local_tree_kernel, dim=dim),
        in_specs=[pl.BlockSpec(memory_space=pltpu.VMEM)] * 2
        + [pl.BlockSpec(memory_space=pltpu.HBM)] * 2,
        out_shape=jax.ShapeDtypeStruct((dim + 16 + skel, LANES), F32),
        scratch_shapes=[
            pltpu.VMEM(leaf_sets.shape, jnp.int32),
            pltpu.VMEM(merge_sets.shape, jnp.int32),
            pltpu.SemaphoreType.DMA((2,)),
        ],
        compiler_params=pltpu.CompilerParams(vmem_limit_bytes=VMEM_BYTES),
        cost_estimate=pl.CostEstimate(
            flops=blocks * 8 * skel * leaf * LANES,
            bytes_accessed=6 * blocks * leaf * LANES,
            transcendentals=blocks * skel * leaf,
        ),
        name="local_tree",
    )(pack, rows, leaf_sets, merge_sets)


def merge_kernel(*refs, dim, blocks, shift, piece):
    merge_sets_in, out, group, merge_sets, sem = refs[-5:]
    parts = refs[:-5]
    count, size = group.shape[:2]
    copy = pltpu.make_async_copy(merge_sets_in, merge_sets, sem)
    copy.start()
    held = dim + 16
    skel = size - held
    rank = lax.axis_index("leaf") * lax.axis_size("sub") + lax.axis_index("sub")
    unit = lax.shift_right_logical(rank, shift)
    place = unit & (count - 1)
    first = unit - place
    span = blocks << shift
    for d, part in enumerate(parts):
        group[place ^ d] = part[...]
    to_rows = form_map(dim, LANES)
    forms = [group[i, :held, :].astype(BF16) for i in range(count)]
    samples = [group[i, held:, :] for i in range(count)]
    copy.wait()
    while len(forms) > 1:
        first = first // 2
        new_forms, new_samples = [], []
        for k in range(len(forms) // 2):
            chosen = merge_sets[pl.ds((2 * (first + k) + 1) * span - 1, 1), :]
            form = jnp.concatenate(forms[2 * k : 2 * k + 2], axis=1)
            form = jnp.concatenate([form, jnp.zeros((LANES - held, 2 * skel), BF16)], axis=0)
            new_form = dot(form, onehot_in(chosen, 2 * skel)).astype(BF16)
            new_rows = dot_t(new_form, to_rows).astype(BF16)
            weights = jnp.exp(dot(new_rows, form))
            picks = onehot_out(column_of(chosen), 2 * skel)
            mixing = picks + weights / jnp.sum(weights, axis=1, keepdims=True)
            new_forms.append(new_form[:held])
            new_samples.append(mix3(mixing, jnp.concatenate(samples[2 * k : 2 * k + 2], axis=0)))
        forms, samples = new_forms, new_samples
        span *= 2
    if piece is None:
        out[:held, :] = forms[0].astype(F32)
        out[held:, :] = samples[0]
    elif piece == 0:
        out[...] = samples[0]
    else:
        column = lax.broadcasted_iota(jnp.int32, (piece, skel), 1)
        row = lax.broadcasted_iota(jnp.int32, (piece, skel), 0) + lax.shift_right_logical(rank, 1) * piece
        take = jnp.where(column == row, 1.0, 0.0).astype(BF16)
        hi, lo = split(samples[0])
        low = (samples[0] - hi.astype(F32) - lo.astype(F32)).astype(BF16)
        out[...] = dot(take, hi) + dot(take, lo) + dot(take, low)


def merge_call(parts, merge_sets, dim, blocks, shift, piece=None):
    count = len(parts)
    size = parts[0].shape[0]
    skel = size - dim - 16
    rows = size if piece is None else (piece or skel)
    return pl.pallas_call(
        functools.partial(merge_kernel, dim=dim, blocks=blocks, shift=shift, piece=piece),
        in_specs=[pl.BlockSpec(memory_space=pltpu.VMEM)] * count
        + [pl.BlockSpec(memory_space=pltpu.HBM)],
        out_shape=jax.ShapeDtypeStruct((rows, LANES), F32),
        scratch_shapes=[
            pltpu.VMEM((count, size, LANES), F32),
            pltpu.VMEM(merge_sets.shape, jnp.int32),
            pltpu.SemaphoreType.DMA(()),
        ],
        compiler_params=pltpu.CompilerParams(vmem_limit_bytes=16 * 1024 * 1024),
        cost_estimate=pl.CostEstimate(
            flops=count * 16 * LANES**3,
            bytes_accessed=4 * count * size * LANES,
            transcendentals=2 * count * LANES**2,
        ),
        name="tree_merge",
    )(*parts, merge_sets)


def near_kernel(*refs, flips, has_acc, sets, tasks, dim):
    refs = list(refs)

    def take(number):
        taken = refs[:number]
        del refs[:number]
        return taken

    lists, rows = take(len(flips)), take(len(flips))
    accs = [take(1)[0] if has else None for has in has_acc]
    buffers = [take(max(which) + 1) for _, which in sets]
    outs, (pair_list,) = take(len(flips)), refs
    blocks, leaf = rows[0].shape[:2]
    near = lists[0].shape[1]
    window = blocks * lax.axis_size("sub")
    sub = lax.axis_index("sub")

    def place(table):
        value = jnp.int32(table[0])
        for i in range(1, len(table)):
            value = jnp.where(sub == i, jnp.int32(table[i]), value)
        return value

    window_first = lax.axis_index("leaf") * window - blocks
    stride = blocks * near + 8
    found = [jnp.int32(0)] * len(tasks)
    for j, flip in enumerate(flips):
        mine = [t for t, (_, group) in enumerate(tasks) if group == j]
        firsts = [window_first + place(sets[tasks[t][0]][0]) for t in mine]
        target_first = lax.axis_index("leaf") * window + (sub ^ flip) * blocks

        def list_block(g, counts, j=j, mine=mine, firsts=firsts, target_first=target_first):
            for s in range(near):
                source = lists[j][g, s]
                used = (source != target_first + g) if s else True
                after = []
                for t, first, count in zip(mine, firsts, counts):
                    local = source - first
                    pair_list[t * stride + count] = g * blocks + local
                    inside = (local >= 0) & (local < blocks) & used
                    after.append(count + jnp.where(inside, 1, 0))
                counts = tuple(after)
            return counts

        counts = lax.fori_loop(0, blocks, list_block, (jnp.int32(0),) * len(mine))
        for t, count in zip(mine, counts):
            found[t] = count
        outs[j][...] = jnp.zeros(outs[j].shape, F32) if accs[j] is None else accs[j][...]

    half = leaf // 2

    def add_all(buffer, t, pairs):
        j = tasks[t][1]

        def add_pair(i):
            code = pair_list[t * stride + i]
            g = code // blocks
            local = code - g * blocks
            form = form_of(buffer.at[local], leaf, dim)
            probes = buffer[local, :leaf, :]
            total = None
            for c in range(0, leaf, half):
                weights = jnp.exp(dot(rows[j][g], form[:, c : c + half])).astype(BF16)
                term = dot(weights, probes[c : c + half])
                total = term if total is None else total + term
            return g, total

        def add_pairs(i, carry):
            for g, total in [add_pair(2 * i), add_pair(2 * i + 1)]:
                outs[j][g] += total
            return carry

        lax.fori_loop(0, pairs // 2, add_pairs, 0)

        @pl.when(pairs % 2 == 1)
        def _():
            g, total = add_pair(pairs - 1)
            outs[j][g] += total

    for t, (number, _) in enumerate(tasks):
        held = place(sets[number][1])
        for k, buffer in enumerate(buffers[number]):
            pairs = found[t] if len(buffers[number]) == 1 else jnp.where(held == k, found[t], 0)
            add_all(buffer, t, pairs)


def near_call(groups, sources, tasks, dim, name):
    flips, lists, rows, accs = zip(*groups)
    blocks, leaf = rows[0].shape[:2]
    held = [acc for acc in accs if acc is not None]
    args = [*lists, *rows, *held, *(b for _, _, buffers in sources for b in buffers)]
    smem = pl.BlockSpec(memory_space=pltpu.SMEM)
    vmem = pl.BlockSpec(memory_space=pltpu.VMEM)
    near = lists[0].shape[1]
    return pl.pallas_call(
        functools.partial(
            near_kernel,
            flips=flips,
            has_acc=tuple(acc is not None for acc in accs),
            sets=tuple((bases, which) for bases, which, _ in sources),
            tasks=tasks,
            dim=dim,
        ),
        in_specs=[smem] * len(lists) + [vmem] * (len(args) - len(lists)),
        out_specs=[vmem] * len(groups),
        out_shape=[jax.ShapeDtypeStruct((blocks, leaf, LANES), F32)] * len(groups),
        scratch_shapes=[pltpu.SMEM((len(tasks) * (blocks * near + 8),), jnp.int32)],
        compiler_params=pltpu.CompilerParams(vmem_limit_bytes=NEAR_BYTES),
        cost_estimate=pl.CostEstimate(flops=1000, bytes_accessed=1000, transcendentals=0),
        name=name,
    )(*args)


def on_device(points, probes, order, near_lists, near_counts, leaf_sets, merge_sets):
    leaf_count = lax.axis_size("leaf")
    sub_count = lax.axis_size("sub")
    blocks, skel = leaf_sets.shape
    npts, dim = points.shape
    leaf = npts // blocks
    axes = ("leaf", "sub")

    def send(x, routes):
        pairs = []
        for place in range(leaf_count):
            for from_sub, step, to_sub in routes:
                if 0 <= place + step < leaf_count:
                    pairs.append((place * sub_count + from_sub, (place + step) * sub_count + to_sub))
        return lax.ppermute(x, axes, pairs)

    count = leaf_count * sub_count
    bits = count.bit_length() - 1
    sub_bits = sub_count.bit_length() - 1

    def exchange(x, shift, stage_bits):
        parts = [x]
        for d in range(1, 1 << stage_bits):
            parts.append(lax.ppermute(x, axes, [(i, i ^ (d << shift)) for i in range(count)]))
        return parts

    def tie(*values):
        return lax.optimization_barrier(values)

    b = blocks
    own_base = (b, 2 * b, 3 * b, 4 * b)
    early_base, late_base = (5 * b, 4 * b, b, 0), (3 * b, 0, 5 * b, 2 * b)
    single, by_edge = (0, 0, 0, 0), (0, 1, 1, 0)

    pack, rows = order_call(points.T, order.reshape(blocks, 1, leaf), probes, blocks)
    outer_across = send(pack, [(3, 0, 1), (0, 0, 2)])
    outer_next = send(pack, [(3, 1, 3), (0, -1, 0)])
    beside_rows = exchange(rows, 0, 1)[1]
    beside_lists = exchange(near_lists, 0, 1)[1]

    node = local_tree_call(pack, rows, leaf_sets, merge_sets, dim)
    node, beside_lists = tie(node, beside_lists)

    def level(parts, bit, piece=None):
        return merge_call(parts, merge_sets, dim, blocks, bit, piece)

    node = level(exchange(node, 0, 1), 0)
    own_pack, node = tie(pack, node)
    other = send(node, [(1, 0, 2), (2, 0, 1)])

    def among_inner(x, shift, stage):
        parts = [x]
        for d in range(1, 1 << stage):
            step = d << shift - sub_bits
            pairs = [
                (place * sub_count + inner, (place ^ step) * sub_count + inner)
                for place in range(leaf_count)
                for inner in (1, 2)
            ]
            parts.append(lax.ppermute(x, axes, pairs))
        return parts

    own_set = (own_base, single, [own_pack])
    (beside,) = near_call(
        [(1, beside_lists, beside_rows, None)], [own_set], ((0, 0),), dim, "near_own"
    )

    other, beside = tie(other, beside)
    node = level([node, other], 1)
    shift, stage = sub_bits, 1
    parts = among_inner(node, shift, stage)
    *parts, outer_across, outer_next, own_pack, beside = tie(
        *parts, outer_across, outer_next, own_pack, beside
    )
    forwarded = send(outer_across, [(1, 1, 1), (2, -1, 2)])
    inner_across = send(own_pack, [(2, 0, 0), (1, 0, 3)])
    while shift + stage < bits:
        node = level(parts, shift)
        shift, stage = shift + stage, min(2, bits - shift - stage)
        parts = among_inner(node, shift, stage)
    own_pack, node = tie(own_pack, node)
    own_set = (own_base, single, [own_pack])
    early_set = (early_base, by_edge, [outer_next, outer_across])
    own, beside = near_call(
        [(0, near_lists, rows, None), (1, beside_lists, beside_rows, beside)],
        [own_set, early_set], ((0, 0), (1, 0), (1, 1)), dim, "near_early",
    )

    *parts, inner_across, forwarded, beside = tie(*parts, inner_across, forwarded, beside)
    late_set = (late_base, by_edge, [inner_across, forwarded])
    (beside,) = near_call(
        [(1, beside_lists, beside_rows, beside)], [late_set], ((0, 0),), dim, "near_beside"
    )
    given = exchange(beside, 0, 1)[1]
    *parts, beside = tie(*parts, beside)
    piece = skel // count
    root_rows = level(parts, shift, 2 * piece)
    shared_rows = send(root_rows, [(1, 0, 0), (2, 0, 3)])
    own, root_rows = tie(own, root_rows)
    (own,) = near_call([(0, near_lists, rows, own)], [late_set], ((0, 0),), dim, "near_last")
    near = (own + given) * (leaf ** -0.5)
    sub_place = lax.axis_index("sub")
    edge = (sub_place == 0) | (sub_place == sub_count - 1)
    rank = lax.axis_index("leaf") * sub_count + sub_place
    size = skel * LANES // count
    root_rows = jnp.where(edge, shared_rows, root_rows).reshape(-1)
    start = (rank % 2 if piece else rank) * size
    root = lax.dynamic_slice_in_dim(root_rows, start, size, 0)
    return near.reshape(npts, LANES), root


def solution(mesh):
    in_specs = (
        P(("leaf", "sub"), None),
        P(("leaf", "sub"), None),
        P(("leaf", "sub")),
        P(("leaf", "sub"), None),
        P(("leaf", "sub")),
        P(("leaf", "sub"), None),
        P(),
    )
    out_specs = (P(("leaf", "sub"), None), P(("leaf", "sub")))
    return jax.shard_map(
        on_device, mesh=mesh, in_specs=in_specs, out_specs=out_specs, check_vma=False
    )
```

```python
import functools

import jax
import jax.numpy as jnp
from jax import lax
from jax.experimental import pallas as pl
from jax.experimental.pallas import tpu as pltpu
from jax.sharding import PartitionSpec as P

LANES = 128
PARTS = 3
VMEM_BYTES = 20 * 1024 * 1024
NEAR_BYTES = 24 * 1024 * 1024
F32 = jnp.float32
BF16 = jnp.bfloat16


def dot(a, b):
    return jnp.dot(a, b, preferred_element_type=F32)


def dot_t(a, b):
    return lax.dot_general(a, b, (((0,), (0,)), ((), ())), preferred_element_type=F32)


def split(x):
    hi = x.astype(BF16)
    return hi, (x - hi.astype(F32)).astype(BF16)


def square_rows(pts):
    x = pts.astype(F32)
    total = jnp.sum(x * x, axis=0, keepdims=True)
    hi = total.astype(BF16).astype(F32)
    mid = (total - hi).astype(BF16).astype(F32)
    low = total - hi - mid
    row = lax.broadcasted_iota(jnp.int32, (16, pts.shape[1]), 0)
    ones = jnp.where(row < 2 * PARTS, 1.0, 0.0)
    return jnp.where(row == 0, hi, jnp.where(row == 1, mid, jnp.where(row == 2, low, ones))).astype(BF16)


def form_map(dim, size):
    k = lax.broadcasted_iota(jnp.int32, (size, size), 0)
    j = lax.broadcasted_iota(jnp.int32, (size, size), 1)
    r = jnp.where((k == j) & (j < dim), 2.0 / dim, 0.0)
    r = jnp.where((j >= dim) & (j < dim + PARTS) & (k == j + PARTS), -1.0 / dim, r)
    r = jnp.where((j >= dim + PARTS) & (j < dim + 2 * PARTS) & (k == j - PARTS), -1.0 / dim, r)
    return r.astype(BF16)


def onehot_in(row, size):
    index = lax.broadcasted_iota(jnp.int32, (size, row.shape[1]), 0)
    return jnp.where(index == row, 1.0, 0.0).astype(BF16)


def column_of(row):
    return jnp.broadcast_to(row.astype(F32), (LANES, row.shape[1])).T


def onehot_out(column, size):
    lane = lax.broadcasted_iota(jnp.int32, column.shape, 1).astype(F32)
    return jnp.concatenate(
        [jnp.where(column == lane + float(i), 1.0, 0.0) for i in range(0, size, LANES)], axis=1
    )


def mix3(m, s):
    m_hi, m_lo = split(m)
    s_hi, s_lo = split(s)
    return dot(m_hi, s_hi) + (dot(m_hi, s_lo) + dot(m_lo, s_hi))


def order_kernel(points_t, order, probes, pack, rows):
    dim = points_t.shape[0]
    many, leaf = rows.shape[:2]
    held = dim + 16
    to_rows = form_map(dim, LANES)
    for b in range(many):
        picks = onehot_in(order[b], leaf)
        tree_t = dot(points_t[:, b * leaf : (b + 1) * leaf], picks).astype(BF16)
        pack[b, :leaf, :] = probes[b * leaf : (b + 1) * leaf, :]
        form = jnp.concatenate([tree_t, square_rows(tree_t)], axis=0)
        for i in range(leaf // LANES):
            pack[b, leaf + i * dim : leaf + (i + 1) * dim, :] = tree_t[:, i * LANES : (i + 1) * LANES]
        form = jnp.concatenate([form, jnp.zeros((LANES - held, leaf), BF16)], axis=0)
        rows[b] = dot_t(form, to_rows).astype(BF16)


def order_call(points_t, order, probes, blocks):
    dim, npts = points_t.shape
    leaf = npts // blocks
    packed = leaf + leaf // LANES * dim
    many = 4 if blocks % 4 == 0 else 1
    return pl.pallas_call(
        order_kernel,
        grid=(blocks // many,),
        in_specs=[
            pl.BlockSpec((dim, many * leaf), lambda b: (0, b)),
            pl.BlockSpec((many, 1, leaf), lambda b: (b, 0, 0)),
            pl.BlockSpec((many * leaf, LANES), lambda b: (b, 0)),
        ],
        out_specs=[
            pl.BlockSpec((many, packed, LANES), lambda b: (b, 0, 0)),
            pl.BlockSpec((many, leaf, LANES), lambda b: (b, 0, 0)),
        ],
        out_shape=[
            jax.ShapeDtypeStruct((blocks, packed, LANES), BF16),
            jax.ShapeDtypeStruct((blocks, leaf, LANES), BF16),
        ],
        compiler_params=pltpu.CompilerParams(vmem_limit_bytes=VMEM_BYTES),
        cost_estimate=pl.CostEstimate(
            flops=blocks * 2 * leaf * leaf * dim, bytes_accessed=10 * npts * LANES, transcendentals=0
        ),
        name="tree_order",
    )(points_t, order, probes)


def form_of(pack_block, leaf, dim):
    columns = []
    for i in range(leaf // LANES):
        pts = pack_block[leaf + i * dim : leaf + (i + 1) * dim, :]
        columns.append(jnp.concatenate([pts, square_rows(pts)], axis=0))
    form = jnp.concatenate(columns, axis=1)
    return jnp.concatenate([form, jnp.zeros((LANES - dim - 16, leaf), BF16)], axis=0)


def condense(form, a_rows, chosen):
    size = form.shape[1]
    picks_out = onehot_out(column_of(chosen), size)
    new_rows = dot(picks_out.astype(BF16), a_rows).astype(BF16)
    new_form = dot(form, onehot_in(chosen, size)).astype(BF16)
    weights = jnp.exp(dot(new_rows, form))
    mixing = picks_out + weights / jnp.sum(weights, axis=1, keepdims=True)
    return new_form, new_rows, mixing


def local_tree_kernel(pack, rows, leaf_sets_in, merge_sets_in, out, leaf_sets, merge_sets, sems, *, dim):
    blocks, leaf = rows.shape[:2]
    leaf_copy = pltpu.make_async_copy(leaf_sets_in, leaf_sets, sems.at[0])
    merge_copy = pltpu.make_async_copy(merge_sets_in, merge_sets, sems.at[1])
    leaf_copy.start()
    merge_copy.start()
    leaf_copy.wait()
    first_block = (lax.axis_index("leaf") * lax.axis_size("sub") + lax.axis_index("sub")) * blocks

    nodes = []
    for b in range(blocks):
        form = form_of(pack.at[b], leaf, dim)
        new_form, new_rows, mixing = condense(form, rows[b], leaf_sets[b : b + 1, :])
        m_hi, m_lo = split(mixing)
        probes = pack[b, :leaf, :]
        nodes.append((new_form, new_rows, dot(m_hi, probes) + dot(m_lo, probes)))
    span = 1
    merge_copy.wait()
    while len(nodes) > 1:
        merged = []
        for k in range(len(nodes) // 2):
            left, right = nodes[2 * k], nodes[2 * k + 1]
            chosen = merge_sets[pl.ds(first_block + (2 * k + 1) * span - 1, 1), :]
            new_form, new_rows, mixing = condense(
                jnp.concatenate([left[0], right[0]], axis=1),
                jnp.concatenate([left[1], right[1]], axis=0),
                chosen,
            )
            samples = mix3(mixing, jnp.concatenate([left[2], right[2]], axis=0))
            merged.append((new_form, new_rows, samples))
        nodes = merged
        span *= 2
    held = dim + 16
    out[:held, :] = nodes[0][0][:held, :].astype(F32)
    out[held:, :] = nodes[0][2]


def local_tree_call(pack, rows, leaf_sets, merge_sets, dim):
    blocks, leaf = rows.shape[:2]
    skel = leaf_sets.shape[1]
    return pl.pallas_call(
        functools.partial(local_tree_kernel, dim=dim),
        in_specs=[pl.BlockSpec(memory_space=pltpu.VMEM)] * 2
        + [pl.BlockSpec(memory_space=pltpu.HBM)] * 2,
        out_shape=jax.ShapeDtypeStruct((dim + 16 + skel, LANES), F32),
        scratch_shapes=[
            pltpu.VMEM(leaf_sets.shape, jnp.int32),
            pltpu.VMEM(merge_sets.shape, jnp.int32),
            pltpu.SemaphoreType.DMA((2,)),
        ],
        compiler_params=pltpu.CompilerParams(vmem_limit_bytes=VMEM_BYTES),
        cost_estimate=pl.CostEstimate(
            flops=blocks * 8 * skel * leaf * LANES,
            bytes_accessed=6 * blocks * leaf * LANES,
            transcendentals=blocks * skel * leaf,
        ),
        name="local_tree",
    )(pack, rows, leaf_sets, merge_sets)


def merge_kernel(*refs, dim, blocks, shift, piece):
    merge_sets_in, out, group, merge_sets, sem = refs[-5:]
    parts = refs[:-5]
    count, size = group.shape[:2]
    copy = pltpu.make_async_copy(merge_sets_in, merge_sets, sem)
    copy.start()
    held = dim + 16
    skel = size - held
    rank = lax.axis_index("leaf") * lax.axis_size("sub") + lax.axis_index("sub")
    unit = lax.shift_right_logical(rank, shift)
    place = unit & (count - 1)
    first = unit - place
    span = blocks << shift
    for d, part in enumerate(parts):
        group[place ^ d] = part[...]
    to_rows = form_map(dim, LANES)
    forms = [group[i, :held, :].astype(BF16) for i in range(count)]
    samples = [group[i, held:, :] for i in range(count)]
    copy.wait()
    while len(forms) > 1:
        first = first // 2
        new_forms, new_samples = [], []
        for k in range(len(forms) // 2):
            chosen = merge_sets[pl.ds((2 * (first + k) + 1) * span - 1, 1), :]
            form = jnp.concatenate(forms[2 * k : 2 * k + 2], axis=1)
            form = jnp.concatenate([form, jnp.zeros((LANES - held, 2 * skel), BF16)], axis=0)
            new_form = dot(form, onehot_in(chosen, 2 * skel)).astype(BF16)
            new_rows = dot_t(new_form, to_rows).astype(BF16)
            weights = jnp.exp(dot(new_rows, form))
            picks = onehot_out(column_of(chosen), 2 * skel)
            mixing = picks + weights / jnp.sum(weights, axis=1, keepdims=True)
            new_forms.append(new_form[:held])
            new_samples.append(mix3(mixing, jnp.concatenate(samples[2 * k : 2 * k + 2], axis=0)))
        forms, samples = new_forms, new_samples
        span *= 2
    if piece is None:
        out[:held, :] = forms[0].astype(F32)
        out[held:, :] = samples[0]
    elif piece == 0:
        out[...] = samples[0]
    else:
        column = lax.broadcasted_iota(jnp.int32, (piece, skel), 1)
        row = lax.broadcasted_iota(jnp.int32, (piece, skel), 0) + rank * piece
        take = jnp.where(column == row, 1.0, 0.0).astype(BF16)
        hi, lo = split(samples[0])
        low = (samples[0] - hi.astype(F32) - lo.astype(F32)).astype(BF16)
        out[...] = dot(take, hi) + dot(take, lo) + dot(take, low)


def merge_call(parts, merge_sets, dim, blocks, shift, piece=None):
    count = len(parts)
    size = parts[0].shape[0]
    skel = size - dim - 16
    rows = size if piece is None else (piece or skel)
    return pl.pallas_call(
        functools.partial(merge_kernel, dim=dim, blocks=blocks, shift=shift, piece=piece),
        in_specs=[pl.BlockSpec(memory_space=pltpu.VMEM)] * count
        + [pl.BlockSpec(memory_space=pltpu.HBM)],
        out_shape=jax.ShapeDtypeStruct((rows, LANES), F32),
        scratch_shapes=[
            pltpu.VMEM((count, size, LANES), F32),
            pltpu.VMEM(merge_sets.shape, jnp.int32),
            pltpu.SemaphoreType.DMA(()),
        ],
        compiler_params=pltpu.CompilerParams(vmem_limit_bytes=16 * 1024 * 1024),
        cost_estimate=pl.CostEstimate(
            flops=count * 16 * LANES**3,
            bytes_accessed=4 * count * size * LANES,
            transcendentals=2 * count * LANES**2,
        ),
        name="tree_merge",
    )(*parts, merge_sets)


def near_kernel(*refs, flips, has_acc, sets, tasks, dim):
    refs = list(refs)

    def take(number):
        taken = refs[:number]
        del refs[:number]
        return taken

    lists, rows = take(len(flips)), take(len(flips))
    accs = [take(1)[0] if has else None for has in has_acc]
    buffers = [take(max(which) + 1) for _, which in sets]
    outs, (pair_list,) = take(len(flips)), refs
    blocks, leaf = rows[0].shape[:2]
    near = lists[0].shape[1]
    window = blocks * lax.axis_size("sub")
    sub = lax.axis_index("sub")

    def place(table):
        value = jnp.int32(table[0])
        for i in range(1, len(table)):
            value = jnp.where(sub == i, jnp.int32(table[i]), value)
        return value

    window_first = lax.axis_index("leaf") * window - blocks
    stride = blocks * near + 8
    found = [jnp.int32(0)] * len(tasks)
    for j, flip in enumerate(flips):
        mine = [t for t, (_, group) in enumerate(tasks) if group == j]
        firsts = [window_first + place(sets[tasks[t][0]][0]) for t in mine]
        target_first = lax.axis_index("leaf") * window + (sub ^ flip) * blocks

        def list_block(g, counts, j=j, mine=mine, firsts=firsts, target_first=target_first):
            for s in range(near):
                source = lists[j][g, s]
                used = (source != target_first + g) if s else True
                after = []
                for t, first, count in zip(mine, firsts, counts):
                    local = source - first
                    pair_list[t * stride + count] = g * blocks + local
                    inside = (local >= 0) & (local < blocks) & used
                    after.append(count + jnp.where(inside, 1, 0))
                counts = tuple(after)
            return counts

        counts = lax.fori_loop(0, blocks, list_block, (jnp.int32(0),) * len(mine))
        for t, count in zip(mine, counts):
            found[t] = count
        outs[j][...] = jnp.zeros(outs[j].shape, F32) if accs[j] is None else accs[j][...]

    half = leaf // 2

    def add_all(buffer, t, pairs):
        j = tasks[t][1]

        def add_pair(i):
            code = pair_list[t * stride + i]
            g = code // blocks
            local = code - g * blocks
            form = form_of(buffer.at[local], leaf, dim)
            probes = buffer[local, :leaf, :]
            total = None
            for c in range(0, leaf, half):
                weights = jnp.exp(dot(rows[j][g], form[:, c : c + half])).astype(BF16)
                term = dot(weights, probes[c : c + half])
                total = term if total is None else total + term
            return g, total

        def add_pairs(i, carry):
            for g, total in [add_pair(2 * i), add_pair(2 * i + 1)]:
                outs[j][g] += total
            return carry

        lax.fori_loop(0, pairs // 2, add_pairs, 0)

        @pl.when(pairs % 2 == 1)
        def _():
            g, total = add_pair(pairs - 1)
            outs[j][g] += total

    for t, (number, _) in enumerate(tasks):
        held = place(sets[number][1])
        for k, buffer in enumerate(buffers[number]):
            pairs = found[t] if len(buffers[number]) == 1 else jnp.where(held == k, found[t], 0)
            add_all(buffer, t, pairs)


def near_call(groups, sources, tasks, dim, name):
    flips, lists, rows, accs = zip(*groups)
    blocks, leaf = rows[0].shape[:2]
    held = [acc for acc in accs if acc is not None]
    args = [*lists, *rows, *held, *(b for _, _, buffers in sources for b in buffers)]
    smem = pl.BlockSpec(memory_space=pltpu.SMEM)
    vmem = pl.BlockSpec(memory_space=pltpu.VMEM)
    near = lists[0].shape[1]
    return pl.pallas_call(
        functools.partial(
            near_kernel,
            flips=flips,
            has_acc=tuple(acc is not None for acc in accs),
            sets=tuple((bases, which) for bases, which, _ in sources),
            tasks=tasks,
            dim=dim,
        ),
        in_specs=[smem] * len(lists) + [vmem] * (len(args) - len(lists)),
        out_specs=[vmem] * len(groups),
        out_shape=[jax.ShapeDtypeStruct((blocks, leaf, LANES), F32)] * len(groups),
        scratch_shapes=[pltpu.SMEM((len(tasks) * (blocks * near + 8),), jnp.int32)],
        compiler_params=pltpu.CompilerParams(vmem_limit_bytes=NEAR_BYTES),
        cost_estimate=pl.CostEstimate(flops=1000, bytes_accessed=1000, transcendentals=0),
        name=name,
    )(*args)


def on_device(points, probes, order, near_lists, near_counts, leaf_sets, merge_sets):
    leaf_count = lax.axis_size("leaf")
    sub_count = lax.axis_size("sub")
    blocks, skel = leaf_sets.shape
    npts, dim = points.shape
    leaf = npts // blocks
    axes = ("leaf", "sub")

    def send(x, routes):
        pairs = []
        for place in range(leaf_count):
            for from_sub, step, to_sub in routes:
                if 0 <= place + step < leaf_count:
                    pairs.append((place * sub_count + from_sub, (place + step) * sub_count + to_sub))
        return lax.ppermute(x, axes, pairs)

    count = leaf_count * sub_count
    bits = count.bit_length() - 1
    sub_bits = sub_count.bit_length() - 1

    def exchange(x, shift, stage_bits):
        parts = [x]
        for d in range(1, 1 << stage_bits):
            parts.append(lax.ppermute(x, axes, [(i, i ^ (d << shift)) for i in range(count)]))
        return parts

    def tie(*values):
        return lax.optimization_barrier(values)

    b = blocks
    own_base = (b, 2 * b, 3 * b, 4 * b)
    early_base, late_base = (5 * b, 4 * b, b, 0), (3 * b, 0, 5 * b, 2 * b)
    single, by_edge = (0, 0, 0, 0), (0, 1, 1, 0)

    pack, rows = order_call(points.T, order.reshape(blocks, 1, leaf), probes, blocks)
    outer_across = send(pack, [(3, 0, 1), (0, 0, 2)])
    outer_next = send(pack, [(3, 1, 3), (0, -1, 0)])
    beside_rows = exchange(rows, 0, 1)[1]
    beside_lists = exchange(near_lists, 0, 1)[1]

    node = local_tree_call(pack, rows, leaf_sets, merge_sets, dim)
    node, beside_lists = tie(node, beside_lists)

    def level(parts, bit, piece=None):
        return merge_call(parts, merge_sets, dim, blocks, bit, piece)

    node = level(exchange(node, 0, 1), 0)
    own_pack, node = tie(pack, node)
    parts = exchange(node, 1, 1)
    own_set = (own_base, single, [own_pack])
    (beside,) = near_call(
        [(1, beside_lists, beside_rows, None)], [own_set], ((0, 0),), dim, "near_own"
    )

    *parts, outer_across, outer_next, own_pack, beside = tie(
        *parts, outer_across, outer_next, own_pack, beside
    )
    inner_across = send(own_pack, [(2, 0, 0), (1, 0, 3)])
    forwarded = send(outer_across, [(1, 1, 1), (2, -1, 2)])
    node = level(parts, 1)
    own_pack, node = tie(own_pack, node)
    parts = exchange(node, 2, 1)
    own_set = (own_base, single, [own_pack])
    early_set = (early_base, by_edge, [outer_next, outer_across])
    own, beside = near_call(
        [(0, near_lists, rows, None), (1, beside_lists, beside_rows, beside)],
        [own_set, early_set], ((0, 0), (1, 0), (1, 1)), dim, "near_early",
    )

    *parts, inner_across, forwarded, beside = tie(*parts, inner_across, forwarded, beside)
    shift, stage = 2, 1
    while shift + stage < bits:
        node = level(parts, shift)
        shift, stage = shift + stage, min(2, bits - shift - stage)
        parts = exchange(node, shift, stage)
    *parts, beside = tie(*parts, beside)
    late_set = (late_base, by_edge, [inner_across, forwarded])
    (beside,) = near_call(
        [(1, beside_lists, beside_rows, beside)], [late_set], ((0, 0),), dim, "near_beside"
    )
    given = exchange(beside, 0, 1)[1]
    (own,) = near_call([(0, near_lists, rows, own)], [late_set], ((0, 0),), dim, "near_last")
    *parts, own = tie(*parts, own)
    node = level(parts, shift, skel // count)
    near = (own + given) * (leaf ** -0.5)
    if skel // count:
        root = node.reshape(-1)
    else:
        size = skel * LANES // count
        rank = lax.axis_index("leaf") * sub_count + lax.axis_index("sub")
        root = lax.dynamic_slice_in_dim(node.reshape(-1), rank * size, size, 0)
    return near.reshape(npts, LANES), root


def solution(mesh):
    in_specs = (
        P(("leaf", "sub"), None),
        P(("leaf", "sub"), None),
        P(("leaf", "sub")),
        P(("leaf", "sub"), None),
        P(("leaf", "sub")),
        P(("leaf", "sub"), None),
        P(),
    )
    out_specs = (P(("leaf", "sub"), None), P(("leaf", "sub")))
    return jax.shard_map(
        on_device, mesh=mesh, in_specs=in_specs, out_specs=out_specs, check_vma=False
    )
```

```python
import functools

import jax
import jax.numpy as jnp
from jax import lax
from jax.experimental import pallas as pl
from jax.experimental.pallas import tpu as pltpu
from jax.sharding import PartitionSpec as P

LANES = 128
PARTS = 3
VMEM_BYTES = 20 * 1024 * 1024
NEAR_BYTES = 24 * 1024 * 1024
F32 = jnp.float32
BF16 = jnp.bfloat16


def dot(a, b):
    return jnp.dot(a, b, preferred_element_type=F32)


def dot_t(a, b):
    return lax.dot_general(a, b, (((0,), (0,)), ((), ())), preferred_element_type=F32)


def split(x):
    hi = x.astype(BF16)
    return hi, (x - hi.astype(F32)).astype(BF16)


def square_rows(pts):
    x = pts.astype(F32)
    total = jnp.sum(x * x, axis=0, keepdims=True)
    hi = total.astype(BF16).astype(F32)
    mid = (total - hi).astype(BF16).astype(F32)
    low = total - hi - mid
    row = lax.broadcasted_iota(jnp.int32, (16, pts.shape[1]), 0)
    ones = jnp.where(row < 2 * PARTS, 1.0, 0.0)
    return jnp.where(row == 0, hi, jnp.where(row == 1, mid, jnp.where(row == 2, low, ones))).astype(BF16)


def form_map(dim, size):
    k = lax.broadcasted_iota(jnp.int32, (size, size), 0)
    j = lax.broadcasted_iota(jnp.int32, (size, size), 1)
    r = jnp.where((k == j) & (j < dim), 2.0 / dim, 0.0)
    r = jnp.where((j >= dim) & (j < dim + PARTS) & (k == j + PARTS), -1.0 / dim, r)
    r = jnp.where((j >= dim + PARTS) & (j < dim + 2 * PARTS) & (k == j - PARTS), -1.0 / dim, r)
    return r.astype(BF16)


def onehot_in(row, size):
    index = lax.broadcasted_iota(jnp.int32, (size, row.shape[1]), 0)
    return jnp.where(index == row, 1.0, 0.0).astype(BF16)


def column_of(row):
    return jnp.broadcast_to(row.astype(F32), (LANES, row.shape[1])).T


def onehot_out(column, size):
    lane = lax.broadcasted_iota(jnp.int32, column.shape, 1).astype(F32)
    return jnp.concatenate(
        [jnp.where(column == lane + float(i), 1.0, 0.0) for i in range(0, size, LANES)], axis=1
    )


def mix3(m, s):
    m_hi, m_lo = split(m)
    s_hi, s_lo = split(s)
    return dot(m_hi, s_hi) + (dot(m_hi, s_lo) + dot(m_lo, s_hi))


def order_kernel(points_t, order, probes, pack, rows):
    dim = points_t.shape[0]
    many, leaf = rows.shape[:2]
    held = dim + 16
    to_rows = form_map(dim, LANES)
    for b in range(many):
        picks = onehot_in(order[b], leaf)
        tree_t = dot(points_t[:, b * leaf : (b + 1) * leaf], picks).astype(BF16)
        pack[b, :leaf, :] = probes[b * leaf : (b + 1) * leaf, :]
        form = jnp.concatenate([tree_t, square_rows(tree_t)], axis=0)
        for i in range(leaf // LANES):
            pack[b, leaf + i * dim : leaf + (i + 1) * dim, :] = tree_t[:, i * LANES : (i + 1) * LANES]
        form = jnp.concatenate([form, jnp.zeros((LANES - held, leaf), BF16)], axis=0)
        rows[b] = dot_t(form, to_rows).astype(BF16)


def order_call(points_t, order, probes, blocks):
    dim, npts = points_t.shape
    leaf = npts // blocks
    packed = leaf + leaf // LANES * dim
    many = 4 if blocks % 4 == 0 else 1
    return pl.pallas_call(
        order_kernel,
        grid=(blocks // many,),
        in_specs=[
            pl.BlockSpec((dim, many * leaf), lambda b: (0, b)),
            pl.BlockSpec((many, 1, leaf), lambda b: (b, 0, 0)),
            pl.BlockSpec((many * leaf, LANES), lambda b: (b, 0)),
        ],
        out_specs=[
            pl.BlockSpec((many, packed, LANES), lambda b: (b, 0, 0)),
            pl.BlockSpec((many, leaf, LANES), lambda b: (b, 0, 0)),
        ],
        out_shape=[
            jax.ShapeDtypeStruct((blocks, packed, LANES), BF16),
            jax.ShapeDtypeStruct((blocks, leaf, LANES), BF16),
        ],
        compiler_params=pltpu.CompilerParams(vmem_limit_bytes=VMEM_BYTES),
        cost_estimate=pl.CostEstimate(
            flops=blocks * 2 * leaf * leaf * dim, bytes_accessed=10 * npts * LANES, transcendentals=0
        ),
        name="tree_order",
    )(points_t, order, probes)


def form_of(pack_block, leaf, dim):
    columns = []
    for i in range(leaf // LANES):
        pts = pack_block[leaf + i * dim : leaf + (i + 1) * dim, :]
        columns.append(jnp.concatenate([pts, square_rows(pts)], axis=0))
    form = jnp.concatenate(columns, axis=1)
    return jnp.concatenate([form, jnp.zeros((LANES - dim - 16, leaf), BF16)], axis=0)


def condense(form, a_rows, chosen):
    size = form.shape[1]
    picks_out = onehot_out(column_of(chosen), size)
    new_rows = dot(picks_out.astype(BF16), a_rows).astype(BF16)
    new_form = dot(form, onehot_in(chosen, size)).astype(BF16)
    weights = jnp.exp(dot(new_rows, form))
    mixing = picks_out + weights / jnp.sum(weights, axis=1, keepdims=True)
    return new_form, new_rows, mixing


def local_tree_kernel(pack, rows, leaf_sets_in, merge_sets_in, out, leaf_sets, merge_sets, sems, *, dim):
    blocks, leaf = rows.shape[:2]
    leaf_copy = pltpu.make_async_copy(leaf_sets_in, leaf_sets, sems.at[0])
    merge_copy = pltpu.make_async_copy(merge_sets_in, merge_sets, sems.at[1])
    leaf_copy.start()
    merge_copy.start()
    leaf_copy.wait()
    first_block = (lax.axis_index("leaf") * lax.axis_size("sub") + lax.axis_index("sub")) * blocks

    nodes = []
    for b in range(blocks):
        form = form_of(pack.at[b], leaf, dim)
        new_form, new_rows, mixing = condense(form, rows[b], leaf_sets[b : b + 1, :])
        m_hi, m_lo = split(mixing)
        probes = pack[b, :leaf, :]
        nodes.append((new_form, new_rows, dot(m_hi, probes) + dot(m_lo, probes)))
    span = 1
    merge_copy.wait()
    while len(nodes) > 1:
        merged = []
        for k in range(len(nodes) // 2):
            left, right = nodes[2 * k], nodes[2 * k + 1]
            chosen = merge_sets[pl.ds(first_block + (2 * k + 1) * span - 1, 1), :]
            new_form, new_rows, mixing = condense(
                jnp.concatenate([left[0], right[0]], axis=1),
                jnp.concatenate([left[1], right[1]], axis=0),
                chosen,
            )
            samples = mix3(mixing, jnp.concatenate([left[2], right[2]], axis=0))
            merged.append((new_form, new_rows, samples))
        nodes = merged
        span *= 2
    held = dim + 16
    out[:held, :] = nodes[0][0][:held, :].astype(F32)
    out[held:, :] = nodes[0][2]


def local_tree_call(pack, rows, leaf_sets, merge_sets, dim):
    blocks, leaf = rows.shape[:2]
    skel = leaf_sets.shape[1]
    return pl.pallas_call(
        functools.partial(local_tree_kernel, dim=dim),
        in_specs=[pl.BlockSpec(memory_space=pltpu.VMEM)] * 2
        + [pl.BlockSpec(memory_space=pltpu.HBM)] * 2,
        out_shape=jax.ShapeDtypeStruct((dim + 16 + skel, LANES), F32),
        scratch_shapes=[
            pltpu.VMEM(leaf_sets.shape, jnp.int32),
            pltpu.VMEM(merge_sets.shape, jnp.int32),
            pltpu.SemaphoreType.DMA((2,)),
        ],
        compiler_params=pltpu.CompilerParams(vmem_limit_bytes=VMEM_BYTES),
        cost_estimate=pl.CostEstimate(
            flops=blocks * 8 * skel * leaf * LANES,
            bytes_accessed=6 * blocks * leaf * LANES,
            transcendentals=blocks * skel * leaf,
        ),
        name="local_tree",
    )(pack, rows, leaf_sets, merge_sets)


def merge_kernel(*refs, dim, blocks, shift, piece):
    merge_sets_in, out, group, merge_sets, sem = refs[-5:]
    parts = refs[:-5]
    count, size = group.shape[:2]
    copy = pltpu.make_async_copy(merge_sets_in, merge_sets, sem)
    copy.start()
    held = dim + 16
    skel = size - held
    rank = lax.axis_index("leaf") * lax.axis_size("sub") + lax.axis_index("sub")
    unit = lax.shift_right_logical(rank, shift)
    place = unit & (count - 1)
    first = unit - place
    span = blocks << shift
    for d, part in enumerate(parts):
        group[place ^ d] = part[...]
    to_rows = form_map(dim, LANES)
    forms = [group[i, :held, :].astype(BF16) for i in range(count)]
    samples = [group[i, held:, :] for i in range(count)]
    copy.wait()
    while len(forms) > 1:
        first = first // 2
        new_forms, new_samples = [], []
        for k in range(len(forms) // 2):
            chosen = merge_sets[pl.ds((2 * (first + k) + 1) * span - 1, 1), :]
            form = jnp.concatenate(forms[2 * k : 2 * k + 2], axis=1)
            form = jnp.concatenate([form, jnp.zeros((LANES - held, 2 * skel), BF16)], axis=0)
            new_form = dot(form, onehot_in(chosen, 2 * skel)).astype(BF16)
            new_rows = dot_t(new_form, to_rows).astype(BF16)
            weights = jnp.exp(dot(new_rows, form))
            picks = onehot_out(column_of(chosen), 2 * skel)
            mixing = picks + weights / jnp.sum(weights, axis=1, keepdims=True)
            new_forms.append(new_form[:held])
            new_samples.append(mix3(mixing, jnp.concatenate(samples[2 * k : 2 * k + 2], axis=0)))
        forms, samples = new_forms, new_samples
        span *= 2
    if piece is None:
        out[:held, :] = forms[0].astype(F32)
        out[held:, :] = samples[0]
    elif piece == 0:
        out[...] = samples[0]
    else:
        column = lax.broadcasted_iota(jnp.int32, (piece, skel), 1)
        row = lax.broadcasted_iota(jnp.int32, (piece, skel), 0) + rank * piece
        take = jnp.where(column == row, 1.0, 0.0).astype(BF16)
        hi, lo = split(samples[0])
        low = (samples[0] - hi.astype(F32) - lo.astype(F32)).astype(BF16)
        out[...] = dot(take, hi) + dot(take, lo) + dot(take, low)


def merge_call(parts, merge_sets, dim, blocks, shift, piece=None):
    count = len(parts)
    size = parts[0].shape[0]
    skel = size - dim - 16
    rows = size if piece is None else (piece or skel)
    return pl.pallas_call(
        functools.partial(merge_kernel, dim=dim, blocks=blocks, shift=shift, piece=piece),
        in_specs=[pl.BlockSpec(memory_space=pltpu.VMEM)] * count
        + [pl.BlockSpec(memory_space=pltpu.HBM)],
        out_shape=jax.ShapeDtypeStruct((rows, LANES), F32),
        scratch_shapes=[
            pltpu.VMEM((count, size, LANES), F32),
            pltpu.VMEM(merge_sets.shape, jnp.int32),
            pltpu.SemaphoreType.DMA(()),
        ],
        compiler_params=pltpu.CompilerParams(vmem_limit_bytes=16 * 1024 * 1024),
        cost_estimate=pl.CostEstimate(
            flops=count * 16 * LANES**3,
            bytes_accessed=4 * count * size * LANES,
            transcendentals=2 * count * LANES**2,
        ),
        name="tree_merge",
    )(*parts, merge_sets)


def near_kernel(*refs, flips, row_counts, has_acc, sets, tasks, span, dim):
    refs = list(refs)

    def take(number):
        taken = refs[:number]
        del refs[:number]
        return taken

    lists, rows = take(len(flips)), [take(number) for number in row_counts]
    accs = [take(1)[0] if has else None for has in has_acc]
    buffers = [take(max(which) + 1) for _, which in sets]
    outs, (pair_list,) = take(len(flips)), refs
    blocks, leaf = rows[0][0].shape[:2]
    near = lists[0].shape[1]
    window = blocks * lax.axis_size("sub")
    sub = lax.axis_index("sub")

    def place(table):
        value = jnp.int32(table[0])
        for i in range(1, len(table)):
            value = jnp.where(sub == i, jnp.int32(table[i]), value)
        return value

    window_first = lax.axis_index("leaf") * window - blocks
    stride = blocks * near + 8
    found = [jnp.int32(0)] * len(tasks)
    for j, flip in enumerate(flips):
        mine = [t for t, (_, group) in enumerate(tasks) if group == j]
        firsts = [window_first + place(sets[tasks[t][0]][0]) for t in mine]
        target_first = lax.axis_index("leaf") * window + (sub ^ flip) * blocks

        def list_block(g, counts, j=j, mine=mine, firsts=firsts, target_first=target_first):
            for s in range(*span):
                source = lists[j][g, s]
                used = (source != target_first + g) if s else True
                after = []
                for t, first, count in zip(mine, firsts, counts):
                    local = source - first
                    pair_list[t * stride + count] = g * blocks + local
                    inside = (local >= 0) & (local < blocks) & used
                    after.append(count + jnp.where(inside, 1, 0))
                counts = tuple(after)
            return counts

        counts = lax.fori_loop(0, blocks, list_block, (jnp.int32(0),) * len(mine))
        for t, count in zip(mine, counts):
            found[t] = count
        outs[j][...] = jnp.zeros(outs[j].shape, F32) if accs[j] is None else accs[j][...]

    half = leaf // 2

    def add_all(buffer, targets, t, pairs):
        j = tasks[t][1]

        def add_pair(i):
            code = pair_list[t * stride + i]
            g = code // blocks
            local = code - g * blocks
            form = form_of(buffer.at[local], leaf, dim)
            probes = buffer[local, :leaf, :]
            total = None
            for c in range(0, leaf, half):
                weights = jnp.exp(dot(targets[g], form[:, c : c + half])).astype(BF16)
                term = dot(weights, probes[c : c + half])
                total = term if total is None else total + term
            return g, total

        def add_pairs(i, carry):
            for g, total in [add_pair(2 * i), add_pair(2 * i + 1)]:
                outs[j][g] += total
            return carry

        lax.fori_loop(0, pairs // 2, add_pairs, 0)

        @pl.when(pairs % 2 == 1)
        def _():
            g, total = add_pair(pairs - 1)
            outs[j][g] += total

    for t, (number, j) in enumerate(tasks):
        held = place(sets[number][1])
        edge = (sub == 0) | (sub == lax.axis_size("sub") - 1)
        for k, buffer in enumerate(buffers[number]):
            for r, targets in enumerate(rows[j]):
                pairs = found[t]
                if len(buffers[number]) > 1:
                    if len(rows[j]) > 1 and r != k:
                        continue
                    pairs = jnp.where(held == k, pairs, 0)
                elif len(rows[j]) > 1:
                    pairs = jnp.where(edge == (r == 0), pairs, 0)
                add_all(buffer, targets, t, pairs)


def near_call(groups, sources, tasks, dim, name, self_tiles=False):
    flips, lists, rows, accs = zip(*groups)
    rows = [r if isinstance(r, tuple) else (r,) for r in rows]
    blocks, leaf = rows[0][0].shape[:2]
    held = [acc for acc in accs if acc is not None]
    args = [*lists, *(r for pair in rows for r in pair), *held, *(b for _, _, buffers in sources for b in buffers)]
    smem = pl.BlockSpec(memory_space=pltpu.SMEM)
    vmem = pl.BlockSpec(memory_space=pltpu.VMEM)
    near = lists[0].shape[1]
    return pl.pallas_call(
        functools.partial(
            near_kernel,
            flips=flips,
            row_counts=tuple(len(pair) for pair in rows),
            has_acc=tuple(acc is not None for acc in accs),
            sets=tuple((bases, which) for bases, which, _ in sources),
            tasks=tasks,
            span=(0, 1) if self_tiles else (1, near),
            dim=dim,
        ),
        in_specs=[smem] * len(lists) + [vmem] * (len(args) - len(lists)),
        out_specs=[vmem] * len(groups),
        out_shape=[jax.ShapeDtypeStruct((blocks, leaf, LANES), F32)] * len(groups),
        scratch_shapes=[pltpu.SMEM((len(tasks) * (blocks * near + 8),), jnp.int32)],
        compiler_params=pltpu.CompilerParams(vmem_limit_bytes=NEAR_BYTES),
        cost_estimate=pl.CostEstimate(flops=1000, bytes_accessed=1000, transcendentals=0),
        name=name,
    )(*args)


def on_device(points, probes, order, near_lists, near_counts, leaf_sets, merge_sets):
    leaf_count = lax.axis_size("leaf")
    sub_count = lax.axis_size("sub")
    blocks, skel = leaf_sets.shape
    npts, dim = points.shape
    leaf = npts // blocks
    axes = ("leaf", "sub")

    def send(x, routes):
        pairs = []
        for place in range(leaf_count):
            for from_sub, step, to_sub in routes:
                if 0 <= place + step < leaf_count:
                    pairs.append((place * sub_count + from_sub, (place + step) * sub_count + to_sub))
        return lax.ppermute(x, axes, pairs)

    count = leaf_count * sub_count
    bits = count.bit_length() - 1
    sub_bits = sub_count.bit_length() - 1

    def exchange(x, shift, stage_bits):
        parts = [x]
        for d in range(1, 1 << stage_bits):
            parts.append(lax.ppermute(x, axes, [(i, i ^ (d << shift)) for i in range(count)]))
        return parts

    def tie(*values):
        return lax.optimization_barrier(values)

    b = blocks
    own_base = (b, 2 * b, 3 * b, 4 * b)
    early_base, late_base = (5 * b, 4 * b, b, 0), (3 * b, 0, 5 * b, 2 * b)
    single, by_edge = (0, 0, 0, 0), (0, 1, 1, 0)

    pack, rows = order_call(points.T, order.reshape(blocks, 1, leaf), probes, blocks)
    outer_across = send(pack, [(3, 0, 1), (0, 0, 2)])
    outer_next = send(pack, [(3, 1, 3), (0, -1, 0)])
    inward, outward = [(1, 0, 0), (2, 0, 3)], [(0, 0, 1), (3, 0, 2)]
    beside_pack = send(pack, inward)
    edge_rows = send(rows, inward)
    beside_lists = exchange(near_lists, 0, 1)[1]

    node = local_tree_call(pack, rows, leaf_sets, merge_sets, dim)
    node, beside_lists = tie(node, beside_lists)

    def level(parts, bit, piece=None):
        return merge_call(parts, merge_sets, dim, blocks, bit, piece)

    node = level(exchange(node, 0, 1), 0)
    own_pack, node = tie(pack, node)
    parts = exchange(node, 1, 1)
    own_set = (own_base, single, [own_pack])
    (own,) = near_call(
        [(0, near_lists, rows, None)], [own_set], ((0, 0),), dim, "near_own", self_tiles=True
    )

    *parts, outer_across, outer_next, beside_pack, edge_rows, late_rows, own = tie(
        *parts, outer_across, outer_next, beside_pack, edge_rows, rows, own
    )
    forwarded = send(outer_across, [(1, 1, 1), (2, -1, 2)])
    inner_across = send(beside_pack, [(0, 0, 3), (3, 0, 0)])
    beside_rows = (edge_rows, send(late_rows, outward))
    node = level(parts, 1)
    own_pack, node = tie(own_pack, node)
    parts = exchange(node, 2, 1)
    own_set = (own_base, single, [own_pack])
    early_set = (early_base, by_edge, [outer_next, outer_across])
    own, beside = near_call(
        [(0, near_lists, rows, own), (1, beside_lists, beside_rows, None)],
        [own_set, early_set], ((0, 0), (1, 0), (0, 1), (1, 1)), dim, "near_early",
    )

    *parts, inner_across, forwarded, beside = tie(*parts, inner_across, forwarded, beside)
    late_set = (late_base, by_edge, [inner_across, forwarded])
    (beside,) = near_call(
        [(1, beside_lists, beside_rows, beside)], [late_set], ((0, 0),), dim, "near_beside"
    )
    given = exchange(beside, 0, 1)[1]
    *parts, beside = tie(*parts, beside)
    shift, stage = 2, 1
    while shift + stage < bits:
        node = level(parts, shift)
        shift, stage = shift + stage, min(2, bits - shift - stage)
        parts = exchange(node, shift, stage)
    (own,) = near_call([(0, near_lists, rows, own)], [late_set], ((0, 0),), dim, "near_last")
    *parts, own = tie(*parts, own)
    node = level(parts, shift, skel // count)
    near = (own + given) * (leaf ** -0.5)
    if skel // count:
        root = node.reshape(-1)
    else:
        size = skel * LANES // count
        rank = lax.axis_index("leaf") * sub_count + lax.axis_index("sub")
        root = lax.dynamic_slice_in_dim(node.reshape(-1), rank * size, size, 0)
    return near.reshape(npts, LANES), root


def solution(mesh):
    in_specs = (
        P(("leaf", "sub"), None),
        P(("leaf", "sub"), None),
        P(("leaf", "sub")),
        P(("leaf", "sub"), None),
        P(("leaf", "sub")),
        P(("leaf", "sub"), None),
        P(),
    )
    out_specs = (P(("leaf", "sub"), None), P(("leaf", "sub")))
    return jax.shard_map(
        on_device, mesh=mesh, in_specs=in_specs, out_specs=out_specs, check_vma=False
    )
```

```python
import functools

import jax
import jax.numpy as jnp
from jax import lax
from jax.experimental import pallas as pl
from jax.experimental.pallas import tpu as pltpu
from jax.sharding import PartitionSpec as P

LANES = 128
PARTS = 3
VMEM_BYTES = 20 * 1024 * 1024
NEAR_BYTES = 24 * 1024 * 1024
F32 = jnp.float32
BF16 = jnp.bfloat16


def dot(a, b):
    return jnp.dot(a, b, preferred_element_type=F32)


def dot_t(a, b):
    return lax.dot_general(a, b, (((0,), (0,)), ((), ())), preferred_element_type=F32)


def split(x):
    hi = x.astype(BF16)
    return hi, (x - hi.astype(F32)).astype(BF16)


def square_rows(pts):
    x = pts.astype(F32)
    total = jnp.sum(x * x, axis=0, keepdims=True)
    hi = total.astype(BF16).astype(F32)
    mid = (total - hi).astype(BF16).astype(F32)
    low = total - hi - mid
    row = lax.broadcasted_iota(jnp.int32, (16, pts.shape[1]), 0)
    ones = jnp.where(row < 2 * PARTS, 1.0, 0.0)
    return jnp.where(row == 0, hi, jnp.where(row == 1, mid, jnp.where(row == 2, low, ones))).astype(BF16)


def form_map(dim, size):
    k = lax.broadcasted_iota(jnp.int32, (size, size), 0)
    j = lax.broadcasted_iota(jnp.int32, (size, size), 1)
    r = jnp.where((k == j) & (j < dim), 2.0 / dim, 0.0)
    r = jnp.where((j >= dim) & (j < dim + PARTS) & (k == j + PARTS), -1.0 / dim, r)
    r = jnp.where((j >= dim + PARTS) & (j < dim + 2 * PARTS) & (k == j - PARTS), -1.0 / dim, r)
    return r.astype(BF16)


def onehot_in(row, size):
    index = lax.broadcasted_iota(jnp.int32, (size, row.shape[1]), 0)
    return jnp.where(index == row, 1.0, 0.0).astype(BF16)


def column_of(row):
    return jnp.broadcast_to(row.astype(F32), (LANES, row.shape[1])).T


def onehot_out(column, size):
    lane = lax.broadcasted_iota(jnp.int32, column.shape, 1).astype(F32)
    return jnp.concatenate(
        [jnp.where(column == lane + float(i), 1.0, 0.0) for i in range(0, size, LANES)], axis=1
    )


def mix3(m, s):
    m_hi, m_lo = split(m)
    s_hi, s_lo = split(s)
    return dot(m_hi, s_hi) + (dot(m_hi, s_lo) + dot(m_lo, s_hi))


def order_kernel(points_t, order, probes, pack, rows):
    dim = points_t.shape[0]
    many, leaf = rows.shape[:2]
    held = dim + 16
    to_rows = form_map(dim, LANES)
    for b in range(many):
        picks = onehot_in(order[b], leaf)
        tree_t = dot(points_t[:, b * leaf : (b + 1) * leaf], picks).astype(BF16)
        pack[b, :leaf, :] = probes[b * leaf : (b + 1) * leaf, :]
        form = jnp.concatenate([tree_t, square_rows(tree_t)], axis=0)
        for i in range(leaf // LANES):
            pack[b, leaf + i * dim : leaf + (i + 1) * dim, :] = tree_t[:, i * LANES : (i + 1) * LANES]
        form = jnp.concatenate([form, jnp.zeros((LANES - held, leaf), BF16)], axis=0)
        rows[b] = dot_t(form, to_rows).astype(BF16)


def order_call(points_t, order, probes, blocks):
    dim, npts = points_t.shape
    leaf = npts // blocks
    packed = leaf + leaf // LANES * dim
    many = 4 if blocks % 4 == 0 else 1
    return pl.pallas_call(
        order_kernel,
        grid=(blocks // many,),
        in_specs=[
            pl.BlockSpec((dim, many * leaf), lambda b: (0, b)),
            pl.BlockSpec((many, 1, leaf), lambda b: (b, 0, 0)),
            pl.BlockSpec((many * leaf, LANES), lambda b: (b, 0)),
        ],
        out_specs=[
            pl.BlockSpec((many, packed, LANES), lambda b: (b, 0, 0)),
            pl.BlockSpec((many, leaf, LANES), lambda b: (b, 0, 0)),
        ],
        out_shape=[
            jax.ShapeDtypeStruct((blocks, packed, LANES), BF16),
            jax.ShapeDtypeStruct((blocks, leaf, LANES), BF16),
        ],
        compiler_params=pltpu.CompilerParams(vmem_limit_bytes=VMEM_BYTES),
        cost_estimate=pl.CostEstimate(
            flops=blocks * 2 * leaf * leaf * dim, bytes_accessed=10 * npts * LANES, transcendentals=0
        ),
        name="tree_order",
    )(points_t, order, probes)


def form_of(pack_block, leaf, dim):
    columns = []
    for i in range(leaf // LANES):
        pts = pack_block[leaf + i * dim : leaf + (i + 1) * dim, :]
        columns.append(jnp.concatenate([pts, square_rows(pts)], axis=0))
    form = jnp.concatenate(columns, axis=1)
    return jnp.concatenate([form, jnp.zeros((LANES - dim - 16, leaf), BF16)], axis=0)


def condense(form, a_rows, chosen):
    size = form.shape[1]
    picks_out = onehot_out(column_of(chosen), size)
    new_rows = dot(picks_out.astype(BF16), a_rows).astype(BF16)
    new_form = dot(form, onehot_in(chosen, size)).astype(BF16)
    weights = jnp.exp(dot(new_rows, form))
    mixing = picks_out + weights / jnp.sum(weights, axis=1, keepdims=True)
    return new_form, new_rows, mixing


def local_tree_kernel(pack, rows, leaf_sets_in, merge_sets_in, out, leaf_sets, merge_sets, sems, *, dim):
    blocks, leaf = rows.shape[:2]
    leaf_copy = pltpu.make_async_copy(leaf_sets_in, leaf_sets, sems.at[0])
    merge_copy = pltpu.make_async_copy(merge_sets_in, merge_sets, sems.at[1])
    leaf_copy.start()
    merge_copy.start()
    leaf_copy.wait()
    first_block = (lax.axis_index("leaf") * lax.axis_size("sub") + lax.axis_index("sub")) * blocks

    nodes = []
    for b in range(blocks):
        form = form_of(pack.at[b], leaf, dim)
        new_form, new_rows, mixing = condense(form, rows[b], leaf_sets[b : b + 1, :])
        m_hi, m_lo = split(mixing)
        probes = pack[b, :leaf, :]
        nodes.append((new_form, new_rows, dot(m_hi, probes) + dot(m_lo, probes)))
    span = 1
    merge_copy.wait()
    while len(nodes) > 1:
        merged = []
        for k in range(len(nodes) // 2):
            left, right = nodes[2 * k], nodes[2 * k + 1]
            chosen = merge_sets[pl.ds(first_block + (2 * k + 1) * span - 1, 1), :]
            new_form, new_rows, mixing = condense(
                jnp.concatenate([left[0], right[0]], axis=1),
                jnp.concatenate([left[1], right[1]], axis=0),
                chosen,
            )
            samples = mix3(mixing, jnp.concatenate([left[2], right[2]], axis=0))
            merged.append((new_form, new_rows, samples))
        nodes = merged
        span *= 2
    held = dim + 16
    out[:held, :] = nodes[0][0][:held, :].astype(F32)
    out[held:, :] = nodes[0][2]


def local_tree_call(pack, rows, leaf_sets, merge_sets, dim):
    blocks, leaf = rows.shape[:2]
    skel = leaf_sets.shape[1]
    return pl.pallas_call(
        functools.partial(local_tree_kernel, dim=dim),
        in_specs=[pl.BlockSpec(memory_space=pltpu.VMEM)] * 2
        + [pl.BlockSpec(memory_space=pltpu.HBM)] * 2,
        out_shape=jax.ShapeDtypeStruct((dim + 16 + skel, LANES), F32),
        scratch_shapes=[
            pltpu.VMEM(leaf_sets.shape, jnp.int32),
            pltpu.VMEM(merge_sets.shape, jnp.int32),
            pltpu.SemaphoreType.DMA((2,)),
        ],
        compiler_params=pltpu.CompilerParams(vmem_limit_bytes=VMEM_BYTES),
        cost_estimate=pl.CostEstimate(
            flops=blocks * 8 * skel * leaf * LANES,
            bytes_accessed=6 * blocks * leaf * LANES,
            transcendentals=blocks * skel * leaf,
        ),
        name="local_tree",
    )(pack, rows, leaf_sets, merge_sets)


def merge_kernel(*refs, dim, blocks, shift, piece):
    merge_sets_in, out, group, merge_sets, sem = refs[-5:]
    parts = refs[:-5]
    count, size = group.shape[:2]
    copy = pltpu.make_async_copy(merge_sets_in, merge_sets, sem)
    copy.start()
    held = dim + 16
    skel = size - held
    rank = lax.axis_index("leaf") * lax.axis_size("sub") + lax.axis_index("sub")
    unit = lax.shift_right_logical(rank, shift)
    place = unit & (count - 1)
    first = unit - place
    span = blocks << shift
    for d, part in enumerate(parts):
        group[place ^ d] = part[...]
    to_rows = form_map(dim, LANES)
    forms = [group[i, :held, :].astype(BF16) for i in range(count)]
    samples = [group[i, held:, :] for i in range(count)]
    copy.wait()
    while len(forms) > 1:
        first = first // 2
        new_forms, new_samples = [], []
        for k in range(len(forms) // 2):
            chosen = merge_sets[pl.ds((2 * (first + k) + 1) * span - 1, 1), :]
            form = jnp.concatenate(forms[2 * k : 2 * k + 2], axis=1)
            form = jnp.concatenate([form, jnp.zeros((LANES - held, 2 * skel), BF16)], axis=0)
            new_form = dot(form, onehot_in(chosen, 2 * skel)).astype(BF16)
            new_rows = dot_t(new_form, to_rows).astype(BF16)
            weights = jnp.exp(dot(new_rows, form))
            picks = onehot_out(column_of(chosen), 2 * skel)
            mixing = picks + weights / jnp.sum(weights, axis=1, keepdims=True)
            new_forms.append(new_form[:held])
            new_samples.append(mix3(mixing, jnp.concatenate(samples[2 * k : 2 * k + 2], axis=0)))
        forms, samples = new_forms, new_samples
        span *= 2
    if piece is None:
        out[:held, :] = forms[0].astype(F32)
        out[held:, :] = samples[0]
    elif piece == 0:
        out[...] = samples[0]
    else:
        column = lax.broadcasted_iota(jnp.int32, (piece, skel), 1)
        row = lax.broadcasted_iota(jnp.int32, (piece, skel), 0) + rank * piece
        take = jnp.where(column == row, 1.0, 0.0).astype(BF16)
        hi, lo = split(samples[0])
        low = (samples[0] - hi.astype(F32) - lo.astype(F32)).astype(BF16)
        out[...] = dot(take, hi) + dot(take, lo) + dot(take, low)


def merge_call(parts, merge_sets, dim, blocks, shift, piece=None):
    count = len(parts)
    size = parts[0].shape[0]
    skel = size - dim - 16
    rows = size if piece is None else (piece or skel)
    return pl.pallas_call(
        functools.partial(merge_kernel, dim=dim, blocks=blocks, shift=shift, piece=piece),
        in_specs=[pl.BlockSpec(memory_space=pltpu.VMEM)] * count
        + [pl.BlockSpec(memory_space=pltpu.HBM)],
        out_shape=jax.ShapeDtypeStruct((rows, LANES), F32),
        scratch_shapes=[
            pltpu.VMEM((count, size, LANES), F32),
            pltpu.VMEM(merge_sets.shape, jnp.int32),
            pltpu.SemaphoreType.DMA(()),
        ],
        compiler_params=pltpu.CompilerParams(vmem_limit_bytes=16 * 1024 * 1024),
        cost_estimate=pl.CostEstimate(
            flops=count * 16 * LANES**3,
            bytes_accessed=4 * count * size * LANES,
            transcendentals=2 * count * LANES**2,
        ),
        name="tree_merge",
    )(*parts, merge_sets)


def near_kernel(*refs, flips, row_counts, has_acc, sets, tasks, span, dim):
    refs = list(refs)

    def take(number):
        taken = refs[:number]
        del refs[:number]
        return taken

    lists, rows = take(len(flips)), [take(number) for number in row_counts]
    accs = [take(1)[0] if has else None for has in has_acc]
    buffers = [take(max(which) + 1) for _, which in sets]
    outs, (pair_list,) = take(len(flips)), refs
    blocks, leaf = rows[0][0].shape[:2]
    near = lists[0].shape[1]
    window = blocks * lax.axis_size("sub")
    sub = lax.axis_index("sub")

    def place(table):
        value = jnp.int32(table[0])
        for i in range(1, len(table)):
            value = jnp.where(sub == i, jnp.int32(table[i]), value)
        return value

    window_first = lax.axis_index("leaf") * window - blocks
    stride = blocks * near + 8
    found = [jnp.int32(0)] * len(tasks)
    for j, flip in enumerate(flips):
        mine = [t for t, (_, group) in enumerate(tasks) if group == j]
        firsts = [window_first + place(sets[tasks[t][0]][0]) for t in mine]
        target_first = lax.axis_index("leaf") * window + (sub ^ flip) * blocks

        def list_block(g, counts, j=j, mine=mine, firsts=firsts, target_first=target_first):
            for s in range(*span):
                source = lists[j][g, s]
                used = (source != target_first + g) if s else True
                after = []
                for t, first, count in zip(mine, firsts, counts):
                    local = source - first
                    pair_list[t * stride + count] = g * blocks + local
                    inside = (local >= 0) & (local < blocks) & used
                    after.append(count + jnp.where(inside, 1, 0))
                counts = tuple(after)
            return counts

        counts = lax.fori_loop(0, blocks, list_block, (jnp.int32(0),) * len(mine))
        for t, count in zip(mine, counts):
            found[t] = count
        outs[j][...] = jnp.zeros(outs[j].shape, F32) if accs[j] is None else accs[j][...]

    half = leaf // 2

    def add_all(buffer, targets, t, pairs):
        j = tasks[t][1]

        def add_pair(i):
            code = pair_list[t * stride + i]
            g = code // blocks
            local = code - g * blocks
            form = form_of(buffer.at[local], leaf, dim)
            probes = buffer[local, :leaf, :]
            total = None
            for c in range(0, leaf, half):
                weights = jnp.exp(dot(targets[g], form[:, c : c + half])).astype(BF16)
                term = dot(weights, probes[c : c + half])
                total = term if total is None else total + term
            return g, total

        def add_pairs(i, carry):
            for g, total in [add_pair(2 * i), add_pair(2 * i + 1)]:
                outs[j][g] += total
            return carry

        lax.fori_loop(0, pairs // 2, add_pairs, 0)

        @pl.when(pairs % 2 == 1)
        def _():
            g, total = add_pair(pairs - 1)
            outs[j][g] += total

    for t, (number, j) in enumerate(tasks):
        held = place(sets[number][1])
        edge = (sub == 0) | (sub == lax.axis_size("sub") - 1)
        for k, buffer in enumerate(buffers[number]):
            for r, targets in enumerate(rows[j]):
                pairs = found[t]
                if len(buffers[number]) > 1:
                    if len(rows[j]) > 1 and r != k:
                        continue
                    pairs = jnp.where(held == k, pairs, 0)
                elif len(rows[j]) > 1:
                    pairs = jnp.where(edge == (r == 0), pairs, 0)
                add_all(buffer, targets, t, pairs)


def near_call(groups, sources, tasks, dim, name):
    flips, lists, rows, accs = zip(*groups)
    rows = [r if isinstance(r, tuple) else (r,) for r in rows]
    blocks, leaf = rows[0][0].shape[:2]
    held = [acc for acc in accs if acc is not None]
    args = [*lists, *(r for pair in rows for r in pair), *held, *(b for _, _, buffers in sources for b in buffers)]
    smem = pl.BlockSpec(memory_space=pltpu.SMEM)
    vmem = pl.BlockSpec(memory_space=pltpu.VMEM)
    near = lists[0].shape[1]
    return pl.pallas_call(
        functools.partial(
            near_kernel,
            flips=flips,
            row_counts=tuple(len(pair) for pair in rows),
            has_acc=tuple(acc is not None for acc in accs),
            sets=tuple((bases, which) for bases, which, _ in sources),
            tasks=tasks,
            span=(0, near),
            dim=dim,
        ),
        in_specs=[smem] * len(lists) + [vmem] * (len(args) - len(lists)),
        out_specs=[vmem] * len(groups),
        out_shape=[jax.ShapeDtypeStruct((blocks, leaf, LANES), F32)] * len(groups),
        scratch_shapes=[pltpu.SMEM((len(tasks) * (blocks * near + 8),), jnp.int32)],
        compiler_params=pltpu.CompilerParams(vmem_limit_bytes=NEAR_BYTES),
        cost_estimate=pl.CostEstimate(flops=1000, bytes_accessed=1000, transcendentals=0),
        name=name,
    )(*args)


def on_device(points, probes, order, near_lists, near_counts, leaf_sets, merge_sets):
    leaf_count = lax.axis_size("leaf")
    sub_count = lax.axis_size("sub")
    blocks, skel = leaf_sets.shape
    npts, dim = points.shape
    leaf = npts // blocks
    axes = ("leaf", "sub")

    def send(x, routes):
        pairs = []
        for place in range(leaf_count):
            for from_sub, step, to_sub in routes:
                if 0 <= place + step < leaf_count:
                    pairs.append((place * sub_count + from_sub, (place + step) * sub_count + to_sub))
        return lax.ppermute(x, axes, pairs)

    count = leaf_count * sub_count
    bits = count.bit_length() - 1
    sub_bits = sub_count.bit_length() - 1

    def exchange(x, shift, stage_bits):
        parts = [x]
        for d in range(1, 1 << stage_bits):
            parts.append(lax.ppermute(x, axes, [(i, i ^ (d << shift)) for i in range(count)]))
        return parts

    def tie(*values):
        return lax.optimization_barrier(values)

    b = blocks
    own_base = (b, 2 * b, 3 * b, 4 * b)
    early_base, late_base = (5 * b, 4 * b, b, 0), (3 * b, 0, 5 * b, 2 * b)
    single, by_edge = (0, 0, 0, 0), (0, 1, 1, 0)

    pack, rows = order_call(points.T, order.reshape(blocks, 1, leaf), probes, blocks)
    outer_across = send(pack, [(3, 0, 1), (0, 0, 2)])
    outer_next = send(pack, [(3, 1, 3), (0, -1, 0)])
    beside_pack = send(pack, [(1, 0, 0), (2, 0, 3)])

    node = local_tree_call(pack, rows, leaf_sets, merge_sets, dim)

    def level(parts, bit, piece=None):
        return merge_call(parts, merge_sets, dim, blocks, bit, piece)

    node = level(exchange(node, 0, 1), 0)
    own_pack, node = tie(pack, node)
    parts = exchange(node, 1, 1)
    *parts, outer_across, outer_next, beside_pack, late_rows, late_lists = tie(
        *parts, outer_across, outer_next, beside_pack, rows, near_lists
    )
    forwarded = send(outer_across, [(1, 1, 1), (2, -1, 2)])
    inner_across = send(beside_pack, [(0, 0, 3), (3, 0, 0)])
    beside_rows = exchange(late_rows, 0, 1)[1]
    beside_lists = exchange(late_lists, 0, 1)[1]
    node = level(parts, 1)
    own_pack, node = tie(own_pack, node)
    parts = exchange(node, 2, 1)
    own_set = (own_base, single, [own_pack])
    early_set = (early_base, by_edge, [outer_next, outer_across])
    (own,) = near_call(
        [(0, near_lists, rows, None)], [own_set, early_set], ((0, 0), (1, 0)), dim, "near_own"
    )
    beside_rows, beside_lists, own = tie(beside_rows, beside_lists, own)
    (beside,) = near_call(
        [(1, beside_lists, beside_rows, None)],
        [own_set, early_set], ((0, 0), (1, 0)), dim, "near_early",
    )

    *parts, inner_across, forwarded, beside = tie(*parts, inner_across, forwarded, beside)
    late_set = (late_base, by_edge, [inner_across, forwarded])
    (beside,) = near_call(
        [(1, beside_lists, beside_rows, beside)], [late_set], ((0, 0),), dim, "near_beside"
    )
    given = exchange(beside, 0, 1)[1]
    *parts, beside = tie(*parts, beside)
    shift, stage = 2, 1
    while shift + stage < bits:
        node = level(parts, shift)
        shift, stage = shift + stage, min(2, bits - shift - stage)
        parts = exchange(node, shift, stage)
    (own,) = near_call([(0, near_lists, rows, own)], [late_set], ((0, 0),), dim, "near_last")
    *parts, own = tie(*parts, own)
    node = level(parts, shift, skel // count)
    near = (own + given) * (leaf ** -0.5)
    if skel // count:
        root = node.reshape(-1)
    else:
        size = skel * LANES // count
        rank = lax.axis_index("leaf") * sub_count + lax.axis_index("sub")
        root = lax.dynamic_slice_in_dim(node.reshape(-1), rank * size, size, 0)
    return near.reshape(npts, LANES), root


def solution(mesh):
    in_specs = (
        P(("leaf", "sub"), None),
        P(("leaf", "sub"), None),
        P(("leaf", "sub")),
        P(("leaf", "sub"), None),
        P(("leaf", "sub")),
        P(("leaf", "sub"), None),
        P(),
    )
    out_specs = (P(("leaf", "sub"), None), P(("leaf", "sub")))
    return jax.shard_map(
        on_device, mesh=mesh, in_specs=in_specs, out_specs=out_specs, check_vma=False
    )
```

```python
import functools

import jax
import jax.numpy as jnp
from jax import lax
from jax.experimental import pallas as pl
from jax.experimental.pallas import tpu as pltpu
from jax.sharding import PartitionSpec as P

LANES = 128
PARTS = 3
VMEM_BYTES = 20 * 1024 * 1024
NEAR_BYTES = 24 * 1024 * 1024
F32 = jnp.float32
BF16 = jnp.bfloat16


def dot(a, b):
    return jnp.dot(a, b, preferred_element_type=F32)


def dot_t(a, b):
    return lax.dot_general(a, b, (((0,), (0,)), ((), ())), preferred_element_type=F32)


def split(x):
    hi = x.astype(BF16)
    return hi, (x - hi.astype(F32)).astype(BF16)


def square_rows(pts):
    x = pts.astype(F32)
    total = jnp.sum(x * x, axis=0, keepdims=True)
    hi = total.astype(BF16).astype(F32)
    mid = (total - hi).astype(BF16).astype(F32)
    low = total - hi - mid
    row = lax.broadcasted_iota(jnp.int32, (16, pts.shape[1]), 0)
    ones = jnp.where(row < 2 * PARTS, 1.0, 0.0)
    return jnp.where(row == 0, hi, jnp.where(row == 1, mid, jnp.where(row == 2, low, ones))).astype(BF16)


def form_map(dim, size):
    k = lax.broadcasted_iota(jnp.int32, (size, size), 0)
    j = lax.broadcasted_iota(jnp.int32, (size, size), 1)
    r = jnp.where((k == j) & (j < dim), 2.0 / dim, 0.0)
    r = jnp.where((j >= dim) & (j < dim + PARTS) & (k == j + PARTS), -1.0 / dim, r)
    r = jnp.where((j >= dim + PARTS) & (j < dim + 2 * PARTS) & (k == j - PARTS), -1.0 / dim, r)
    return r.astype(BF16)


def onehot_in(row, size):
    index = lax.broadcasted_iota(jnp.int32, (size, row.shape[1]), 0)
    return jnp.where(index == row, 1.0, 0.0).astype(BF16)


def column_of(row):
    return jnp.broadcast_to(row.astype(F32), (LANES, row.shape[1])).T


def onehot_out(column, size):
    lane = lax.broadcasted_iota(jnp.int32, column.shape, 1).astype(F32)
    return jnp.concatenate(
        [jnp.where(column == lane + float(i), 1.0, 0.0) for i in range(0, size, LANES)], axis=1
    )


def mix3(m, s):
    m_hi, m_lo = split(m)
    s_hi, s_lo = split(s)
    return dot(m_hi, s_hi) + (dot(m_hi, s_lo) + dot(m_lo, s_hi))


def order_kernel(points_t, order, probes, pack, rows):
    dim = points_t.shape[0]
    many, leaf = rows.shape[:2]
    held = dim + 16
    to_rows = form_map(dim, LANES)
    for b in range(many):
        picks = onehot_in(order[b], leaf)
        tree_t = dot(points_t[:, b * leaf : (b + 1) * leaf], picks).astype(BF16)
        pack[b, :leaf, :] = probes[b * leaf : (b + 1) * leaf, :]
        form = jnp.concatenate([tree_t, square_rows(tree_t)], axis=0)
        for i in range(leaf // LANES):
            pack[b, leaf + i * dim : leaf + (i + 1) * dim, :] = tree_t[:, i * LANES : (i + 1) * LANES]
        form = jnp.concatenate([form, jnp.zeros((LANES - held, leaf), BF16)], axis=0)
        rows[b] = dot_t(form, to_rows).astype(BF16)


def order_call(points_t, order, probes, blocks):
    dim, npts = points_t.shape
    leaf = npts // blocks
    packed = leaf + leaf // LANES * dim
    many = 4 if blocks % 4 == 0 else 1
    return pl.pallas_call(
        order_kernel,
        grid=(blocks // many,),
        in_specs=[
            pl.BlockSpec((dim, many * leaf), lambda b: (0, b)),
            pl.BlockSpec((many, 1, leaf), lambda b: (b, 0, 0)),
            pl.BlockSpec((many * leaf, LANES), lambda b: (b, 0)),
        ],
        out_specs=[
            pl.BlockSpec((many, packed, LANES), lambda b: (b, 0, 0)),
            pl.BlockSpec((many, leaf, LANES), lambda b: (b, 0, 0)),
        ],
        out_shape=[
            jax.ShapeDtypeStruct((blocks, packed, LANES), BF16),
            jax.ShapeDtypeStruct((blocks, leaf, LANES), BF16),
        ],
        compiler_params=pltpu.CompilerParams(vmem_limit_bytes=VMEM_BYTES),
        cost_estimate=pl.CostEstimate(
            flops=blocks * 2 * leaf * leaf * dim, bytes_accessed=10 * npts * LANES, transcendentals=0
        ),
        name="tree_order",
    )(points_t, order, probes)


def form_of(pack_block, leaf, dim):
    columns = []
    for i in range(leaf // LANES):
        pts = pack_block[leaf + i * dim : leaf + (i + 1) * dim, :]
        columns.append(jnp.concatenate([pts, square_rows(pts)], axis=0))
    form = jnp.concatenate(columns, axis=1)
    return jnp.concatenate([form, jnp.zeros((LANES - dim - 16, leaf), BF16)], axis=0)


def condense(form, a_rows, chosen):
    size = form.shape[1]
    picks_out = onehot_out(column_of(chosen), size)
    new_rows = dot(picks_out.astype(BF16), a_rows).astype(BF16)
    new_form = dot(form, onehot_in(chosen, size)).astype(BF16)
    weights = jnp.exp(dot(new_rows, form))
    mixing = picks_out + weights / jnp.sum(weights, axis=1, keepdims=True)
    return new_form, new_rows, mixing


def local_tree_kernel(pack, rows, leaf_sets_in, merge_sets_in, out, leaf_sets, merge_sets, sems, *, dim):
    blocks, leaf = rows.shape[:2]
    leaf_copy = pltpu.make_async_copy(leaf_sets_in, leaf_sets, sems.at[0])
    merge_copy = pltpu.make_async_copy(merge_sets_in, merge_sets, sems.at[1])
    leaf_copy.start()
    merge_copy.start()
    leaf_copy.wait()
    first_block = (lax.axis_index("leaf") * lax.axis_size("sub") + lax.axis_index("sub")) * blocks

    nodes = []
    for b in range(blocks):
        form = form_of(pack.at[b], leaf, dim)
        new_form, new_rows, mixing = condense(form, rows[b], leaf_sets[b : b + 1, :])
        m_hi, m_lo = split(mixing)
        probes = pack[b, :leaf, :]
        nodes.append((new_form, new_rows, dot(m_hi, probes) + dot(m_lo, probes)))
    span = 1
    merge_copy.wait()
    while len(nodes) > 1:
        merged = []
        for k in range(len(nodes) // 2):
            left, right = nodes[2 * k], nodes[2 * k + 1]
            chosen = merge_sets[pl.ds(first_block + (2 * k + 1) * span - 1, 1), :]
            new_form, new_rows, mixing = condense(
                jnp.concatenate([left[0], right[0]], axis=1),
                jnp.concatenate([left[1], right[1]], axis=0),
                chosen,
            )
            samples = mix3(mixing, jnp.concatenate([left[2], right[2]], axis=0))
            merged.append((new_form, new_rows, samples))
        nodes = merged
        span *= 2
    held = dim + 16
    out[:held, :] = nodes[0][0][:held, :].astype(F32)
    out[held:, :] = nodes[0][2]


def local_tree_call(pack, rows, leaf_sets, merge_sets, dim):
    blocks, leaf = rows.shape[:2]
    skel = leaf_sets.shape[1]
    return pl.pallas_call(
        functools.partial(local_tree_kernel, dim=dim),
        in_specs=[pl.BlockSpec(memory_space=pltpu.VMEM)] * 2
        + [pl.BlockSpec(memory_space=pltpu.HBM)] * 2,
        out_shape=jax.ShapeDtypeStruct((dim + 16 + skel, LANES), F32),
        scratch_shapes=[
            pltpu.VMEM(leaf_sets.shape, jnp.int32),
            pltpu.VMEM(merge_sets.shape, jnp.int32),
            pltpu.SemaphoreType.DMA((2,)),
        ],
        compiler_params=pltpu.CompilerParams(vmem_limit_bytes=VMEM_BYTES),
        cost_estimate=pl.CostEstimate(
            flops=blocks * 8 * skel * leaf * LANES,
            bytes_accessed=6 * blocks * leaf * LANES,
            transcendentals=blocks * skel * leaf,
        ),
        name="local_tree",
    )(pack, rows, leaf_sets, merge_sets)


def merge_kernel(*refs, dim, blocks, shift, piece):
    merge_sets_in, out, group, merge_sets, sem = refs[-5:]
    parts = refs[:-5]
    count, size = group.shape[:2]
    copy = pltpu.make_async_copy(merge_sets_in, merge_sets, sem)
    copy.start()
    held = dim + 16
    skel = size - held
    rank = lax.axis_index("leaf") * lax.axis_size("sub") + lax.axis_index("sub")
    unit = lax.shift_right_logical(rank, shift)
    place = unit & (count - 1)
    first = unit - place
    span = blocks << shift
    for d, part in enumerate(parts):
        group[place ^ d] = part[...]
    to_rows = form_map(dim, LANES)
    forms = [group[i, :held, :].astype(BF16) for i in range(count)]
    samples = [group[i, held:, :] for i in range(count)]
    copy.wait()
    while len(forms) > 1:
        first = first // 2
        new_forms, new_samples = [], []
        for k in range(len(forms) // 2):
            chosen = merge_sets[pl.ds((2 * (first + k) + 1) * span - 1, 1), :]
            form = jnp.concatenate(forms[2 * k : 2 * k + 2], axis=1)
            form = jnp.concatenate([form, jnp.zeros((LANES - held, 2 * skel), BF16)], axis=0)
            new_form = dot(form, onehot_in(chosen, 2 * skel)).astype(BF16)
            new_rows = dot_t(new_form, to_rows).astype(BF16)
            weights = jnp.exp(dot(new_rows, form))
            picks = onehot_out(column_of(chosen), 2 * skel)
            mixing = picks + weights / jnp.sum(weights, axis=1, keepdims=True)
            new_forms.append(new_form[:held])
            new_samples.append(mix3(mixing, jnp.concatenate(samples[2 * k : 2 * k + 2], axis=0)))
        forms, samples = new_forms, new_samples
        span *= 2
    if piece is None:
        out[:held, :] = forms[0].astype(F32)
        out[held:, :] = samples[0]
    elif piece == 0:
        out[...] = samples[0]
    else:
        column = lax.broadcasted_iota(jnp.int32, (piece, skel), 1)
        row = lax.broadcasted_iota(jnp.int32, (piece, skel), 0) + rank * piece
        take = jnp.where(column == row, 1.0, 0.0).astype(BF16)
        hi, lo = split(samples[0])
        low = (samples[0] - hi.astype(F32) - lo.astype(F32)).astype(BF16)
        out[...] = dot(take, hi) + dot(take, lo) + dot(take, low)


def merge_call(parts, merge_sets, dim, blocks, shift, piece=None):
    count = len(parts)
    size = parts[0].shape[0]
    skel = size - dim - 16
    rows = size if piece is None else (piece or skel)
    return pl.pallas_call(
        functools.partial(merge_kernel, dim=dim, blocks=blocks, shift=shift, piece=piece),
        in_specs=[pl.BlockSpec(memory_space=pltpu.VMEM)] * count
        + [pl.BlockSpec(memory_space=pltpu.HBM)],
        out_shape=jax.ShapeDtypeStruct((rows, LANES), F32),
        scratch_shapes=[
            pltpu.VMEM((count, size, LANES), F32),
            pltpu.VMEM(merge_sets.shape, jnp.int32),
            pltpu.SemaphoreType.DMA(()),
        ],
        compiler_params=pltpu.CompilerParams(vmem_limit_bytes=16 * 1024 * 1024),
        cost_estimate=pl.CostEstimate(
            flops=count * 16 * LANES**3,
            bytes_accessed=4 * count * size * LANES,
            transcendentals=2 * count * LANES**2,
        ),
        name="tree_merge",
    )(*parts, merge_sets)


def near_kernel(*refs, flips, row_counts, has_acc, sets, tasks, span, dim):
    refs = list(refs)

    def take(number):
        taken = refs[:number]
        del refs[:number]
        return taken

    lists, rows = take(len(flips)), [take(number) for number in row_counts]
    accs = [take(1)[0] if has else None for has in has_acc]
    buffers = [take(max(which) + 1) for _, which in sets]
    outs, (pair_list,) = take(len(flips)), refs
    blocks, leaf = rows[0][0].shape[:2]
    near = lists[0].shape[1]
    window = blocks * lax.axis_size("sub")
    sub = lax.axis_index("sub")

    def place(table):
        value = jnp.int32(table[0])
        for i in range(1, len(table)):
            value = jnp.where(sub == i, jnp.int32(table[i]), value)
        return value

    window_first = lax.axis_index("leaf") * window - blocks
    stride = blocks * near + 8
    found = [jnp.int32(0)] * len(tasks)
    for j, flip in enumerate(flips):
        mine = [t for t, (_, group) in enumerate(tasks) if group == j]
        firsts = [window_first + place(sets[tasks[t][0]][0]) for t in mine]
        target_first = lax.axis_index("leaf") * window + (sub ^ flip) * blocks

        def list_block(g, counts, j=j, mine=mine, firsts=firsts, target_first=target_first):
            for s in range(*span):
                source = lists[j][g, s]
                used = (source != target_first + g) if s else True
                after = []
                for t, first, count in zip(mine, firsts, counts):
                    local = source - first
                    pair_list[t * stride + count] = g * blocks + local
                    inside = (local >= 0) & (local < blocks) & used
                    after.append(count + jnp.where(inside, 1, 0))
                counts = tuple(after)
            return counts

        counts = lax.fori_loop(0, blocks, list_block, (jnp.int32(0),) * len(mine))
        for t, count in zip(mine, counts):
            found[t] = count
        outs[j][...] = jnp.zeros(outs[j].shape, F32) if accs[j] is None else accs[j][...]

    half = leaf // 2

    def add_all(buffer, targets, t, pairs):
        j = tasks[t][1]

        def add_pair(i):
            code = pair_list[t * stride + i]
            g = code // blocks
            local = code - g * blocks
            form = form_of(buffer.at[local], leaf, dim)
            probes = buffer[local, :leaf, :]
            total = None
            for c in range(0, leaf, half):
                weights = jnp.exp(dot(targets[g], form[:, c : c + half])).astype(BF16)
                term = dot(weights, probes[c : c + half])
                total = term if total is None else total + term
            return g, total

        def add_pairs(i, carry):
            for g, total in [add_pair(2 * i), add_pair(2 * i + 1)]:
                outs[j][g] += total
            return carry

        lax.fori_loop(0, pairs // 2, add_pairs, 0)

        @pl.when(pairs % 2 == 1)
        def _():
            g, total = add_pair(pairs - 1)
            outs[j][g] += total

    for t, (number, j) in enumerate(tasks):
        held = place(sets[number][1])
        edge = (sub == 0) | (sub == lax.axis_size("sub") - 1)
        for k, buffer in enumerate(buffers[number]):
            for r, targets in enumerate(rows[j]):
                pairs = found[t]
                if len(buffers[number]) > 1:
                    if len(rows[j]) > 1 and r != k:
                        continue
                    pairs = jnp.where(held == k, pairs, 0)
                elif len(rows[j]) > 1:
                    pairs = jnp.where(edge == (r == 0), pairs, 0)
                add_all(buffer, targets, t, pairs)


def near_call(groups, sources, tasks, dim, name):
    flips, lists, rows, accs = zip(*groups)
    rows = [r if isinstance(r, tuple) else (r,) for r in rows]
    blocks, leaf = rows[0][0].shape[:2]
    held = [acc for acc in accs if acc is not None]
    args = [*lists, *(r for pair in rows for r in pair), *held, *(b for _, _, buffers in sources for b in buffers)]
    smem = pl.BlockSpec(memory_space=pltpu.SMEM)
    vmem = pl.BlockSpec(memory_space=pltpu.VMEM)
    near = lists[0].shape[1]
    return pl.pallas_call(
        functools.partial(
            near_kernel,
            flips=flips,
            row_counts=tuple(len(pair) for pair in rows),
            has_acc=tuple(acc is not None for acc in accs),
            sets=tuple((bases, which) for bases, which, _ in sources),
            tasks=tasks,
            span=(0, near),
            dim=dim,
        ),
        in_specs=[smem] * len(lists) + [vmem] * (len(args) - len(lists)),
        out_specs=[vmem] * len(groups),
        out_shape=[jax.ShapeDtypeStruct((blocks, leaf, LANES), F32)] * len(groups),
        scratch_shapes=[pltpu.SMEM((len(tasks) * (blocks * near + 8),), jnp.int32)],
        compiler_params=pltpu.CompilerParams(vmem_limit_bytes=NEAR_BYTES),
        cost_estimate=pl.CostEstimate(flops=1000, bytes_accessed=1000, transcendentals=0),
        name=name,
    )(*args)


def on_device(points, probes, order, near_lists, near_counts, leaf_sets, merge_sets):
    leaf_count = lax.axis_size("leaf")
    sub_count = lax.axis_size("sub")
    blocks, skel = leaf_sets.shape
    npts, dim = points.shape
    leaf = npts // blocks
    axes = ("leaf", "sub")

    def send(x, routes):
        pairs = []
        for place in range(leaf_count):
            for from_sub, step, to_sub in routes:
                if 0 <= place + step < leaf_count:
                    pairs.append((place * sub_count + from_sub, (place + step) * sub_count + to_sub))
        return lax.ppermute(x, axes, pairs)

    count = leaf_count * sub_count
    bits = count.bit_length() - 1
    sub_bits = sub_count.bit_length() - 1

    def exchange(x, shift, stage_bits):
        parts = [x]
        for d in range(1, 1 << stage_bits):
            parts.append(lax.ppermute(x, axes, [(i, i ^ (d << shift)) for i in range(count)]))
        return parts

    def tie(*values):
        return lax.optimization_barrier(values)

    b = blocks
    own_base = (b, 2 * b, 3 * b, 4 * b)
    early_base, late_base = (5 * b, 4 * b, b, 0), (3 * b, 0, 5 * b, 2 * b)
    single, by_edge = (0, 0, 0, 0), (0, 1, 1, 0)

    pack, rows = order_call(points.T, order.reshape(blocks, 1, leaf), probes, blocks)
    outer_across = send(pack, [(3, 0, 1), (0, 0, 2)])
    outer_next = send(pack, [(3, 1, 3), (0, -1, 0)])
    beside_pack = send(pack, [(1, 0, 0), (2, 0, 3)])

    node = local_tree_call(pack, rows, leaf_sets, merge_sets, dim)

    def level(parts, bit, piece=None):
        return merge_call(parts, merge_sets, dim, blocks, bit, piece)

    node = level(exchange(node, 0, 1), 0)
    own_pack, node = tie(pack, node)
    parts = exchange(node, 1, 1)
    *parts, outer_across, outer_next, beside_pack, late_rows, late_lists = tie(
        *parts, outer_across, outer_next, beside_pack, rows, near_lists
    )
    forwarded = send(outer_across, [(1, 1, 1), (2, -1, 2)])
    inner_across = send(beside_pack, [(0, 0, 3), (3, 0, 0)])
    beside_rows = exchange(late_rows, 0, 1)[1]
    beside_lists = exchange(late_lists, 0, 1)[1]
    node = level(parts, 1)
    own_pack, node = tie(own_pack, node)
    parts = exchange(node, 2, 1)
    own_set = (own_base, single, [own_pack])
    early_set = (early_base, by_edge, [outer_next, outer_across])
    (own,) = near_call(
        [(0, near_lists, rows, None)], [own_set, early_set], ((0, 0), (1, 0)), dim, "near_own"
    )
    beside_rows, beside_lists, own = tie(beside_rows, beside_lists, own)
    (beside,) = near_call(
        [(1, beside_lists, beside_rows, None)],
        [own_set, early_set], ((0, 0), (1, 0)), dim, "near_early",
    )

    *parts, inner_across, forwarded, beside, own = tie(
        *parts, inner_across, forwarded, beside, own
    )
    late_set = (late_base, by_edge, [inner_across, forwarded])
    bit = 2
    while bit < bits - 2:
        node = level(parts, bit)
        bit += 1
        parts = exchange(node, bit, 1)
    (own,) = near_call([(0, near_lists, rows, own)], [late_set], ((0, 0),), dim, "near_last")
    *parts, own = tie(*parts, own)
    node = level(parts, bit)
    bit += 1
    beside, node = tie(beside, node)
    (beside,) = near_call(
        [(1, beside_lists, beside_rows, beside)], [late_set], ((0, 0),), dim, "near_beside"
    )
    given = exchange(beside, 0, 1)[1]
    node, beside = tie(node, beside)
    node = level(exchange(node, bit, 1), bit, skel // count)
    near = (own + given) * (leaf ** -0.5)
    if skel // count:
        root = node.reshape(-1)
    else:
        size = skel * LANES // count
        rank = lax.axis_index("leaf") * sub_count + lax.axis_index("sub")
        root = lax.dynamic_slice_in_dim(node.reshape(-1), rank * size, size, 0)
    return near.reshape(npts, LANES), root


def solution(mesh):
    in_specs = (
        P(("leaf", "sub"), None),
        P(("leaf", "sub"), None),
        P(("leaf", "sub")),
        P(("leaf", "sub"), None),
        P(("leaf", "sub")),
        P(("leaf", "sub"), None),
        P(),
    )
    out_specs = (P(("leaf", "sub"), None), P(("leaf", "sub")))
    return jax.shard_map(
        on_device, mesh=mesh, in_specs=in_specs, out_specs=out_specs, check_vma=False
    )
```

```python
import functools

import jax
import jax.numpy as jnp
from jax import lax
from jax.experimental import pallas as pl
from jax.experimental.pallas import tpu as pltpu
from jax.sharding import PartitionSpec as P

LANES = 128
PARTS = 3
VMEM_BYTES = 20 * 1024 * 1024
NEAR_BYTES = 24 * 1024 * 1024
F32 = jnp.float32
BF16 = jnp.bfloat16


def dot(a, b):
    return jnp.dot(a, b, preferred_element_type=F32)


def dot_t(a, b):
    return lax.dot_general(a, b, (((0,), (0,)), ((), ())), preferred_element_type=F32)


def split(x):
    hi = x.astype(BF16)
    return hi, (x - hi.astype(F32)).astype(BF16)


def square_rows(pts):
    x = pts.astype(F32)
    total = jnp.sum(x * x, axis=0, keepdims=True)
    hi = total.astype(BF16).astype(F32)
    mid = (total - hi).astype(BF16).astype(F32)
    low = total - hi - mid
    row = lax.broadcasted_iota(jnp.int32, (16, pts.shape[1]), 0)
    ones = jnp.where(row < 2 * PARTS, 1.0, 0.0)
    return jnp.where(row == 0, hi, jnp.where(row == 1, mid, jnp.where(row == 2, low, ones))).astype(BF16)


def form_map(dim, size):
    k = lax.broadcasted_iota(jnp.int32, (size, size), 0)
    j = lax.broadcasted_iota(jnp.int32, (size, size), 1)
    r = jnp.where((k == j) & (j < dim), 2.0 / dim, 0.0)
    r = jnp.where((j >= dim) & (j < dim + PARTS) & (k == j + PARTS), -1.0 / dim, r)
    r = jnp.where((j >= dim + PARTS) & (j < dim + 2 * PARTS) & (k == j - PARTS), -1.0 / dim, r)
    return r.astype(BF16)


def onehot_in(row, size):
    index = lax.broadcasted_iota(jnp.int32, (size, row.shape[1]), 0)
    return jnp.where(index == row, 1.0, 0.0).astype(BF16)


def column_of(row):
    return jnp.broadcast_to(row.astype(F32), (LANES, row.shape[1])).T


def onehot_out(column, size):
    lane = lax.broadcasted_iota(jnp.int32, column.shape, 1).astype(F32)
    return jnp.concatenate(
        [jnp.where(column == lane + float(i), 1.0, 0.0) for i in range(0, size, LANES)], axis=1
    )


def mix3(m, s):
    m_hi, m_lo = split(m)
    s_hi, s_lo = split(s)
    return dot(m_hi, s_hi) + (dot(m_hi, s_lo) + dot(m_lo, s_hi))


def order_kernel(points_t, order, probes, pack, rows):
    dim = points_t.shape[0]
    many, leaf = rows.shape[:2]
    held = dim + 16
    to_rows = form_map(dim, LANES)
    for b in range(many):
        picks = onehot_in(order[b], leaf)
        tree_t = dot(points_t[:, b * leaf : (b + 1) * leaf], picks).astype(BF16)
        pack[b, :leaf, :] = probes[b * leaf : (b + 1) * leaf, :]
        form = jnp.concatenate([tree_t, square_rows(tree_t)], axis=0)
        for i in range(leaf // LANES):
            pack[b, leaf + i * dim : leaf + (i + 1) * dim, :] = tree_t[:, i * LANES : (i + 1) * LANES]
        form = jnp.concatenate([form, jnp.zeros((LANES - held, leaf), BF16)], axis=0)
        rows[b] = dot_t(form, to_rows).astype(BF16)


def order_call(points_t, order, probes, blocks):
    dim, npts = points_t.shape
    leaf = npts // blocks
    packed = leaf + leaf // LANES * dim
    many = 4 if blocks % 4 == 0 else 1
    return pl.pallas_call(
        order_kernel,
        grid=(blocks // many,),
        in_specs=[
            pl.BlockSpec((dim, many * leaf), lambda b: (0, b)),
            pl.BlockSpec((many, 1, leaf), lambda b: (b, 0, 0)),
            pl.BlockSpec((many * leaf, LANES), lambda b: (b, 0)),
        ],
        out_specs=[
            pl.BlockSpec((many, packed, LANES), lambda b: (b, 0, 0)),
            pl.BlockSpec((many, leaf, LANES), lambda b: (b, 0, 0)),
        ],
        out_shape=[
            jax.ShapeDtypeStruct((blocks, packed, LANES), BF16),
            jax.ShapeDtypeStruct((blocks, leaf, LANES), BF16),
        ],
        compiler_params=pltpu.CompilerParams(vmem_limit_bytes=VMEM_BYTES),
        cost_estimate=pl.CostEstimate(
            flops=blocks * 2 * leaf * leaf * dim, bytes_accessed=10 * npts * LANES, transcendentals=0
        ),
        name="tree_order",
    )(points_t, order, probes)


def form_of(pack_block, leaf, dim):
    columns = []
    for i in range(leaf // LANES):
        pts = pack_block[leaf + i * dim : leaf + (i + 1) * dim, :]
        columns.append(jnp.concatenate([pts, square_rows(pts)], axis=0))
    form = jnp.concatenate(columns, axis=1)
    return jnp.concatenate([form, jnp.zeros((LANES - dim - 16, leaf), BF16)], axis=0)


def condense(form, a_rows, chosen):
    size = form.shape[1]
    picks_out = onehot_out(column_of(chosen), size)
    new_rows = dot(picks_out.astype(BF16), a_rows).astype(BF16)
    new_form = dot(form, onehot_in(chosen, size)).astype(BF16)
    weights = jnp.exp(dot(new_rows, form))
    mixing = picks_out + weights / jnp.sum(weights, axis=1, keepdims=True)
    return new_form, new_rows, mixing


def local_tree_kernel(pack, rows, leaf_sets_in, merge_sets_in, out, leaf_sets, merge_sets, sems, *, dim):
    blocks, leaf = rows.shape[:2]
    leaf_copy = pltpu.make_async_copy(leaf_sets_in, leaf_sets, sems.at[0])
    merge_copy = pltpu.make_async_copy(merge_sets_in, merge_sets, sems.at[1])
    leaf_copy.start()
    merge_copy.start()
    leaf_copy.wait()
    first_block = (lax.axis_index("leaf") * lax.axis_size("sub") + lax.axis_index("sub")) * blocks

    nodes = []
    for b in range(blocks):
        form = form_of(pack.at[b], leaf, dim)
        new_form, new_rows, mixing = condense(form, rows[b], leaf_sets[b : b + 1, :])
        m_hi, m_lo = split(mixing)
        probes = pack[b, :leaf, :]
        nodes.append((new_form, new_rows, dot(m_hi, probes) + dot(m_lo, probes)))
    span = 1
    merge_copy.wait()
    while len(nodes) > 1:
        merged = []
        for k in range(len(nodes) // 2):
            left, right = nodes[2 * k], nodes[2 * k + 1]
            chosen = merge_sets[pl.ds(first_block + (2 * k + 1) * span - 1, 1), :]
            new_form, new_rows, mixing = condense(
                jnp.concatenate([left[0], right[0]], axis=1),
                jnp.concatenate([left[1], right[1]], axis=0),
                chosen,
            )
            samples = mix3(mixing, jnp.concatenate([left[2], right[2]], axis=0))
            merged.append((new_form, new_rows, samples))
        nodes = merged
        span *= 2
    held = dim + 16
    out[:held, :] = nodes[0][0][:held, :].astype(F32)
    out[held:, :] = nodes[0][2]


def local_tree_call(pack, rows, leaf_sets, merge_sets, dim):
    blocks, leaf = rows.shape[:2]
    skel = leaf_sets.shape[1]
    return pl.pallas_call(
        functools.partial(local_tree_kernel, dim=dim),
        in_specs=[pl.BlockSpec(memory_space=pltpu.VMEM)] * 2
        + [pl.BlockSpec(memory_space=pltpu.HBM)] * 2,
        out_shape=jax.ShapeDtypeStruct((dim + 16 + skel, LANES), F32),
        scratch_shapes=[
            pltpu.VMEM(leaf_sets.shape, jnp.int32),
            pltpu.VMEM(merge_sets.shape, jnp.int32),
            pltpu.SemaphoreType.DMA((2,)),
        ],
        compiler_params=pltpu.CompilerParams(vmem_limit_bytes=VMEM_BYTES),
        cost_estimate=pl.CostEstimate(
            flops=blocks * 8 * skel * leaf * LANES,
            bytes_accessed=6 * blocks * leaf * LANES,
            transcendentals=blocks * skel * leaf,
        ),
        name="local_tree",
    )(pack, rows, leaf_sets, merge_sets)


def merge_kernel(*refs, dim, blocks, shift, piece):
    merge_sets_in, out, group, merge_sets, sem = refs[-5:]
    parts = refs[:-5]
    count, size = group.shape[:2]
    copy = pltpu.make_async_copy(merge_sets_in, merge_sets, sem)
    copy.start()
    held = dim + 16
    skel = size - held
    rank = lax.axis_index("leaf") * lax.axis_size("sub") + lax.axis_index("sub")
    unit = lax.shift_right_logical(rank, shift)
    place = unit & (count - 1)
    first = unit - place
    span = blocks << shift
    for d, part in enumerate(parts):
        group[place ^ d] = part[...]
    to_rows = form_map(dim, LANES)
    forms = [group[i, :held, :].astype(BF16) for i in range(count)]
    samples = [group[i, held:, :] for i in range(count)]
    copy.wait()
    while len(forms) > 1:
        first = first // 2
        new_forms, new_samples = [], []
        for k in range(len(forms) // 2):
            chosen = merge_sets[pl.ds((2 * (first + k) + 1) * span - 1, 1), :]
            form = jnp.concatenate(forms[2 * k : 2 * k + 2], axis=1)
            form = jnp.concatenate([form, jnp.zeros((LANES - held, 2 * skel), BF16)], axis=0)
            new_form = dot(form, onehot_in(chosen, 2 * skel)).astype(BF16)
            new_rows = dot_t(new_form, to_rows).astype(BF16)
            weights = jnp.exp(dot(new_rows, form))
            picks = onehot_out(column_of(chosen), 2 * skel)
            mixing = picks + weights / jnp.sum(weights, axis=1, keepdims=True)
            new_forms.append(new_form[:held])
            new_samples.append(mix3(mixing, jnp.concatenate(samples[2 * k : 2 * k + 2], axis=0)))
        forms, samples = new_forms, new_samples
        span *= 2
    if piece is None:
        out[:held, :] = forms[0].astype(F32)
        out[held:, :] = samples[0]
    elif piece == 0:
        out[...] = samples[0]
    else:
        column = lax.broadcasted_iota(jnp.int32, (piece, skel), 1)
        row = lax.broadcasted_iota(jnp.int32, (piece, skel), 0) + rank * piece
        take = jnp.where(column == row, 1.0, 0.0).astype(BF16)
        hi, lo = split(samples[0])
        low = (samples[0] - hi.astype(F32) - lo.astype(F32)).astype(BF16)
        out[...] = dot(take, hi) + dot(take, lo) + dot(take, low)


def merge_call(parts, merge_sets, dim, blocks, shift, piece=None):
    count = len(parts)
    size = parts[0].shape[0]
    skel = size - dim - 16
    rows = size if piece is None else (piece or skel)
    return pl.pallas_call(
        functools.partial(merge_kernel, dim=dim, blocks=blocks, shift=shift, piece=piece),
        in_specs=[pl.BlockSpec(memory_space=pltpu.VMEM)] * count
        + [pl.BlockSpec(memory_space=pltpu.HBM)],
        out_shape=jax.ShapeDtypeStruct((rows, LANES), F32),
        scratch_shapes=[
            pltpu.VMEM((count, size, LANES), F32),
            pltpu.VMEM(merge_sets.shape, jnp.int32),
            pltpu.SemaphoreType.DMA(()),
        ],
        compiler_params=pltpu.CompilerParams(vmem_limit_bytes=16 * 1024 * 1024),
        cost_estimate=pl.CostEstimate(
            flops=count * 16 * LANES**3,
            bytes_accessed=4 * count * size * LANES,
            transcendentals=2 * count * LANES**2,
        ),
        name="tree_merge",
    )(*parts, merge_sets)


def near_kernel(*refs, flips, row_counts, has_acc, sets, tasks, span, dim):
    refs = list(refs)

    def take(number):
        taken = refs[:number]
        del refs[:number]
        return taken

    lists, rows = take(len(flips)), [take(number) for number in row_counts]
    accs = [take(1)[0] if has else None for has in has_acc]
    buffers = [take(max(which) + 1) for _, which in sets]
    outs, (pair_list,) = take(len(flips)), refs
    blocks, leaf = rows[0][0].shape[:2]
    near = lists[0].shape[1]
    window = blocks * lax.axis_size("sub")
    sub = lax.axis_index("sub")

    def place(table):
        value = jnp.int32(table[0])
        for i in range(1, len(table)):
            value = jnp.where(sub == i, jnp.int32(table[i]), value)
        return value

    window_first = lax.axis_index("leaf") * window - blocks
    stride = blocks * near + 8
    found = [jnp.int32(0)] * len(tasks)
    for j, flip in enumerate(flips):
        mine = [t for t, (_, group) in enumerate(tasks) if group == j]
        firsts = [window_first + place(sets[tasks[t][0]][0]) for t in mine]
        target_first = lax.axis_index("leaf") * window + (sub ^ flip) * blocks

        def list_block(g, counts, j=j, mine=mine, firsts=firsts, target_first=target_first):
            for s in range(*span):
                source = lists[j][g, s]
                used = (source != target_first + g) if s else True
                after = []
                for t, first, count in zip(mine, firsts, counts):
                    local = source - first
                    pair_list[t * stride + count] = g * blocks + local
                    inside = (local >= 0) & (local < blocks) & used
                    after.append(count + jnp.where(inside, 1, 0))
                counts = tuple(after)
            return counts

        counts = lax.fori_loop(0, blocks, list_block, (jnp.int32(0),) * len(mine))
        for t, count in zip(mine, counts):
            found[t] = count
        outs[j][...] = jnp.zeros(outs[j].shape, F32) if accs[j] is None else accs[j][...]

    half = leaf // 2

    def add_all(buffer, targets, t, pairs):
        j = tasks[t][1]

        def add_pair(i):
            code = pair_list[t * stride + i]
            g = code // blocks
            local = code - g * blocks
            form = form_of(buffer.at[local], leaf, dim)
            probes = buffer[local, :leaf, :]
            total = None
            for c in range(0, leaf, half):
                weights = jnp.exp(dot(targets[g], form[:, c : c + half])).astype(BF16)
                term = dot(weights, probes[c : c + half])
                total = term if total is None else total + term
            return g, total

        def add_pairs(i, carry):
            for g, total in [add_pair(2 * i), add_pair(2 * i + 1)]:
                outs[j][g] += total
            return carry

        lax.fori_loop(0, pairs // 2, add_pairs, 0)

        @pl.when(pairs % 2 == 1)
        def _():
            g, total = add_pair(pairs - 1)
            outs[j][g] += total

    for t, (number, j) in enumerate(tasks):
        held = place(sets[number][1])
        edge = (sub == 0) | (sub == lax.axis_size("sub") - 1)
        for k, buffer in enumerate(buffers[number]):
            for r, targets in enumerate(rows[j]):
                pairs = found[t]
                if len(buffers[number]) > 1:
                    if len(rows[j]) > 1 and r != k:
                        continue
                    pairs = jnp.where(held == k, pairs, 0)
                elif len(rows[j]) > 1:
                    pairs = jnp.where(edge == (r == 0), pairs, 0)
                add_all(buffer, targets, t, pairs)


def near_call(groups, sources, tasks, dim, name):
    flips, lists, rows, accs = zip(*groups)
    rows = [r if isinstance(r, tuple) else (r,) for r in rows]
    blocks, leaf = rows[0][0].shape[:2]
    held = [acc for acc in accs if acc is not None]
    args = [*lists, *(r for pair in rows for r in pair), *held, *(b for _, _, buffers in sources for b in buffers)]
    smem = pl.BlockSpec(memory_space=pltpu.SMEM)
    vmem = pl.BlockSpec(memory_space=pltpu.VMEM)
    near = lists[0].shape[1]
    return pl.pallas_call(
        functools.partial(
            near_kernel,
            flips=flips,
            row_counts=tuple(len(pair) for pair in rows),
            has_acc=tuple(acc is not None for acc in accs),
            sets=tuple((bases, which) for bases, which, _ in sources),
            tasks=tasks,
            span=(0, near),
            dim=dim,
        ),
        in_specs=[smem] * len(lists) + [vmem] * (len(args) - len(lists)),
        out_specs=[vmem] * len(groups),
        out_shape=[jax.ShapeDtypeStruct((blocks, leaf, LANES), F32)] * len(groups),
        scratch_shapes=[pltpu.SMEM((len(tasks) * (blocks * near + 8),), jnp.int32)],
        compiler_params=pltpu.CompilerParams(vmem_limit_bytes=NEAR_BYTES),
        cost_estimate=pl.CostEstimate(flops=1000, bytes_accessed=1000, transcendentals=0),
        name=name,
    )(*args)


def on_device(points, probes, order, near_lists, near_counts, leaf_sets, merge_sets):
    leaf_count = lax.axis_size("leaf")
    sub_count = lax.axis_size("sub")
    blocks, skel = leaf_sets.shape
    npts, dim = points.shape
    leaf = npts // blocks
    axes = ("leaf", "sub")

    def send(x, routes):
        pairs = []
        for place in range(leaf_count):
            for from_sub, step, to_sub in routes:
                if 0 <= place + step < leaf_count:
                    pairs.append((place * sub_count + from_sub, (place + step) * sub_count + to_sub))
        return lax.ppermute(x, axes, pairs)

    count = leaf_count * sub_count
    bits = count.bit_length() - 1
    sub_bits = sub_count.bit_length() - 1

    def exchange(x, shift, stage_bits):
        parts = [x]
        for d in range(1, 1 << stage_bits):
            parts.append(lax.ppermute(x, axes, [(i, i ^ (d << shift)) for i in range(count)]))
        return parts

    def tie(*values):
        return lax.optimization_barrier(values)

    b = blocks
    own_base = (b, 2 * b, 3 * b, 4 * b)
    early_base, late_base = (5 * b, 4 * b, b, 0), (3 * b, 0, 5 * b, 2 * b)
    single, by_edge = (0, 0, 0, 0), (0, 1, 1, 0)

    pack, rows = order_call(points.T, order.reshape(blocks, 1, leaf), probes, blocks)
    outer_across = send(pack, [(3, 0, 1), (0, 0, 2)])
    outer_next = send(pack, [(3, 1, 3), (0, -1, 0)])
    beside_pack = send(pack, [(1, 0, 0), (2, 0, 3)])

    node = local_tree_call(pack, rows, leaf_sets, merge_sets, dim)

    def level(parts, bit, piece=None):
        return merge_call(parts, merge_sets, dim, blocks, bit, piece)

    node = level(exchange(node, 0, 1), 0)
    own_pack, node = tie(pack, node)
    parts = exchange(node, 1, 1)
    *parts, outer_across, outer_next, beside_pack, late_rows, late_lists = tie(
        *parts, outer_across, outer_next, beside_pack, rows, near_lists
    )
    forwarded = send(outer_across, [(1, 1, 1), (2, -1, 2)])
    inner_across = send(beside_pack, [(0, 0, 3), (3, 0, 0)])
    beside_rows = exchange(late_rows, 0, 1)[1]
    beside_lists = exchange(late_lists, 0, 1)[1]
    node = level(parts, 1)
    own_pack, node = tie(own_pack, node)
    parts = exchange(node, 2, 1)
    own_set = (own_base, single, [own_pack])
    early_set = (early_base, by_edge, [outer_next, outer_across])
    (own,) = near_call(
        [(0, near_lists, rows, None)], [own_set, early_set], ((0, 0), (1, 0)), dim, "near_own"
    )
    beside_rows, beside_lists, own = tie(beside_rows, beside_lists, own)
    (beside,) = near_call(
        [(1, beside_lists, beside_rows, None)],
        [own_set, early_set], ((0, 0), (1, 0)), dim, "near_early",
    )

    *parts, inner_across, forwarded, beside, own = tie(
        *parts, inner_across, forwarded, beside, own
    )
    late_set = (late_base, by_edge, [inner_across, forwarded])
    bit = 2
    while bit < bits - 2:
        node = level(parts, bit)
        bit += 1
        parts = exchange(node, bit, 1)
    (own,) = near_call([(0, near_lists, rows, own)], [late_set], ((0, 0),), dim, "near_last")
    *parts, own = tie(*parts, own)
    node = level(parts, bit)
    bit += 1
    beside, *parts = tie(beside, *exchange(node, bit, 1))
    (beside,) = near_call(
        [(1, beside_lists, beside_rows, beside)], [late_set], ((0, 0),), dim, "near_beside"
    )
    given = exchange(beside, 0, 1)[1]
    *parts, beside = tie(*parts, beside)
    node = level(parts, bit, skel // count)
    near = (own + given) * (leaf ** -0.5)
    if skel // count:
        root = node.reshape(-1)
    else:
        size = skel * LANES // count
        rank = lax.axis_index("leaf") * sub_count + lax.axis_index("sub")
        root = lax.dynamic_slice_in_dim(node.reshape(-1), rank * size, size, 0)
    return near.reshape(npts, LANES), root


def solution(mesh):
    in_specs = (
        P(("leaf", "sub"), None),
        P(("leaf", "sub"), None),
        P(("leaf", "sub")),
        P(("leaf", "sub"), None),
        P(("leaf", "sub")),
        P(("leaf", "sub"), None),
        P(),
    )
    out_specs = (P(("leaf", "sub"), None), P(("leaf", "sub")))
    return jax.shard_map(
        on_device, mesh=mesh, in_specs=in_specs, out_specs=out_specs, check_vma=False
    )
```

```python
import functools

import jax
import jax.numpy as jnp
from jax import lax
from jax.experimental import pallas as pl
from jax.experimental.pallas import tpu as pltpu
from jax.sharding import PartitionSpec as P

LANES = 128
PARTS = 3
VMEM_BYTES = 20 * 1024 * 1024
NEAR_BYTES = 24 * 1024 * 1024
F32 = jnp.float32
BF16 = jnp.bfloat16


def dot(a, b):
    return jnp.dot(a, b, preferred_element_type=F32)


def dot_t(a, b):
    return lax.dot_general(a, b, (((0,), (0,)), ((), ())), preferred_element_type=F32)


def split(x):
    hi = x.astype(BF16)
    return hi, (x - hi.astype(F32)).astype(BF16)


def square_rows(pts):
    x = pts.astype(F32)
    total = jnp.sum(x * x, axis=0, keepdims=True)
    hi = total.astype(BF16).astype(F32)
    mid = (total - hi).astype(BF16).astype(F32)
    low = total - hi - mid
    row = lax.broadcasted_iota(jnp.int32, (16, pts.shape[1]), 0)
    ones = jnp.where(row < 2 * PARTS, 1.0, 0.0)
    return jnp.where(row == 0, hi, jnp.where(row == 1, mid, jnp.where(row == 2, low, ones))).astype(BF16)


def form_map(dim, size):
    k = lax.broadcasted_iota(jnp.int32, (size, size), 0)
    j = lax.broadcasted_iota(jnp.int32, (size, size), 1)
    r = jnp.where((k == j) & (j < dim), 2.0 / dim, 0.0)
    r = jnp.where((j >= dim) & (j < dim + PARTS) & (k == j + PARTS), -1.0 / dim, r)
    r = jnp.where((j >= dim + PARTS) & (j < dim + 2 * PARTS) & (k == j - PARTS), -1.0 / dim, r)
    return r.astype(BF16)


def onehot_in(row, size):
    index = lax.broadcasted_iota(jnp.int32, (size, row.shape[1]), 0)
    return jnp.where(index == row, 1.0, 0.0).astype(BF16)


def column_of(row):
    return jnp.broadcast_to(row.astype(F32), (LANES, row.shape[1])).T


def onehot_out(column, size):
    lane = lax.broadcasted_iota(jnp.int32, column.shape, 1).astype(F32)
    return jnp.concatenate(
        [jnp.where(column == lane + float(i), 1.0, 0.0) for i in range(0, size, LANES)], axis=1
    )


def mix3(m, s):
    m_hi, m_lo = split(m)
    s_hi, s_lo = split(s)
    return dot(m_hi, s_hi) + (dot(m_hi, s_lo) + dot(m_lo, s_hi))


def order_kernel(points_t, order, probes, pack, rows):
    dim = points_t.shape[0]
    many, leaf = rows.shape[:2]
    held = dim + 16
    to_rows = form_map(dim, LANES)
    for b in range(many):
        picks = onehot_in(order[b], leaf)
        tree_t = dot(points_t[:, b * leaf : (b + 1) * leaf], picks).astype(BF16)
        pack[b, :leaf, :] = probes[b * leaf : (b + 1) * leaf, :]
        form = jnp.concatenate([tree_t, square_rows(tree_t)], axis=0)
        for i in range(leaf // LANES):
            pack[b, leaf + i * dim : leaf + (i + 1) * dim, :] = tree_t[:, i * LANES : (i + 1) * LANES]
        form = jnp.concatenate([form, jnp.zeros((LANES - held, leaf), BF16)], axis=0)
        rows[b] = dot_t(form, to_rows).astype(BF16)


def order_call(points_t, order, probes, blocks):
    dim, npts = points_t.shape
    leaf = npts // blocks
    packed = leaf + leaf // LANES * dim
    many = 4 if blocks % 4 == 0 else 1
    return pl.pallas_call(
        order_kernel,
        grid=(blocks // many,),
        in_specs=[
            pl.BlockSpec((dim, many * leaf), lambda b: (0, b)),
            pl.BlockSpec((many, 1, leaf), lambda b: (b, 0, 0)),
            pl.BlockSpec((many * leaf, LANES), lambda b: (b, 0)),
        ],
        out_specs=[
            pl.BlockSpec((many, packed, LANES), lambda b: (b, 0, 0)),
            pl.BlockSpec((many, leaf, LANES), lambda b: (b, 0, 0)),
        ],
        out_shape=[
            jax.ShapeDtypeStruct((blocks, packed, LANES), BF16),
            jax.ShapeDtypeStruct((blocks, leaf, LANES), BF16),
        ],
        compiler_params=pltpu.CompilerParams(vmem_limit_bytes=VMEM_BYTES),
        cost_estimate=pl.CostEstimate(
            flops=blocks * 2 * leaf * leaf * dim, bytes_accessed=10 * npts * LANES, transcendentals=0
        ),
        name="tree_order",
    )(points_t, order, probes)


def form_of(pack_block, leaf, dim):
    columns = []
    for i in range(leaf // LANES):
        pts = pack_block[leaf + i * dim : leaf + (i + 1) * dim, :]
        columns.append(jnp.concatenate([pts, square_rows(pts)], axis=0))
    form = jnp.concatenate(columns, axis=1)
    return jnp.concatenate([form, jnp.zeros((LANES - dim - 16, leaf), BF16)], axis=0)


def condense(form, a_rows, chosen):
    size = form.shape[1]
    picks_out = onehot_out(column_of(chosen), size)
    new_rows = dot(picks_out.astype(BF16), a_rows).astype(BF16)
    new_form = dot(form, onehot_in(chosen, size)).astype(BF16)
    weights = jnp.exp(dot(new_rows, form))
    mixing = picks_out + weights / jnp.sum(weights, axis=1, keepdims=True)
    return new_form, new_rows, mixing


def local_tree_kernel(pack, rows, leaf_sets_in, merge_sets_in, out, leaf_sets, merge_sets, sems, *, dim):
    blocks, leaf = rows.shape[:2]
    leaf_copy = pltpu.make_async_copy(leaf_sets_in, leaf_sets, sems.at[0])
    merge_copy = pltpu.make_async_copy(merge_sets_in, merge_sets, sems.at[1])
    leaf_copy.start()
    merge_copy.start()
    leaf_copy.wait()
    first_block = (lax.axis_index("leaf") * lax.axis_size("sub") + lax.axis_index("sub")) * blocks

    nodes = []
    for b in range(blocks):
        form = form_of(pack.at[b], leaf, dim)
        new_form, new_rows, mixing = condense(form, rows[b], leaf_sets[b : b + 1, :])
        m_hi, m_lo = split(mixing)
        probes = pack[b, :leaf, :]
        nodes.append((new_form, new_rows, dot(m_hi, probes) + dot(m_lo, probes)))
    span = 1
    merge_copy.wait()
    while len(nodes) > 1:
        merged = []
        for k in range(len(nodes) // 2):
            left, right = nodes[2 * k], nodes[2 * k + 1]
            chosen = merge_sets[pl.ds(first_block + (2 * k + 1) * span - 1, 1), :]
            new_form, new_rows, mixing = condense(
                jnp.concatenate([left[0], right[0]], axis=1),
                jnp.concatenate([left[1], right[1]], axis=0),
                chosen,
            )
            samples = mix3(mixing, jnp.concatenate([left[2], right[2]], axis=0))
            merged.append((new_form, new_rows, samples))
        nodes = merged
        span *= 2
    held = dim + 16
    out[:held, :] = nodes[0][0][:held, :].astype(F32)
    out[held:, :] = nodes[0][2]


def local_tree_call(pack, rows, leaf_sets, merge_sets, dim):
    blocks, leaf = rows.shape[:2]
    skel = leaf_sets.shape[1]
    return pl.pallas_call(
        functools.partial(local_tree_kernel, dim=dim),
        in_specs=[pl.BlockSpec(memory_space=pltpu.VMEM)] * 2
        + [pl.BlockSpec(memory_space=pltpu.HBM)] * 2,
        out_shape=jax.ShapeDtypeStruct((dim + 16 + skel, LANES), F32),
        scratch_shapes=[
            pltpu.VMEM(leaf_sets.shape, jnp.int32),
            pltpu.VMEM(merge_sets.shape, jnp.int32),
            pltpu.SemaphoreType.DMA((2,)),
        ],
        compiler_params=pltpu.CompilerParams(vmem_limit_bytes=VMEM_BYTES),
        cost_estimate=pl.CostEstimate(
            flops=blocks * 8 * skel * leaf * LANES,
            bytes_accessed=6 * blocks * leaf * LANES,
            transcendentals=blocks * skel * leaf,
        ),
        name="local_tree",
    )(pack, rows, leaf_sets, merge_sets)


def merge_kernel(*refs, dim, blocks, shift, piece):
    merge_sets_in, out, group, merge_sets, sem = refs[-5:]
    parts = refs[:-5]
    count, size = group.shape[:2]
    copy = pltpu.make_async_copy(merge_sets_in, merge_sets, sem)
    copy.start()
    held = dim + 16
    skel = size - held
    rank = lax.axis_index("leaf") * lax.axis_size("sub") + lax.axis_index("sub")
    unit = lax.shift_right_logical(rank, shift)
    place = unit & (count - 1)
    first = unit - place
    span = blocks << shift
    for d, part in enumerate(parts):
        group[place ^ d] = part[...]
    to_rows = form_map(dim, LANES)
    forms = [group[i, :held, :].astype(BF16) for i in range(count)]
    samples = [group[i, held:, :] for i in range(count)]
    copy.wait()
    while len(forms) > 1:
        first = first // 2
        new_forms, new_samples = [], []
        for k in range(len(forms) // 2):
            chosen = merge_sets[pl.ds((2 * (first + k) + 1) * span - 1, 1), :]
            form = jnp.concatenate(forms[2 * k : 2 * k + 2], axis=1)
            form = jnp.concatenate([form, jnp.zeros((LANES - held, 2 * skel), BF16)], axis=0)
            new_form = dot(form, onehot_in(chosen, 2 * skel)).astype(BF16)
            new_rows = dot_t(new_form, to_rows).astype(BF16)
            weights = jnp.exp(dot(new_rows, form))
            picks = onehot_out(column_of(chosen), 2 * skel)
            mixing = picks + weights / jnp.sum(weights, axis=1, keepdims=True)
            new_forms.append(new_form[:held])
            new_samples.append(mix3(mixing, jnp.concatenate(samples[2 * k : 2 * k + 2], axis=0)))
        forms, samples = new_forms, new_samples
        span *= 2
    if piece is None:
        out[:held, :] = forms[0].astype(F32)
        out[held:, :] = samples[0]
    elif piece == 0:
        out[...] = samples[0]
    else:
        column = lax.broadcasted_iota(jnp.int32, (piece, skel), 1)
        row = lax.broadcasted_iota(jnp.int32, (piece, skel), 0) + rank * piece
        take = jnp.where(column == row, 1.0, 0.0).astype(BF16)
        hi, lo = split(samples[0])
        low = (samples[0] - hi.astype(F32) - lo.astype(F32)).astype(BF16)
        out[...] = dot(take, hi) + dot(take, lo) + dot(take, low)


def merge_call(parts, merge_sets, dim, blocks, shift, piece=None):
    count = len(parts)
    size = parts[0].shape[0]
    skel = size - dim - 16
    rows = size if piece is None else (piece or skel)
    return pl.pallas_call(
        functools.partial(merge_kernel, dim=dim, blocks=blocks, shift=shift, piece=piece),
        in_specs=[pl.BlockSpec(memory_space=pltpu.VMEM)] * count
        + [pl.BlockSpec(memory_space=pltpu.HBM)],
        out_shape=jax.ShapeDtypeStruct((rows, LANES), F32),
        scratch_shapes=[
            pltpu.VMEM((count, size, LANES), F32),
            pltpu.VMEM(merge_sets.shape, jnp.int32),
            pltpu.SemaphoreType.DMA(()),
        ],
        compiler_params=pltpu.CompilerParams(vmem_limit_bytes=16 * 1024 * 1024),
        cost_estimate=pl.CostEstimate(
            flops=count * 16 * LANES**3,
            bytes_accessed=4 * count * size * LANES,
            transcendentals=2 * count * LANES**2,
        ),
        name="tree_merge",
    )(*parts, merge_sets)


def near_kernel(*refs, flips, row_counts, has_acc, sets, tasks, span, dim):
    refs = list(refs)

    def take(number):
        taken = refs[:number]
        del refs[:number]
        return taken

    lists, rows = take(len(flips)), [take(number) for number in row_counts]
    accs = [take(1)[0] if has else None for has in has_acc]
    buffers = [take(max(which) + 1) for _, which in sets]
    outs, (pair_list,) = take(len(flips)), refs
    blocks, leaf = rows[0][0].shape[:2]
    near = lists[0].shape[1]
    window = blocks * lax.axis_size("sub")
    sub = lax.axis_index("sub")

    def place(table):
        value = jnp.int32(table[0])
        for i in range(1, len(table)):
            value = jnp.where(sub == i, jnp.int32(table[i]), value)
        return value

    window_first = lax.axis_index("leaf") * window - blocks
    stride = blocks * near + 8
    found = [jnp.int32(0)] * len(tasks)
    for j, flip in enumerate(flips):
        mine = [t for t, (_, group) in enumerate(tasks) if group == j]
        firsts = [window_first + place(sets[tasks[t][0]][0]) for t in mine]
        target_first = lax.axis_index("leaf") * window + (sub ^ flip) * blocks

        def list_block(g, counts, j=j, mine=mine, firsts=firsts, target_first=target_first):
            for s in range(*span):
                source = lists[j][g, s]
                used = (source != target_first + g) if s else True
                after = []
                for t, first, count in zip(mine, firsts, counts):
                    local = source - first
                    pair_list[t * stride + count] = g * blocks + local
                    inside = (local >= 0) & (local < blocks) & used
                    after.append(count + jnp.where(inside, 1, 0))
                counts = tuple(after)
            return counts

        counts = lax.fori_loop(0, blocks, list_block, (jnp.int32(0),) * len(mine))
        for t, count in zip(mine, counts):
            found[t] = count
        outs[j][...] = jnp.zeros(outs[j].shape, F32) if accs[j] is None else accs[j][...]

    half = leaf // 2

    def add_all(buffer, targets, t, pairs):
        j = tasks[t][1]

        def add_pair(i):
            code = pair_list[t * stride + i]
            g = code // blocks
            local = code - g * blocks
            form = form_of(buffer.at[local], leaf, dim)
            probes = buffer[local, :leaf, :]
            total = None
            for c in range(0, leaf, half):
                weights = jnp.exp(dot(targets[g], form[:, c : c + half])).astype(BF16)
                term = dot(weights, probes[c : c + half])
                total = term if total is None else total + term
            return g, total

        def add_pairs(i, carry):
            for g, total in [add_pair(2 * i), add_pair(2 * i + 1)]:
                outs[j][g] += total
            return carry

        lax.fori_loop(0, pairs // 2, add_pairs, 0)

        @pl.when(pairs % 2 == 1)
        def _():
            g, total = add_pair(pairs - 1)
            outs[j][g] += total

    for t, (number, j) in enumerate(tasks):
        held = place(sets[number][1])
        edge = (sub == 0) | (sub == lax.axis_size("sub") - 1)
        for k, buffer in enumerate(buffers[number]):
            for r, targets in enumerate(rows[j]):
                pairs = found[t]
                if len(buffers[number]) > 1:
                    if len(rows[j]) > 1 and r != k:
                        continue
                    pairs = jnp.where(held == k, pairs, 0)
                elif len(rows[j]) > 1:
                    pairs = jnp.where(edge == (r == 0), pairs, 0)
                add_all(buffer, targets, t, pairs)


def near_call(groups, sources, tasks, dim, name):
    flips, lists, rows, accs = zip(*groups)
    rows = [r if isinstance(r, tuple) else (r,) for r in rows]
    blocks, leaf = rows[0][0].shape[:2]
    held = [acc for acc in accs if acc is not None]
    args = [*lists, *(r for pair in rows for r in pair), *held, *(b for _, _, buffers in sources for b in buffers)]
    smem = pl.BlockSpec(memory_space=pltpu.SMEM)
    vmem = pl.BlockSpec(memory_space=pltpu.VMEM)
    near = lists[0].shape[1]
    return pl.pallas_call(
        functools.partial(
            near_kernel,
            flips=flips,
            row_counts=tuple(len(pair) for pair in rows),
            has_acc=tuple(acc is not None for acc in accs),
            sets=tuple((bases, which) for bases, which, _ in sources),
            tasks=tasks,
            span=(0, near),
            dim=dim,
        ),
        in_specs=[smem] * len(lists) + [vmem] * (len(args) - len(lists)),
        out_specs=[vmem] * len(groups),
        out_shape=[jax.ShapeDtypeStruct((blocks, leaf, LANES), F32)] * len(groups),
        scratch_shapes=[pltpu.SMEM((len(tasks) * (blocks * near + 8),), jnp.int32)],
        compiler_params=pltpu.CompilerParams(vmem_limit_bytes=NEAR_BYTES),
        cost_estimate=pl.CostEstimate(flops=1000, bytes_accessed=1000, transcendentals=0),
        name=name,
    )(*args)


def on_device(points, probes, order, near_lists, near_counts, leaf_sets, merge_sets):
    leaf_count = lax.axis_size("leaf")
    sub_count = lax.axis_size("sub")
    blocks, skel = leaf_sets.shape
    npts, dim = points.shape
    leaf = npts // blocks
    axes = ("leaf", "sub")

    def send(x, routes):
        pairs = []
        for place in range(leaf_count):
            for from_sub, step, to_sub in routes:
                if 0 <= place + step < leaf_count:
                    pairs.append((place * sub_count + from_sub, (place + step) * sub_count + to_sub))
        return lax.ppermute(x, axes, pairs)

    count = leaf_count * sub_count
    bits = count.bit_length() - 1
    sub_bits = sub_count.bit_length() - 1

    def exchange(x, shift, stage_bits):
        parts = [x]
        for d in range(1, 1 << stage_bits):
            parts.append(lax.ppermute(x, axes, [(i, i ^ (d << shift)) for i in range(count)]))
        return parts

    def tie(*values):
        return lax.optimization_barrier(values)

    b = blocks
    own_base = (b, 2 * b, 3 * b, 4 * b)
    early_base, late_base = (5 * b, 4 * b, b, 0), (3 * b, 0, 5 * b, 2 * b)
    single, by_edge = (0, 0, 0, 0), (0, 1, 1, 0)

    pack, rows = order_call(points.T, order.reshape(blocks, 1, leaf), probes, blocks)
    outer_across = send(pack, [(3, 0, 1), (0, 0, 2)])
    outer_next = send(pack, [(3, 1, 3), (0, -1, 0)])
    beside_pack = send(pack, [(1, 0, 0), (2, 0, 3)])

    node = local_tree_call(pack, rows, leaf_sets, merge_sets, dim)

    def level(parts, bit, piece=None):
        return merge_call(parts, merge_sets, dim, blocks, bit, piece)

    node = level(exchange(node, 0, 1), 0)
    own_pack, node = tie(pack, node)
    parts = exchange(node, 1, 1)
    *parts, outer_across, outer_next, beside_pack, late_rows, late_lists = tie(
        *parts, outer_across, outer_next, beside_pack, rows, near_lists
    )
    forwarded = send(outer_across, [(1, 1, 1), (2, -1, 2)])
    inner_across = send(beside_pack, [(0, 0, 3), (3, 0, 0)])
    beside_rows = exchange(late_rows, 0, 1)[1]
    beside_lists = exchange(late_lists, 0, 1)[1]
    node = level(parts, 1)
    own_pack, node = tie(own_pack, node)
    parts = exchange(node, 2, 1)
    own_set = (own_base, single, [own_pack])
    early_set = (early_base, by_edge, [outer_next, outer_across])
    (own,) = near_call(
        [(0, near_lists, rows, None)], [own_set, early_set], ((0, 0), (1, 0)), dim, "near_own"
    )
    beside_rows, beside_lists, own = tie(beside_rows, beside_lists, own)
    (beside,) = near_call(
        [(1, beside_lists, beside_rows, None)],
        [own_set, early_set], ((0, 0), (1, 0)), dim, "near_early",
    )

    *parts, inner_across, forwarded, beside, own = tie(
        *parts, inner_across, forwarded, beside, own
    )
    late_set = (late_base, by_edge, [inner_across, forwarded])
    bit = 2
    while bit < bits - 2:
        node = level(parts, bit)
        bit += 1
        parts = exchange(node, bit, 1)
    (own,) = near_call([(0, near_lists, rows, own)], [late_set], ((0, 0),), dim, "near_last")
    *parts, own = tie(*parts, own)
    node = level(parts, bit)
    bit += 1
    beside, node = tie(beside, node)
    parts = exchange(node, bit, 1)
    (beside,) = near_call(
        [(1, beside_lists, beside_rows, beside)], [late_set], ((0, 0),), dim, "near_beside"
    )
    *parts, beside = tie(*parts, beside)
    given = exchange(beside, 0, 1)[1]
    node = level(parts, bit, skel // count)
    near = (own + given) * (leaf ** -0.5)
    if skel // count:
        root = node.reshape(-1)
    else:
        size = skel * LANES // count
        rank = lax.axis_index("leaf") * sub_count + lax.axis_index("sub")
        root = lax.dynamic_slice_in_dim(node.reshape(-1), rank * size, size, 0)
    return near.reshape(npts, LANES), root


def solution(mesh):
    in_specs = (
        P(("leaf", "sub"), None),
        P(("leaf", "sub"), None),
        P(("leaf", "sub")),
        P(("leaf", "sub"), None),
        P(("leaf", "sub")),
        P(("leaf", "sub"), None),
        P(),
    )
    out_specs = (P(("leaf", "sub"), None), P(("leaf", "sub")))
    return jax.shard_map(
        on_device, mesh=mesh, in_specs=in_specs, out_specs=out_specs, check_vma=False
    )
```

```python
import functools

import jax
import jax.numpy as jnp
from jax import lax
from jax.experimental import pallas as pl
from jax.experimental.pallas import tpu as pltpu
from jax.sharding import PartitionSpec as P

LANES = 128
PARTS = 3
VMEM_BYTES = 20 * 1024 * 1024
NEAR_BYTES = 24 * 1024 * 1024
F32 = jnp.float32
BF16 = jnp.bfloat16


def dot(a, b):
    return jnp.dot(a, b, preferred_element_type=F32)


def dot_t(a, b):
    return lax.dot_general(a, b, (((0,), (0,)), ((), ())), preferred_element_type=F32)


def split(x):
    hi = x.astype(BF16)
    return hi, (x - hi.astype(F32)).astype(BF16)


def square_rows(pts):
    x = pts.astype(F32)
    total = jnp.sum(x * x, axis=0, keepdims=True)
    hi = total.astype(BF16).astype(F32)
    mid = (total - hi).astype(BF16).astype(F32)
    low = total - hi - mid
    row = lax.broadcasted_iota(jnp.int32, (16, pts.shape[1]), 0)
    ones = jnp.where(row < 2 * PARTS, 1.0, 0.0)
    return jnp.where(row == 0, hi, jnp.where(row == 1, mid, jnp.where(row == 2, low, ones))).astype(BF16)


def form_map(dim, size):
    k = lax.broadcasted_iota(jnp.int32, (size, size), 0)
    j = lax.broadcasted_iota(jnp.int32, (size, size), 1)
    r = jnp.where((k == j) & (j < dim), 2.0 / dim, 0.0)
    r = jnp.where((j >= dim) & (j < dim + PARTS) & (k == j + PARTS), -1.0 / dim, r)
    r = jnp.where((j >= dim + PARTS) & (j < dim + 2 * PARTS) & (k == j - PARTS), -1.0 / dim, r)
    return r.astype(BF16)


def onehot_in(row, size):
    index = lax.broadcasted_iota(jnp.int32, (size, row.shape[1]), 0)
    return jnp.where(index == row, 1.0, 0.0).astype(BF16)


def column_of(row):
    return jnp.broadcast_to(row.astype(F32), (LANES, row.shape[1])).T


def onehot_out(column, size):
    lane = lax.broadcasted_iota(jnp.int32, column.shape, 1).astype(F32)
    return jnp.concatenate(
        [jnp.where(column == lane + float(i), 1.0, 0.0) for i in range(0, size, LANES)], axis=1
    )


def mix3(m, s):
    m_hi, m_lo = split(m)
    s_hi, s_lo = split(s)
    return dot(m_hi, s_hi) + (dot(m_hi, s_lo) + dot(m_lo, s_hi))


def order_kernel(points_t, order, probes, pack, rows):
    dim = points_t.shape[0]
    many, leaf = rows.shape[:2]
    held = dim + 16
    to_rows = form_map(dim, LANES)
    for b in range(many):
        picks = onehot_in(order[b], leaf)
        tree_t = dot(points_t[:, b * leaf : (b + 1) * leaf], picks).astype(BF16)
        pack[b, :leaf, :] = probes[b * leaf : (b + 1) * leaf, :]
        form = jnp.concatenate([tree_t, square_rows(tree_t)], axis=0)
        for i in range(leaf // LANES):
            pack[b, leaf + i * dim : leaf + (i + 1) * dim, :] = tree_t[:, i * LANES : (i + 1) * LANES]
        form = jnp.concatenate([form, jnp.zeros((LANES - held, leaf), BF16)], axis=0)
        rows[b] = dot_t(form, to_rows).astype(BF16)


def order_call(points_t, order, probes, blocks):
    dim, npts = points_t.shape
    leaf = npts // blocks
    packed = leaf + leaf // LANES * dim
    many = 4 if blocks % 4 == 0 else 1
    return pl.pallas_call(
        order_kernel,
        grid=(blocks // many,),
        in_specs=[
            pl.BlockSpec((dim, many * leaf), lambda b: (0, b)),
            pl.BlockSpec((many, 1, leaf), lambda b: (b, 0, 0)),
            pl.BlockSpec((many * leaf, LANES), lambda b: (b, 0)),
        ],
        out_specs=[
            pl.BlockSpec((many, packed, LANES), lambda b: (b, 0, 0)),
            pl.BlockSpec((many, leaf, LANES), lambda b: (b, 0, 0)),
        ],
        out_shape=[
            jax.ShapeDtypeStruct((blocks, packed, LANES), BF16),
            jax.ShapeDtypeStruct((blocks, leaf, LANES), BF16),
        ],
        compiler_params=pltpu.CompilerParams(vmem_limit_bytes=VMEM_BYTES),
        cost_estimate=pl.CostEstimate(
            flops=blocks * 2 * leaf * leaf * dim, bytes_accessed=10 * npts * LANES, transcendentals=0
        ),
        name="tree_order",
    )(points_t, order, probes)


def form_of(pack_block, leaf, dim):
    columns = []
    for i in range(leaf // LANES):
        pts = pack_block[leaf + i * dim : leaf + (i + 1) * dim, :]
        columns.append(jnp.concatenate([pts, square_rows(pts)], axis=0))
    form = jnp.concatenate(columns, axis=1)
    return jnp.concatenate([form, jnp.zeros((LANES - dim - 16, leaf), BF16)], axis=0)


def condense(form, a_rows, chosen):
    size = form.shape[1]
    picks_out = onehot_out(column_of(chosen), size)
    new_rows = dot(picks_out.astype(BF16), a_rows).astype(BF16)
    new_form = dot(form, onehot_in(chosen, size)).astype(BF16)
    weights = jnp.exp(dot(new_rows, form))
    mixing = picks_out + weights / jnp.sum(weights, axis=1, keepdims=True)
    return new_form, new_rows, mixing


def local_tree_kernel(pack, rows, leaf_sets_in, merge_sets_in, out, leaf_sets, merge_sets, sems, *, dim):
    blocks, leaf = rows.shape[:2]
    leaf_copy = pltpu.make_async_copy(leaf_sets_in, leaf_sets, sems.at[0])
    merge_copy = pltpu.make_async_copy(merge_sets_in, merge_sets, sems.at[1])
    leaf_copy.start()
    merge_copy.start()
    leaf_copy.wait()
    first_block = (lax.axis_index("leaf") * lax.axis_size("sub") + lax.axis_index("sub")) * blocks

    nodes = []
    for b in range(blocks):
        form = form_of(pack.at[b], leaf, dim)
        new_form, new_rows, mixing = condense(form, rows[b], leaf_sets[b : b + 1, :])
        m_hi, m_lo = split(mixing)
        probes = pack[b, :leaf, :]
        nodes.append((new_form, new_rows, dot(m_hi, probes) + dot(m_lo, probes)))
    span = 1
    merge_copy.wait()
    while len(nodes) > 1:
        merged = []
        for k in range(len(nodes) // 2):
            left, right = nodes[2 * k], nodes[2 * k + 1]
            chosen = merge_sets[pl.ds(first_block + (2 * k + 1) * span - 1, 1), :]
            new_form, new_rows, mixing = condense(
                jnp.concatenate([left[0], right[0]], axis=1),
                jnp.concatenate([left[1], right[1]], axis=0),
                chosen,
            )
            samples = mix3(mixing, jnp.concatenate([left[2], right[2]], axis=0))
            merged.append((new_form, new_rows, samples))
        nodes = merged
        span *= 2
    held = dim + 16
    out[:held, :] = nodes[0][0][:held, :].astype(F32)
    out[held:, :] = nodes[0][2]


def local_tree_call(pack, rows, leaf_sets, merge_sets, dim):
    blocks, leaf = rows.shape[:2]
    skel = leaf_sets.shape[1]
    return pl.pallas_call(
        functools.partial(local_tree_kernel, dim=dim),
        in_specs=[pl.BlockSpec(memory_space=pltpu.VMEM)] * 2
        + [pl.BlockSpec(memory_space=pltpu.HBM)] * 2,
        out_shape=jax.ShapeDtypeStruct((dim + 16 + skel, LANES), F32),
        scratch_shapes=[
            pltpu.VMEM(leaf_sets.shape, jnp.int32),
            pltpu.VMEM(merge_sets.shape, jnp.int32),
            pltpu.SemaphoreType.DMA((2,)),
        ],
        compiler_params=pltpu.CompilerParams(vmem_limit_bytes=VMEM_BYTES),
        cost_estimate=pl.CostEstimate(
            flops=blocks * 8 * skel * leaf * LANES,
            bytes_accessed=6 * blocks * leaf * LANES,
            transcendentals=blocks * skel * leaf,
        ),
        name="local_tree",
    )(pack, rows, leaf_sets, merge_sets)


def merge_kernel(*refs, dim, blocks, shift, piece):
    merge_sets_in, out, group, merge_sets, sem = refs[-5:]
    parts = refs[:-5]
    count, size = group.shape[:2]
    copy = pltpu.make_async_copy(merge_sets_in, merge_sets, sem)
    copy.start()
    held = dim + 16
    skel = size - held
    rank = lax.axis_index("leaf") * lax.axis_size("sub") + lax.axis_index("sub")
    unit = lax.shift_right_logical(rank, shift)
    place = unit & (count - 1)
    first = unit - place
    span = blocks << shift
    for d, part in enumerate(parts):
        group[place ^ d] = part[...]
    to_rows = form_map(dim, LANES)
    forms = [group[i, :held, :].astype(BF16) for i in range(count)]
    samples = [group[i, held:, :] for i in range(count)]
    copy.wait()
    while len(forms) > 1:
        first = first // 2
        new_forms, new_samples = [], []
        for k in range(len(forms) // 2):
            chosen = merge_sets[pl.ds((2 * (first + k) + 1) * span - 1, 1), :]
            form = jnp.concatenate(forms[2 * k : 2 * k + 2], axis=1)
            form = jnp.concatenate([form, jnp.zeros((LANES - held, 2 * skel), BF16)], axis=0)
            new_form = dot(form, onehot_in(chosen, 2 * skel)).astype(BF16)
            new_rows = dot_t(new_form, to_rows).astype(BF16)
            weights = jnp.exp(dot(new_rows, form))
            picks = onehot_out(column_of(chosen), 2 * skel)
            mixing = picks + weights / jnp.sum(weights, axis=1, keepdims=True)
            new_forms.append(new_form[:held])
            new_samples.append(mix3(mixing, jnp.concatenate(samples[2 * k : 2 * k + 2], axis=0)))
        forms, samples = new_forms, new_samples
        span *= 2
    if piece is None:
        out[:held, :] = forms[0].astype(F32)
        out[held:, :] = samples[0]
    elif piece == 0:
        out[...] = samples[0]
    else:
        column = lax.broadcasted_iota(jnp.int32, (piece, skel), 1)
        row = lax.broadcasted_iota(jnp.int32, (piece, skel), 0) + rank * piece
        take = jnp.where(column == row, 1.0, 0.0).astype(BF16)
        hi, lo = split(samples[0])
        low = (samples[0] - hi.astype(F32) - lo.astype(F32)).astype(BF16)
        out[...] = dot(take, hi) + dot(take, lo) + dot(take, low)


def merge_call(parts, merge_sets, dim, blocks, shift, piece=None):
    count = len(parts)
    size = parts[0].shape[0]
    skel = size - dim - 16
    rows = size if piece is None else (piece or skel)
    return pl.pallas_call(
        functools.partial(merge_kernel, dim=dim, blocks=blocks, shift=shift, piece=piece),
        in_specs=[pl.BlockSpec(memory_space=pltpu.VMEM)] * count
        + [pl.BlockSpec(memory_space=pltpu.HBM)],
        out_shape=jax.ShapeDtypeStruct((rows, LANES), F32),
        scratch_shapes=[
            pltpu.VMEM((count, size, LANES), F32),
            pltpu.VMEM(merge_sets.shape, jnp.int32),
            pltpu.SemaphoreType.DMA(()),
        ],
        compiler_params=pltpu.CompilerParams(vmem_limit_bytes=16 * 1024 * 1024),
        cost_estimate=pl.CostEstimate(
            flops=count * 16 * LANES**3,
            bytes_accessed=4 * count * size * LANES,
            transcendentals=2 * count * LANES**2,
        ),
        name="tree_merge",
    )(*parts, merge_sets)


def near_kernel(*refs, flips, row_counts, has_acc, sets, tasks, span, dim):
    refs = list(refs)

    def take(number):
        taken = refs[:number]
        del refs[:number]
        return taken

    lists, rows = take(len(flips)), [take(number) for number in row_counts]
    accs = [take(1)[0] if has else None for has in has_acc]
    buffers = [take(max(which) + 1) for _, which in sets]
    outs, (pair_list,) = take(len(flips)), refs
    blocks, leaf = rows[0][0].shape[:2]
    near = lists[0].shape[1]
    window = blocks * lax.axis_size("sub")
    sub = lax.axis_index("sub")

    def place(table):
        value = jnp.int32(table[0])
        for i in range(1, len(table)):
            value = jnp.where(sub == i, jnp.int32(table[i]), value)
        return value

    window_first = lax.axis_index("leaf") * window - blocks
    stride = blocks * near + 8
    found = [jnp.int32(0)] * len(tasks)
    for j, flip in enumerate(flips):
        mine = [t for t, (_, group) in enumerate(tasks) if group == j]
        firsts = [window_first + place(sets[tasks[t][0]][0]) for t in mine]
        target_first = lax.axis_index("leaf") * window + (sub ^ flip) * blocks

        def list_block(g, counts, j=j, mine=mine, firsts=firsts, target_first=target_first):
            for s in range(*span):
                source = lists[j][g, s]
                used = (source != target_first + g) if s else True
                after = []
                for t, first, count in zip(mine, firsts, counts):
                    local = source - first
                    pair_list[t * stride + count] = g * blocks + local
                    inside = (local >= 0) & (local < blocks) & used
                    after.append(count + jnp.where(inside, 1, 0))
                counts = tuple(after)
            return counts

        counts = lax.fori_loop(0, blocks, list_block, (jnp.int32(0),) * len(mine))
        for t, count in zip(mine, counts):
            found[t] = count
        outs[j][...] = jnp.zeros(outs[j].shape, F32) if accs[j] is None else accs[j][...]

    half = leaf // 2

    def add_all(buffer, targets, t, pairs):
        j = tasks[t][1]

        def add_pair(i):
            code = pair_list[t * stride + i]
            g = code // blocks
            local = code - g * blocks
            form = form_of(buffer.at[local], leaf, dim)
            probes = buffer[local, :leaf, :]
            total = None
            for c in range(0, leaf, half):
                weights = jnp.exp(dot(targets[g], form[:, c : c + half])).astype(BF16)
                term = dot(weights, probes[c : c + half])
                total = term if total is None else total + term
            return g, total

        def add_four(i, carry):
            for g, total in [add_pair(4 * i + k) for k in range(4)]:
                outs[j][g] += total
            return carry

        def add_one(i, carry):
            g, total = add_pair(i)
            outs[j][g] += total
            return carry

        lax.fori_loop(0, pairs // 4, add_four, 0)
        lax.fori_loop(pairs // 4 * 4, pairs, add_one, 0)

    for t, (number, j) in enumerate(tasks):
        held = place(sets[number][1])
        edge = (sub == 0) | (sub == lax.axis_size("sub") - 1)
        for k, buffer in enumerate(buffers[number]):
            for r, targets in enumerate(rows[j]):
                pairs = found[t]
                if len(buffers[number]) > 1:
                    if len(rows[j]) > 1 and r != k:
                        continue
                    pairs = jnp.where(held == k, pairs, 0)
                elif len(rows[j]) > 1:
                    pairs = jnp.where(edge == (r == 0), pairs, 0)
                add_all(buffer, targets, t, pairs)


def near_call(groups, sources, tasks, dim, name):
    flips, lists, rows, accs = zip(*groups)
    rows = [r if isinstance(r, tuple) else (r,) for r in rows]
    blocks, leaf = rows[0][0].shape[:2]
    held = [acc for acc in accs if acc is not None]
    args = [*lists, *(r for pair in rows for r in pair), *held, *(b for _, _, buffers in sources for b in buffers)]
    smem = pl.BlockSpec(memory_space=pltpu.SMEM)
    vmem = pl.BlockSpec(memory_space=pltpu.VMEM)
    near = lists[0].shape[1]
    return pl.pallas_call(
        functools.partial(
            near_kernel,
            flips=flips,
            row_counts=tuple(len(pair) for pair in rows),
            has_acc=tuple(acc is not None for acc in accs),
            sets=tuple((bases, which) for bases, which, _ in sources),
            tasks=tasks,
            span=(0, near),
            dim=dim,
        ),
        in_specs=[smem] * len(lists) + [vmem] * (len(args) - len(lists)),
        out_specs=[vmem] * len(groups),
        out_shape=[jax.ShapeDtypeStruct((blocks, leaf, LANES), F32)] * len(groups),
        scratch_shapes=[pltpu.SMEM((len(tasks) * (blocks * near + 8),), jnp.int32)],
        compiler_params=pltpu.CompilerParams(vmem_limit_bytes=NEAR_BYTES),
        cost_estimate=pl.CostEstimate(flops=1000, bytes_accessed=1000, transcendentals=0),
        name=name,
    )(*args)


def on_device(points, probes, order, near_lists, near_counts, leaf_sets, merge_sets):
    leaf_count = lax.axis_size("leaf")
    sub_count = lax.axis_size("sub")
    blocks, skel = leaf_sets.shape
    npts, dim = points.shape
    leaf = npts // blocks
    axes = ("leaf", "sub")

    def send(x, routes):
        pairs = []
        for place in range(leaf_count):
            for from_sub, step, to_sub in routes:
                if 0 <= place + step < leaf_count:
                    pairs.append((place * sub_count + from_sub, (place + step) * sub_count + to_sub))
        return lax.ppermute(x, axes, pairs)

    count = leaf_count * sub_count
    bits = count.bit_length() - 1
    sub_bits = sub_count.bit_length() - 1

    def exchange(x, shift, stage_bits):
        parts = [x]
        for d in range(1, 1 << stage_bits):
            parts.append(lax.ppermute(x, axes, [(i, i ^ (d << shift)) for i in range(count)]))
        return parts

    def tie(*values):
        return lax.optimization_barrier(values)

    b = blocks
    own_base = (b, 2 * b, 3 * b, 4 * b)
    early_base, late_base = (5 * b, 4 * b, b, 0), (3 * b, 0, 5 * b, 2 * b)
    single, by_edge = (0, 0, 0, 0), (0, 1, 1, 0)

    pack, rows = order_call(points.T, order.reshape(blocks, 1, leaf), probes, blocks)
    outer_across = send(pack, [(3, 0, 1), (0, 0, 2)])
    outer_next = send(pack, [(3, 1, 3), (0, -1, 0)])
    beside_pack = send(pack, [(1, 0, 0), (2, 0, 3)])

    node = local_tree_call(pack, rows, leaf_sets, merge_sets, dim)

    def level(parts, bit, piece=None):
        return merge_call(parts, merge_sets, dim, blocks, bit, piece)

    node = level(exchange(node, 0, 1), 0)
    own_pack, node = tie(pack, node)
    parts = exchange(node, 1, 1)
    *parts, outer_across, outer_next, beside_pack, late_rows, late_lists = tie(
        *parts, outer_across, outer_next, beside_pack, rows, near_lists
    )
    forwarded = send(outer_across, [(1, 1, 1), (2, -1, 2)])
    inner_across = send(beside_pack, [(0, 0, 3), (3, 0, 0)])
    beside_rows = exchange(late_rows, 0, 1)[1]
    beside_lists = exchange(late_lists, 0, 1)[1]
    node = level(parts, 1)
    own_pack, node = tie(own_pack, node)
    parts = exchange(node, 2, 1)
    own_set = (own_base, single, [own_pack])
    early_set = (early_base, by_edge, [outer_next, outer_across])
    (own,) = near_call(
        [(0, near_lists, rows, None)], [own_set, early_set], ((0, 0), (1, 0)), dim, "near_own"
    )
    beside_rows, beside_lists, own = tie(beside_rows, beside_lists, own)
    (beside,) = near_call(
        [(1, beside_lists, beside_rows, None)],
        [own_set, early_set], ((0, 0), (1, 0)), dim, "near_early",
    )

    *parts, inner_across, forwarded, beside, own = tie(
        *parts, inner_across, forwarded, beside, own
    )
    late_set = (late_base, by_edge, [inner_across, forwarded])
    bit = 2
    while bit < bits - 2:
        node = level(parts, bit)
        bit += 1
        parts = exchange(node, bit, 1)
    (own,) = near_call([(0, near_lists, rows, own)], [late_set], ((0, 0),), dim, "near_last")
    *parts, own = tie(*parts, own)
    node = level(parts, bit)
    bit += 1
    beside, node = tie(beside, node)
    parts = exchange(node, bit, 1)
    (beside,) = near_call(
        [(1, beside_lists, beside_rows, beside)], [late_set], ((0, 0),), dim, "near_beside"
    )
    *parts, beside = tie(*parts, beside)
    given = exchange(beside, 0, 1)[1]
    node = level(parts, bit, skel // count)
    near = (own + given) * (leaf ** -0.5)
    if skel // count:
        root = node.reshape(-1)
    else:
        size = skel * LANES // count
        rank = lax.axis_index("leaf") * sub_count + lax.axis_index("sub")
        root = lax.dynamic_slice_in_dim(node.reshape(-1), rank * size, size, 0)
    return near.reshape(npts, LANES), root


def solution(mesh):
    in_specs = (
        P(("leaf", "sub"), None),
        P(("leaf", "sub"), None),
        P(("leaf", "sub")),
        P(("leaf", "sub"), None),
        P(("leaf", "sub")),
        P(("leaf", "sub"), None),
        P(),
    )
    out_specs = (P(("leaf", "sub"), None), P(("leaf", "sub")))
    return jax.shard_map(
        on_device, mesh=mesh, in_specs=in_specs, out_specs=out_specs, check_vma=False
    )
```
